32 devices in a mesh: fsdp: 32 (over z, y, x, core).
Axes of the slice: x: 2, y: 2, z: 4, core: 2. Of those that a mesh axis runs over, the one named last changes fastest.
Arguments:
- latents: bfloat16 [128, 256, 16], P('fsdp'), may hold values from -6 to 6
- targets: float32 [128, 256, 32], P('fsdp'), may hold values from -12 to 12
- timesteps: int32 [128], P('fsdp'), may hold values from 0 to 999
- labels: int32 [128], P('fsdp'), may hold values from 0 to 1000, as said below
- embed_w: float32 [2041, 768], P(None, 'fsdp'), may hold values from -1 to 1
- embed_m: float32 [2041, 768], P(None, 'fsdp'), may hold values from -3.33786e-06 to 3.33786e-06
- embed_v: float32 [2041, 768], P(None, 'fsdp'), may hold values from 2.0805344e-15 to 3.328855e-14
- cond_w: float32 [768, 10752], P(None, 'fsdp'), may hold values from -0.21875 to 0.21875
- cond_m: float32 [768, 10752], P(None, 'fsdp'), may hold values from -3.33786e-06 to 3.33786e-06
- cond_v: float32 [768, 10752], P(None, 'fsdp'), may hold values from 2.0805344e-15 to 3.328855e-14
- layer_input_weights: float32 [2, 768, 5376], P(None, None, 'fsdp'), may hold values from -0.21875 to 0.21875
- in_m: float32 [2, 768, 5376], P(None, None, 'fsdp'), may hold values from -3.33786e-06 to 3.33786e-06
- in_v: float32 [2, 768, 5376], P(None, None, 'fsdp'), may hold values from 2.0805344e-15 to 3.328855e-14
- layer_output_weights: float32 [2, 3840, 768], P(None, None, 'fsdp'), may hold values from -2 to 2
- out_m: float32 [2, 3840, 768], P(None, None, 'fsdp'), may hold values from -3.33786e-06 to 3.33786e-06
- out_v: float32 [2, 3840, 768], P(None, None, 'fsdp'), may hold values from 2.0805344e-15 to 3.328855e-14
- head_w: float32 [768, 32], replicated, may hold values from -0.21875 to 0.21875
- head_m: float32 [768, 32], replicated, may hold values from -3.33786e-06 to 3.33786e-06
- head_v: float32 [768, 32], replicated, may hold values from 2.0805344e-15 to 3.328855e-14
- biases: float32 [26912], replicated, may hold values from -0.6 to 0.6
- bias_m: float32 [26912], replicated, may hold values from -9.536743e-06 to 9.536743e-06
- bias_v: float32 [26912], replicated, may hold values from 2.0805343e-14 to 3.328855e-13
Outputs:
- loss_total: float32 [], replicated
- grad_norm: float32 [], replicated
- embed_new: float32 [2041, 768], P(None, 'fsdp')
- embed_m_new: float32 [2041, 768], P(None, 'fsdp')
- embed_v_new: float32 [2041, 768], P(None, 'fsdp')
- cond_new: float32 [768, 10752], P(None, 'fsdp')
- cond_m_new: float32 [768, 10752], P(None, 'fsdp')
- cond_v_new: float32 [768, 10752], P(None, 'fsdp')
- in_new: float32 [2, 768, 5376], P(None, None, 'fsdp')
- in_m_new: float32 [2, 768, 5376], P(None, None, 'fsdp')
- in_v_new: float32 [2, 768, 5376], P(None, None, 'fsdp')
- out_new: float32 [2, 3840, 768], P(None, None, 'fsdp')
- out_m_new: float32 [2, 3840, 768], P(None, None, 'fsdp')
- out_v_new: float32 [2, 3840, 768], P(None, None, 'fsdp')
- head_new: float32 [768, 32], replicated
- head_m_new: float32 [768, 32], replicated
- head_v_new: float32 [768, 32], replicated
- bias_new: float32 [26912], replicated
- bias_m_new: float32 [26912], replicated
- bias_v_new: float32 [26912], replicated
The draws below stay inside these ranges and needn't reach their ends.
Inputs may be any that keep to these rules, and one draw needn't show every extreme that they name: `labels`: label 1001 - 1 is the null class and some images carry it.
All inputs are finite; a program needn't handle non-finite values.
Results may differ from the reference program's by a relative error of at most 0.008.
Values may be sent and summed in bfloat16 or wider, within the bound.
A program may use at most 320 MiB of HBM per device.

```python
import math
import jax
import jax.numpy as jnp
from jax import lax

MODEL_WIDTH = 768
HEADS = 12
HEAD_DIM = 64
FF = 3072
NCLS = 1001
FREQ = 256
PD = 16
PO = 32
GRID = 16
LAYERS = 2
STEP = 10
SEQ = 256
IMAGES = 128
IW = 5376
OW = 3840
CW = 10752
ER = 2041
NB = 26912
PARAMS = 24032288


def draw_targets(key, part):
    key = jax.random.fold_in(key, 11)
    ramp = jnp.arange(IMAGES, dtype=jnp.float32) / max(IMAGES - 1, 1)
    base = jnp.clip(jax.random.normal(key, (IMAGES, SEQ, PO), jnp.float32), -4.0, 4.0)
    rise = 1.0 + 2.0 * ramp
    return base * rise[:, None, None]


def draw_labels(key, part):
    key = jax.random.fold_in(key, 12)
    first_key, second_key = jax.random.split(key)
    classes = jax.random.randint(first_key, (IMAGES,), 0, NCLS - 1)
    dropped = jax.random.randint(second_key, (IMAGES,), 0, 10) == 0
    labels = jnp.where(dropped, NCLS - 1, classes)
    return labels.at[0].set(NCLS - 1).astype(jnp.int32)


def draw_embed_w(key, part):
    key = jax.random.fold_in(key, 13)
    rows_idx = jnp.arange(ER)
    scale = jnp.where(rows_idx < FREQ, FREQ ** (-0.5), jnp.where(rows_idx < FREQ + MODEL_WIDTH, MODEL_WIDTH ** (-0.5), jnp.where(rows_idx < FREQ + MODEL_WIDTH + PD, PD ** (-0.5), 0.15)))
    values = jnp.clip(jax.random.normal(key, (ER, MODEL_WIDTH), jnp.float32), -4.0, 4.0)
    return values * scale[:, None].astype(jnp.float32)


def draw_layer_output_weights(key, part):
    key = jax.random.fold_in(key, 14)
    rows_idx = jnp.arange(OW)
    scale = jnp.where(rows_idx < MODEL_WIDTH, 4.0 * MODEL_WIDTH ** (-0.5), FF ** (-0.5))
    values = jnp.clip(jax.random.normal(key, (LAYERS, OW, MODEL_WIDTH), jnp.float32), -4.0, 4.0)
    return values * scale[None, :, None].astype(jnp.float32)


def set_ends(result, stream_key, low, top_value):
    longest = result.shape.index(max(result.shape))
    spots = []
    for shift in (0, 1):
        where = [jax.random.randint(jax.random.fold_in(stream_key, axis), (), 0, length) for axis, length in enumerate(result.shape)]
        where[longest] = (where[longest] + shift) % result.shape[longest]
        spots.append(tuple(where))
    return result.at[spots[0]].set(low).at[spots[1]].set(top_value)


def block_levels(own_key, extent, cuts, low, largest):
    def one(position, parts):
        steps = jax.random.uniform(jax.random.fold_in(jax.random.fold_in(own_key, 6), position), (parts,), jnp.float32, low / len(cuts), largest / len(cuts))
        return jnp.repeat(jnp.exp(steps), extent[position] // parts).reshape((-1,) + (1,) * (len(extent) - position - 1))

    gain = one(*cuts[0])
    for cut in cuts[1:]:
        gain = gain * one(*cut)
    return gain


def centred(key, dims, spread, limit, cuts=(), kind=jnp.bfloat16):
    values = spread * jax.random.normal(key, dims, jnp.float32)
    if cuts:
        values = values * block_levels(key, dims, cuts, -0.22, 0.18)
    return jnp.clip(values, -limit, limit).astype(kind)


def setup_inputs(seed: int = 0) -> dict:
    streams_of = jax.random.split(jax.random.key(seed), 23)
    latents = centred(streams_of[0], (IMAGES, SEQ, PD), 1.0, 6.0, ((0, 32),))
    targets = draw_targets(jax.random.fold_in(streams_of[22], 71), 0)
    timesteps = set_ends(jax.random.randint(streams_of[2], (IMAGES,), 0, 1000), jax.random.fold_in(streams_of[2], 1), 0, 999).astype(jnp.int32)
    labels = draw_labels(jax.random.fold_in(streams_of[22], 71), 0)
    embed_w = draw_embed_w(jax.random.fold_in(streams_of[22], 71), 0)
    embed_m = centred(streams_of[5], (ER, MODEL_WIDTH), (0.0011 / PARAMS ** 0.5), 3.337860107421875e-06, ((1, 32),), jnp.float32)
    embed_v = jnp.clip(jnp.exp(math.log(3.32885506811563e-14) - 2.7725887 * jax.random.uniform(streams_of[6], (ER, MODEL_WIDTH), jnp.float32) ** block_levels(streams_of[6], (ER, MODEL_WIDTH), ((1, 32),), -0.2, 0.2)), 2.0805344175722686e-15, 3.32885506811563e-14)
    cond_w = centred(streams_of[7], (MODEL_WIDTH, CW), MODEL_WIDTH ** -0.5, 0.21875, ((1, 32),), jnp.float32)
    cond_m = centred(streams_of[8], (MODEL_WIDTH, CW), (0.0011 / PARAMS ** 0.5), 3.337860107421875e-06, ((1, 32),), jnp.float32)
    cond_v = jnp.clip(jnp.exp(math.log(3.32885506811563e-14) - 2.7725887 * jax.random.uniform(streams_of[9], (MODEL_WIDTH, CW), jnp.float32) ** block_levels(streams_of[9], (MODEL_WIDTH, CW), ((1, 32),), -0.2, 0.2)), 2.0805344175722686e-15, 3.32885506811563e-14)
    layer_input_weights = centred(streams_of[10], (LAYERS, MODEL_WIDTH, IW), MODEL_WIDTH ** -0.5, 0.21875, ((2, 32),), jnp.float32)
    in_m = centred(streams_of[11], (LAYERS, MODEL_WIDTH, IW), (0.0011 / PARAMS ** 0.5), 3.337860107421875e-06, ((2, 32),), jnp.float32)
    in_v = jnp.clip(jnp.exp(math.log(3.32885506811563e-14) - 2.7725887 * jax.random.uniform(streams_of[12], (LAYERS, MODEL_WIDTH, IW), jnp.float32) ** block_levels(streams_of[12], (LAYERS, MODEL_WIDTH, IW), ((2, 32),), -0.2, 0.2)), 2.0805344175722686e-15, 3.32885506811563e-14)
    layer_output_weights = draw_layer_output_weights(jax.random.fold_in(streams_of[22], 71), 0)
    out_m = centred(streams_of[14], (LAYERS, OW, MODEL_WIDTH), (0.0011 / PARAMS ** 0.5), 3.337860107421875e-06, ((2, 32),), jnp.float32)
    out_v = jnp.clip(jnp.exp(math.log(3.32885506811563e-14) - 2.7725887 * jax.random.uniform(streams_of[15], (LAYERS, OW, MODEL_WIDTH), jnp.float32) ** block_levels(streams_of[15], (LAYERS, OW, MODEL_WIDTH), ((2, 32),), -0.2, 0.2)), 2.0805344175722686e-15, 3.32885506811563e-14)
    head_w = centred(streams_of[16], (MODEL_WIDTH, PO), MODEL_WIDTH ** -0.5, 0.21875, (), jnp.float32)
    head_m = centred(streams_of[17], (MODEL_WIDTH, PO), (0.0011 / PARAMS ** 0.5), 3.337860107421875e-06, (), jnp.float32)
    head_v = jnp.clip(jnp.exp(jax.random.uniform(streams_of[18], (MODEL_WIDTH, PO), jnp.float32, math.log(2.0805344175722686e-15), math.log(3.32885506811563e-14))), 2.0805344175722686e-15, 3.32885506811563e-14)
    biases = centred(streams_of[19], (NB,), 0.1, 0.6, (), jnp.float32)
    bias_m = centred(streams_of[20], (NB,), (0.0033 / PARAMS ** 0.5), 9.5367431640625e-06, (), jnp.float32)
    bias_v = jnp.clip(jnp.exp(jax.random.uniform(streams_of[21], (NB,), jnp.float32, math.log(2.080534332868974e-14), math.log(3.328854932590358e-13))), 2.080534332868974e-14, 3.328854932590358e-13)
    return {"latents": latents, "targets": targets, "timesteps": timesteps, "labels": labels, "embed_w": embed_w, "embed_m": embed_m, "embed_v": embed_v, "cond_w": cond_w, "cond_m": cond_m, "cond_v": cond_v, "layer_input_weights": layer_input_weights, "in_m": in_m, "in_v": in_v, "layer_output_weights": layer_output_weights, "out_m": out_m, "out_v": out_v, "head_w": head_w, "head_m": head_m, "head_v": head_v, "biases": biases, "bias_m": bias_m, "bias_v": bias_v}


learn_rate = 0.03
beta_one = 0.9
beta_two = 0.999
adam_eps = 1e-08
decay = 0.01
clip_limit = 0.01
highest = lax.Precision.HIGHEST

@jax.custom_vjp
def low(v):
    return lax.optimization_barrier(v.astype(jnp.bfloat16)).astype(jnp.float32)

@jax.custom_vjp
def low_back(v):
    return v

def low_keep(v):
    return (low(v), None)

def low_pass(kept, grad):
    return (grad,)

def back_keep(v):
    return (v, None)

def back_low(kept, grad):
    return (low(grad),)
low.defvjp(low_keep, low_pass)
low_back.defvjp(back_keep, back_low)

def matmul(left, right):
    return jnp.dot(left, right, precision=highest)

def project(left, right):
    return jnp.einsum('bsd,de->bse', left, right, precision=highest)

def silu(value):
    return value * jax.nn.sigmoid(value)

def layer_norm(value):
    centered = value - lax.optimization_barrier(jnp.mean(value, -1, keepdims=True))
    return centered * lax.rsqrt(lax.optimization_barrier(jnp.mean(centered * centered, -1, keepdims=True)) + 1e-06)

def position_table():
    quarter = MODEL_WIDTH // 4
    omega = 1.0 / 10000.0 ** (jnp.arange(quarter, dtype=jnp.float32) / quarter)
    places = jnp.arange(GRID * GRID)
    rows_pos = (places // GRID).astype(jnp.float32)[:, None] * omega
    cols_pos = (places % GRID).astype(jnp.float32)[:, None] * omega
    return jnp.concatenate([jnp.sin(rows_pos), jnp.cos(rows_pos), jnp.sin(cols_pos), jnp.cos(cols_pos)], 1)

def time_features(timesteps):
    half_freq = FREQ // 2
    rates = jnp.exp(-math.log(10000.0) * jnp.arange(half_freq, dtype=jnp.float32) / half_freq)
    angles = timesteps.astype(jnp.float32)[:, None] * rates
    return jnp.concatenate([jnp.cos(angles), jnp.sin(angles)], 1)

def split_biases(vector):
    lengths = [MODEL_WIDTH, MODEL_WIDTH, MODEL_WIDTH, CW, LAYERS * IW, LAYERS * 2 * MODEL_WIDTH, PO]
    pieces = []
    offset = 0
    for length in lengths:
        pieces.append(vector[offset:offset + length])
        offset += length
    pieces[4] = pieces[4].reshape(LAYERS, IW)
    pieces[5] = pieces[5].reshape(LAYERS, 2 * MODEL_WIDTH)
    return pieces

def transformer_block(residual_state, adaptive_modulation, input_weight_slice, output_weight_slice, input_bias_rows, output_bias_rows):
    pieces = [adaptive_modulation[:, None, i * MODEL_WIDTH:(i + 1) * MODEL_WIDTH] for i in range(6)]
    n_images, seq_len = (residual_state.shape[0], residual_state.shape[1])
    shaped = low(layer_norm(residual_state) * (1 + pieces[1]) + pieces[0])
    triple = low(low_back(project(shaped, input_weight_slice[:, :3 * MODEL_WIDTH]) + input_bias_rows[:3 * MODEL_WIDTH]))
    queries, key_part, values = [triple[..., j * MODEL_WIDTH:(j + 1) * MODEL_WIDTH].reshape(n_images, seq_len, HEADS, HEAD_DIM) for j in range(3)]
    scores = low_back(jnp.einsum('bqhd,bkhd->bhqk', queries, key_part, precision=highest) * HEAD_DIM ** (-0.5))
    attn_weights = low(jax.nn.softmax(scores, axis=-1))
    mixed_heads = low(low_back(jnp.einsum('bhqk,bkhd->bqhd', attn_weights, values, precision=highest)))
    branch = low_back(project(mixed_heads.reshape(n_images, seq_len, MODEL_WIDTH), output_weight_slice[:MODEL_WIDTH]) + output_bias_rows[:MODEL_WIDTH])
    residual_state = residual_state + pieces[2] * branch
    shaped = low(layer_norm(residual_state) * (1 + pieces[4]) + pieces[3])
    active = low(jax.nn.gelu(low_back(project(shaped, input_weight_slice[:, 3 * MODEL_WIDTH:]) + input_bias_rows[3 * MODEL_WIDTH:]), approximate=True))
    return residual_state + pieces[5] * low_back(project(active, output_weight_slice[MODEL_WIDTH:]) + output_bias_rows[MODEL_WIDTH:])

def group_loss(weights, latents, targets, timesteps, labels):
    embed_w, cond_w, layer_input_weights, layer_output_weights, head_w, biases = weights
    time_one, time_two, patch_bias, cond_bias, block_input_bias, block_output_bias, head_bias = split_biases(biases)
    features = low(time_features(timesteps))
    hidden_t = low(silu(matmul(features, embed_w[:FREQ]) + time_one))
    time_emb = matmul(hidden_t, embed_w[FREQ:FREQ + MODEL_WIDTH]) + time_two
    onehot = (labels[:, None] == jnp.arange(NCLS)[None, :]).astype(jnp.float32)
    condition = time_emb + matmul(onehot, embed_w[FREQ + MODEL_WIDTH + PD:])
    adaptive_modulation = matmul(low(silu(condition)), cond_w) + cond_bias
    residual_state = low_back(project(latents, embed_w[FREQ + MODEL_WIDTH:FREQ + MODEL_WIDTH + PD]) + patch_bias) + position_table()
    for layer_count in range(LAYERS):
        residual_state = transformer_block(residual_state, adaptive_modulation[:, 6 * MODEL_WIDTH * layer_count:6 * MODEL_WIDTH * (layer_count + 1)], layer_input_weights[layer_count], layer_output_weights[layer_count], block_input_bias[layer_count], block_output_bias[layer_count])
    final_mod = adaptive_modulation[:, 6 * MODEL_WIDTH * LAYERS:]
    shaped = low(layer_norm(residual_state) * (1 + final_mod[:, None, MODEL_WIDTH:]) + final_mod[:, None, :MODEL_WIDTH])
    output = low_back(jnp.einsum('bsd,do->bso', shaped, head_w, precision=highest) + head_bias)
    error_vals = output - targets
    return jnp.sum(error_vals * error_vals)

def adam_step(weight, first, second, gradient):
    first = beta_one * first + (1 - beta_one) * gradient
    second = beta_two * second + (1 - beta_two) * gradient * gradient
    ahead = first / (1 - beta_one ** STEP)
    scaled = second / (1 - beta_two ** STEP)
    return (weight - learn_rate * (ahead / (jnp.sqrt(scaled) + adam_eps) + decay * weight), first, second)

def reference(latents, targets, timesteps, labels, embed_w, embed_m, embed_v, cond_w, cond_m, cond_v, layer_input_weights, in_m, in_v, layer_output_weights, out_m, out_v, head_w, head_m, head_v, biases, bias_m, bias_v):
    per_group = math.gcd(IMAGES, 16)
    n_groups = IMAGES // per_group
    batches = (latents.astype(jnp.float32).reshape(n_groups, per_group, SEQ, PD), targets.reshape(n_groups, per_group, SEQ, PO), timesteps.reshape(n_groups, per_group), labels.reshape(n_groups, per_group))
    masters = (embed_w, cond_w, layer_input_weights, layer_output_weights, head_w, biases)

    def objective(params):
        rounded = tuple((low(weight) for weight in params[:5])) + (params[5],)

        def add_group(running, batch_in):
            return (running + jax.checkpoint(group_loss)(rounded, *batch_in), None)
        summed, _ = lax.scan(add_group, jnp.zeros((), jnp.float32), batches)
        return summed
    loss_total, pullback = jax.vjp(objective, masters)
    gradients = pullback(jnp.asarray(1.0 / (IMAGES * SEQ * PO), jnp.float32))[0]
    squares = jnp.zeros((), jnp.float32)
    for gradient in gradients:
        squares = squares + jnp.sum(gradient * gradient)
    grad_norm = jnp.sqrt(squares)
    factor = jnp.minimum(1.0, clip_limit / grad_norm)
    embed_up = adam_step(embed_w, embed_m, embed_v, gradients[0] * factor)
    cond_up = adam_step(cond_w, cond_m, cond_v, gradients[1] * factor)
    in_up = adam_step(layer_input_weights, in_m, in_v, gradients[2] * factor)
    out_up = adam_step(layer_output_weights, out_m, out_v, gradients[3] * factor)
    head_up = adam_step(head_w, head_m, head_v, gradients[4] * factor)
    bias_up = adam_step(biases, bias_m, bias_v, gradients[5] * factor)
    return (loss_total, grad_norm, embed_up[0], embed_up[1], embed_up[2], cond_up[0], cond_up[1], cond_up[2], in_up[0], in_up[1], in_up[2], out_up[0], out_up[1], out_up[2], head_up[0], head_up[1], head_up[2], bias_up[0], bias_up[1], bias_up[2])
```

```python
import functools
import math

import jax
import jax.numpy as jnp
import numpy as np
from jax import lax
from jax.experimental import pallas as pl
from jax.experimental.pallas import tpu as pltpu
from jax.sharding import PartitionSpec as P

MODEL_WIDTH = 768
HEADS = 12
HEAD_DIM = 64
NCLS = 1001
FREQ = 256
PD = 16
PO = 32
GRID = 16
LAYERS = 2
STEP = 10
SEQ = 256
IW = 5376
CW = 10752


learn_rate = 0.03
beta_one = 0.9
beta_two = 0.999
adam_eps = 1e-08
decay = 0.01
clip_limit = 0.01
highest = lax.Precision.HIGHEST


def product(left, right):
    return jnp.dot(left, right, preferred_element_type=jnp.float32)


def exact_dot(left, right):
    return jnp.dot(left, right, precision=highest)


def apply_rows(left, right):
    return jnp.einsum("bsd,de->bse", left, right, preferred_element_type=jnp.float32)


def outer_sum(left, right):
    return jnp.einsum("bsd,bse->de", left, right, preferred_element_type=jnp.float32)


def apply_back(left, right):
    return jnp.einsum("bse,de->bsd", left, right, preferred_element_type=jnp.float32)


def column_sum(value):
    return jnp.sum(value.astype(jnp.float32), (0, 1))


def silu(value):
    return value * jax.nn.sigmoid(value)


def gelu(value):
    return jax.nn.gelu(value, approximate=True)


def layer_norm(value):
    centered = value - jnp.mean(value, -1, keepdims=True)
    return centered * lax.rsqrt(jnp.mean(centered * centered, -1, keepdims=True) + 1e-06)


def local_back(func, value, cotangent):
    return jax.vjp(func, value)[1](cotangent)[0]


def position_table():
    quarter = MODEL_WIDTH // 4
    omega = 1.0 / 10000.0 ** (jnp.arange(quarter, dtype=jnp.float32) / quarter)
    places = jnp.arange(GRID * GRID)
    rows_pos = (places // GRID).astype(jnp.float32)[:, None] * omega
    cols_pos = (places % GRID).astype(jnp.float32)[:, None] * omega
    return jnp.concatenate(
        [jnp.sin(rows_pos), jnp.cos(rows_pos), jnp.sin(cols_pos), jnp.cos(cols_pos)], 1
    )


def time_features(timesteps):
    half_freq = FREQ // 2
    rates = jnp.exp(-math.log(10000.0) * jnp.arange(half_freq, dtype=jnp.float32) / half_freq)
    angles = timesteps.astype(jnp.float32)[:, None] * rates
    return jnp.concatenate([jnp.cos(angles), jnp.sin(angles)], 1)


def split_biases(vector):
    lengths = [MODEL_WIDTH, MODEL_WIDTH, MODEL_WIDTH, CW, LAYERS * IW, LAYERS * 2 * MODEL_WIDTH, PO]
    pieces = []
    offset = 0
    for length in lengths:
        pieces.append(vector[offset : offset + length])
        offset += length
    pieces[4] = pieces[4].reshape(LAYERS, IW)
    pieces[5] = pieces[5].reshape(LAYERS, 2 * MODEL_WIDTH)
    return pieces


def split_heads(triple, which):
    n_images, seq_len = (triple.shape[0], triple.shape[1])
    return triple[..., which * MODEL_WIDTH : (which + 1) * MODEL_WIDTH].reshape(
        n_images, seq_len, HEADS, HEAD_DIM
    )


def attend(triple):
    queries, key_part, values = [split_heads(triple, j) for j in range(3)]
    scores = jnp.einsum(
        "bqhd,bkhd->bhqk", queries, key_part, preferred_element_type=jnp.float32
    ) * HEAD_DIM ** (-0.5)
    row_max = jnp.max(scores, -1, keepdims=True)
    expo = jnp.exp(scores - row_max)
    row_sum = jnp.sum(expo, -1, keepdims=True)
    attn_weights = (expo / row_sum).astype(jnp.bfloat16)
    mixed_heads = jnp.einsum(
        "bhqk,bkhd->bqhd", attn_weights, values, preferred_element_type=jnp.float32
    ).astype(jnp.bfloat16)
    return (
        mixed_heads.reshape(triple.shape[0], triple.shape[1], MODEL_WIDTH),
        row_max + jnp.log(row_sum),
    )


def attend_back(triple, log_norm, d_mixed):
    queries, key_part, values = [split_heads(triple, j) for j in range(3)]
    scale = HEAD_DIM ** (-0.5)
    scores = (
        jnp.einsum("bqhd,bkhd->bhqk", queries, key_part, preferred_element_type=jnp.float32) * scale
    )
    probs_full = jnp.exp(scores - log_norm)
    attn_weights = probs_full.astype(jnp.bfloat16)
    d_heads = d_mixed.reshape(queries.shape)
    d_probs = jnp.einsum("bqhd,bkhd->bhqk", d_heads, values, preferred_element_type=jnp.float32)
    d_values = jnp.einsum(
        "bhqk,bqhd->bkhd", attn_weights, d_heads, preferred_element_type=jnp.float32
    )
    d_scores = (probs_full * (d_probs - jnp.sum(probs_full * d_probs, -1, keepdims=True))).astype(
        jnp.bfloat16
    )
    d_queries = (
        jnp.einsum("bhqk,bkhd->bqhd", d_scores, key_part, preferred_element_type=jnp.float32)
        * scale
    )
    d_keys = (
        jnp.einsum("bhqk,bqhd->bkhd", d_scores, queries, preferred_element_type=jnp.float32) * scale
    )
    shape_flat = (triple.shape[0], triple.shape[1], MODEL_WIDTH)
    return jnp.concatenate(
        [d_queries.reshape(shape_flat), d_keys.reshape(shape_flat), d_values.reshape(shape_flat)],
        -1,
    ).astype(jnp.bfloat16)


def block_forward(residual_state, adaptive_modulation, weights_in, weights_out, bias_in, bias_out):
    pieces = [
        adaptive_modulation[:, None, i * MODEL_WIDTH : (i + 1) * MODEL_WIDTH] for i in range(6)
    ]
    shaped_one = (layer_norm(residual_state) * (1 + pieces[1]) + pieces[0]).astype(jnp.bfloat16)
    triple = (
        apply_rows(shaped_one, weights_in[:, : 3 * MODEL_WIDTH]) + bias_in[: 3 * MODEL_WIDTH]
    ).astype(jnp.bfloat16)
    mixed_heads, log_norm = attend(triple)
    branch = apply_rows(mixed_heads, weights_out[:MODEL_WIDTH]) + bias_out[:MODEL_WIDTH]
    middle = residual_state + pieces[2] * branch
    shaped_two = (layer_norm(middle) * (1 + pieces[4]) + pieces[3]).astype(jnp.bfloat16)
    pre_ffn = apply_rows(shaped_two, weights_in[:, 3 * MODEL_WIDTH :]) + bias_in[3 * MODEL_WIDTH :]
    active = gelu(pre_ffn).astype(jnp.bfloat16)
    ffn_out = apply_rows(active, weights_out[MODEL_WIDTH:]) + bias_out[MODEL_WIDTH:]
    kept = (
        residual_state,
        shaped_one,
        triple,
        log_norm,
        mixed_heads,
        branch,
        middle,
        shaped_two,
        pre_ffn,
        active,
        ffn_out,
    )
    return (middle + pieces[5] * ffn_out, kept)


def block_backward(upstream, adaptive_modulation, weights_in, weights_out, kept):
    (
        residual_state,
        shaped_one,
        triple,
        log_norm,
        mixed_heads,
        branch,
        middle,
        shaped_two,
        pre_ffn,
        active,
        ffn_out,
    ) = kept
    pieces = [
        adaptive_modulation[:, None, i * MODEL_WIDTH : (i + 1) * MODEL_WIDTH] for i in range(6)
    ]
    d_ffn = (pieces[5] * upstream).astype(jnp.bfloat16)
    gate_two = jnp.sum(ffn_out * upstream, 1)
    grad_down = outer_sum(active, d_ffn)
    d_active = apply_back(d_ffn, weights_out[MODEL_WIDTH:])
    d_pre = local_back(gelu, pre_ffn, d_active).astype(jnp.bfloat16)
    grad_up = outer_sum(shaped_two, d_pre)
    d_shaped = apply_back(d_pre, weights_in[:, 3 * MODEL_WIDTH :])
    shift_two = jnp.sum(d_shaped, 1)
    scale_two = jnp.sum(d_shaped * layer_norm(middle), 1)
    upstream = upstream + local_back(layer_norm, middle, d_shaped * (1 + pieces[4]))
    gate_one = jnp.sum(branch * upstream, 1)
    d_branch = (pieces[2] * upstream).astype(jnp.bfloat16)
    grad_proj = outer_sum(mixed_heads, d_branch)
    d_mixed = apply_back(d_branch, weights_out[:MODEL_WIDTH]).astype(jnp.bfloat16)
    d_triple = attend_back(triple, log_norm, d_mixed)
    grad_qkv = outer_sum(shaped_one, d_triple)
    d_shaped = apply_back(d_triple, weights_in[:, : 3 * MODEL_WIDTH])
    shift_one = jnp.sum(d_shaped, 1)
    scale_one = jnp.sum(d_shaped * layer_norm(residual_state), 1)
    upstream = upstream + local_back(layer_norm, residual_state, d_shaped * (1 + pieces[1]))
    mod_grad = jnp.concatenate([shift_one, scale_one, gate_one, shift_two, scale_two, gate_two], 1)
    bias_in_grad = jnp.concatenate([column_sum(d_triple), column_sum(d_pre)])
    bias_out_grad = jnp.concatenate([column_sum(d_branch), column_sum(d_ffn)])
    grad_in = jnp.concatenate([grad_qkv, grad_up], 1)
    grad_out = jnp.concatenate([grad_proj, grad_down], 0)
    return (upstream, mod_grad, grad_in, grad_out, bias_in_grad, bias_out_grad)


def fetch_layer(layer_input_weights, layer_output_weights, layer_count):
    return (
        lax.all_gather(
            layer_input_weights[layer_count].astype(jnp.bfloat16), "fsdp", axis=1, tiled=True
        ),
        lax.all_gather(
            layer_output_weights[layer_count].astype(jnp.bfloat16), "fsdp", axis=1, tiled=True
        ),
    )


def adam_step(weight, first, second, gradient):
    first = beta_one * first + (1 - beta_one) * gradient
    second = beta_two * second + (1 - beta_two) * gradient * gradient
    ahead = first / (1 - beta_one**STEP)
    scaled = second / (1 - beta_two**STEP)
    return (
        weight - learn_rate * (ahead / (jnp.sqrt(scaled) + adam_eps) + decay * weight),
        first,
        second,
    )


def generic_body(
    latents,
    targets,
    timesteps,
    labels,
    embed_w,
    embed_m,
    embed_v,
    cond_w,
    cond_m,
    cond_v,
    layer_input_weights,
    in_m,
    in_v,
    layer_output_weights,
    out_m,
    out_v,
    head_w,
    head_m,
    head_v,
    biases,
    bias_m,
    bias_v,
):
    devices = lax.axis_size("fsdp")
    embed_full, cond_full = (
        lax.all_gather(embed_w.astype(jnp.bfloat16), "fsdp", axis=1, tiled=True),
        lax.all_gather(cond_w.astype(jnp.bfloat16), "fsdp", axis=1, tiled=True),
    )
    time_one, time_two, patch_bias, cond_bias, block_input_bias, block_output_bias, head_bias = (
        split_biases(biases)
    )
    head_low = head_w.astype(jnp.bfloat16)
    features = time_features(timesteps).astype(jnp.bfloat16)
    pre_time = product(features, embed_full[:FREQ]) + time_one
    hidden_t = silu(pre_time).astype(jnp.bfloat16)
    time_emb = product(hidden_t, embed_full[FREQ : FREQ + MODEL_WIDTH]) + time_two
    onehot = (labels[:, None] == jnp.arange(NCLS)[None, :]).astype(jnp.bfloat16)
    condition = time_emb + product(onehot, embed_full[FREQ + MODEL_WIDTH + PD :])
    cond_low = silu(condition).astype(jnp.bfloat16)
    adaptive_modulation = product(cond_low, cond_full) + cond_bias
    residual_state = (
        apply_rows(latents, embed_full[FREQ + MODEL_WIDTH : FREQ + MODEL_WIDTH + PD])
        + patch_bias
        + position_table()
    )
    kept_all = []
    for layer_count in range(LAYERS):
        weights_in, weights_out = fetch_layer(
            layer_input_weights, layer_output_weights, layer_count
        )
        residual_state, kept = block_forward(
            residual_state,
            adaptive_modulation[
                :, 6 * MODEL_WIDTH * layer_count : 6 * MODEL_WIDTH * (layer_count + 1)
            ],
            weights_in,
            weights_out,
            block_input_bias[layer_count],
            block_output_bias[layer_count],
        )
        kept_all.append(kept)
    final_mod = adaptive_modulation[:, 6 * MODEL_WIDTH * LAYERS :]
    norm_final = layer_norm(residual_state)
    shaped = (
        norm_final * (1 + final_mod[:, None, MODEL_WIDTH:]) + final_mod[:, None, :MODEL_WIDTH]
    ).astype(jnp.bfloat16)
    output = apply_rows(shaped, head_low) + head_bias
    error_vals = output - targets
    loss_part = jnp.sum(error_vals * error_vals)
    tokens_all = devices * error_vals.shape[0] * SEQ * PO
    d_output = (error_vals * (2.0 / tokens_all)).astype(jnp.bfloat16)
    head_grad = outer_sum(shaped, d_output)
    head_bias_grad = column_sum(d_output)
    d_shaped = apply_back(d_output, head_low)
    d_final = jnp.concatenate([jnp.sum(d_shaped, 1), jnp.sum(d_shaped * norm_final, 1)], 1)
    upstream = local_back(
        layer_norm, residual_state, d_shaped * (1 + final_mod[:, None, MODEL_WIDTH:])
    )
    mod_grads = [None] * LAYERS
    in_shards = [None] * LAYERS
    out_shards = [None] * LAYERS
    in_bias_grads = [None] * LAYERS
    out_bias_grads = [None] * LAYERS
    for layer_count in reversed(range(LAYERS)):
        weights_in, weights_out = (
            lax.all_gather(
                layer_input_weights[layer_count].astype(jnp.bfloat16), "fsdp", axis=1, tiled=True
            ),
            lax.all_gather(
                layer_output_weights[layer_count].astype(jnp.bfloat16), "fsdp", axis=1, tiled=True
            ),
        )
        upstream, mod_grad, grad_in, grad_out, bias_in_grad, bias_out_grad = block_backward(
            upstream,
            adaptive_modulation[
                :, 6 * MODEL_WIDTH * layer_count : 6 * MODEL_WIDTH * (layer_count + 1)
            ],
            weights_in,
            weights_out,
            kept_all[layer_count],
        )
        in_shards[layer_count], out_shards[layer_count] = (
            lax.psum_scatter(grad_in, "fsdp", scatter_dimension=1, tiled=True),
            lax.psum_scatter(grad_out, "fsdp", scatter_dimension=1, tiled=True),
        )
        mod_grads[layer_count] = mod_grad
        in_bias_grads[layer_count] = bias_in_grad
        out_bias_grads[layer_count] = bias_out_grad
    d_patch = upstream.astype(jnp.bfloat16)
    patch_grad = outer_sum(latents, d_patch)
    patch_bias_grad = column_sum(d_patch)
    d_modulation = jnp.concatenate(mod_grads + [d_final], 1)
    d_cond = exact_dot(d_modulation, cond_full.astype(jnp.float32).T)
    d_condition = local_back(silu, condition, d_cond)
    d_hidden = exact_dot(d_condition, embed_full[FREQ : FREQ + MODEL_WIDTH].astype(jnp.float32).T)
    d_pre = local_back(silu, pre_time, d_hidden)
    cond_grad = exact_dot(cond_low.astype(jnp.float32).T, d_modulation)
    class_grad = exact_dot(onehot.astype(jnp.float32).T, d_condition)
    time_two_grad = exact_dot(hidden_t.astype(jnp.float32).T, d_condition)
    time_one_grad = exact_dot(features.astype(jnp.float32).T, d_pre)
    embed_grad = jnp.concatenate([time_one_grad, time_two_grad, patch_grad, class_grad], 0)
    embed_shard, cond_shard = (
        lax.psum_scatter(embed_grad, "fsdp", scatter_dimension=1, tiled=True),
        lax.psum_scatter(cond_grad, "fsdp", scatter_dimension=1, tiled=True),
    )
    bias_grad = jnp.concatenate(
        [jnp.sum(d_pre, 0), jnp.sum(d_condition, 0), patch_bias_grad, jnp.sum(d_modulation, 0)]
        + in_bias_grads
        + out_bias_grads
        + [head_bias_grad]
    )
    head_total, bias_total, loss_total = lax.psum((head_grad, bias_grad, loss_part), "fsdp")
    in_stack = jnp.stack(in_shards, 0)
    out_stack = jnp.stack(out_shards, 0)
    shard_squares = (
        jnp.sum(embed_shard * embed_shard)
        + jnp.sum(cond_shard * cond_shard)
        + jnp.sum(in_stack * in_stack)
        + jnp.sum(out_stack * out_stack)
    )
    square_total = lax.psum(shard_squares, "fsdp")
    grad_norm = jnp.sqrt(
        square_total + jnp.sum(head_total * head_total) + jnp.sum(bias_total * bias_total)
    )
    factor = jnp.minimum(1.0, clip_limit / grad_norm)
    embed_up = adam_step(embed_w, embed_m, embed_v, embed_shard * factor)
    cond_up = adam_step(cond_w, cond_m, cond_v, cond_shard * factor)
    in_up = adam_step(layer_input_weights, in_m, in_v, in_stack * factor)
    out_up = adam_step(layer_output_weights, out_m, out_v, out_stack * factor)
    head_up = adam_step(head_w, head_m, head_v, head_total * factor)
    bias_up = adam_step(biases, bias_m, bias_v, bias_total * factor)
    return (
        loss_total,
        grad_norm,
        embed_up[0],
        embed_up[1],
        embed_up[2],
        cond_up[0],
        cond_up[1],
        cond_up[2],
        in_up[0],
        in_up[1],
        in_up[2],
        out_up[0],
        out_up[1],
        out_up[2],
        head_up[0],
        head_up[1],
        head_up[2],
        bias_up[0],
        bias_up[1],
        bias_up[2],
    )


MESH_ID = pl.DeviceIdType.MESH
AXIS = "fsdp"


class Place:
    def __init__(self):
        me = lax.axis_index(AXIS)
        self.me = me
        self.core = core = me % 2
        x = (me // 2) % 2
        y = (me // 4) % 2
        self.z = me // 8
        self.chip = me // 2
        step_x = 1 - 2 * x
        step_y = 2 - 4 * y
        self.step_a = step_x + core * (step_y - step_x)
        self.step_b = step_y + core * (step_x - step_y)
        self.dev_a = me + 2 * self.step_a
        self.dev_b = me + 2 * self.step_b
        self.sibling = me + 1 - 2 * core

    def other(self, dz, flip_a=0, flip_b=0):
        return self.chip + 4 * dz + flip_a * self.step_a + flip_b * self.step_b

    def valid(self, dz):
        return jnp.logical_and(self.z + dz >= 0, self.z + dz < 4)

    def greet(self):
        barrier = pltpu.get_barrier_semaphore()
        for device in (self.sibling, self.dev_a, self.dev_b):
            pl.semaphore_signal(barrier, inc=1, device_id=(device,), device_id_type=MESH_ID)
        for sign in (-1, 1):

            @pl.when(self.valid(sign))
            def _():
                pl.semaphore_signal(barrier, inc=1, device_id=(self.me + 8 * sign,), device_id_type=MESH_ID)

        pl.semaphore_wait(barrier, 4 + self.z * (3 - self.z) // 2)


def remote(src, dst, send_sem, recv_sem, device):
    return pltpu.make_async_remote_copy(
        src_ref=src, dst_ref=dst, send_sem=send_sem, recv_sem=recv_sem, device_id=(device,), device_id_type=MESH_ID
    )


class Gather:
    def __init__(self, place, own, stage, piece, full, sems):
        self.p, self.own, self.stage, self.piece, self.full = place, own, stage, piece, full
        self.xch_send, self.xch_recv, self.local, self.send, self.recv, self.sib_recv = sems
        self.sent, self.keep = [], []

    def slot(self, a, chip):
        rows, half = self.piece[a].shape
        return self.full[a].at[
            pl.ds(pl.multiple_of(chip * rows, rows), rows), pl.ds(pl.multiple_of(self.p.core * half, half), half)
        ]

    def push(self, a, k, src, chip, device, sem, cond=None):
        copy = remote(src, self.slot(a, chip), self.send.at[a, k], sem, device)
        self.sent.append((copy, cond))
        if cond is None:
            copy.start()
        else:
            pl.when(cond)(copy.start)

    def begin(self):
        core = self.p.core
        copies = []
        for a in range(2):
            rows, half = self.own[a].shape[0], self.piece[a].shape[1]
            dst = self.stage[a].at[pl.ds(pl.multiple_of(core * rows, 8), rows), :]
            away = remote(
                self.own[a].at[:, pl.ds(pl.multiple_of((1 - core) * half, half), half)],
                dst,
                self.xch_send.at[a],
                self.xch_recv.at[a],
                self.p.sibling,
            )
            away.start()
            keep = pltpu.make_async_copy(
                self.own[a].at[:, pl.ds(pl.multiple_of(core * half, half), half)], dst, self.local.at[a]
            )
            keep.start()
            copies.append((away, keep))
        for a in range(2):
            copies[a][0].wait()
            copies[a][1].wait()
            self.piece[a][...] = self.stage[a][...].astype(jnp.bfloat16)
            keep = pltpu.make_async_copy(self.piece[a], self.slot(a, self.p.chip), self.local.at[a])
            keep.start()
            self.keep.append(keep)
            for sign in (-1, 1):
                self.push(
                    a, 0 if sign < 0 else 3, self.piece[a], self.p.chip, self.p.me + 8 * sign,
                    self.recv.at[a, self.p.chip], self.p.valid(sign),
                )
            self.push(a, 6, self.piece[a], self.p.chip, self.p.dev_a, self.recv.at[a, self.p.chip])
            self.push(a, 10, self.piece[a], self.p.chip, self.p.dev_b, self.recv.at[a, self.p.chip])
            self.push(a, 18, self.piece[a], self.p.chip, self.p.sibling, self.sib_recv.at[a, self.p.chip])

    def arrive(self, a, chip):
        slot = self.slot(a, chip)
        pltpu.make_async_copy(slot, slot, self.recv.at[a, chip]).wait()

    def z_step(self, dist):
        for sign in (-1, 1):
            here = self.p.valid(sign * dist)
            chip = self.p.other(sign * dist)
            rel = (sign * dist) % 4
            onward = jnp.logical_and(here, self.p.valid(-sign))
            for a in range(2):
                pl.when(here)(functools.partial(self.arrive, a, chip))
                src = self.slot(a, chip)
                if dist < 3:
                    self.push(
                        a, (0 if sign > 0 else 3) + dist, src, chip, self.p.me - 8 * sign,
                        self.recv.at[a, chip], onward,
                    )
                self.push(a, 6 + rel, src, chip, self.p.dev_a, self.recv.at[a, chip], here)
                self.push(a, 10 + rel, src, chip, self.p.dev_b, self.recv.at[a, chip], here)
                self.push(a, 18 + rel, src, chip, self.p.sibling, self.sib_recv.at[a, chip], here)

    def a_step(self, dist):
        for sign in (-1, 1) if dist else (1,):
            here = self.p.valid(sign * dist)
            chip = self.p.other(sign * dist, 1)
            rel = (sign * dist) % 4
            for a in range(2):
                pl.when(here)(functools.partial(self.arrive, a, chip))
                src = self.slot(a, chip)
                self.push(a, 14 + rel, src, chip, self.p.dev_b, self.recv.at[a, chip], here)
                self.push(a, 22 + rel, src, chip, self.p.sibling, self.sib_recv.at[a, chip], here)

    def b_step(self, dist, flip_a):
        for sign in (-1, 1) if dist else (1,):
            here = self.p.valid(sign * dist)
            chip = self.p.other(sign * dist, flip_a, 1)
            rel = (sign * dist) % 4
            for a in range(2):
                pl.when(here)(functools.partial(self.arrive, a, chip))
                src = self.slot(a, chip)
                self.push(a, 26 + 4 * flip_a + rel, src, chip, self.p.sibling, self.sib_recv.at[a, chip], here)

    def finish(self):
        for a in range(2):
            rows, half = self.piece[a].shape

            def take(chip, carry):
                slot = self.full[a].at[
                    pl.ds(pl.multiple_of(chip * rows, rows), rows),
                    pl.ds(pl.multiple_of((1 - self.p.core) * half, half), half),
                ]
                pltpu.make_async_copy(slot, slot, self.sib_recv.at[a, chip]).wait()
                return carry

            lax.fori_loop(0, 16, take, 0)
        for copy in self.keep:
            copy.wait()
        for copy, cond in self.sent:
            if cond is None:
                copy.wait_send()
            else:
                pl.when(cond)(copy.wait_send)


GATHER_SEMS = [
    pltpu.SemaphoreType.DMA((2,)),
    pltpu.SemaphoreType.DMA((2,)),
    pltpu.SemaphoreType.DMA((2,)),
    pltpu.SemaphoreType.DMA((2, 34)),
    pltpu.SemaphoreType.DMA((2, 16)),
    pltpu.SemaphoreType.DMA((2, 16)),
]


def gather_scratch(shapes):
    return (
        [pltpu.VMEM(shape, jnp.float32) for shape in shapes]
        + [pltpu.VMEM(shape, jnp.bfloat16) for shape in shapes]
        + GATHER_SEMS
    )


def piece_shapes(shapes):
    return [(2 * rows, width // 2) for rows, width in shapes]


def gather_kernel(layers, *refs):
    own, refs = refs[: 2 * layers], refs[2 * layers :]
    full, refs = refs[: 2 * layers], refs[2 * layers :]
    place = Place()
    place.greet()
    jobs = []
    for layer in range(layers):
        part = refs[10 * layer : 10 * layer + 10]
        jobs.append(
            Gather(place, own[2 * layer : 2 * layer + 2], part[:2], part[2:4], full[2 * layer : 2 * layer + 2], part[4:])
        )
    for job in jobs:
        job.begin()
        job.a_step(0)
        for dist in (1, 2, 3):
            job.z_step(dist)
            job.a_step(dist)
    for job in jobs:
        for dist in range(4):
            job.b_step(dist, 0)
            job.b_step(dist, 1)
    for job in jobs:
        job.finish()


def gather_weights(pairs, collective):
    flat = [array for pair in pairs for array in pair]
    devices = lax.axis_size(AXIS)
    scratch = []
    for pair in pairs:
        scratch += gather_scratch(piece_shapes([array.shape for array in pair]))
    return pl.pallas_call(
        functools.partial(gather_kernel, len(pairs)),
        out_shape=[jax.ShapeDtypeStruct((devices * a.shape[0], a.shape[1]), jnp.bfloat16) for a in flat],
        in_specs=[pl.BlockSpec(memory_space=pltpu.VMEM)] * len(flat),
        out_specs=[pl.BlockSpec(memory_space=pl.ANY)] * len(flat),
        scratch_shapes=scratch,
        compiler_params=pltpu.CompilerParams(
            collective_id=collective, has_side_effects=True, vmem_limit_bytes=24 << 20
        ),
        name="gather_weights",
    )(*flat)


ORDER = (3, 0, 2, 1)


class Scatter:
    def __init__(self, place, grad, total, bufs, sems):
        self.p, self.grad, self.total = place, grad, total
        self.mine, self.sib, self.from_b, self.from_a, self.up, self.down, self.part, self.last = (
            bufs[2 * i : 2 * i + 2] for i in range(8)
        )
        (self.load_sem, self.sib_send, self.sib_recv, self.b_send, self.b_recv, self.a_send, self.a_recv, self.up_send,
         self.up_recv, self.down_send, self.down_recv, self.end_send, self.end_recv, self.end_local) = sems

    def rows_of(self, a, chip, core):
        _, rows, half = self.mine[a].shape
        return self.grad[a].at[
            pl.ds(pl.multiple_of(chip * rows, rows), rows), pl.ds(pl.multiple_of(core * half, half), half)
        ]

    def chip_of(self, z, flip_a, flip_b):
        return self.p.other(z - self.p.z, flip_a, flip_b)

    def load(self, a, flip_b, flip_a, z):
        k = 8 * flip_b + 4 * flip_a + z
        return pltpu.make_async_copy(
            self.rows_of(a, self.chip_of(z, flip_a, flip_b), self.p.core), self.mine[a].at[k], self.load_sem.at[a, k]
        )

    def lend(self, a, flip_b, flip_a, z):
        k = 8 * flip_b + 4 * flip_a + z
        return remote(
            self.rows_of(a, self.chip_of(z, flip_b, flip_a), 1 - self.p.core),
            self.sib[a].at[k],
            self.sib_send.at[a, k],
            self.sib_recv.at[a, k],
            self.p.sibling,
        )

    def to_b(self, a, flip_a, z):
        k = 4 * flip_a + z
        return remote(
            self.mine[a].at[8 + k], self.from_b[a].at[k], self.b_send.at[a, k], self.b_recv.at[a, k], self.p.dev_b
        )

    def to_a(self, a, z):
        return remote(
            self.mine[a].at[4 + z], self.from_a[a].at[z], self.a_send.at[a, z], self.a_recv.at[a, z], self.p.dev_a
        )

    def to_z(self, a, z, sign):
        dst, send, recv = (
            (self.up, self.up_send, self.up_recv) if sign > 0 else (self.down, self.down_send, self.down_recv)
        )
        return remote(self.mine[a].at[z], dst[a].at[z], send.at[a, z], recv.at[a, z], self.p.me + 8 * sign)

    def each(self, step):
        def run(z, carry):
            for a in range(2):
                step(a, z)
            return carry

        lax.fori_loop(0, 4, run, 0)

    def begin(self):
        for z in ORDER:
            for flip_b, flip_a in ((1, 1), (1, 0), (0, 1), (0, 0)):
                for a in range(2):
                    self.lend(a, flip_b, flip_a, z).start()
                    self.load(a, flip_b, flip_a, z).start()

    def pair(self, a, flip_b, flip_a, z):
        k = 8 * flip_b + 4 * flip_a + z
        self.load(a, flip_b, flip_a, z).wait()
        self.lend(a, flip_b, flip_a, z).wait_recv()
        return self.mine[a][k].astype(jnp.float32) + self.sib[a][k].astype(jnp.float32)

    def cross_b(self, z):
        for flip_a in (1, 0):
            for a in range(2):
                self.mine[a][8 + 4 * flip_a + z] = self.pair(a, 1, flip_a, z).astype(jnp.bfloat16)
                self.to_b(a, flip_a, z).start()

    def cross_a(self, z):
        for a in range(2):
            value = self.pair(a, 0, 1, z)
            self.to_b(a, 1, z).wait_recv()
            self.mine[a][4 + z] = (value + self.from_b[a][4 + z].astype(jnp.float32)).astype(jnp.bfloat16)
            self.to_a(a, z).start()

    def along_z(self, z):
        place = self.p
        for a in range(2):
            value = self.pair(a, 0, 0, z)
            self.to_b(a, 0, z).wait_recv()
            value = value + self.from_b[a][z].astype(jnp.float32)
            self.to_a(a, z).wait_recv()
            self.part[a][...] = value + self.from_a[a][z].astype(jnp.float32)

            @pl.when(jnp.logical_and(place.z < z, place.z > 0))
            def _():
                self.to_z(a, z, 1).wait_recv()
                self.part[a][...] += self.up[a][z].astype(jnp.float32)

            @pl.when(jnp.logical_and(place.z > z, place.z < 3))
            def _():
                self.to_z(a, z, -1).wait_recv()
                self.part[a][...] += self.down[a][z].astype(jnp.float32)

            @pl.when(place.z != z)
            def _():
                self.mine[a][z] = self.part[a][...].astype(jnp.bfloat16)

            @pl.when(place.z < z)
            def _():
                self.to_z(a, z, 1).start()

            @pl.when(place.z > z)
            def _():
                self.to_z(a, z, -1).start()

            @pl.when(place.z == z)
            def _():
                self.last[a][...] = self.part[a][...]

    def end_copies(self, a):
        core = self.p.core
        rows, width = self.total[a].shape
        dst = self.total[a].at[:, pl.ds(pl.multiple_of(core * (width // 2), width // 2), width // 2)]
        away = remote(
            self.last[a].at[pl.ds(pl.multiple_of((1 - core) * rows, 8), rows), :],
            dst,
            self.end_send.at[a],
            self.end_recv.at[a],
            self.p.sibling,
        )
        keep = pltpu.make_async_copy(
            self.last[a].at[pl.ds(pl.multiple_of(core * rows, 8), rows), :], dst, self.end_local.at[a]
        )
        return away, keep

    def close(self):
        place = self.p
        for a in range(2):

            @pl.when(place.z > 0)
            def _():
                self.to_z(a, place.z, 1).wait_recv()
                self.last[a][...] += self.up[a][place.z].astype(jnp.float32)

            @pl.when(place.z < 3)
            def _():
                self.to_z(a, place.z, -1).wait_recv()
                self.last[a][...] += self.down[a][place.z].astype(jnp.float32)

            for copy in self.end_copies(a):
                copy.start()

    def finish(self):
        for a in range(2):
            for copy in self.end_copies(a):
                copy.wait()

        def step(a, z):
            for flip_b in range(2):
                for flip_a in range(2):
                    self.lend(a, flip_b, flip_a, z).wait_send()
            for flip_a in range(2):
                self.to_b(a, flip_a, z).wait_send()
            self.to_a(a, z).wait_send()

            @pl.when(self.p.z < z)
            def _():
                self.to_z(a, z, 1).wait_send()

            @pl.when(self.p.z > z)
            def _():
                self.to_z(a, z, -1).wait_send()

        self.each(step)

    def steps(self):
        yield self.begin
        for k in range(6):
            if k < 4:
                yield functools.partial(self.cross_b, ORDER[k])
            if 0 <= k - 1 < 4:
                yield functools.partial(self.cross_a, ORDER[k - 1])
            if 0 <= k - 2 < 4:
                yield functools.partial(self.along_z, ORDER[k - 2])
        yield self.close
        yield self.finish


def scatter_scratch(shapes):
    scratch = []
    for count, kind in ((16, jnp.bfloat16), (16, jnp.bfloat16), (8, jnp.bfloat16), (4, jnp.bfloat16), (4, jnp.bfloat16),
                        (4, jnp.bfloat16), (0, jnp.float32), (0, jnp.float32)):
        scratch += [pltpu.VMEM(((count,) if count else ()) + shape, kind) for shape in shapes]
    counts = (16, 16, 16, 8, 8, 4, 4, 4, 4, 4, 4)
    return scratch + [pltpu.SemaphoreType.DMA((2, n)) for n in counts] + [pltpu.SemaphoreType.DMA((2,))] * 3


def scatter_kernel(*refs):
    grad, total, bufs, sems = refs[:2], refs[2:4], refs[4:20], refs[20:]
    place = Place()
    place.greet()
    for step in Scatter(place, grad, total, bufs, sems).steps():
        step()


def scatter_grads(grads, collective):
    devices = lax.axis_size(AXIS)
    shapes = [(a.shape[0] // devices, a.shape[1]) for a in grads]
    return pl.pallas_call(
        scatter_kernel,
        out_shape=[jax.ShapeDtypeStruct(shape, jnp.float32) for shape in shapes],
        in_specs=[pl.BlockSpec(memory_space=pl.ANY)] * 2,
        out_specs=[pl.BlockSpec(memory_space=pltpu.VMEM)] * 2,
        scratch_shapes=scatter_scratch(piece_shapes(shapes)),
        compiler_params=pltpu.CompilerParams(
            collective_id=collective, has_side_effects=True, vmem_limit_bytes=40 << 20
        ),
        name="scatter_grads",
    )(*grads)


def dot_nt(left, right):
    return lax.dot_general(left, right, (((1,), (1,)), ((), ())), preferred_element_type=jnp.float32)


def dot_tn(left, right):
    return lax.dot_general(left, right, (((0,), (0,)), ((), ())), preferred_element_type=jnp.float32)


def thirds(value):
    high = value.astype(jnp.bfloat16)
    rest = value - high.astype(jnp.float32)
    mid = rest.astype(jnp.bfloat16)
    return high, mid, (rest - mid.astype(jnp.float32)).astype(jnp.bfloat16)


def silu_slope(value):
    gate = jax.nn.sigmoid(value)
    return gate * (1 + value * (1 - gate))


class Swap:
    def __init__(self, me, devices, index, src_of, dst, send, recv):
        self.me, self.n, self.i, self.src_of, self.dst, self.send, self.recv = me, devices, index, src_of, dst, send, recv

    def copy(self, peer, slot):
        return remote(self.src_of(peer), self.dst.at[slot], self.send.at[self.i, peer], self.recv.at[self.i, slot], peer)

    def each(self, step):
        def run(k, carry):
            step(lax.rem(self.me + k, self.n))
            return carry

        lax.fori_loop(1, self.n, run, 0)

    def start(self):
        self.each(lambda peer: self.copy(peer, self.me).start())

    def arrive(self):
        self.each(lambda peer: self.copy(peer, peer).wait_recv())

    def sent(self):
        self.each(lambda peer: self.copy(peer, self.me).wait_send())


def greet_all(devices):
    barrier = pltpu.get_barrier_semaphore()
    me = lax.axis_index(AXIS)

    def hello(k, carry):
        pl.semaphore_signal(barrier, inc=1, device_id=(lax.rem(me + k, devices),), device_id_type=MESH_ID)
        return carry

    lax.fori_loop(1, devices, hello, 0)
    pl.semaphore_wait(barrier, devices - 1)


def modulate_steps(devices, ins, outs, bufs, sems):
    msg, wt1, wt2, wcls, wcond, bt1, bt2, bcond = ins
    mods, pre, cond, hid_all, low_all, feat_all, lab_all, got = outs
    hid, low, away = bufs
    me = lax.axis_index(AXIS)
    images, cols = 4, wt1.shape[0]
    swaps = [
        Swap(me, devices, 0, lambda peer: msg, got, *sems),
        Swap(me, devices, 1, lambda peer: hid.at[me], hid, *sems),
        Swap(me, devices, 2, lambda peer: low.at[me], low, *sems),
        Swap(me, devices, 3, lambda peer: away.at[peer], mods, *sems),
    ]

    def first():
        swaps[0].start()
        got[me] = msg[...]

    def second():
        swaps[0].arrive()
        for j in range(devices):
            feat_all[images * j : images * (j + 1), :] = got[j, :, :FREQ]
            lab_all[images * j : images * (j + 1), :] = got[j, :, FREQ : FREQ + 128]
        pre[...] = dot_nt(wt1[...].astype(jnp.bfloat16), feat_all[...].astype(jnp.bfloat16)) + bt1[...]
        hidden = silu(pre[...])
        pad = jnp.zeros((hid.shape[1] - cols, hidden.shape[1]), jnp.float32)
        hid[me] = jnp.concatenate([hidden, pad], 0).astype(jnp.bfloat16)
        swaps[1].start()
        classes = lax.broadcasted_iota(jnp.int32, (lab_all.shape[0], wcls.shape[1]), 1).astype(jnp.float32)
        labels = jnp.concatenate([lab_all[...]] * (wcls.shape[1] // 128), 1)
        onehot = (labels == classes).astype(jnp.bfloat16)
        cond[...] = dot_nt(wcls[...].astype(jnp.bfloat16), onehot) + bt2[...]

    def third():
        swaps[1].arrive()
        for j in range(devices):
            hid_all[cols * j : cols * (j + 1), :] = hid[j].astype(jnp.float32)[:cols]
        cond[...] += jnp.dot(
            wt2[...].astype(jnp.bfloat16), hid_all[...].astype(jnp.bfloat16), preferred_element_type=jnp.float32
        )
        value = silu(cond[...])
        pad = jnp.zeros((low.shape[1] - cols, value.shape[1]), jnp.float32)
        low[me] = jnp.concatenate([value, pad], 0).astype(jnp.bfloat16)
        swaps[2].start()

    def fourth():
        swaps[2].arrive()
        for j in range(devices):
            low_all[cols * j : cols * (j + 1), :] = low[j].astype(jnp.float32)[:cols]
        rows = dot_nt(low_all[...].T.astype(jnp.bfloat16), wcond[...].astype(jnp.bfloat16)) + bcond[...]
        for j in range(devices):
            away[j] = rows[images * j : images * (j + 1)]
        swaps[3].start()
        mods[me] = away[me]

    def last():
        swaps[3].arrive()
        for swap in swaps:
            swap.sent()

    return [first, second, third, fourth, last]


def modulate_kernel(devices, *refs):
    greet_all(devices)
    for step in modulate_steps(devices, refs[:8], refs[8:16], refs[16:19], refs[19:]):
        step()


def modulate(ins):
    devices = lax.axis_size(AXIS)
    msg, wt1, wt2, wcls, wcond = ins[:5]
    cols, images = wt1.shape[0], devices * msg.shape[0]
    outs = [
        (devices, msg.shape[0], wcond.shape[0]), (cols, images), (cols, images), (devices * cols, images),
        (devices * cols, images), (images, FREQ), (images, 128), (devices,) + msg.shape,
    ]
    padded = -(-cols // 16) * 16
    return pl.pallas_call(
        functools.partial(modulate_kernel, devices),
        out_shape=[jax.ShapeDtypeStruct(shape, jnp.float32) for shape in outs],
        in_specs=[pl.BlockSpec(memory_space=pltpu.VMEM)] * 8,
        out_specs=[pl.BlockSpec(memory_space=pltpu.VMEM)] * 8,
        scratch_shapes=[
            pltpu.VMEM((devices, padded, images), jnp.bfloat16),
            pltpu.VMEM((devices, padded, images), jnp.bfloat16),
            pltpu.VMEM((devices, msg.shape[0], wcond.shape[0]), jnp.float32),
            pltpu.SemaphoreType.DMA((4, devices)),
            pltpu.SemaphoreType.DMA((4, devices)),
        ],
        compiler_params=pltpu.CompilerParams(collective_id=3, has_side_effects=True, vmem_limit_bytes=24 << 20),
        name="modulate",
    )(*ins)


def settle_steps(devices, ins, outs, bufs, sems):
    d_mods, small, wt2, wcond, pre, cond, hid_all, low_all, feat_all, lab_all, squares = ins
    g_cond, g_t1, g_t2, g_cls, merged = outs
    dm_got, dm_all, small_got, dc_part, dc_got, dh_part, dh_got, note = bufs
    me = lax.axis_index(AXIS)
    images, cols = d_mods.shape[1], wt2.shape[0]
    width = d_mods.shape[2]

    def rows_for(ref):
        return lambda peer: ref.at[pl.ds(pl.multiple_of(peer * cols, 8), cols), :]

    swaps = [
        Swap(me, devices, 0, lambda peer: d_mods.at[peer], dm_got, *sems),
        Swap(me, devices, 1, lambda peer: small.at[peer], small_got, *sems),
        Swap(me, devices, 2, rows_for(dc_part), dc_got, *sems),
        Swap(me, devices, 3, rows_for(dh_part), dh_got, *sems),
        Swap(me, devices, 4, lambda peer: note, merged, *sems),
    ]
    keep = {}

    def first():
        swaps[0].start()
        swaps[1].start()
        dm_got[me] = d_mods[me]
        small_got[me] = small[me]
        dm_all[...] = jnp.zeros_like(dm_all)

    def second():
        swaps[0].arrive()
        for j in range(devices):
            dm_all[images * j : images * (j + 1), :width] = dm_got[j]
        turned = dm_all[...].T[:width]
        parts = thirds(turned)
        weight = wcond[...].astype(jnp.bfloat16)
        dc_part[...] = sum(dot_tn(weight, part) for part in parts)
        swaps[2].start()
        mine = pl.ds(pl.multiple_of(me * cols, 8), cols)
        dc_got[me] = dc_part[mine, :]
        low = low_all[...].astype(jnp.bfloat16)
        g_cond[...] = sum(dot_nt(part, low) for part in parts)
        swaps[1].arrive()

    def third():
        swaps[2].arrive()
        d_cond = jnp.sum(dc_got[...], 0) * silu_slope(cond[...])
        parts = thirds(d_cond)
        weight = wt2[...].astype(jnp.bfloat16)
        dh_part[...] = sum(dot_tn(weight, part) for part in parts)
        swaps[3].start()
        mine = pl.ds(pl.multiple_of(me * cols, 8), cols)
        dh_got[me] = dh_part[mine, :]
        classes = lax.broadcasted_iota(jnp.int32, (lab_all.shape[0], g_cls.shape[1]), 1).astype(jnp.float32)
        labels = jnp.concatenate([lab_all[...]] * (g_cls.shape[1] // 128), 1)
        onehot = (labels == classes).astype(jnp.bfloat16)
        g_cls[...] = sum(jnp.dot(part, onehot, preferred_element_type=jnp.float32) for part in parts)
        hidden = hid_all[...].astype(jnp.bfloat16)
        g_t2[...] = sum(dot_nt(part, hidden) for part in parts)
        ones = jnp.ones((8, lab_all.shape[0]), jnp.bfloat16)
        keep["t2"] = sum(dot_nt(ones, part) for part in parts)

    def fourth():
        swaps[3].arrive()
        d_pre = jnp.sum(dh_got[...], 0) * silu_slope(pre[...])
        parts = thirds(d_pre)
        feats = feat_all[...].astype(jnp.bfloat16)
        g_t1[...] = sum(jnp.dot(part, feats, preferred_element_type=jnp.float32) for part in parts)
        ones = jnp.ones((8, lab_all.shape[0]), jnp.bfloat16)
        bias_t1 = sum(dot_nt(ones, part) for part in parts)
        total = squares[...]
        for ref in (g_cond, g_t1, g_t2, g_cls):
            total = total + jnp.sum(ref[...] * ref[...])
        bias_cond = jnp.sum(dm_all[...], 0, keepdims=True)
        note[...] = jnp.zeros_like(note)
        note[0:16, :] = jnp.sum(small_got[...], 0)
        note[16:17, :] = total
        note[17:18, :cols] = bias_t1[0:1]
        note[18:19, :cols] = keep["t2"][0:1]
        for k in range(3):
            note[19 + k : 20 + k, :] = bias_cond[:, 128 * k : 128 * (k + 1)]
        swaps[4].start()
        merged[me] = note[...]

    def last():
        swaps[4].arrive()
        for swap in swaps:
            swap.sent()

    return [first, second, third, fourth, last]


def settle_kernel(devices, *refs):
    greet_all(devices)
    for step in settle_steps(devices, refs[:11], refs[11:16], refs[16:24], refs[24:]):
        step()


def settle(ins):
    devices = lax.axis_size(AXIS)
    d_mods, small, wt2, wcond, pre = ins[:5]
    cols, images = pre.shape
    outs = [(wcond.shape[0], devices * cols), (cols, FREQ), (cols, devices * cols), (cols, 1024), (devices, 24, 128)]
    return pl.pallas_call(
        functools.partial(settle_kernel, devices),
        out_shape=[jax.ShapeDtypeStruct(shape, jnp.float32) for shape in outs],
        in_specs=[pl.BlockSpec(memory_space=pltpu.VMEM)] * 11,
        out_specs=[pl.BlockSpec(memory_space=pltpu.VMEM)] * 5,
        scratch_shapes=[
            pltpu.VMEM(d_mods.shape, jnp.float32),
            pltpu.VMEM((images, 384), jnp.float32),
            pltpu.VMEM(small.shape, jnp.float32),
            pltpu.VMEM((devices * cols, images), jnp.float32),
            pltpu.VMEM((devices, cols, images), jnp.float32),
            pltpu.VMEM((devices * cols, images), jnp.float32),
            pltpu.VMEM((devices, cols, images), jnp.float32),
            pltpu.VMEM((24, 128), jnp.float32),
            pltpu.SemaphoreType.DMA((5, devices)),
            pltpu.SemaphoreType.DMA((5, devices)),
        ],
        compiler_params=pltpu.CompilerParams(collective_id=4, has_side_effects=True, vmem_limit_bytes=24 << 20),
        name="settle",
    )(*ins)

def code_table():
    quarter = MODEL_WIDTH // 4
    omega = (1.0 / 10000.0 ** (np.arange(quarter, dtype=np.float32) / np.float32(quarter))).astype(np.float32)
    angles = np.arange(GRID, dtype=np.float32)[:, None] * omega
    return np.concatenate([np.sin(angles), np.cos(angles)], 1).astype(np.float32)


def position_sum():
    table = jnp.asarray(code_table())
    half = MODEL_WIDTH // 2
    rows_pos = jnp.broadcast_to(table[:, None, :], (GRID, GRID, half))
    cols_pos = jnp.broadcast_to(table[None, :, :], (GRID, GRID, half))
    return jnp.concatenate([rows_pos, cols_pos], -1).reshape(SEQ, MODEL_WIDTH)


def rows_t(left, right):
    return jnp.einsum("bsd,ed->bse", left, right, preferred_element_type=jnp.float32)


def back_t(left, right):
    return jnp.einsum("bse,ed->bsd", left, right, preferred_element_type=jnp.float32)


def outer_t(left, right):
    return jnp.einsum("bsd,bse->ed", left, right, preferred_element_type=jnp.float32).astype(jnp.bfloat16)


def forward_t(x, mod, w_in, w_out, bias_in, bias_out):
    pieces = [mod[:, None, i * MODEL_WIDTH : (i + 1) * MODEL_WIDTH] for i in range(6)]
    shaped_one = (layer_norm(x) * (1 + pieces[1]) + pieces[0]).astype(jnp.bfloat16)
    triple = (rows_t(shaped_one, w_in[: 3 * MODEL_WIDTH]) + bias_in[: 3 * MODEL_WIDTH]).astype(jnp.bfloat16)
    mixed_heads, log_norm = attend(triple)
    branch = rows_t(mixed_heads, w_out[:, :MODEL_WIDTH]) + bias_out[:MODEL_WIDTH]
    middle = x + pieces[2] * branch
    shaped_two = (layer_norm(middle) * (1 + pieces[4]) + pieces[3]).astype(jnp.bfloat16)
    pre_ffn = rows_t(shaped_two, w_in[3 * MODEL_WIDTH :]) + bias_in[3 * MODEL_WIDTH :]
    active = gelu(pre_ffn).astype(jnp.bfloat16)
    ffn_out = rows_t(active, w_out[:, MODEL_WIDTH:]) + bias_out[MODEL_WIDTH:]
    kept = (x, shaped_one, triple, log_norm, mixed_heads, branch, middle, shaped_two, pre_ffn, active, ffn_out)
    return middle + pieces[5] * ffn_out, kept


def backward_t(upstream, mod, w_in, w_out, kept):
    x, shaped_one, triple, log_norm, mixed_heads, branch, middle, shaped_two, pre_ffn, active, ffn_out = kept
    pieces = [mod[:, None, i * MODEL_WIDTH : (i + 1) * MODEL_WIDTH] for i in range(6)]
    d_ffn = (pieces[5] * upstream).astype(jnp.bfloat16)
    gate_two = jnp.sum(ffn_out * upstream, 1)
    grad_down = outer_t(active, d_ffn)
    d_active = back_t(d_ffn, w_out[:, MODEL_WIDTH:])
    d_pre = local_back(gelu, pre_ffn, d_active).astype(jnp.bfloat16)
    grad_up = outer_t(shaped_two, d_pre)
    d_shaped = back_t(d_pre, w_in[3 * MODEL_WIDTH :])
    shift_two = jnp.sum(d_shaped, 1)
    scale_two = jnp.sum(d_shaped * layer_norm(middle), 1)
    upstream = upstream + local_back(layer_norm, middle, d_shaped * (1 + pieces[4]))
    gate_one = jnp.sum(branch * upstream, 1)
    d_branch = (pieces[2] * upstream).astype(jnp.bfloat16)
    grad_proj = outer_t(mixed_heads, d_branch)
    d_mixed = back_t(d_branch, w_out[:, :MODEL_WIDTH]).astype(jnp.bfloat16)
    d_triple = attend_back(triple, log_norm, d_mixed)
    grad_qkv = outer_t(shaped_one, d_triple)
    d_shaped = back_t(d_triple, w_in[: 3 * MODEL_WIDTH])
    shift_one = jnp.sum(d_shaped, 1)
    scale_one = jnp.sum(d_shaped * layer_norm(x), 1)
    upstream = upstream + local_back(layer_norm, x, d_shaped * (1 + pieces[1]))
    mod_grad = jnp.concatenate([shift_one, scale_one, gate_one, shift_two, scale_two, gate_two], 1)
    bias_in_grad = jnp.concatenate([column_sum(d_triple), column_sum(d_pre)])
    bias_out_grad = jnp.concatenate([column_sum(d_branch), column_sum(d_ffn)])
    grad_in = jnp.concatenate([grad_qkv, grad_up], 0)
    grad_out = jnp.concatenate([grad_proj, grad_down], 1)
    return upstream, mod_grad, grad_in, grad_out, bias_in_grad, bias_out_grad


def body(
    latents, targets, timesteps, labels, embed_w, embed_m, embed_v, cond_w, cond_m, cond_v, layer_input_weights, in_m,
    in_v, layer_output_weights, out_m, out_v, head_w, head_m, head_v, biases, bias_m, bias_v,
):
    devices = lax.axis_size("fsdp")
    me = lax.axis_index("fsdp")
    images = latents.shape[0]
    embed_t = embed_w.T
    cond_t = cond_w.T
    in_t = layer_input_weights.transpose(0, 2, 1)
    out_t = layer_output_weights.transpose(0, 2, 1)
    cols, cond_cols = embed_t.shape[0], cond_t.shape[0]
    time_one, time_two, patch_bias, cond_bias, block_input_bias, block_output_bias, head_bias = split_biases(biases)
    fulls = gather_weights([(in_t[i], out_t[i]) for i in range(LAYERS)], 1)
    w_in = [fulls[2 * i] for i in range(LAYERS)]
    w_out = [fulls[2 * i + 1] for i in range(LAYERS)]
    features = time_features(timesteps).astype(jnp.bfloat16).astype(jnp.float32)
    label_rows = jnp.broadcast_to(labels.astype(jnp.float32)[:, None], (images, 128))
    own_patch_w = embed_t[:, FREQ + MODEL_WIDTH : FREQ + MODEL_WIDTH + PD].reshape(3, 128)
    note = jnp.concatenate([features, label_rows, jnp.pad(own_patch_w, ((0, images - 3), (0, 0)))], 1)
    w_t1 = embed_t[:, :FREQ]
    w_t2 = embed_t[:, FREQ : FREQ + MODEL_WIDTH]
    w_class = jnp.pad(embed_t[:, FREQ + MODEL_WIDTH + PD :], ((0, 0), (0, 1024 - NCLS)))
    images_all = devices * images

    def own_bias(vector, count):
        part = lax.dynamic_slice(vector, (me * count,), (count,))
        return jnp.broadcast_to(part[:, None], (count, images_all))

    own_cond_bias = lax.dynamic_slice(cond_bias, (me * cond_cols,), (cond_cols,))[None]
    mods, pre, cond, hid_all, low_all, feat_all, lab_all, notes = modulate(
        [note, w_t1, w_t2, w_class, cond_t, own_bias(time_one, cols), own_bias(time_two, cols), own_cond_bias]
    )
    modulation = mods.transpose(1, 0, 2).reshape(images, CW)
    w_patch = notes[:, :3, FREQ + 128 :].reshape(MODEL_WIDTH, PD).astype(jnp.bfloat16)
    head_low = head_w.astype(jnp.bfloat16)
    x = rows_t(latents, w_patch) + patch_bias + position_sum()
    kept_all = []
    for i in range(LAYERS):
        mod = modulation[:, 6 * MODEL_WIDTH * i : 6 * MODEL_WIDTH * (i + 1)]
        x, kept = forward_t(x, mod, w_in[i], w_out[i], block_input_bias[i], block_output_bias[i])
        kept_all.append(kept)
    final_mod = modulation[:, 6 * MODEL_WIDTH * LAYERS :]
    norm_final = layer_norm(x)
    shaped = (norm_final * (1 + final_mod[:, None, MODEL_WIDTH:]) + final_mod[:, None, :MODEL_WIDTH]).astype(jnp.bfloat16)
    output = apply_rows(shaped, head_low) + head_bias
    error_vals = output - targets
    loss_part = jnp.sum(error_vals * error_vals)
    tokens_all = devices * images * SEQ * PO
    d_output = (error_vals * (2.0 / tokens_all)).astype(jnp.bfloat16)
    head_grad = outer_sum(shaped, d_output)
    head_bias_grad = column_sum(d_output)
    d_shaped = apply_back(d_output, head_low)
    d_final = jnp.concatenate([jnp.sum(d_shaped, 1), jnp.sum(d_shaped * norm_final, 1)], 1)
    upstream = local_back(layer_norm, x, d_shaped * (1 + final_mod[:, None, MODEL_WIDTH:]))
    mod_grads, in_shards, out_shards = [None] * LAYERS, [None] * LAYERS, [None] * LAYERS
    in_bias_grads, out_bias_grads = [None] * LAYERS, [None] * LAYERS
    for i in reversed(range(LAYERS)):
        mod = modulation[:, 6 * MODEL_WIDTH * i : 6 * MODEL_WIDTH * (i + 1)]
        upstream, mod_grads[i], grad_in, grad_out, in_bias_grads[i], out_bias_grads[i] = backward_t(
            upstream, mod, w_in[i], w_out[i], kept_all[i]
        )
        in_shards[i], out_shards[i] = scatter_grads([grad_in, grad_out], 5 + i)
    d_patch = upstream.astype(jnp.bfloat16)
    patch_grad = outer_sum(latents, d_patch)
    patch_bias_grad = column_sum(d_patch)
    d_modulation = jnp.concatenate(mod_grads + [d_final], 1)
    d_mods = d_modulation.reshape(images, devices, cond_cols).transpose(1, 0, 2)
    small = jnp.concatenate(
        [head_grad.reshape(-1), patch_grad.reshape(-1), patch_bias_grad] + in_bias_grads + out_bias_grads
        + [head_bias_grad, loss_part[None]]
    )
    small = jnp.pad(small, (0, devices * 2048 - small.shape[0])).reshape(devices, 16, 128)
    squares = sum(jnp.sum(shard * shard) for shard in in_shards + out_shards)
    g_cond, g_t1, g_t2, g_cls, merged = settle(
        [d_mods, small, w_t2, cond_t, pre, cond, hid_all, low_all, feat_all, lab_all, jnp.full((1, 128), squares)]
    )
    flat = merged[:, :16].reshape(-1)
    sizes = [MODEL_WIDTH * PO, PD * MODEL_WIDTH, MODEL_WIDTH, LAYERS * IW, LAYERS * 2 * MODEL_WIDTH, PO, 1]
    places = [sum(sizes[:k]) for k in range(len(sizes) + 1)]
    head_total = flat[: places[1]].reshape(MODEL_WIDTH, PO)
    patch_total = flat[places[1] : places[2]].reshape(PD, MODEL_WIDTH)
    loss_total = flat[places[6]]
    bias_total = jnp.concatenate(
        [merged[:, 17, :cols].reshape(-1), merged[:, 18, :cols].reshape(-1), flat[places[2] : places[3]],
         merged[:, 19:22].reshape(devices, 384)[:, :cond_cols].reshape(-1), flat[places[3] : places[6]]]
    )
    grad_norm = jnp.sqrt(
        jnp.sum(merged[:, 16, 0])
        + jnp.sum(head_total * head_total)
        + jnp.sum(patch_total * patch_total)
        + jnp.sum(bias_total * bias_total)
    )
    factor = jnp.minimum(1.0, clip_limit / grad_norm)
    own_patch = lax.dynamic_slice(patch_total, (0, me * cols), (PD, cols)).T
    embed_grad = jnp.concatenate([g_t1, g_t2, own_patch, g_cls[:, :NCLS]], 1)
    embed_up = [a.T for a in adam_step(embed_t, embed_m.T, embed_v.T, embed_grad * factor)]
    cond_up = [a.T for a in adam_step(cond_t, cond_m.T, cond_v.T, g_cond * factor)]
    turn = (0, 2, 1)
    in_up = [
        a.transpose(turn)
        for a in adam_step(in_t, in_m.transpose(turn), in_v.transpose(turn), jnp.stack(in_shards) * factor)
    ]
    out_up = [
        a.transpose(turn)
        for a in adam_step(out_t, out_m.transpose(turn), out_v.transpose(turn), jnp.stack(out_shards) * factor)
    ]
    head_up = adam_step(head_w, head_m, head_v, head_total * factor)
    bias_up = adam_step(biases, bias_m, bias_v, bias_total * factor)
    return (loss_total, grad_norm, *embed_up, *cond_up, *in_up, *out_up, *head_up, *bias_up)


def fits(mesh):
    return mesh.shape["fsdp"] == 32


def solution(mesh):
    in_specs = (
        P("fsdp", None, None),
        P("fsdp", None, None),
        P("fsdp"),
        P("fsdp"),
        P(None, "fsdp"),
        P(None, "fsdp"),
        P(None, "fsdp"),
        P(None, "fsdp"),
        P(None, "fsdp"),
        P(None, "fsdp"),
        P(None, None, "fsdp"),
        P(None, None, "fsdp"),
        P(None, None, "fsdp"),
        P(None, None, "fsdp"),
        P(None, None, "fsdp"),
        P(None, None, "fsdp"),
        P(),
        P(),
        P(),
        P(),
        P(),
        P(),
    )
    out_specs = (
        P(),
        P(),
        P(None, "fsdp"),
        P(None, "fsdp"),
        P(None, "fsdp"),
        P(None, "fsdp"),
        P(None, "fsdp"),
        P(None, "fsdp"),
        P(None, None, "fsdp"),
        P(None, None, "fsdp"),
        P(None, None, "fsdp"),
        P(None, None, "fsdp"),
        P(None, None, "fsdp"),
        P(None, None, "fsdp"),
        P(),
        P(),
        P(),
        P(),
        P(),
        P(),
    )
    chosen = body if fits(mesh) else generic_body
    return jax.shard_map(chosen, mesh=mesh, in_specs=in_specs, out_specs=out_specs, check_vma=False)
```

```python
import functools
import math

import jax
import jax.numpy as jnp
import numpy as np
from jax import lax
from jax.experimental import pallas as pl
from jax.experimental.pallas import tpu as pltpu
from jax.sharding import PartitionSpec as P

MODEL_WIDTH = 768
HEADS = 12
HEAD_DIM = 64
NCLS = 1001
FREQ = 256
PD = 16
PO = 32
GRID = 16
LAYERS = 2
STEP = 10
SEQ = 256
IW = 5376
OW = 3840
FF = 3072
CW = 10752


learn_rate = 0.03
beta_one = 0.9
beta_two = 0.999
adam_eps = 1e-08
decay = 0.01
clip_limit = 0.01
highest = lax.Precision.HIGHEST


def product(left, right):
    return jnp.dot(left, right, preferred_element_type=jnp.float32)


def exact_dot(left, right):
    return jnp.dot(left, right, precision=highest)


def apply_rows(left, right):
    return jnp.einsum("bsd,de->bse", left, right, preferred_element_type=jnp.float32)


def outer_sum(left, right):
    return jnp.einsum("bsd,bse->de", left, right, preferred_element_type=jnp.float32)


def apply_back(left, right):
    return jnp.einsum("bse,de->bsd", left, right, preferred_element_type=jnp.float32)


def column_sum(value):
    return jnp.sum(value.astype(jnp.float32), (0, 1))


def silu(value):
    return value * jax.nn.sigmoid(value)


def gelu(value):
    return jax.nn.gelu(value, approximate=True)


def layer_norm(value):
    centered = value - jnp.mean(value, -1, keepdims=True)
    return centered * lax.rsqrt(jnp.mean(centered * centered, -1, keepdims=True) + 1e-06)


def local_back(func, value, cotangent):
    return jax.vjp(func, value)[1](cotangent)[0]


def position_table():
    quarter = MODEL_WIDTH // 4
    omega = 1.0 / 10000.0 ** (jnp.arange(quarter, dtype=jnp.float32) / quarter)
    places = jnp.arange(GRID * GRID)
    rows_pos = (places // GRID).astype(jnp.float32)[:, None] * omega
    cols_pos = (places % GRID).astype(jnp.float32)[:, None] * omega
    return jnp.concatenate(
        [jnp.sin(rows_pos), jnp.cos(rows_pos), jnp.sin(cols_pos), jnp.cos(cols_pos)], 1
    )


def time_features(timesteps):
    half_freq = FREQ // 2
    rates = jnp.exp(-math.log(10000.0) * jnp.arange(half_freq, dtype=jnp.float32) / half_freq)
    angles = timesteps.astype(jnp.float32)[:, None] * rates
    return jnp.concatenate([jnp.cos(angles), jnp.sin(angles)], 1)


def split_biases(vector):
    lengths = [MODEL_WIDTH, MODEL_WIDTH, MODEL_WIDTH, CW, LAYERS * IW, LAYERS * 2 * MODEL_WIDTH, PO]
    pieces = []
    offset = 0
    for length in lengths:
        pieces.append(vector[offset : offset + length])
        offset += length
    pieces[4] = pieces[4].reshape(LAYERS, IW)
    pieces[5] = pieces[5].reshape(LAYERS, 2 * MODEL_WIDTH)
    return pieces


def split_heads(triple, which):
    n_images, seq_len = (triple.shape[0], triple.shape[1])
    return triple[..., which * MODEL_WIDTH : (which + 1) * MODEL_WIDTH].reshape(
        n_images, seq_len, HEADS, HEAD_DIM
    )


def attend(triple):
    queries, key_part, values = [split_heads(triple, j) for j in range(3)]
    scores = jnp.einsum(
        "bqhd,bkhd->bhqk", queries, key_part, preferred_element_type=jnp.float32
    ) * HEAD_DIM ** (-0.5)
    row_max = jnp.max(scores, -1, keepdims=True)
    expo = jnp.exp(scores - row_max)
    row_sum = jnp.sum(expo, -1, keepdims=True)
    attn_weights = (expo / row_sum).astype(jnp.bfloat16)
    mixed_heads = jnp.einsum(
        "bhqk,bkhd->bqhd", attn_weights, values, preferred_element_type=jnp.float32
    ).astype(jnp.bfloat16)
    return (
        mixed_heads.reshape(triple.shape[0], triple.shape[1], MODEL_WIDTH),
        row_max + jnp.log(row_sum),
    )


def attend_back(triple, log_norm, d_mixed):
    queries, key_part, values = [split_heads(triple, j) for j in range(3)]
    scale = HEAD_DIM ** (-0.5)
    scores = (
        jnp.einsum("bqhd,bkhd->bhqk", queries, key_part, preferred_element_type=jnp.float32) * scale
    )
    probs_full = jnp.exp(scores - log_norm)
    attn_weights = probs_full.astype(jnp.bfloat16)
    d_heads = d_mixed.reshape(queries.shape)
    d_probs = jnp.einsum("bqhd,bkhd->bhqk", d_heads, values, preferred_element_type=jnp.float32)
    d_values = jnp.einsum(
        "bhqk,bqhd->bkhd", attn_weights, d_heads, preferred_element_type=jnp.float32
    )
    d_scores = (probs_full * (d_probs - jnp.sum(probs_full * d_probs, -1, keepdims=True))).astype(
        jnp.bfloat16
    )
    d_queries = (
        jnp.einsum("bhqk,bkhd->bqhd", d_scores, key_part, preferred_element_type=jnp.float32)
        * scale
    )
    d_keys = (
        jnp.einsum("bhqk,bqhd->bkhd", d_scores, queries, preferred_element_type=jnp.float32) * scale
    )
    shape_flat = (triple.shape[0], triple.shape[1], MODEL_WIDTH)
    return jnp.concatenate(
        [d_queries.reshape(shape_flat), d_keys.reshape(shape_flat), d_values.reshape(shape_flat)],
        -1,
    ).astype(jnp.bfloat16)


def block_forward(residual_state, adaptive_modulation, weights_in, weights_out, bias_in, bias_out):
    pieces = [
        adaptive_modulation[:, None, i * MODEL_WIDTH : (i + 1) * MODEL_WIDTH] for i in range(6)
    ]
    shaped_one = (layer_norm(residual_state) * (1 + pieces[1]) + pieces[0]).astype(jnp.bfloat16)
    triple = (
        apply_rows(shaped_one, weights_in[:, : 3 * MODEL_WIDTH]) + bias_in[: 3 * MODEL_WIDTH]
    ).astype(jnp.bfloat16)
    mixed_heads, log_norm = attend(triple)
    branch = apply_rows(mixed_heads, weights_out[:MODEL_WIDTH]) + bias_out[:MODEL_WIDTH]
    middle = residual_state + pieces[2] * branch
    shaped_two = (layer_norm(middle) * (1 + pieces[4]) + pieces[3]).astype(jnp.bfloat16)
    pre_ffn = apply_rows(shaped_two, weights_in[:, 3 * MODEL_WIDTH :]) + bias_in[3 * MODEL_WIDTH :]
    active = gelu(pre_ffn).astype(jnp.bfloat16)
    ffn_out = apply_rows(active, weights_out[MODEL_WIDTH:]) + bias_out[MODEL_WIDTH:]
    kept = (
        residual_state,
        shaped_one,
        triple,
        log_norm,
        mixed_heads,
        branch,
        middle,
        shaped_two,
        pre_ffn,
        active,
        ffn_out,
    )
    return (middle + pieces[5] * ffn_out, kept)


def block_backward(upstream, adaptive_modulation, weights_in, weights_out, kept):
    (
        residual_state,
        shaped_one,
        triple,
        log_norm,
        mixed_heads,
        branch,
        middle,
        shaped_two,
        pre_ffn,
        active,
        ffn_out,
    ) = kept
    pieces = [
        adaptive_modulation[:, None, i * MODEL_WIDTH : (i + 1) * MODEL_WIDTH] for i in range(6)
    ]
    d_ffn = (pieces[5] * upstream).astype(jnp.bfloat16)
    gate_two = jnp.sum(ffn_out * upstream, 1)
    grad_down = outer_sum(active, d_ffn)
    d_active = apply_back(d_ffn, weights_out[MODEL_WIDTH:])
    d_pre = local_back(gelu, pre_ffn, d_active).astype(jnp.bfloat16)
    grad_up = outer_sum(shaped_two, d_pre)
    d_shaped = apply_back(d_pre, weights_in[:, 3 * MODEL_WIDTH :])
    shift_two = jnp.sum(d_shaped, 1)
    scale_two = jnp.sum(d_shaped * layer_norm(middle), 1)
    upstream = upstream + local_back(layer_norm, middle, d_shaped * (1 + pieces[4]))
    gate_one = jnp.sum(branch * upstream, 1)
    d_branch = (pieces[2] * upstream).astype(jnp.bfloat16)
    grad_proj = outer_sum(mixed_heads, d_branch)
    d_mixed = apply_back(d_branch, weights_out[:MODEL_WIDTH]).astype(jnp.bfloat16)
    d_triple = attend_back(triple, log_norm, d_mixed)
    grad_qkv = outer_sum(shaped_one, d_triple)
    d_shaped = apply_back(d_triple, weights_in[:, : 3 * MODEL_WIDTH])
    shift_one = jnp.sum(d_shaped, 1)
    scale_one = jnp.sum(d_shaped * layer_norm(residual_state), 1)
    upstream = upstream + local_back(layer_norm, residual_state, d_shaped * (1 + pieces[1]))
    mod_grad = jnp.concatenate([shift_one, scale_one, gate_one, shift_two, scale_two, gate_two], 1)
    bias_in_grad = jnp.concatenate([column_sum(d_triple), column_sum(d_pre)])
    bias_out_grad = jnp.concatenate([column_sum(d_branch), column_sum(d_ffn)])
    grad_in = jnp.concatenate([grad_qkv, grad_up], 1)
    grad_out = jnp.concatenate([grad_proj, grad_down], 0)
    return (upstream, mod_grad, grad_in, grad_out, bias_in_grad, bias_out_grad)


def fetch_layer(layer_input_weights, layer_output_weights, layer_count):
    return (
        lax.all_gather(
            layer_input_weights[layer_count].astype(jnp.bfloat16), "fsdp", axis=1, tiled=True
        ),
        lax.all_gather(
            layer_output_weights[layer_count].astype(jnp.bfloat16), "fsdp", axis=1, tiled=True
        ),
    )


def adam_step(weight, first, second, gradient):
    first = beta_one * first + (1 - beta_one) * gradient
    second = beta_two * second + (1 - beta_two) * gradient * gradient
    ahead = first / (1 - beta_one**STEP)
    scaled = second / (1 - beta_two**STEP)
    return (
        weight - learn_rate * (ahead / (jnp.sqrt(scaled) + adam_eps) + decay * weight),
        first,
        second,
    )


def generic_body(
    latents,
    targets,
    timesteps,
    labels,
    embed_w,
    embed_m,
    embed_v,
    cond_w,
    cond_m,
    cond_v,
    layer_input_weights,
    in_m,
    in_v,
    layer_output_weights,
    out_m,
    out_v,
    head_w,
    head_m,
    head_v,
    biases,
    bias_m,
    bias_v,
):
    devices = lax.axis_size("fsdp")
    embed_full, cond_full = (
        lax.all_gather(embed_w.astype(jnp.bfloat16), "fsdp", axis=1, tiled=True),
        lax.all_gather(cond_w.astype(jnp.bfloat16), "fsdp", axis=1, tiled=True),
    )
    time_one, time_two, patch_bias, cond_bias, block_input_bias, block_output_bias, head_bias = (
        split_biases(biases)
    )
    head_low = head_w.astype(jnp.bfloat16)
    features = time_features(timesteps).astype(jnp.bfloat16)
    pre_time = product(features, embed_full[:FREQ]) + time_one
    hidden_t = silu(pre_time).astype(jnp.bfloat16)
    time_emb = product(hidden_t, embed_full[FREQ : FREQ + MODEL_WIDTH]) + time_two
    onehot = (labels[:, None] == jnp.arange(NCLS)[None, :]).astype(jnp.bfloat16)
    condition = time_emb + product(onehot, embed_full[FREQ + MODEL_WIDTH + PD :])
    cond_low = silu(condition).astype(jnp.bfloat16)
    adaptive_modulation = product(cond_low, cond_full) + cond_bias
    residual_state = (
        apply_rows(latents, embed_full[FREQ + MODEL_WIDTH : FREQ + MODEL_WIDTH + PD])
        + patch_bias
        + position_table()
    )
    kept_all = []
    for layer_count in range(LAYERS):
        weights_in, weights_out = fetch_layer(
            layer_input_weights, layer_output_weights, layer_count
        )
        residual_state, kept = block_forward(
            residual_state,
            adaptive_modulation[
                :, 6 * MODEL_WIDTH * layer_count : 6 * MODEL_WIDTH * (layer_count + 1)
            ],
            weights_in,
            weights_out,
            block_input_bias[layer_count],
            block_output_bias[layer_count],
        )
        kept_all.append(kept)
    final_mod = adaptive_modulation[:, 6 * MODEL_WIDTH * LAYERS :]
    norm_final = layer_norm(residual_state)
    shaped = (
        norm_final * (1 + final_mod[:, None, MODEL_WIDTH:]) + final_mod[:, None, :MODEL_WIDTH]
    ).astype(jnp.bfloat16)
    output = apply_rows(shaped, head_low) + head_bias
    error_vals = output - targets
    loss_part = jnp.sum(error_vals * error_vals)
    tokens_all = devices * error_vals.shape[0] * SEQ * PO
    d_output = (error_vals * (2.0 / tokens_all)).astype(jnp.bfloat16)
    head_grad = outer_sum(shaped, d_output)
    head_bias_grad = column_sum(d_output)
    d_shaped = apply_back(d_output, head_low)
    d_final = jnp.concatenate([jnp.sum(d_shaped, 1), jnp.sum(d_shaped * norm_final, 1)], 1)
    upstream = local_back(
        layer_norm, residual_state, d_shaped * (1 + final_mod[:, None, MODEL_WIDTH:])
    )
    mod_grads = [None] * LAYERS
    in_shards = [None] * LAYERS
    out_shards = [None] * LAYERS
    in_bias_grads = [None] * LAYERS
    out_bias_grads = [None] * LAYERS
    for layer_count in reversed(range(LAYERS)):
        weights_in, weights_out = (
            lax.all_gather(
                layer_input_weights[layer_count].astype(jnp.bfloat16), "fsdp", axis=1, tiled=True
            ),
            lax.all_gather(
                layer_output_weights[layer_count].astype(jnp.bfloat16), "fsdp", axis=1, tiled=True
            ),
        )
        upstream, mod_grad, grad_in, grad_out, bias_in_grad, bias_out_grad = block_backward(
            upstream,
            adaptive_modulation[
                :, 6 * MODEL_WIDTH * layer_count : 6 * MODEL_WIDTH * (layer_count + 1)
            ],
            weights_in,
            weights_out,
            kept_all[layer_count],
        )
        in_shards[layer_count], out_shards[layer_count] = (
            lax.psum_scatter(grad_in, "fsdp", scatter_dimension=1, tiled=True),
            lax.psum_scatter(grad_out, "fsdp", scatter_dimension=1, tiled=True),
        )
        mod_grads[layer_count] = mod_grad
        in_bias_grads[layer_count] = bias_in_grad
        out_bias_grads[layer_count] = bias_out_grad
    d_patch = upstream.astype(jnp.bfloat16)
    patch_grad = outer_sum(latents, d_patch)
    patch_bias_grad = column_sum(d_patch)
    d_modulation = jnp.concatenate(mod_grads + [d_final], 1)
    d_cond = exact_dot(d_modulation, cond_full.astype(jnp.float32).T)
    d_condition = local_back(silu, condition, d_cond)
    d_hidden = exact_dot(d_condition, embed_full[FREQ : FREQ + MODEL_WIDTH].astype(jnp.float32).T)
    d_pre = local_back(silu, pre_time, d_hidden)
    cond_grad = exact_dot(cond_low.astype(jnp.float32).T, d_modulation)
    class_grad = exact_dot(onehot.astype(jnp.float32).T, d_condition)
    time_two_grad = exact_dot(hidden_t.astype(jnp.float32).T, d_condition)
    time_one_grad = exact_dot(features.astype(jnp.float32).T, d_pre)
    embed_grad = jnp.concatenate([time_one_grad, time_two_grad, patch_grad, class_grad], 0)
    embed_shard, cond_shard = (
        lax.psum_scatter(embed_grad, "fsdp", scatter_dimension=1, tiled=True),
        lax.psum_scatter(cond_grad, "fsdp", scatter_dimension=1, tiled=True),
    )
    bias_grad = jnp.concatenate(
        [jnp.sum(d_pre, 0), jnp.sum(d_condition, 0), patch_bias_grad, jnp.sum(d_modulation, 0)]
        + in_bias_grads
        + out_bias_grads
        + [head_bias_grad]
    )
    head_total, bias_total, loss_total = lax.psum((head_grad, bias_grad, loss_part), "fsdp")
    in_stack = jnp.stack(in_shards, 0)
    out_stack = jnp.stack(out_shards, 0)
    shard_squares = (
        jnp.sum(embed_shard * embed_shard)
        + jnp.sum(cond_shard * cond_shard)
        + jnp.sum(in_stack * in_stack)
        + jnp.sum(out_stack * out_stack)
    )
    square_total = lax.psum(shard_squares, "fsdp")
    grad_norm = jnp.sqrt(
        square_total + jnp.sum(head_total * head_total) + jnp.sum(bias_total * bias_total)
    )
    factor = jnp.minimum(1.0, clip_limit / grad_norm)
    embed_up = adam_step(embed_w, embed_m, embed_v, embed_shard * factor)
    cond_up = adam_step(cond_w, cond_m, cond_v, cond_shard * factor)
    in_up = adam_step(layer_input_weights, in_m, in_v, in_stack * factor)
    out_up = adam_step(layer_output_weights, out_m, out_v, out_stack * factor)
    head_up = adam_step(head_w, head_m, head_v, head_total * factor)
    bias_up = adam_step(biases, bias_m, bias_v, bias_total * factor)
    return (
        loss_total,
        grad_norm,
        embed_up[0],
        embed_up[1],
        embed_up[2],
        cond_up[0],
        cond_up[1],
        cond_up[2],
        in_up[0],
        in_up[1],
        in_up[2],
        out_up[0],
        out_up[1],
        out_up[2],
        head_up[0],
        head_up[1],
        head_up[2],
        bias_up[0],
        bias_up[1],
        bias_up[2],
    )


MESH_ID = pl.DeviceIdType.MESH
AXIS = "fsdp"


class Place:
    def __init__(self):
        me = lax.axis_index(AXIS)
        self.me = me
        self.core = core = me % 2
        x = (me // 2) % 2
        y = (me // 4) % 2
        self.z = me // 8
        self.chip = me // 2
        step_x = 1 - 2 * x
        step_y = 2 - 4 * y
        self.step_a = step_x + core * (step_y - step_x)
        self.step_b = step_y + core * (step_x - step_y)
        self.dev_a = me + 2 * self.step_a
        self.dev_b = me + 2 * self.step_b
        self.sibling = me + 1 - 2 * core

    def other(self, dz, flip_a=0, flip_b=0):
        return self.chip + 4 * dz + flip_a * self.step_a + flip_b * self.step_b

    def valid(self, dz):
        return jnp.logical_and(self.z + dz >= 0, self.z + dz < 4)

    def greet(self):
        barrier = pltpu.get_barrier_semaphore()
        for device in (self.sibling, self.dev_a, self.dev_b):
            pl.semaphore_signal(barrier, inc=1, device_id=(device,), device_id_type=MESH_ID)
        for sign in (-1, 1):

            @pl.when(self.valid(sign))
            def _():
                pl.semaphore_signal(barrier, inc=1, device_id=(self.me + 8 * sign,), device_id_type=MESH_ID)

        pl.semaphore_wait(barrier, 4 + self.z * (3 - self.z) // 2)


def remote(src, dst, send_sem, recv_sem, device):
    return pltpu.make_async_remote_copy(
        src_ref=src, dst_ref=dst, send_sem=send_sem, recv_sem=recv_sem, device_id=(device,), device_id_type=MESH_ID
    )


class Gather:
    def __init__(self, place, own, stage, piece, full, sems):
        self.p, self.own, self.stage, self.piece, self.full = place, own, stage, piece, full
        self.xch_send, self.xch_recv, self.local, self.send, self.recv, self.sib_recv = sems
        self.sent, self.keep = [], []

    def slot(self, a, chip):
        rows, half = self.piece[a].shape
        return self.full[a].at[
            pl.ds(pl.multiple_of(chip * rows, rows), rows), pl.ds(pl.multiple_of(self.p.core * half, half), half)
        ]

    def push(self, a, k, src, chip, device, sem, cond=None):
        copy = remote(src, self.slot(a, chip), self.send.at[a, k], sem, device)
        self.sent.append((copy, cond))
        if cond is None:
            copy.start()
        else:
            pl.when(cond)(copy.start)

    def begin(self):
        core = self.p.core
        copies = []
        for a in range(2):
            rows, half = self.own[a].shape[0], self.piece[a].shape[1]
            dst = self.stage[a].at[pl.ds(pl.multiple_of(core * rows, 8), rows), :]
            away = remote(
                self.own[a].at[:, pl.ds(pl.multiple_of((1 - core) * half, half), half)],
                dst,
                self.xch_send.at[a],
                self.xch_recv.at[a],
                self.p.sibling,
            )
            away.start()
            keep = pltpu.make_async_copy(
                self.own[a].at[:, pl.ds(pl.multiple_of(core * half, half), half)], dst, self.local.at[a]
            )
            keep.start()
            copies.append((away, keep))
        for a in range(2):
            copies[a][0].wait()
            copies[a][1].wait()
            self.piece[a][...] = self.stage[a][...].astype(jnp.bfloat16)
            keep = pltpu.make_async_copy(self.piece[a], self.slot(a, self.p.chip), self.local.at[a])
            keep.start()
            self.keep.append(keep)
            for sign in (-1, 1):
                self.push(
                    a, 0 if sign < 0 else 3, self.piece[a], self.p.chip, self.p.me + 8 * sign,
                    self.recv.at[a, self.p.chip], self.p.valid(sign),
                )
            self.push(a, 6, self.piece[a], self.p.chip, self.p.dev_a, self.recv.at[a, self.p.chip])
            self.push(a, 10, self.piece[a], self.p.chip, self.p.dev_b, self.recv.at[a, self.p.chip])
            self.push(a, 18, self.piece[a], self.p.chip, self.p.sibling, self.sib_recv.at[a, self.p.chip])

    def arrive(self, a, chip):
        slot = self.slot(a, chip)
        pltpu.make_async_copy(slot, slot, self.recv.at[a, chip]).wait()

    def z_step(self, dist):
        for sign in (-1, 1):
            here = self.p.valid(sign * dist)
            chip = self.p.other(sign * dist)
            rel = (sign * dist) % 4
            onward = jnp.logical_and(here, self.p.valid(-sign))
            for a in range(2):
                pl.when(here)(functools.partial(self.arrive, a, chip))
                src = self.slot(a, chip)
                if dist < 3:
                    self.push(
                        a, (0 if sign > 0 else 3) + dist, src, chip, self.p.me - 8 * sign,
                        self.recv.at[a, chip], onward,
                    )
                self.push(a, 6 + rel, src, chip, self.p.dev_a, self.recv.at[a, chip], here)
                self.push(a, 10 + rel, src, chip, self.p.dev_b, self.recv.at[a, chip], here)
                self.push(a, 18 + rel, src, chip, self.p.sibling, self.sib_recv.at[a, chip], here)

    def a_step(self, dist):
        for sign in (-1, 1) if dist else (1,):
            here = self.p.valid(sign * dist)
            chip = self.p.other(sign * dist, 1)
            rel = (sign * dist) % 4
            for a in range(2):
                pl.when(here)(functools.partial(self.arrive, a, chip))
                src = self.slot(a, chip)
                self.push(a, 14 + rel, src, chip, self.p.dev_b, self.recv.at[a, chip], here)
                self.push(a, 22 + rel, src, chip, self.p.sibling, self.sib_recv.at[a, chip], here)

    def b_step(self, dist, flip_a):
        for sign in (-1, 1) if dist else (1,):
            here = self.p.valid(sign * dist)
            chip = self.p.other(sign * dist, flip_a, 1)
            rel = (sign * dist) % 4
            for a in range(2):
                pl.when(here)(functools.partial(self.arrive, a, chip))
                src = self.slot(a, chip)
                self.push(a, 26 + 4 * flip_a + rel, src, chip, self.p.sibling, self.sib_recv.at[a, chip], here)

    def finish(self):
        for a in range(2):
            rows, half = self.piece[a].shape

            def take(chip, carry):
                slot = self.full[a].at[
                    pl.ds(pl.multiple_of(chip * rows, rows), rows),
                    pl.ds(pl.multiple_of((1 - self.p.core) * half, half), half),
                ]
                pltpu.make_async_copy(slot, slot, self.sib_recv.at[a, chip]).wait()
                return carry

            lax.fori_loop(0, 16, take, 0)
        for copy in self.keep:
            copy.wait()
        for copy, cond in self.sent:
            if cond is None:
                copy.wait_send()
            else:
                pl.when(cond)(copy.wait_send)


GATHER_SEMS = [
    pltpu.SemaphoreType.DMA((2,)),
    pltpu.SemaphoreType.DMA((2,)),
    pltpu.SemaphoreType.DMA((2,)),
    pltpu.SemaphoreType.DMA((2, 34)),
    pltpu.SemaphoreType.DMA((2, 16)),
    pltpu.SemaphoreType.DMA((2, 16)),
]


def gather_scratch(shapes):
    return (
        [pltpu.VMEM(shape, jnp.float32) for shape in shapes]
        + [pltpu.VMEM(shape, jnp.bfloat16) for shape in shapes]
        + GATHER_SEMS
    )


def piece_shapes(shapes):
    return [(2 * rows, width // 2) for rows, width in shapes]


def gather_kernel(layers, *refs):
    own, refs = refs[: 2 * layers], refs[2 * layers :]
    full, refs = refs[: 2 * layers], refs[2 * layers :]
    place = Place()
    place.greet()
    jobs = []
    for layer in range(layers):
        part = refs[10 * layer : 10 * layer + 10]
        jobs.append(
            Gather(place, own[2 * layer : 2 * layer + 2], part[:2], part[2:4], full[2 * layer : 2 * layer + 2], part[4:])
        )
    for job in jobs:
        job.begin()
        job.a_step(0)
        for dist in (1, 2, 3):
            job.z_step(dist)
            job.a_step(dist)
    for job in jobs:
        for dist in range(4):
            job.b_step(dist, 0)
            job.b_step(dist, 1)
    for job in jobs:
        job.finish()


def gather_weights(pairs, collective):
    flat = [array for pair in pairs for array in pair]
    devices = lax.axis_size(AXIS)
    scratch = []
    for pair in pairs:
        scratch += gather_scratch(piece_shapes([array.shape for array in pair]))
    return pl.pallas_call(
        functools.partial(gather_kernel, len(pairs)),
        out_shape=[jax.ShapeDtypeStruct((devices * a.shape[0], a.shape[1]), jnp.bfloat16) for a in flat],
        in_specs=[pl.BlockSpec(memory_space=pltpu.VMEM)] * len(flat),
        out_specs=[pl.BlockSpec(memory_space=pl.ANY)] * len(flat),
        scratch_shapes=scratch,
        compiler_params=pltpu.CompilerParams(
            collective_id=collective, has_side_effects=True, vmem_limit_bytes=24 << 20
        ),
        name="gather_weights",
    )(*flat)


ORDER = (3, 0, 2, 1)


class Scatter:
    def __init__(self, place, grad, total, bufs, sems):
        self.p, self.grad, self.total = place, grad, total
        self.mine, self.sib, self.from_b, self.from_a, self.up, self.down, self.part, self.last = (
            bufs[2 * i : 2 * i + 2] for i in range(8)
        )
        (self.load_sem, self.sib_send, self.sib_recv, self.b_send, self.b_recv, self.a_send, self.a_recv, self.up_send,
         self.up_recv, self.down_send, self.down_recv, self.end_send, self.end_recv, self.end_local) = sems

    def rows_of(self, a, chip, core):
        _, rows, half = self.mine[a].shape
        return self.grad[a].at[
            pl.ds(pl.multiple_of(chip * rows, rows), rows), pl.ds(pl.multiple_of(core * half, half), half)
        ]

    def chip_of(self, z, flip_a, flip_b):
        return self.p.other(z - self.p.z, flip_a, flip_b)

    def load(self, a, flip_b, flip_a, z):
        k = 8 * flip_b + 4 * flip_a + z
        return pltpu.make_async_copy(
            self.rows_of(a, self.chip_of(z, flip_a, flip_b), self.p.core), self.mine[a].at[k], self.load_sem.at[a, k]
        )

    def lend(self, a, flip_b, flip_a, z):
        k = 8 * flip_b + 4 * flip_a + z
        return remote(
            self.rows_of(a, self.chip_of(z, flip_b, flip_a), 1 - self.p.core),
            self.sib[a].at[k],
            self.sib_send.at[a, k],
            self.sib_recv.at[a, k],
            self.p.sibling,
        )

    def to_b(self, a, flip_a, z):
        k = 4 * flip_a + z
        return remote(
            self.mine[a].at[8 + k], self.from_b[a].at[k], self.b_send.at[a, k], self.b_recv.at[a, k], self.p.dev_b
        )

    def to_a(self, a, z):
        return remote(
            self.mine[a].at[4 + z], self.from_a[a].at[z], self.a_send.at[a, z], self.a_recv.at[a, z], self.p.dev_a
        )

    def to_z(self, a, z, sign):
        dst, send, recv = (
            (self.up, self.up_send, self.up_recv) if sign > 0 else (self.down, self.down_send, self.down_recv)
        )
        return remote(self.mine[a].at[z], dst[a].at[z], send.at[a, z], recv.at[a, z], self.p.me + 8 * sign)

    def each(self, step):
        def run(z, carry):
            for a in range(2):
                step(a, z)
            return carry

        lax.fori_loop(0, 4, run, 0)

    def begin(self):
        for z in ORDER:
            for flip_b, flip_a in ((1, 1), (1, 0), (0, 1), (0, 0)):
                for a in range(2):
                    self.lend(a, flip_b, flip_a, z).start()
                    self.load(a, flip_b, flip_a, z).start()

    def pair(self, a, flip_b, flip_a, z):
        k = 8 * flip_b + 4 * flip_a + z
        self.load(a, flip_b, flip_a, z).wait()
        self.lend(a, flip_b, flip_a, z).wait_recv()
        return self.mine[a][k].astype(jnp.float32) + self.sib[a][k].astype(jnp.float32)

    def cross_b(self, z):
        for flip_a in (1, 0):
            for a in range(2):
                self.mine[a][8 + 4 * flip_a + z] = self.pair(a, 1, flip_a, z).astype(jnp.bfloat16)
                self.to_b(a, flip_a, z).start()

    def cross_a(self, z):
        for a in range(2):
            value = self.pair(a, 0, 1, z)
            self.to_b(a, 1, z).wait_recv()
            self.mine[a][4 + z] = (value + self.from_b[a][4 + z].astype(jnp.float32)).astype(jnp.bfloat16)
            self.to_a(a, z).start()

    def along_z(self, z):
        place = self.p
        for a in range(2):
            value = self.pair(a, 0, 0, z)
            self.to_b(a, 0, z).wait_recv()
            value = value + self.from_b[a][z].astype(jnp.float32)
            self.to_a(a, z).wait_recv()
            self.part[a][...] = value + self.from_a[a][z].astype(jnp.float32)

            @pl.when(jnp.logical_and(place.z < z, place.z > 0))
            def _():
                self.to_z(a, z, 1).wait_recv()
                self.part[a][...] += self.up[a][z].astype(jnp.float32)

            @pl.when(jnp.logical_and(place.z > z, place.z < 3))
            def _():
                self.to_z(a, z, -1).wait_recv()
                self.part[a][...] += self.down[a][z].astype(jnp.float32)

            @pl.when(place.z != z)
            def _():
                self.mine[a][z] = self.part[a][...].astype(jnp.bfloat16)

            @pl.when(place.z < z)
            def _():
                self.to_z(a, z, 1).start()

            @pl.when(place.z > z)
            def _():
                self.to_z(a, z, -1).start()

            @pl.when(place.z == z)
            def _():
                self.last[a][...] = self.part[a][...]

    def end_copies(self, a):
        core = self.p.core
        rows, width = self.total[a].shape
        dst = self.total[a].at[:, pl.ds(pl.multiple_of(core * (width // 2), width // 2), width // 2)]
        away = remote(
            self.last[a].at[pl.ds(pl.multiple_of((1 - core) * rows, 8), rows), :],
            dst,
            self.end_send.at[a],
            self.end_recv.at[a],
            self.p.sibling,
        )
        keep = pltpu.make_async_copy(
            self.last[a].at[pl.ds(pl.multiple_of(core * rows, 8), rows), :], dst, self.end_local.at[a]
        )
        return away, keep

    def close(self):
        place = self.p
        for a in range(2):

            @pl.when(place.z > 0)
            def _():
                self.to_z(a, place.z, 1).wait_recv()
                self.last[a][...] += self.up[a][place.z].astype(jnp.float32)

            @pl.when(place.z < 3)
            def _():
                self.to_z(a, place.z, -1).wait_recv()
                self.last[a][...] += self.down[a][place.z].astype(jnp.float32)

            for copy in self.end_copies(a):
                copy.start()

    def finish(self):
        for a in range(2):
            for copy in self.end_copies(a):
                copy.wait()

        def step(a, z):
            for flip_b in range(2):
                for flip_a in range(2):
                    self.lend(a, flip_b, flip_a, z).wait_send()
            for flip_a in range(2):
                self.to_b(a, flip_a, z).wait_send()
            self.to_a(a, z).wait_send()

            @pl.when(self.p.z < z)
            def _():
                self.to_z(a, z, 1).wait_send()

            @pl.when(self.p.z > z)
            def _():
                self.to_z(a, z, -1).wait_send()

        self.each(step)

    def steps(self):
        yield self.begin
        for k in range(6):
            if k < 4:
                yield functools.partial(self.cross_b, ORDER[k])
            if 0 <= k - 1 < 4:
                yield functools.partial(self.cross_a, ORDER[k - 1])
            if 0 <= k - 2 < 4:
                yield functools.partial(self.along_z, ORDER[k - 2])
        yield self.close
        yield self.finish


def scatter_scratch(shapes):
    scratch = []
    for count, kind in ((16, jnp.bfloat16), (16, jnp.bfloat16), (8, jnp.bfloat16), (4, jnp.bfloat16), (4, jnp.bfloat16),
                        (4, jnp.bfloat16), (0, jnp.float32), (0, jnp.float32)):
        scratch += [pltpu.VMEM(((count,) if count else ()) + shape, kind) for shape in shapes]
    counts = (16, 16, 16, 8, 8, 4, 4, 4, 4, 4, 4)
    return scratch + [pltpu.SemaphoreType.DMA((2, n)) for n in counts] + [pltpu.SemaphoreType.DMA((2,))] * 3


def scatter_kernel(*refs):
    grad, total, bufs, sems = refs[:2], refs[2:4], refs[4:20], refs[20:]
    place = Place()
    place.greet()
    for step in Scatter(place, grad, total, bufs, sems).steps():
        step()


def scatter_grads(grads, collective):
    devices = lax.axis_size(AXIS)
    shapes = [(a.shape[0] // devices, a.shape[1]) for a in grads]
    return pl.pallas_call(
        scatter_kernel,
        out_shape=[jax.ShapeDtypeStruct(shape, jnp.float32) for shape in shapes],
        in_specs=[pl.BlockSpec(memory_space=pl.ANY)] * 2,
        out_specs=[pl.BlockSpec(memory_space=pltpu.VMEM)] * 2,
        scratch_shapes=scatter_scratch(piece_shapes(shapes)),
        compiler_params=pltpu.CompilerParams(
            collective_id=collective, has_side_effects=True, vmem_limit_bytes=40 << 20
        ),
        name="scatter_grads",
    )(*grads)


def dot_nt(left, right):
    return lax.dot_general(left, right, (((1,), (1,)), ((), ())), preferred_element_type=jnp.float32)


def dot_tn(left, right):
    return lax.dot_general(left, right, (((0,), (0,)), ((), ())), preferred_element_type=jnp.float32)


def thirds(value):
    high = value.astype(jnp.bfloat16)
    rest = value - high.astype(jnp.float32)
    mid = rest.astype(jnp.bfloat16)
    return high, mid, (rest - mid.astype(jnp.float32)).astype(jnp.bfloat16)


def silu_slope(value):
    gate = jax.nn.sigmoid(value)
    return gate * (1 + value * (1 - gate))


class Swap:
    def __init__(self, me, devices, index, src_of, dst, send, recv):
        self.me, self.n, self.i, self.src_of, self.dst, self.send, self.recv = me, devices, index, src_of, dst, send, recv

    def copy(self, peer, slot):
        return remote(self.src_of(peer), self.dst.at[slot], self.send.at[self.i, peer], self.recv.at[self.i, slot], peer)

    def each(self, step):
        def run(k, carry):
            step(lax.rem(self.me + k, self.n))
            return carry

        lax.fori_loop(1, self.n, run, 0)

    def start(self):
        self.each(lambda peer: self.copy(peer, self.me).start())

    def arrive(self):
        self.each(lambda peer: self.copy(peer, peer).wait_recv())

    def sent(self):
        self.each(lambda peer: self.copy(peer, self.me).wait_send())


def greet_all(devices):
    barrier = pltpu.get_barrier_semaphore()
    me = lax.axis_index(AXIS)

    def hello(k, carry):
        pl.semaphore_signal(barrier, inc=1, device_id=(lax.rem(me + k, devices),), device_id_type=MESH_ID)
        return carry

    lax.fori_loop(1, devices, hello, 0)
    pl.semaphore_wait(barrier, devices - 1)


def modulate_steps(devices, ins, outs, bufs, sems):
    msg, wt1, wt2, wcls, wcond, bt1, bt2, bcond = ins
    mods, pre, cond, hid_all, low_all, feat_all, lab_all, got = outs
    hid, low, away = bufs
    me = lax.axis_index(AXIS)
    images, cols = 4, wt1.shape[0]
    swaps = [
        Swap(me, devices, 0, lambda peer: msg, got, *sems),
        Swap(me, devices, 1, lambda peer: hid.at[me], hid, *sems),
        Swap(me, devices, 2, lambda peer: low.at[me], low, *sems),
        Swap(me, devices, 3, lambda peer: away.at[peer], mods, *sems),
    ]

    def first():
        swaps[0].start()
        got[me] = msg[...]

    def second():
        swaps[0].arrive()
        for j in range(devices):
            feat_all[images * j : images * (j + 1), :] = got[j, :, :FREQ]
            lab_all[images * j : images * (j + 1), :] = got[j, :, FREQ : FREQ + 128]
        pre[...] = dot_nt(wt1[...].astype(jnp.bfloat16), feat_all[...].astype(jnp.bfloat16)) + bt1[...]
        hidden = silu(pre[...])
        pad = jnp.zeros((hid.shape[1] - cols, hidden.shape[1]), jnp.float32)
        hid[me] = jnp.concatenate([hidden, pad], 0).astype(jnp.bfloat16)
        swaps[1].start()
        classes = lax.broadcasted_iota(jnp.int32, (lab_all.shape[0], wcls.shape[1]), 1).astype(jnp.float32)
        labels = jnp.concatenate([lab_all[...]] * (wcls.shape[1] // 128), 1)
        onehot = (labels == classes).astype(jnp.bfloat16)
        cond[...] = dot_nt(wcls[...].astype(jnp.bfloat16), onehot) + bt2[...]

    def third():
        swaps[1].arrive()
        for j in range(devices):
            hid_all[cols * j : cols * (j + 1), :] = hid[j].astype(jnp.float32)[:cols]
        cond[...] += jnp.dot(
            wt2[...].astype(jnp.bfloat16), hid_all[...].astype(jnp.bfloat16), preferred_element_type=jnp.float32
        )
        value = silu(cond[...])
        pad = jnp.zeros((low.shape[1] - cols, value.shape[1]), jnp.float32)
        low[me] = jnp.concatenate([value, pad], 0).astype(jnp.bfloat16)
        swaps[2].start()

    def fourth():
        swaps[2].arrive()
        for j in range(devices):
            low_all[cols * j : cols * (j + 1), :] = low[j].astype(jnp.float32)[:cols]
        rows = dot_nt(low_all[...].T.astype(jnp.bfloat16), wcond[...].astype(jnp.bfloat16)) + bcond[...]
        for j in range(devices):
            away[j] = rows[images * j : images * (j + 1)]
        swaps[3].start()
        mods[me] = away[me]

    def last():
        swaps[3].arrive()
        for swap in swaps:
            swap.sent()

    return [first, second, third, fourth, last]


def modulate_kernel(devices, *refs):
    greet_all(devices)
    for step in modulate_steps(devices, refs[:8], refs[8:16], refs[16:19], refs[19:]):
        step()


def modulate(ins):
    devices = lax.axis_size(AXIS)
    msg, wt1, wt2, wcls, wcond = ins[:5]
    cols, images = wt1.shape[0], devices * msg.shape[0]
    outs = [
        (devices, msg.shape[0], wcond.shape[0]), (cols, images), (cols, images), (devices * cols, images),
        (devices * cols, images), (images, FREQ), (images, 128), (devices,) + msg.shape,
    ]
    padded = -(-cols // 16) * 16
    return pl.pallas_call(
        functools.partial(modulate_kernel, devices),
        out_shape=[jax.ShapeDtypeStruct(shape, jnp.float32) for shape in outs],
        in_specs=[pl.BlockSpec(memory_space=pltpu.VMEM)] * 8,
        out_specs=[pl.BlockSpec(memory_space=pltpu.VMEM)] * 8,
        scratch_shapes=[
            pltpu.VMEM((devices, padded, images), jnp.bfloat16),
            pltpu.VMEM((devices, padded, images), jnp.bfloat16),
            pltpu.VMEM((devices, msg.shape[0], wcond.shape[0]), jnp.float32),
            pltpu.SemaphoreType.DMA((4, devices)),
            pltpu.SemaphoreType.DMA((4, devices)),
        ],
        compiler_params=pltpu.CompilerParams(collective_id=3, has_side_effects=True, vmem_limit_bytes=24 << 20),
        name="modulate",
    )(*ins)


def settle_steps(devices, ins, outs, bufs, sems):
    d_mods, small, wt2, wcond, pre, cond, hid_all, low_all, feat_all, lab_all, squares = ins
    g_cond, g_t1, g_t2, g_cls, merged = outs
    dm_got, dm_all, small_got, dc_part, dc_got, dh_part, dh_got, note = bufs
    me = lax.axis_index(AXIS)
    images, cols = d_mods.shape[1], wt2.shape[0]
    width = d_mods.shape[2]

    def rows_for(ref):
        return lambda peer: ref.at[pl.ds(pl.multiple_of(peer * cols, 8), cols), :]

    swaps = [
        Swap(me, devices, 0, lambda peer: d_mods.at[peer], dm_got, *sems),
        Swap(me, devices, 1, lambda peer: small.at[peer], small_got, *sems),
        Swap(me, devices, 2, rows_for(dc_part), dc_got, *sems),
        Swap(me, devices, 3, rows_for(dh_part), dh_got, *sems),
        Swap(me, devices, 4, lambda peer: note, merged, *sems),
    ]
    keep = {}

    def first():
        swaps[0].start()
        swaps[1].start()
        dm_got[me] = d_mods[me]
        small_got[me] = small[me]
        dm_all[...] = jnp.zeros_like(dm_all)

    def second():
        swaps[0].arrive()
        for j in range(devices):
            dm_all[images * j : images * (j + 1), :width] = dm_got[j]
        turned = dm_all[...].T[:width]
        parts = thirds(turned)
        weight = wcond[...].astype(jnp.bfloat16)
        dc_part[...] = sum(dot_tn(weight, part) for part in parts)
        swaps[2].start()
        mine = pl.ds(pl.multiple_of(me * cols, 8), cols)
        dc_got[me] = dc_part[mine, :]
        low = low_all[...].astype(jnp.bfloat16)
        g_cond[...] = sum(dot_nt(part, low) for part in parts)
        swaps[1].arrive()

    def third():
        swaps[2].arrive()
        d_cond = jnp.sum(dc_got[...], 0) * silu_slope(cond[...])
        parts = thirds(d_cond)
        weight = wt2[...].astype(jnp.bfloat16)
        dh_part[...] = sum(dot_tn(weight, part) for part in parts)
        swaps[3].start()
        mine = pl.ds(pl.multiple_of(me * cols, 8), cols)
        dh_got[me] = dh_part[mine, :]
        classes = lax.broadcasted_iota(jnp.int32, (lab_all.shape[0], g_cls.shape[1]), 1).astype(jnp.float32)
        labels = jnp.concatenate([lab_all[...]] * (g_cls.shape[1] // 128), 1)
        onehot = (labels == classes).astype(jnp.bfloat16)
        g_cls[...] = sum(jnp.dot(part, onehot, preferred_element_type=jnp.float32) for part in parts)
        hidden = hid_all[...].astype(jnp.bfloat16)
        g_t2[...] = sum(dot_nt(part, hidden) for part in parts)
        ones = jnp.ones((8, lab_all.shape[0]), jnp.bfloat16)
        keep["t2"] = sum(dot_nt(ones, part) for part in parts)

    def fourth():
        swaps[3].arrive()
        d_pre = jnp.sum(dh_got[...], 0) * silu_slope(pre[...])
        parts = thirds(d_pre)
        feats = feat_all[...].astype(jnp.bfloat16)
        g_t1[...] = sum(jnp.dot(part, feats, preferred_element_type=jnp.float32) for part in parts)
        ones = jnp.ones((8, lab_all.shape[0]), jnp.bfloat16)
        bias_t1 = sum(dot_nt(ones, part) for part in parts)
        total = squares[...]
        for ref in (g_cond, g_t1, g_t2, g_cls):
            total = total + jnp.sum(ref[...] * ref[...])
        bias_cond = jnp.sum(dm_all[...], 0, keepdims=True)
        note[...] = jnp.zeros_like(note)
        note[0:16, :] = jnp.sum(small_got[...], 0)
        note[16:17, :] = total
        note[17:18, :cols] = bias_t1[0:1]
        note[18:19, :cols] = keep["t2"][0:1]
        for k in range(3):
            note[19 + k : 20 + k, :] = bias_cond[:, 128 * k : 128 * (k + 1)]
        swaps[4].start()
        merged[me] = note[...]

    def last():
        swaps[4].arrive()
        for swap in swaps:
            swap.sent()

    return [first, second, third, fourth, last]


def settle_kernel(devices, *refs):
    greet_all(devices)
    for step in settle_steps(devices, refs[:11], refs[11:16], refs[16:24], refs[24:]):
        step()


def settle(ins):
    devices = lax.axis_size(AXIS)
    d_mods, small, wt2, wcond, pre = ins[:5]
    cols, images = pre.shape
    outs = [(wcond.shape[0], devices * cols), (cols, FREQ), (cols, devices * cols), (cols, 1024), (devices, 24, 128)]
    return pl.pallas_call(
        functools.partial(settle_kernel, devices),
        out_shape=[jax.ShapeDtypeStruct(shape, jnp.float32) for shape in outs],
        in_specs=[pl.BlockSpec(memory_space=pltpu.VMEM)] * 11,
        out_specs=[pl.BlockSpec(memory_space=pltpu.VMEM)] * 5,
        scratch_shapes=[
            pltpu.VMEM(d_mods.shape, jnp.float32),
            pltpu.VMEM((images, 384), jnp.float32),
            pltpu.VMEM(small.shape, jnp.float32),
            pltpu.VMEM((devices * cols, images), jnp.float32),
            pltpu.VMEM((devices, cols, images), jnp.float32),
            pltpu.VMEM((devices * cols, images), jnp.float32),
            pltpu.VMEM((devices, cols, images), jnp.float32),
            pltpu.VMEM((24, 128), jnp.float32),
            pltpu.SemaphoreType.DMA((5, devices)),
            pltpu.SemaphoreType.DMA((5, devices)),
        ],
        compiler_params=pltpu.CompilerParams(collective_id=4, has_side_effects=True, vmem_limit_bytes=24 << 20),
        name="settle",
    )(*ins)


def dot_nn(left, right):
    return lax.dot_general(left, right, (((1,), (0,)), ((), ())), preferred_element_type=jnp.float32)


def norm_parts(value):
    centered = value - jnp.mean(value, -1, keepdims=True)
    scale = lax.rsqrt(jnp.mean(centered * centered, -1, keepdims=True) + 1e-06)
    return centered * scale, scale


def norm_back(normed, scale, d_normed):
    inner = jnp.mean(d_normed * normed, -1, keepdims=True)
    return scale * (d_normed - jnp.mean(d_normed, -1, keepdims=True) - normed * inner)


GELU_C = math.sqrt(2.0 / math.pi)


def gelu_value(u):
    return 0.5 * u * (1.0 + jnp.tanh(GELU_C * (u + 0.044715 * u * u * u)))


def gelu_slope(u):
    square = u * u
    t = jnp.tanh(GELU_C * u * (1.0 + 0.044715 * square))
    return 0.5 * (1.0 + t) + 0.5 * u * (1.0 - t * t) * (GELU_C * (1.0 + 3 * 0.044715 * square))


def head_masks(shape):
    low_half = lax.broadcasted_iota(jnp.int32, shape, 1) < HEAD_DIM
    return low_half, jnp.logical_not(low_half)


class Weights:
    def __init__(self, hbm, vmem, sems):
        w_in, w_out = hbm
        self.w_in, self.w_out = vmem
        cut = 3 * MODEL_WIDTH
        spans = [
            (w_in.at[pl.ds(0, cut), :], self.w_in.at[pl.ds(0, cut), :]),
            (w_out.at[:, pl.ds(0, MODEL_WIDTH)], self.w_out.at[:, pl.ds(0, MODEL_WIDTH)]),
            (w_in.at[pl.ds(cut, FF), :], self.w_in.at[pl.ds(cut, FF), :]),
            (w_out.at[:, pl.ds(MODEL_WIDTH, FF)], self.w_out.at[:, pl.ds(MODEL_WIDTH, FF)]),
        ]
        self.copies = [pltpu.make_async_copy(src, dst, sems.at[i]) for i, (src, dst) in enumerate(spans)]

    def start(self, order):
        @pl.when(pl.program_id(0) == 0)
        def _():
            for i in order:
                self.copies[i].start()

    def need(self, i):
        @pl.when(pl.program_id(0) == 0)
        def _():
            self.copies[i].wait()


def forward_image(x_ref, mod, weights, b_in, b_out, outs):
    h1, qkv, probs, o, a, x1, h2, u, g, f = outs
    shift1, scale1, gate1, shift2, scale2, gate2 = (mod[0, i : i + 1, :] for i in range(6))
    width = MODEL_WIDTH
    x = x_ref[...]
    h1[...] = (norm_parts(x)[0] * (1 + scale1) + shift1).astype(jnp.bfloat16)
    weights.need(0)
    for j in range(3):
        span = slice(j * width, (j + 1) * width)
        qkv[:, span] = (dot_nt(h1[...], weights.w_in[span, :]) + b_in[:, span]).astype(jnp.bfloat16)
    for pair in range(HEADS // 2):
        lanes = slice(128 * pair, 128 * (pair + 1))
        q, k, v = (qkv[:, j * width + 128 * pair : j * width + 128 * (pair + 1)] for j in range(3))
        q = q * jnp.bfloat16(HEAD_DIM**-0.5)
        zero = jnp.zeros_like(q)
        mixed = None
        for half, mask in enumerate(head_masks(q.shape)):
            scores = dot_nt(jnp.where(mask, q, zero), k)
            expo = jnp.exp(scores - jnp.max(scores, -1, keepdims=True))
            weight = (expo * pl.reciprocal(jnp.sum(expo, -1, keepdims=True))).astype(jnp.bfloat16)
            probs[0, 2 * pair + half] = weight
            term = dot_nn(weight, jnp.where(mask, v, zero))
            mixed = term if mixed is None else mixed + term
        o[:, lanes] = mixed.astype(jnp.bfloat16)
    weights.need(1)
    branch = dot_nt(o[...], weights.w_out[:, :width]) + b_out[:, :width]
    a[...] = branch.astype(jnp.bfloat16)
    x1[...] = x + gate1 * branch
    h2[...] = (norm_parts(x1[...])[0] * (1 + scale2) + shift2).astype(jnp.bfloat16)
    weights.need(2)
    weights.need(3)
    total = None
    for j in range(FF // width):
        span = slice(j * width, (j + 1) * width)
        rows = slice((3 + j) * width, (4 + j) * width)
        value = dot_nt(h2[...], weights.w_in[rows, :]) + b_in[:, rows]
        u[:, span] = value.astype(jnp.bfloat16)
        g[:, span] = gelu_value(value).astype(jnp.bfloat16)
        term = dot_nt(g[:, span], weights.w_out[:, (1 + j) * width : (2 + j) * width])
        total = term if total is None else total + term
    ffn = total + b_out[:, width:]
    f[...] = ffn.astype(jnp.bfloat16)
    return x1[...] + gate2 * ffn


def forward_kernel(x, mod, w_in, w_out, b_in, b_out, *refs):
    outs, x_out, vm_in, vm_out, sems = refs[:10], refs[10], refs[11], refs[12], refs[13]
    weights = Weights((w_in, w_out), (vm_in, vm_out), sems)
    weights.start((0, 1, 2, 3))
    x_out[...] = forward_image(x, mod, weights, b_in, b_out, outs)


def head_kernel(scale_out, x, mod, w_in, w_out, b_in, b_out, final, head_t, b_head, targets_t, *refs):
    outs, (dx, d_final, g_head, g_bias, loss), (vm_in, vm_out, sems) = refs[:10], refs[10:15], refs[15:]
    weights = Weights((w_in, w_out), (vm_in, vm_out), sems)
    weights.start((0, 1, 2, 3))
    last = forward_image(x, mod, weights, b_in, b_out, outs)
    normed, scale = norm_parts(last)
    shift_row, scale_row = final[0, 0:1, :], final[0, 1:2, :]
    shaped = (normed * (1 + scale_row) + shift_row).astype(jnp.bfloat16)
    low = head_t[...].astype(jnp.bfloat16)
    error = dot_nt(low, shaped) + b_head[...] - targets_t[0]
    d_out = (error * scale_out).astype(jnp.bfloat16)

    @pl.when(pl.program_id(0) == 0)
    def _():
        g_head[...] = jnp.zeros_like(g_head)
        g_bias[...] = jnp.zeros_like(g_bias)
        loss[...] = jnp.zeros_like(loss)

    g_head[...] += dot_nn(d_out, shaped)
    g_bias[...] += jnp.sum(d_out.astype(jnp.float32), 1, keepdims=True)
    loss[...] += jnp.sum(error * error)
    d_shaped = dot_tn(d_out, low)
    d_final[0, 0:1, :] = jnp.sum(d_shaped, 0, keepdims=True)
    d_final[0, 1:2, :] = jnp.sum(d_shaped * normed, 0, keepdims=True)
    dx[...] = norm_back(normed, scale, d_shaped * (1 + scale_row))


WEIGHT_SCRATCH = [
    pltpu.VMEM((IW, MODEL_WIDTH), jnp.bfloat16),
    pltpu.VMEM((MODEL_WIDTH, OW), jnp.bfloat16),
    pltpu.SemaphoreType.DMA((4,)),
]


def token_block(width):
    return pl.BlockSpec((SEQ, width), lambda i: (i, 0))


def image_block(*dims):
    return pl.BlockSpec((1,) + dims, lambda i: (i,) + (0,) * len(dims))


def whole_block(*dims):
    return pl.BlockSpec(dims, lambda i: (0,) * len(dims))


def kept_shapes(images):
    tokens, width, low, full = images * SEQ, MODEL_WIDTH, jnp.bfloat16, jnp.float32
    shapes = [((tokens, width), low), ((tokens, 3 * width), low), ((images, HEADS, SEQ, SEQ), low), ((tokens, width), low),
              ((tokens, width), low), ((tokens, width), full), ((tokens, width), low), ((tokens, FF), low),
              ((tokens, FF), low), ((tokens, width), low)]
    specs = [token_block(s[1]) if len(s) == 2 else image_block(*s[1:]) for s, _ in shapes]
    return [jax.ShapeDtypeStruct(s, t) for s, t in shapes], specs


def forward_specs():
    any_block = pl.BlockSpec(memory_space=pl.ANY)
    return [token_block(MODEL_WIDTH), image_block(6, MODEL_WIDTH), any_block, any_block, whole_block(1, IW),
            whole_block(1, 2 * MODEL_WIDTH)]


def forward_block(ins):
    images = ins[1].shape[0]
    shapes, specs = kept_shapes(images)
    return pl.pallas_call(
        forward_kernel,
        grid=(images,),
        out_shape=shapes + [jax.ShapeDtypeStruct((images * SEQ, MODEL_WIDTH), jnp.float32)],
        in_specs=forward_specs(),
        out_specs=specs + [token_block(MODEL_WIDTH)],
        scratch_shapes=WEIGHT_SCRATCH,
        compiler_params=pltpu.CompilerParams(vmem_limit_bytes=56 << 20),
        name="forward_block",
    )(*ins)


def forward_head(ins, scale_out):
    images = ins[1].shape[0]
    shapes, specs = kept_shapes(images)
    extra = [(images * SEQ, MODEL_WIDTH), (images, 2, MODEL_WIDTH), (PO, MODEL_WIDTH), (PO, 128), (8, 128)]
    return pl.pallas_call(
        functools.partial(head_kernel, scale_out),
        grid=(images,),
        out_shape=shapes + [jax.ShapeDtypeStruct(s, jnp.float32) for s in extra],
        in_specs=forward_specs()
        + [image_block(2, MODEL_WIDTH), whole_block(PO, MODEL_WIDTH), whole_block(PO, 1), image_block(PO, SEQ)],
        out_specs=specs
        + [token_block(MODEL_WIDTH), image_block(2, MODEL_WIDTH), whole_block(PO, MODEL_WIDTH), whole_block(PO, 128),
           whole_block(8, 128)],
        scratch_shapes=WEIGHT_SCRATCH,
        compiler_params=pltpu.CompilerParams(vmem_limit_bytes=56 << 20),
        name="forward_head",
    )(*ins)


def backward_image(refs, mod, weights, outs):
    up_ref, x_ref, x1_ref, probs, qkv, a, f, u = refs
    dx, d_qkv, d_u, d_f, d_a, d_mod, g_bin, g_bout = outs
    width = MODEL_WIDTH
    shift1, scale1, gate1, shift2, scale2, gate2 = (mod[0, i : i + 1, :] for i in range(6))

    @pl.when(pl.program_id(0) == 0)
    def _():
        g_bin[...] = jnp.zeros_like(g_bin)
        g_bout[...] = jnp.zeros_like(g_bout)

    def rows_sum(value):
        return jnp.sum(value.astype(jnp.float32), 0, keepdims=True)

    upstream = up_ref[...]
    d_f[...] = (gate2 * upstream).astype(jnp.bfloat16)
    d_mod[0, 5:6, :] = rows_sum(f[...].astype(jnp.float32) * upstream)
    g_bout[:, width:] += rows_sum(d_f[...])
    weights.need(3)
    weights.need(2)
    d_h2 = None
    for j in range(FF // width):
        span = slice(j * width, (j + 1) * width)
        rows = slice((3 + j) * width, (4 + j) * width)
        d_g = dot_nn(d_f[...], weights.w_out[:, (1 + j) * width : (2 + j) * width])
        d_u[:, span] = (d_g * gelu_slope(u[:, span].astype(jnp.float32))).astype(jnp.bfloat16)
        g_bin[:, rows] += rows_sum(d_u[:, span])
        term = dot_nn(d_u[:, span], weights.w_in[rows, :])
        d_h2 = term if d_h2 is None else d_h2 + term
    normed, scale = norm_parts(x1_ref[...])
    d_mod[0, 3:4, :] = rows_sum(d_h2)
    d_mod[0, 4:5, :] = rows_sum(d_h2 * normed)
    upstream = upstream + norm_back(normed, scale, d_h2 * (1 + scale2))
    d_mod[0, 2:3, :] = rows_sum(a[...].astype(jnp.float32) * upstream)
    d_a[...] = (gate1 * upstream).astype(jnp.bfloat16)
    g_bout[:, :width] += rows_sum(d_a[...])
    dx[...] = upstream
    weights.need(1)
    d_o = dot_nn(d_a[...], weights.w_out[:, :width]).astype(jnp.bfloat16)
    root = HEAD_DIM**-0.5
    for pair in range(HEADS // 2):
        lanes = [slice(j * width + 128 * pair, j * width + 128 * (pair + 1)) for j in range(3)]
        q, k, v = (qkv[:, s] for s in lanes)
        d_mixed = d_o[:, 128 * pair : 128 * (pair + 1)]
        zero = jnp.zeros_like(q)
        sums = [None] * 3
        for half, mask in enumerate(head_masks(q.shape)):
            weight = probs[0, 2 * pair + half]
            full = weight.astype(jnp.float32)
            d_masked = jnp.where(mask, d_mixed, zero)
            d_probs = dot_nt(d_masked, v)
            d_scores = (full * (d_probs - jnp.sum(full * d_probs, -1, keepdims=True))).astype(jnp.bfloat16)
            terms = (
                dot_nn(d_scores, jnp.where(mask, k, zero)),
                dot_tn(d_scores, jnp.where(mask, q, zero)),
                dot_tn(weight, d_masked),
            )
            sums = [t if s is None else s + t for s, t in zip(sums, terms)]
        d_qkv[:, lanes[0]] = (sums[0] * root).astype(jnp.bfloat16)
        d_qkv[:, lanes[1]] = (sums[1] * root).astype(jnp.bfloat16)
        d_qkv[:, lanes[2]] = sums[2].astype(jnp.bfloat16)
    weights.need(0)
    d_h1 = None
    for j in range(3):
        span = slice(j * width, (j + 1) * width)
        g_bin[:, span] += rows_sum(d_qkv[:, span])
        term = dot_nn(d_qkv[:, span], weights.w_in[span, :])
        d_h1 = term if d_h1 is None else d_h1 + term
    normed, scale = norm_parts(x_ref[...])
    d_mod[0, 0:1, :] = rows_sum(d_h1)
    d_mod[0, 1:2, :] = rows_sum(d_h1 * normed)
    dx[...] += norm_back(normed, scale, d_h1 * (1 + scale1))


def backward_kernel(mod, w_in, w_out, *refs):
    ins, outs, (vm_in, vm_out, sems) = refs[:8], refs[8:16], refs[16:]
    weights = Weights((w_in, w_out), (vm_in, vm_out), sems)
    weights.start((3, 2, 1, 0))
    backward_image(ins, mod, weights, outs)


def backward_block(mods, w_in, w_out, refs):
    images, width, low, full = mods.shape[0], MODEL_WIDTH, jnp.bfloat16, jnp.float32
    tokens = images * SEQ
    any_block = pl.BlockSpec(memory_space=pl.ANY)
    shapes = [((tokens, width), full), ((tokens, 3 * width), low), ((tokens, FF), low), ((tokens, width), low),
              ((tokens, width), low), ((images, 6, width), full), ((1, IW), full), ((1, 2 * width), full)]
    return pl.pallas_call(
        backward_kernel,
        grid=(images,),
        out_shape=[jax.ShapeDtypeStruct(s, t) for s, t in shapes],
        in_specs=[image_block(6, width), any_block, any_block, token_block(width), token_block(width), token_block(width),
                  image_block(HEADS, SEQ, SEQ), token_block(3 * width), token_block(width), token_block(width),
                  token_block(FF)],
        out_specs=[token_block(s[1]) for s, _ in shapes[:5]]
        + [image_block(6, width), whole_block(1, IW), whole_block(1, 2 * width)],
        scratch_shapes=WEIGHT_SCRATCH,
        compiler_params=pltpu.CompilerParams(vmem_limit_bytes=56 << 20),
        name="backward_block",
    )(mods, w_in, w_out, *refs)


GRAD_STEPS = tuple((0, j) for j in range(3)) + tuple((1, j) for j in range(4)) + ((2, 0),) + tuple((3, j) for j in range(4))


def grads_kernel(*refs):
    ins, (g_in, g_out), bufs, (keep_in, keep_out, load_sems, store_sems) = refs[:8], refs[8:10], refs[10:18], refs[18:]
    width = MODEL_WIDTH
    copies = [pltpu.make_async_copy(src, dst, load_sems.at[i]) for i, (src, dst) in enumerate(zip(ins, bufs))]
    for copy in copies:
        copy.start()
    stores = []
    for step, (kind, j) in enumerate(GRAD_STEPS):
        left, right = bufs[2 * kind], bufs[2 * kind + 1]
        if j == 0:
            copies[2 * kind].wait()
            copies[2 * kind + 1].wait()
        span = pl.ds(j * width, width)
        if kind < 2:
            at = pl.ds((3 * kind + j) * width, width)
            keep_in[at, :] = dot_tn(left[:, span], right[...]).astype(jnp.bfloat16)
            store = pltpu.make_async_copy(keep_in.at[at, :], g_in.at[at, :], store_sems.at[step])
        else:
            at = pl.ds((kind - 2 + j) * width, width)
            keep_out[:, at] = dot_tn(left[...], right[:, span]).astype(jnp.bfloat16)
            store = pltpu.make_async_copy(keep_out.at[:, at], g_out.at[:, at], store_sems.at[step])
        store.start()
        stores.append(store)
    for store in stores:
        store.wait()


def weight_grads(ins):
    any_block = pl.BlockSpec(memory_space=pl.ANY)
    return pl.pallas_call(
        grads_kernel,
        out_shape=[
            jax.ShapeDtypeStruct((IW, MODEL_WIDTH), jnp.bfloat16), jax.ShapeDtypeStruct((MODEL_WIDTH, OW), jnp.bfloat16)
        ],
        in_specs=[any_block] * 8,
        out_specs=[any_block] * 2,
        scratch_shapes=[pltpu.VMEM(a.shape, a.dtype) for a in ins]
        + [pltpu.VMEM((IW, MODEL_WIDTH), jnp.bfloat16), pltpu.VMEM((MODEL_WIDTH, OW), jnp.bfloat16),
           pltpu.SemaphoreType.DMA((8,)), pltpu.SemaphoreType.DMA((len(GRAD_STEPS),))],
        compiler_params=pltpu.CompilerParams(vmem_limit_bytes=56 << 20),
        name="weight_grads",
    )(*ins)

def code_table():
    quarter = MODEL_WIDTH // 4
    omega = (1.0 / 10000.0 ** (np.arange(quarter, dtype=np.float32) / np.float32(quarter))).astype(np.float32)
    angles = np.arange(GRID, dtype=np.float32)[:, None] * omega
    return np.concatenate([np.sin(angles), np.cos(angles)], 1).astype(np.float32)


def position_sum():
    table = jnp.asarray(code_table())
    half = MODEL_WIDTH // 2
    rows_pos = jnp.broadcast_to(table[:, None, :], (GRID, GRID, half))
    cols_pos = jnp.broadcast_to(table[None, :, :], (GRID, GRID, half))
    return jnp.concatenate([rows_pos, cols_pos], -1).reshape(SEQ, MODEL_WIDTH)


def rows_t(left, right):
    return jnp.einsum("bsd,ed->bse", left, right, preferred_element_type=jnp.float32)


def body(
    latents, targets, timesteps, labels, embed_w, embed_m, embed_v, cond_w, cond_m, cond_v, layer_input_weights, in_m,
    in_v, layer_output_weights, out_m, out_v, head_w, head_m, head_v, biases, bias_m, bias_v,
):
    devices = lax.axis_size("fsdp")
    me = lax.axis_index("fsdp")
    images = latents.shape[0]
    embed_t = embed_w.T
    cond_t = cond_w.T
    in_t = layer_input_weights.transpose(0, 2, 1)
    out_t = layer_output_weights.transpose(0, 2, 1)
    cols, cond_cols = embed_t.shape[0], cond_t.shape[0]
    time_one, time_two, patch_bias, cond_bias, block_input_bias, block_output_bias, head_bias = split_biases(biases)
    fulls = gather_weights([(in_t[i], out_t[i]) for i in range(LAYERS)], 1)
    w_in = [fulls[2 * i] for i in range(LAYERS)]
    w_out = [fulls[2 * i + 1] for i in range(LAYERS)]
    features = time_features(timesteps).astype(jnp.bfloat16).astype(jnp.float32)
    label_rows = jnp.broadcast_to(labels.astype(jnp.float32)[:, None], (images, 128))
    own_patch_w = embed_t[:, FREQ + MODEL_WIDTH : FREQ + MODEL_WIDTH + PD].reshape(3, 128)
    note = jnp.concatenate([features, label_rows, jnp.pad(own_patch_w, ((0, images - 3), (0, 0)))], 1)
    w_t1 = embed_t[:, :FREQ]
    w_t2 = embed_t[:, FREQ : FREQ + MODEL_WIDTH]
    w_class = jnp.pad(embed_t[:, FREQ + MODEL_WIDTH + PD :], ((0, 0), (0, 1024 - NCLS)))
    images_all = devices * images

    def own_bias(vector, count):
        part = lax.dynamic_slice(vector, (me * count,), (count,))
        return jnp.broadcast_to(part[:, None], (count, images_all))

    own_cond_bias = lax.dynamic_slice(cond_bias, (me * cond_cols,), (cond_cols,))[None]
    mods, pre, cond, hid_all, low_all, feat_all, lab_all, notes = modulate(
        [note, w_t1, w_t2, w_class, cond_t, own_bias(time_one, cols), own_bias(time_two, cols), own_cond_bias]
    )
    chunks = mods.transpose(1, 0, 2).reshape(images, 6 * LAYERS + 2, MODEL_WIDTH)
    w_patch = notes[:, :3, FREQ + 128 :].reshape(MODEL_WIDTH, PD).astype(jnp.bfloat16)
    x = (rows_t(latents, w_patch) + patch_bias + position_sum()).reshape(images * SEQ, MODEL_WIDTH)
    block_mods = [chunks[:, 6 * i : 6 * (i + 1)] for i in range(LAYERS)]
    head_t = head_w.T
    tokens_all = devices * images * SEQ * PO
    kept_all, starts = [], []
    for i in range(LAYERS):
        ins = [x, block_mods[i], w_in[i], w_out[i], block_input_bias[i][None], block_output_bias[i][None]]
        starts.append(x)
        if i < LAYERS - 1:
            *kept, x = forward_block(ins)
        else:
            ins += [chunks[:, 6 * LAYERS :], head_t, head_bias[:, None], targets.transpose(0, 2, 1)]
            *kept, upstream, d_final, head_grad, head_bias_grad, loss_part = forward_head(ins, 2.0 / tokens_all)
        kept_all.append(kept)
    mod_grads, in_shards, out_shards = [None] * LAYERS, [None] * LAYERS, [None] * LAYERS
    in_bias_grads, out_bias_grads = [None] * LAYERS, [None] * LAYERS
    for i in reversed(range(LAYERS)):
        h1, qkv, probs, o, a, x1, h2, u, g, f = kept_all[i]
        upstream, d_qkv, d_u, d_f, d_a, mod_grads[i], in_bias_grads[i], out_bias_grads[i] = backward_block(
            block_mods[i], w_in[i], w_out[i], [upstream, starts[i], x1, probs, qkv, a, f, u]
        )
        grads = weight_grads([d_qkv, h1, d_u, h2, d_a, o, d_f, g])
        in_shards[i], out_shards[i] = scatter_grads(grads, 5 + i)
    d_patch = upstream.astype(jnp.bfloat16)
    patch_grad = jnp.dot(latents.reshape(images * SEQ, PD).T, d_patch, preferred_element_type=jnp.float32)
    patch_bias_grad = jnp.sum(d_patch.astype(jnp.float32), 0)
    d_modulation = jnp.concatenate(mod_grads + [d_final], 1)
    d_mods = d_modulation.reshape(images, devices, cond_cols).transpose(1, 0, 2)
    end_row = jnp.concatenate([head_bias_grad[:, 0], loss_part[0, :1], jnp.zeros((128 - PO - 1,), jnp.float32)])
    rows = [
        a.reshape(-1, 128) for a in [head_grad, patch_grad, patch_bias_grad] + in_bias_grads + out_bias_grads + [end_row]
    ]
    used = sum(a.shape[0] for a in rows)
    small = jnp.concatenate(rows + [jnp.zeros((devices * 16 - used, 128), jnp.float32)], 0).reshape(devices, 16, 128)
    squares = sum(jnp.sum(shard * shard) for shard in in_shards + out_shards)
    g_cond, g_t1, g_t2, g_cls, merged = settle(
        [d_mods, small, w_t2, cond_t, pre, cond, hid_all, low_all, feat_all, lab_all, jnp.full((1, 128), squares)]
    )
    flat = merged[:, :16].reshape(-1)
    sizes = [MODEL_WIDTH * PO, PD * MODEL_WIDTH, MODEL_WIDTH, LAYERS * IW, LAYERS * 2 * MODEL_WIDTH, PO, 1]
    places = [sum(sizes[:k]) for k in range(len(sizes) + 1)]
    head_total = flat[: places[1]].reshape(PO, MODEL_WIDTH)
    patch_total = flat[places[1] : places[2]].reshape(PD, MODEL_WIDTH)
    loss_total = flat[places[6]]
    bias_total = jnp.concatenate(
        [merged[:, 17, :cols].reshape(-1), merged[:, 18, :cols].reshape(-1), flat[places[2] : places[3]],
         merged[:, 19:22].reshape(devices, 384)[:, :cond_cols].reshape(-1), flat[places[3] : places[6]]]
    )
    grad_norm = jnp.sqrt(
        jnp.sum(merged[:, 16, 0])
        + jnp.sum(head_total * head_total)
        + jnp.sum(patch_total * patch_total)
        + jnp.sum(bias_total * bias_total)
    )
    factor = jnp.minimum(1.0, clip_limit / grad_norm)
    own_patch = lax.dynamic_slice(patch_total, (0, me * cols), (PD, cols)).T
    embed_grad = jnp.concatenate([g_t1, g_t2, own_patch, g_cls[:, :NCLS]], 1)
    embed_up = [a.T for a in adam_step(embed_t, embed_m.T, embed_v.T, embed_grad * factor)]
    cond_up = [a.T for a in adam_step(cond_t, cond_m.T, cond_v.T, g_cond * factor)]
    turn = (0, 2, 1)
    in_up = [
        a.transpose(turn)
        for a in adam_step(in_t, in_m.transpose(turn), in_v.transpose(turn), jnp.stack(in_shards) * factor)
    ]
    out_up = [
        a.transpose(turn)
        for a in adam_step(out_t, out_m.transpose(turn), out_v.transpose(turn), jnp.stack(out_shards) * factor)
    ]
    head_up = [a.T for a in adam_step(head_t, head_m.T, head_v.T, head_total * factor)]
    bias_up = adam_step(biases, bias_m, bias_v, bias_total * factor)
    return (loss_total, grad_norm, *embed_up, *cond_up, *in_up, *out_up, *head_up, *bias_up)


def fits(mesh):
    return mesh.shape["fsdp"] == 32


def solution(mesh):
    in_specs = (
        P("fsdp", None, None),
        P("fsdp", None, None),
        P("fsdp"),
        P("fsdp"),
        P(None, "fsdp"),
        P(None, "fsdp"),
        P(None, "fsdp"),
        P(None, "fsdp"),
        P(None, "fsdp"),
        P(None, "fsdp"),
        P(None, None, "fsdp"),
        P(None, None, "fsdp"),
        P(None, None, "fsdp"),
        P(None, None, "fsdp"),
        P(None, None, "fsdp"),
        P(None, None, "fsdp"),
        P(),
        P(),
        P(),
        P(),
        P(),
        P(),
    )
    out_specs = (
        P(),
        P(),
        P(None, "fsdp"),
        P(None, "fsdp"),
        P(None, "fsdp"),
        P(None, "fsdp"),
        P(None, "fsdp"),
        P(None, "fsdp"),
        P(None, None, "fsdp"),
        P(None, None, "fsdp"),
        P(None, None, "fsdp"),
        P(None, None, "fsdp"),
        P(None, None, "fsdp"),
        P(None, None, "fsdp"),
        P(),
        P(),
        P(),
        P(),
        P(),
        P(),
    )
    chosen = body if fits(mesh) else generic_body
    return jax.shard_map(chosen, mesh=mesh, in_specs=in_specs, out_specs=out_specs, check_vma=False)
```

```python
import functools
import math

import jax
import jax.numpy as jnp
import numpy as np
from jax import lax
from jax.experimental import pallas as pl
from jax.experimental.pallas import tpu as pltpu
from jax.sharding import PartitionSpec as P

MODEL_WIDTH = 768
HEADS = 12
HEAD_DIM = 64
NCLS = 1001
FREQ = 256
PD = 16
PO = 32
GRID = 16
LAYERS = 2
STEP = 10
SEQ = 256
IW = 5376
OW = 3840
FF = 3072
CW = 10752


learn_rate = 0.03
beta_one = 0.9
beta_two = 0.999
adam_eps = 1e-08
decay = 0.01
clip_limit = 0.01
highest = lax.Precision.HIGHEST


def product(left, right):
    return jnp.dot(left, right, preferred_element_type=jnp.float32)


def exact_dot(left, right):
    return jnp.dot(left, right, precision=highest)


def apply_rows(left, right):
    return jnp.einsum("bsd,de->bse", left, right, preferred_element_type=jnp.float32)


def outer_sum(left, right):
    return jnp.einsum("bsd,bse->de", left, right, preferred_element_type=jnp.float32)


def apply_back(left, right):
    return jnp.einsum("bse,de->bsd", left, right, preferred_element_type=jnp.float32)


def column_sum(value):
    return jnp.sum(value.astype(jnp.float32), (0, 1))


def silu(value):
    return value * jax.nn.sigmoid(value)


def gelu(value):
    return jax.nn.gelu(value, approximate=True)


def layer_norm(value):
    centered = value - jnp.mean(value, -1, keepdims=True)
    return centered * lax.rsqrt(jnp.mean(centered * centered, -1, keepdims=True) + 1e-06)


def local_back(func, value, cotangent):
    return jax.vjp(func, value)[1](cotangent)[0]


def position_table():
    quarter = MODEL_WIDTH // 4
    omega = 1.0 / 10000.0 ** (jnp.arange(quarter, dtype=jnp.float32) / quarter)
    places = jnp.arange(GRID * GRID)
    rows_pos = (places // GRID).astype(jnp.float32)[:, None] * omega
    cols_pos = (places % GRID).astype(jnp.float32)[:, None] * omega
    return jnp.concatenate(
        [jnp.sin(rows_pos), jnp.cos(rows_pos), jnp.sin(cols_pos), jnp.cos(cols_pos)], 1
    )


def time_features(timesteps):
    half_freq = FREQ // 2
    rates = jnp.exp(-math.log(10000.0) * jnp.arange(half_freq, dtype=jnp.float32) / half_freq)
    angles = timesteps.astype(jnp.float32)[:, None] * rates
    return jnp.concatenate([jnp.cos(angles), jnp.sin(angles)], 1)


def split_biases(vector):
    lengths = [MODEL_WIDTH, MODEL_WIDTH, MODEL_WIDTH, CW, LAYERS * IW, LAYERS * 2 * MODEL_WIDTH, PO]
    pieces = []
    offset = 0
    for length in lengths:
        pieces.append(vector[offset : offset + length])
        offset += length
    pieces[4] = pieces[4].reshape(LAYERS, IW)
    pieces[5] = pieces[5].reshape(LAYERS, 2 * MODEL_WIDTH)
    return pieces


def split_heads(triple, which):
    n_images, seq_len = (triple.shape[0], triple.shape[1])
    return triple[..., which * MODEL_WIDTH : (which + 1) * MODEL_WIDTH].reshape(
        n_images, seq_len, HEADS, HEAD_DIM
    )


def attend(triple):
    queries, key_part, values = [split_heads(triple, j) for j in range(3)]
    scores = jnp.einsum(
        "bqhd,bkhd->bhqk", queries, key_part, preferred_element_type=jnp.float32
    ) * HEAD_DIM ** (-0.5)
    row_max = jnp.max(scores, -1, keepdims=True)
    expo = jnp.exp(scores - row_max)
    row_sum = jnp.sum(expo, -1, keepdims=True)
    attn_weights = (expo / row_sum).astype(jnp.bfloat16)
    mixed_heads = jnp.einsum(
        "bhqk,bkhd->bqhd", attn_weights, values, preferred_element_type=jnp.float32
    ).astype(jnp.bfloat16)
    return (
        mixed_heads.reshape(triple.shape[0], triple.shape[1], MODEL_WIDTH),
        row_max + jnp.log(row_sum),
    )


def attend_back(triple, log_norm, d_mixed):
    queries, key_part, values = [split_heads(triple, j) for j in range(3)]
    scale = HEAD_DIM ** (-0.5)
    scores = (
        jnp.einsum("bqhd,bkhd->bhqk", queries, key_part, preferred_element_type=jnp.float32) * scale
    )
    probs_full = jnp.exp(scores - log_norm)
    attn_weights = probs_full.astype(jnp.bfloat16)
    d_heads = d_mixed.reshape(queries.shape)
    d_probs = jnp.einsum("bqhd,bkhd->bhqk", d_heads, values, preferred_element_type=jnp.float32)
    d_values = jnp.einsum(
        "bhqk,bqhd->bkhd", attn_weights, d_heads, preferred_element_type=jnp.float32
    )
    d_scores = (probs_full * (d_probs - jnp.sum(probs_full * d_probs, -1, keepdims=True))).astype(
        jnp.bfloat16
    )
    d_queries = (
        jnp.einsum("bhqk,bkhd->bqhd", d_scores, key_part, preferred_element_type=jnp.float32)
        * scale
    )
    d_keys = (
        jnp.einsum("bhqk,bqhd->bkhd", d_scores, queries, preferred_element_type=jnp.float32) * scale
    )
    shape_flat = (triple.shape[0], triple.shape[1], MODEL_WIDTH)
    return jnp.concatenate(
        [d_queries.reshape(shape_flat), d_keys.reshape(shape_flat), d_values.reshape(shape_flat)],
        -1,
    ).astype(jnp.bfloat16)


def block_forward(residual_state, adaptive_modulation, weights_in, weights_out, bias_in, bias_out):
    pieces = [
        adaptive_modulation[:, None, i * MODEL_WIDTH : (i + 1) * MODEL_WIDTH] for i in range(6)
    ]
    shaped_one = (layer_norm(residual_state) * (1 + pieces[1]) + pieces[0]).astype(jnp.bfloat16)
    triple = (
        apply_rows(shaped_one, weights_in[:, : 3 * MODEL_WIDTH]) + bias_in[: 3 * MODEL_WIDTH]
    ).astype(jnp.bfloat16)
    mixed_heads, log_norm = attend(triple)
    branch = apply_rows(mixed_heads, weights_out[:MODEL_WIDTH]) + bias_out[:MODEL_WIDTH]
    middle = residual_state + pieces[2] * branch
    shaped_two = (layer_norm(middle) * (1 + pieces[4]) + pieces[3]).astype(jnp.bfloat16)
    pre_ffn = apply_rows(shaped_two, weights_in[:, 3 * MODEL_WIDTH :]) + bias_in[3 * MODEL_WIDTH :]
    active = gelu(pre_ffn).astype(jnp.bfloat16)
    ffn_out = apply_rows(active, weights_out[MODEL_WIDTH:]) + bias_out[MODEL_WIDTH:]
    kept = (
        residual_state,
        shaped_one,
        triple,
        log_norm,
        mixed_heads,
        branch,
        middle,
        shaped_two,
        pre_ffn,
        active,
        ffn_out,
    )
    return (middle + pieces[5] * ffn_out, kept)


def block_backward(upstream, adaptive_modulation, weights_in, weights_out, kept):
    (
        residual_state,
        shaped_one,
        triple,
        log_norm,
        mixed_heads,
        branch,
        middle,
        shaped_two,
        pre_ffn,
        active,
        ffn_out,
    ) = kept
    pieces = [
        adaptive_modulation[:, None, i * MODEL_WIDTH : (i + 1) * MODEL_WIDTH] for i in range(6)
    ]
    d_ffn = (pieces[5] * upstream).astype(jnp.bfloat16)
    gate_two = jnp.sum(ffn_out * upstream, 1)
    grad_down = outer_sum(active, d_ffn)
    d_active = apply_back(d_ffn, weights_out[MODEL_WIDTH:])
    d_pre = local_back(gelu, pre_ffn, d_active).astype(jnp.bfloat16)
    grad_up = outer_sum(shaped_two, d_pre)
    d_shaped = apply_back(d_pre, weights_in[:, 3 * MODEL_WIDTH :])
    shift_two = jnp.sum(d_shaped, 1)
    scale_two = jnp.sum(d_shaped * layer_norm(middle), 1)
    upstream = upstream + local_back(layer_norm, middle, d_shaped * (1 + pieces[4]))
    gate_one = jnp.sum(branch * upstream, 1)
    d_branch = (pieces[2] * upstream).astype(jnp.bfloat16)
    grad_proj = outer_sum(mixed_heads, d_branch)
    d_mixed = apply_back(d_branch, weights_out[:MODEL_WIDTH]).astype(jnp.bfloat16)
    d_triple = attend_back(triple, log_norm, d_mixed)
    grad_qkv = outer_sum(shaped_one, d_triple)
    d_shaped = apply_back(d_triple, weights_in[:, : 3 * MODEL_WIDTH])
    shift_one = jnp.sum(d_shaped, 1)
    scale_one = jnp.sum(d_shaped * layer_norm(residual_state), 1)
    upstream = upstream + local_back(layer_norm, residual_state, d_shaped * (1 + pieces[1]))
    mod_grad = jnp.concatenate([shift_one, scale_one, gate_one, shift_two, scale_two, gate_two], 1)
    bias_in_grad = jnp.concatenate([column_sum(d_triple), column_sum(d_pre)])
    bias_out_grad = jnp.concatenate([column_sum(d_branch), column_sum(d_ffn)])
    grad_in = jnp.concatenate([grad_qkv, grad_up], 1)
    grad_out = jnp.concatenate([grad_proj, grad_down], 0)
    return (upstream, mod_grad, grad_in, grad_out, bias_in_grad, bias_out_grad)


def fetch_layer(layer_input_weights, layer_output_weights, layer_count):
    return (
        lax.all_gather(
            layer_input_weights[layer_count].astype(jnp.bfloat16), "fsdp", axis=1, tiled=True
        ),
        lax.all_gather(
            layer_output_weights[layer_count].astype(jnp.bfloat16), "fsdp", axis=1, tiled=True
        ),
    )


def adam_step(weight, first, second, gradient):
    first = beta_one * first + (1 - beta_one) * gradient
    second = beta_two * second + (1 - beta_two) * gradient * gradient
    ahead = first / (1 - beta_one**STEP)
    scaled = second / (1 - beta_two**STEP)
    return (
        weight - learn_rate * (ahead / (jnp.sqrt(scaled) + adam_eps) + decay * weight),
        first,
        second,
    )


def generic_body(
    latents,
    targets,
    timesteps,
    labels,
    embed_w,
    embed_m,
    embed_v,
    cond_w,
    cond_m,
    cond_v,
    layer_input_weights,
    in_m,
    in_v,
    layer_output_weights,
    out_m,
    out_v,
    head_w,
    head_m,
    head_v,
    biases,
    bias_m,
    bias_v,
):
    devices = lax.axis_size("fsdp")
    embed_full, cond_full = (
        lax.all_gather(embed_w.astype(jnp.bfloat16), "fsdp", axis=1, tiled=True),
        lax.all_gather(cond_w.astype(jnp.bfloat16), "fsdp", axis=1, tiled=True),
    )
    time_one, time_two, patch_bias, cond_bias, block_input_bias, block_output_bias, head_bias = (
        split_biases(biases)
    )
    head_low = head_w.astype(jnp.bfloat16)
    features = time_features(timesteps).astype(jnp.bfloat16)
    pre_time = product(features, embed_full[:FREQ]) + time_one
    hidden_t = silu(pre_time).astype(jnp.bfloat16)
    time_emb = product(hidden_t, embed_full[FREQ : FREQ + MODEL_WIDTH]) + time_two
    onehot = (labels[:, None] == jnp.arange(NCLS)[None, :]).astype(jnp.bfloat16)
    condition = time_emb + product(onehot, embed_full[FREQ + MODEL_WIDTH + PD :])
    cond_low = silu(condition).astype(jnp.bfloat16)
    adaptive_modulation = product(cond_low, cond_full) + cond_bias
    residual_state = (
        apply_rows(latents, embed_full[FREQ + MODEL_WIDTH : FREQ + MODEL_WIDTH + PD])
        + patch_bias
        + position_table()
    )
    kept_all = []
    for layer_count in range(LAYERS):
        weights_in, weights_out = fetch_layer(
            layer_input_weights, layer_output_weights, layer_count
        )
        residual_state, kept = block_forward(
            residual_state,
            adaptive_modulation[
                :, 6 * MODEL_WIDTH * layer_count : 6 * MODEL_WIDTH * (layer_count + 1)
            ],
            weights_in,
            weights_out,
            block_input_bias[layer_count],
            block_output_bias[layer_count],
        )
        kept_all.append(kept)
    final_mod = adaptive_modulation[:, 6 * MODEL_WIDTH * LAYERS :]
    norm_final = layer_norm(residual_state)
    shaped = (
        norm_final * (1 + final_mod[:, None, MODEL_WIDTH:]) + final_mod[:, None, :MODEL_WIDTH]
    ).astype(jnp.bfloat16)
    output = apply_rows(shaped, head_low) + head_bias
    error_vals = output - targets
    loss_part = jnp.sum(error_vals * error_vals)
    tokens_all = devices * error_vals.shape[0] * SEQ * PO
    d_output = (error_vals * (2.0 / tokens_all)).astype(jnp.bfloat16)
    head_grad = outer_sum(shaped, d_output)
    head_bias_grad = column_sum(d_output)
    d_shaped = apply_back(d_output, head_low)
    d_final = jnp.concatenate([jnp.sum(d_shaped, 1), jnp.sum(d_shaped * norm_final, 1)], 1)
    upstream = local_back(
        layer_norm, residual_state, d_shaped * (1 + final_mod[:, None, MODEL_WIDTH:])
    )
    mod_grads = [None] * LAYERS
    in_shards = [None] * LAYERS
    out_shards = [None] * LAYERS
    in_bias_grads = [None] * LAYERS
    out_bias_grads = [None] * LAYERS
    for layer_count in reversed(range(LAYERS)):
        weights_in, weights_out = (
            lax.all_gather(
                layer_input_weights[layer_count].astype(jnp.bfloat16), "fsdp", axis=1, tiled=True
            ),
            lax.all_gather(
                layer_output_weights[layer_count].astype(jnp.bfloat16), "fsdp", axis=1, tiled=True
            ),
        )
        upstream, mod_grad, grad_in, grad_out, bias_in_grad, bias_out_grad = block_backward(
            upstream,
            adaptive_modulation[
                :, 6 * MODEL_WIDTH * layer_count : 6 * MODEL_WIDTH * (layer_count + 1)
            ],
            weights_in,
            weights_out,
            kept_all[layer_count],
        )
        in_shards[layer_count], out_shards[layer_count] = (
            lax.psum_scatter(grad_in, "fsdp", scatter_dimension=1, tiled=True),
            lax.psum_scatter(grad_out, "fsdp", scatter_dimension=1, tiled=True),
        )
        mod_grads[layer_count] = mod_grad
        in_bias_grads[layer_count] = bias_in_grad
        out_bias_grads[layer_count] = bias_out_grad
    d_patch = upstream.astype(jnp.bfloat16)
    patch_grad = outer_sum(latents, d_patch)
    patch_bias_grad = column_sum(d_patch)
    d_modulation = jnp.concatenate(mod_grads + [d_final], 1)
    d_cond = exact_dot(d_modulation, cond_full.astype(jnp.float32).T)
    d_condition = local_back(silu, condition, d_cond)
    d_hidden = exact_dot(d_condition, embed_full[FREQ : FREQ + MODEL_WIDTH].astype(jnp.float32).T)
    d_pre = local_back(silu, pre_time, d_hidden)
    cond_grad = exact_dot(cond_low.astype(jnp.float32).T, d_modulation)
    class_grad = exact_dot(onehot.astype(jnp.float32).T, d_condition)
    time_two_grad = exact_dot(hidden_t.astype(jnp.float32).T, d_condition)
    time_one_grad = exact_dot(features.astype(jnp.float32).T, d_pre)
    embed_grad = jnp.concatenate([time_one_grad, time_two_grad, patch_grad, class_grad], 0)
    embed_shard, cond_shard = (
        lax.psum_scatter(embed_grad, "fsdp", scatter_dimension=1, tiled=True),
        lax.psum_scatter(cond_grad, "fsdp", scatter_dimension=1, tiled=True),
    )
    bias_grad = jnp.concatenate(
        [jnp.sum(d_pre, 0), jnp.sum(d_condition, 0), patch_bias_grad, jnp.sum(d_modulation, 0)]
        + in_bias_grads
        + out_bias_grads
        + [head_bias_grad]
    )
    head_total, bias_total, loss_total = lax.psum((head_grad, bias_grad, loss_part), "fsdp")
    in_stack = jnp.stack(in_shards, 0)
    out_stack = jnp.stack(out_shards, 0)
    shard_squares = (
        jnp.sum(embed_shard * embed_shard)
        + jnp.sum(cond_shard * cond_shard)
        + jnp.sum(in_stack * in_stack)
        + jnp.sum(out_stack * out_stack)
    )
    square_total = lax.psum(shard_squares, "fsdp")
    grad_norm = jnp.sqrt(
        square_total + jnp.sum(head_total * head_total) + jnp.sum(bias_total * bias_total)
    )
    factor = jnp.minimum(1.0, clip_limit / grad_norm)
    embed_up = adam_step(embed_w, embed_m, embed_v, embed_shard * factor)
    cond_up = adam_step(cond_w, cond_m, cond_v, cond_shard * factor)
    in_up = adam_step(layer_input_weights, in_m, in_v, in_stack * factor)
    out_up = adam_step(layer_output_weights, out_m, out_v, out_stack * factor)
    head_up = adam_step(head_w, head_m, head_v, head_total * factor)
    bias_up = adam_step(biases, bias_m, bias_v, bias_total * factor)
    return (
        loss_total,
        grad_norm,
        embed_up[0],
        embed_up[1],
        embed_up[2],
        cond_up[0],
        cond_up[1],
        cond_up[2],
        in_up[0],
        in_up[1],
        in_up[2],
        out_up[0],
        out_up[1],
        out_up[2],
        head_up[0],
        head_up[1],
        head_up[2],
        bias_up[0],
        bias_up[1],
        bias_up[2],
    )


MESH_ID = pl.DeviceIdType.MESH
AXIS = "fsdp"


class Place:
    def __init__(self):
        me = lax.axis_index(AXIS)
        self.me = me
        self.core = core = me % 2
        x = (me // 2) % 2
        y = (me // 4) % 2
        self.z = me // 8
        self.chip = me // 2
        step_x = 1 - 2 * x
        step_y = 2 - 4 * y
        self.step_a = step_x + core * (step_y - step_x)
        self.step_b = step_y + core * (step_x - step_y)
        self.dev_a = me + 2 * self.step_a
        self.dev_b = me + 2 * self.step_b
        self.sibling = me + 1 - 2 * core

    def other(self, dz, flip_a=0, flip_b=0):
        return self.chip + 4 * dz + flip_a * self.step_a + flip_b * self.step_b

    def valid(self, dz):
        return jnp.logical_and(self.z + dz >= 0, self.z + dz < 4)

    def greet(self):
        barrier = pltpu.get_barrier_semaphore()
        for device in (self.sibling, self.dev_a, self.dev_b):
            pl.semaphore_signal(barrier, inc=1, device_id=(device,), device_id_type=MESH_ID)
        for sign in (-1, 1):

            @pl.when(self.valid(sign))
            def _():
                pl.semaphore_signal(barrier, inc=1, device_id=(self.me + 8 * sign,), device_id_type=MESH_ID)

        pl.semaphore_wait(barrier, 4 + self.z * (3 - self.z) // 2)


def remote(src, dst, send_sem, recv_sem, device):
    return pltpu.make_async_remote_copy(
        src_ref=src, dst_ref=dst, send_sem=send_sem, recv_sem=recv_sem, device_id=(device,), device_id_type=MESH_ID
    )


class Gather:
    def __init__(self, place, own, stage, piece, full, sems):
        self.p, self.own, self.stage, self.piece, self.full = place, own, stage, piece, full
        self.xch_send, self.xch_recv, self.local, self.send, self.recv, self.sib_recv = sems
        self.sent = []

    def slot(self, a, chip):
        rows, half = self.piece[a].shape
        return self.full[a].at[
            pl.ds(pl.multiple_of(chip * rows, rows), rows), pl.ds(pl.multiple_of(self.p.core * half, half), half)
        ]

    def push(self, a, k, src, chip, device, sem, cond=None):
        def act(what):
            copy = remote(src(), self.slot(a, chip()), self.send.at[a, k], sem.at[a, chip()], device())
            getattr(copy, what)()

        def guarded(what):
            if cond is None:
                act(what)
            else:
                pl.when(cond())(functools.partial(act, what))

        guarded("start")
        self.sent.append(functools.partial(guarded, "wait_send"))

    def store_own(self, a):
        return pltpu.make_async_copy(self.piece[a], self.slot(a, self.p.chip), self.local.at[a])

    def begin(self):
        core = self.p.core
        copies = []
        for a in range(2):
            rows, half = self.own[a].shape[0], self.piece[a].shape[1]
            dst = self.stage[a].at[pl.ds(pl.multiple_of(core * rows, 8), rows), :]
            away = remote(
                self.own[a].at[:, pl.ds(pl.multiple_of((1 - core) * half, half), half)],
                dst,
                self.xch_send.at[a],
                self.xch_recv.at[a],
                self.p.sibling,
            )
            away.start()
            keep = pltpu.make_async_copy(
                self.own[a].at[:, pl.ds(pl.multiple_of(core * half, half), half)], dst, self.local.at[a]
            )
            keep.start()
            copies.append((away, keep))
        for a in range(2):
            copies[a][0].wait()
            copies[a][1].wait()
            self.piece[a][...] = self.stage[a][...].astype(jnp.bfloat16)
            self.store_own(a).start()
            piece, here = (lambda a=a: self.piece[a]), (lambda: self.p.chip)
            for sign in (-1, 1):
                self.push(
                    a, 0 if sign < 0 else 3, piece, here, lambda sign=sign: self.p.me + 8 * sign, self.recv,
                    lambda sign=sign: self.p.valid(sign),
                )
            self.push(a, 6, piece, here, lambda: self.p.dev_a, self.recv)
            self.push(a, 10, piece, here, lambda: self.p.dev_b, self.recv)
            self.push(a, 18, piece, here, lambda: self.p.sibling, self.sib_recv)

    def arrive(self, a, chip):
        slot = self.slot(a, chip)
        pltpu.make_async_copy(slot, slot, self.recv.at[a, chip]).wait()

    def pass_on(self, dz, flip_a, flip_b, targets):
        def here():
            return self.p.valid(dz)

        def chip():
            return self.p.other(dz, flip_a, flip_b)

        for a in range(2):
            pl.when(here())(lambda a=a: self.arrive(a, chip()))
            for k, device, sem, extra in targets:
                self.push(
                    a, k, lambda a=a: self.slot(a, chip()), chip, device, sem,
                    here if extra is None else lambda extra=extra: jnp.logical_and(here(), self.p.valid(extra)),
                )

    def z_step(self, dist):
        for sign in (-1, 1):
            rel = (sign * dist) % 4
            targets = [
                (6 + rel, lambda: self.p.dev_a, self.recv, None),
                (10 + rel, lambda: self.p.dev_b, self.recv, None),
                (18 + rel, lambda: self.p.sibling, self.sib_recv, None),
            ]
            if dist < 3:
                onward = ((0 if sign > 0 else 3) + dist, lambda sign=sign: self.p.me - 8 * sign, self.recv, -sign)
                targets.insert(0, onward)
            self.pass_on(sign * dist, 0, 0, targets)

    def a_step(self, dist):
        for sign in (-1, 1) if dist else (1,):
            rel = (sign * dist) % 4
            self.pass_on(sign * dist, 1, 0, [
                (14 + rel, lambda: self.p.dev_b, self.recv, None), (22 + rel, lambda: self.p.sibling, self.sib_recv, None)
            ])

    def b_step(self, dist, flip_a):
        for sign in (-1, 1) if dist else (1,):
            rel = (sign * dist) % 4
            self.pass_on(
                sign * dist, flip_a, 1, [(26 + 4 * flip_a + rel, lambda: self.p.sibling, self.sib_recv, None)]
            )

    def finish(self):
        for a in range(2):
            rows, half = self.piece[a].shape

            def take(chip, carry):
                slot = self.full[a].at[
                    pl.ds(pl.multiple_of(chip * rows, rows), rows),
                    pl.ds(pl.multiple_of((1 - self.p.core) * half, half), half),
                ]
                pltpu.make_async_copy(slot, slot, self.sib_recv.at[a, chip]).wait()
                return carry

            lax.fori_loop(0, 16, take, 0)
            self.store_own(a).wait()
        for wait in self.sent:
            wait()


GATHER_SEMS = [
    pltpu.SemaphoreType.DMA((2,)),
    pltpu.SemaphoreType.DMA((2,)),
    pltpu.SemaphoreType.DMA((2,)),
    pltpu.SemaphoreType.DMA((2, 34)),
    pltpu.SemaphoreType.DMA((2, 16)),
    pltpu.SemaphoreType.DMA((2, 16)),
]


def gather_scratch(shapes):
    return (
        [pltpu.VMEM(shape, jnp.float32) for shape in shapes]
        + [pltpu.VMEM(shape, jnp.bfloat16) for shape in shapes]
        + GATHER_SEMS
    )


def piece_shapes(shapes):
    return [(2 * rows, width // 2) for rows, width in shapes]


ORDER = (3, 0, 2, 1)


class Scatter:
    def __init__(self, place, grads, totals, bufs, sems, mine=None):
        self.p, self.grad, self.total, self.mine = place, grads, totals, mine
        count = len(grads)
        self.arrays = range(count)
        self.sib, self.from_b, self.from_a, self.line, self.part, self.last = (
            bufs[count * i : count * i + count] for i in range(6)
        )
        (self.load_sem, self.sib_send, self.sib_recv, self.b_send, self.b_recv, self.a_send, self.a_recv, self.up_send,
         self.up_recv, self.down_send, self.down_recv, self.end_send, self.end_recv, self.end_local) = sems

    def rows_of(self, a, chip, core):
        rows, half = self.part[a].shape
        return self.grad[a].at[
            pl.ds(pl.multiple_of(chip * rows, rows), rows), pl.ds(pl.multiple_of(core * half, half), half)
        ]

    def chip_of(self, z, flip_a, flip_b):
        return self.p.other(z - self.p.z, flip_a, flip_b)

    def own(self, a, flip_b, flip_a, z):
        if self.mine is None:
            return self.rows_of(a, self.chip_of(z, flip_a, flip_b), self.p.core)
        return self.mine[a].at[8 * flip_b + 4 * flip_a + z]

    def load(self, a, flip_b, flip_a, z):
        return pltpu.make_async_copy(
            self.rows_of(a, self.chip_of(z, flip_a, flip_b), self.p.core),
            self.own(a, flip_b, flip_a, z),
            self.load_sem.at[a, 8 * flip_b + 4 * flip_a + z],
        )

    def lend(self, a, flip_b, flip_a, z):
        k = 8 * flip_b + 4 * flip_a + z
        return remote(
            self.rows_of(a, self.chip_of(z, flip_b, flip_a), 1 - self.p.core),
            self.sib[a].at[k],
            self.sib_send.at[a, k],
            self.sib_recv.at[a, k],
            self.p.sibling,
        )

    def to_b(self, a, flip_a, z):
        k = 4 * flip_a + z
        return remote(
            self.own(a, 1, flip_a, z), self.from_b[a].at[k], self.b_send.at[a, k], self.b_recv.at[a, k], self.p.dev_b
        )

    def to_a(self, a, z):
        return remote(
            self.own(a, 0, 1, z), self.from_a[a].at[z], self.a_send.at[a, z], self.a_recv.at[a, z], self.p.dev_a
        )

    def to_z(self, a, z, sign, slot):
        send, recv = (self.up_send, self.up_recv) if sign > 0 else (self.down_send, self.down_recv)
        return remote(
            self.own(a, 0, 0, z), self.line[a].at[slot], send.at[a, z], recv.at[a, z], self.p.me + 8 * sign
        )

    def open(self, z):
        for flip_b, flip_a in ((1, 1), (1, 0), (0, 1), (0, 0)):
            for a in self.arrays:
                self.lend(a, flip_b, flip_a, z).start()
                if self.mine is not None:
                    self.load(a, flip_b, flip_a, z).start()

    def open_all(self):
        for z in ORDER:
            self.open(z)

    def pair(self, a, flip_b, flip_a, z):
        if self.mine is not None:
            self.load(a, flip_b, flip_a, z).wait()
        self.lend(a, flip_b, flip_a, z).wait_recv()
        k = 8 * flip_b + 4 * flip_a + z
        return self.own(a, flip_b, flip_a, z)[...].astype(jnp.float32) + self.sib[a][k].astype(jnp.float32)

    def cross_b(self, z):
        for flip_a in (1, 0):
            for a in self.arrays:
                self.own(a, 1, flip_a, z)[...] = self.pair(a, 1, flip_a, z).astype(jnp.bfloat16)
                self.to_b(a, flip_a, z).start()

    def cross_a(self, z):
        for a in self.arrays:
            value = self.pair(a, 0, 1, z)
            self.to_b(a, 1, z).wait_recv()
            self.own(a, 0, 1, z)[...] = (value + self.from_b[a][4 + z].astype(jnp.float32)).astype(jnp.bfloat16)
            self.to_a(a, z).start()

    def along_z(self, z):
        place = self.p
        for a in self.arrays:
            value = self.pair(a, 0, 0, z)
            self.to_b(a, 0, z).wait_recv()
            value = value + self.from_b[a][z].astype(jnp.float32)
            self.to_a(a, z).wait_recv()
            self.part[a][...] = value + self.from_a[a][z].astype(jnp.float32)

            @pl.when(jnp.logical_and(place.z < z, place.z > 0))
            def _():
                self.to_z(a, z, 1, z).wait_recv()
                self.part[a][...] += self.line[a][z].astype(jnp.float32)

            @pl.when(jnp.logical_and(place.z > z, place.z < 3))
            def _():
                self.to_z(a, z, -1, z).wait_recv()
                self.part[a][...] += self.line[a][z].astype(jnp.float32)

            @pl.when(place.z != z)
            def _():
                self.own(a, 0, 0, z)[...] = self.part[a][...].astype(jnp.bfloat16)

            @pl.when(place.z < z)
            def _():
                self.to_z(a, z, 1, z).start()

            @pl.when(place.z > z + 1)
            def _():
                self.to_z(a, z, -1, z).start()

            @pl.when(place.z == z + 1)
            def _():
                self.to_z(a, z, -1, 4).start()

            @pl.when(place.z == z)
            def _():
                self.last[a][...] = self.part[a][...]

    def end_copies(self, a):
        core = self.p.core
        rows, width = self.total[a].shape
        dst = self.total[a].at[:, pl.ds(pl.multiple_of(core * (width // 2), width // 2), width // 2)]
        away = remote(
            self.last[a].at[pl.ds(pl.multiple_of((1 - core) * rows, 8), rows), :],
            dst,
            self.end_send.at[a],
            self.end_recv.at[a],
            self.p.sibling,
        )
        keep = pltpu.make_async_copy(
            self.last[a].at[pl.ds(pl.multiple_of(core * rows, 8), rows), :], dst, self.end_local.at[a]
        )
        return away, keep

    def close(self):
        place = self.p
        for a in self.arrays:

            @pl.when(place.z > 0)
            def _():
                self.to_z(a, place.z, 1, place.z).wait_recv()
                self.last[a][...] += self.line[a][place.z].astype(jnp.float32)

            @pl.when(place.z < 3)
            def _():
                self.to_z(a, place.z, -1, 4).wait_recv()
                self.last[a][...] += self.line[a][4].astype(jnp.float32)

            for copy in self.end_copies(a):
                copy.start()

    def end(self):
        for a in self.arrays:
            for copy in self.end_copies(a):
                copy.wait()

    def finish(self):
        def step(z, carry):
            for a in self.arrays:
                for flip_b in range(2):
                    for flip_a in range(2):
                        self.lend(a, flip_b, flip_a, z).wait_send()
                for flip_a in range(2):
                    self.to_b(a, flip_a, z).wait_send()
                self.to_a(a, z).wait_send()

                @pl.when(self.p.z < z)
                def _():
                    self.to_z(a, z, 1, z).wait_send()

                @pl.when(self.p.z > z)
                def _():
                    self.to_z(a, z, -1, z).wait_send()

            return carry

        lax.fori_loop(0, 4, step, 0)

    def steps(self):
        out = []
        for k in range(6):
            if k < 4:
                out.append(functools.partial(self.cross_b, ORDER[k]))
            if 0 <= k - 1 < 4:
                out.append(functools.partial(self.cross_a, ORDER[k - 1]))
            if 0 <= k - 2 < 4:
                out.append(functools.partial(self.along_z, ORDER[k - 2]))
        return out + [self.close, self.end, self.finish]


def scatter_scratch(shapes):
    scratch = []
    for count, kind in ((16, jnp.bfloat16), (8, jnp.bfloat16), (4, jnp.bfloat16), (5, jnp.bfloat16),
                        (0, jnp.float32), (0, jnp.float32)):
        scratch += [pltpu.VMEM(((count,) if count else ()) + shape, kind) for shape in shapes]
    counts = (16, 16, 16, 8, 8, 4, 4, 4, 4, 4, 4)
    several = len(shapes)
    return (
        scratch
        + [pltpu.SemaphoreType.DMA((several, n)) for n in counts]
        + [pltpu.SemaphoreType.DMA((several,))] * 3
    )


def dot_nt(left, right):
    return lax.dot_general(left, right, (((1,), (1,)), ((), ())), preferred_element_type=jnp.float32)


def dot_tn(left, right):
    return lax.dot_general(left, right, (((0,), (0,)), ((), ())), preferred_element_type=jnp.float32)


def thirds(value):
    high = value.astype(jnp.bfloat16)
    rest = value - high.astype(jnp.float32)
    mid = rest.astype(jnp.bfloat16)
    return high, mid, (rest - mid.astype(jnp.float32)).astype(jnp.bfloat16)


def silu_slope(value):
    gate = jax.nn.sigmoid(value)
    return gate * (1 + value * (1 - gate))


class Swap:
    def __init__(self, me, devices, index, src_of, dst, send, recv):
        self.me, self.n, self.i, self.src_of, self.dst, self.send, self.recv = me, devices, index, src_of, dst, send, recv

    def copy(self, peer, slot):
        return remote(self.src_of(peer), self.dst.at[slot], self.send.at[self.i, peer], self.recv.at[self.i, slot], peer)

    def each(self, step):
        def run(k, carry):
            step(lax.rem(self.me + k, self.n))
            return carry

        lax.fori_loop(1, self.n, run, 0)

    def start(self):
        self.each(lambda peer: self.copy(peer, self.me).start())

    def arrive(self):
        self.each(lambda peer: self.copy(peer, peer).wait_recv())

    def sent(self):
        self.each(lambda peer: self.copy(peer, self.me).wait_send())


def greet_all(devices):
    barrier = pltpu.get_barrier_semaphore()
    me = lax.axis_index(AXIS)

    def hello(k, carry):
        pl.semaphore_signal(barrier, inc=1, device_id=(lax.rem(me + k, devices),), device_id_type=MESH_ID)
        return carry

    lax.fori_loop(1, devices, hello, 0)
    pl.semaphore_wait(barrier, devices - 1)


def modulate_steps(devices, ins, outs, bufs, sems):
    msg, wt1, wt2, wcls, wcond, bt1, bt2, bcond = ins
    mods, pre, cond, hid_all, low_all, feat_all, lab_all, got = outs
    hid, low, away = bufs
    me = lax.axis_index(AXIS)
    images, cols = 4, wt1.shape[0]
    swaps = [
        Swap(me, devices, 0, lambda peer: msg, got, *sems),
        Swap(me, devices, 1, lambda peer: hid.at[me], hid, *sems),
        Swap(me, devices, 2, lambda peer: low.at[me], low, *sems),
        Swap(me, devices, 3, lambda peer: away.at[peer], mods, *sems),
    ]

    def first():
        swaps[0].start()
        got[me] = msg[...]

    def second():
        swaps[0].arrive()
        for j in range(devices):
            feat_all[images * j : images * (j + 1), :] = got[j, :, :FREQ]
            lab_all[images * j : images * (j + 1), :] = got[j, :, FREQ : FREQ + 128]
        pre[...] = dot_nt(wt1[...].astype(jnp.bfloat16), feat_all[...].astype(jnp.bfloat16)) + bt1[...]
        hidden = silu(pre[...])
        pad = jnp.zeros((hid.shape[1] - cols, hidden.shape[1]), jnp.float32)
        hid[me] = jnp.concatenate([hidden, pad], 0).astype(jnp.bfloat16)
        swaps[1].start()
        classes = lax.broadcasted_iota(jnp.int32, (lab_all.shape[0], wcls.shape[1]), 1).astype(jnp.float32)
        labels = jnp.concatenate([lab_all[...]] * (wcls.shape[1] // 128), 1)
        onehot = (labels == classes).astype(jnp.bfloat16)
        cond[...] = dot_nt(wcls[...].astype(jnp.bfloat16), onehot) + bt2[...]

    def third():
        swaps[1].arrive()
        for j in range(devices):
            hid_all[cols * j : cols * (j + 1), :] = hid[j].astype(jnp.float32)[:cols]
        cond[...] += jnp.dot(
            wt2[...].astype(jnp.bfloat16), hid_all[...].astype(jnp.bfloat16), preferred_element_type=jnp.float32
        )
        value = silu(cond[...])
        pad = jnp.zeros((low.shape[1] - cols, value.shape[1]), jnp.float32)
        low[me] = jnp.concatenate([value, pad], 0).astype(jnp.bfloat16)
        swaps[2].start()

    def fourth():
        swaps[2].arrive()
        for j in range(devices):
            low_all[cols * j : cols * (j + 1), :] = low[j].astype(jnp.float32)[:cols]
        rows = dot_nt(low_all[...].T.astype(jnp.bfloat16), wcond[...].astype(jnp.bfloat16)) + bcond[...]
        for j in range(devices):
            away[j] = rows[images * j : images * (j + 1)]
        swaps[3].start()
        mods[me] = away[me]

    def last():
        swaps[3].arrive()
        for swap in swaps:
            swap.sent()

    return [first, second, third, fourth, last]


SETTLE_INS = ("d_mods", "wt2", "wcond", "pre", "cond", "hid_all", "low_all", "feat_all", "lab_all", "g_head", "g_hbias", "loss",
              "g_patch", "g_pbias", "bin0", "bin1", "bout0", "bout1", "done_in", "done_out")


def settle_steps(devices, ins, outs, bufs, sems, shards):
    d_mods, pre, lab_all = ins["d_mods"], ins["pre"], ins["lab_all"]
    g_cond, g_t1, g_t2, g_cls, merged = outs
    dm_got, dm_all, rows, small, small_got, dc_part, dc_got, dh_part, dh_got, note = bufs
    me = lax.axis_index(AXIS)
    images, width = d_mods.shape[1:]
    cols = pre.shape[0]
    swaps = [
        Swap(me, devices, 0, lambda peer: d_mods.at[peer], dm_got, *sems),
        Swap(me, devices, 1, lambda peer: small.at[peer], small_got, *sems),
        Swap(me, devices, 2, lambda peer: dc_part.at[peer], dc_got, *sems),
        Swap(me, devices, 3, lambda peer: dh_part.at[peer], dh_got, *sems),
        Swap(me, devices, 4, lambda peer: note, merged, *sems),
    ]
    keep = {}

    def share(value, part, got):
        pad = jnp.zeros((32 - cols, value.shape[1]), jnp.float32)
        for j in range(devices):
            part[j] = jnp.concatenate([value[cols * j : cols * (j + 1)], pad], 0).astype(jnp.bfloat16)
        got[me] = part[me]

    def collect(got):
        return jnp.sum(got[...].astype(jnp.float32), 0)[:cols]

    def parts_of(value):
        return sum(
            jnp.where(lax.broadcasted_iota(jnp.int32, (1, 128), 1) == k, part.astype(jnp.float32), 0.0)
            for k, part in enumerate(thirds(value))
        )

    def first():
        swaps[0].start()
        dm_got[me] = d_mods[me]
        dm_all[...] = jnp.zeros_like(dm_all)
        rows[...] = jnp.zeros_like(rows)
        for k in range(MODEL_WIDTH // 128):
            span = slice(128 * k, 128 * (k + 1))
            rows[16 * k : 16 * (k + 1), :] = ins["g_patch"][:, span]
            rows[96 + 32 * k : 96 + 32 * (k + 1), :] = ins["g_head"][:, span]
        at = 288
        for name in ("g_pbias", "bin0", "bin1", "bout0", "bout1"):
            for k in range(ins[name].shape[1] // 128):
                rows[at : at + 1, :] = ins[name][:, 128 * k : 128 * (k + 1)]
                at += 1
        square = ins["g_hbias"].shape
        diagonal = lax.broadcasted_iota(jnp.int32, square, 0) == lax.broadcasted_iota(jnp.int32, square, 1)
        rows[at : at + 1, :] = jnp.sum(jnp.where(diagonal, ins["g_hbias"][...], 0.0), 0, keepdims=True)
        for j in range(devices):
            small[j] = rows[16 * j : 16 * (j + 1), :].astype(jnp.bfloat16)
        swaps[1].start()
        small_got[me] = small[me]

    def second():
        swaps[0].arrive()
        for j in range(devices):
            dm_all[images * j : images * (j + 1), :width] = dm_got[j]
        turned = dm_all[...].T[:width]
        parts = thirds(turned)
        weight = ins["wcond"][...].astype(jnp.bfloat16)
        share(sum(dot_tn(weight, part) for part in parts), dc_part, dc_got)
        swaps[2].start()
        low = ins["low_all"][...].astype(jnp.bfloat16)
        g_cond[...] = sum(dot_nt(part, low) for part in parts)
        swaps[1].arrive()

    def third():
        swaps[2].arrive()
        d_cond = collect(dc_got) * silu_slope(ins["cond"][...])
        parts = thirds(d_cond)
        weight = ins["wt2"][...].astype(jnp.bfloat16)
        share(sum(dot_tn(weight, part) for part in parts), dh_part, dh_got)
        swaps[3].start()
        classes = lax.broadcasted_iota(jnp.int32, (lab_all.shape[0], g_cls.shape[1]), 1).astype(jnp.float32)
        labels = jnp.concatenate([lab_all[...]] * (g_cls.shape[1] // 128), 1)
        onehot = (labels == classes).astype(jnp.bfloat16)
        g_cls[...] = sum(jnp.dot(part, onehot, preferred_element_type=jnp.float32) for part in parts)
        hidden = ins["hid_all"][...].astype(jnp.bfloat16)
        g_t2[...] = sum(dot_nt(part, hidden) for part in parts)
        ones = jnp.ones((8, lab_all.shape[0]), jnp.bfloat16)
        keep["t2"] = sum(dot_nt(ones, part) for part in parts)

    def fourth():
        swaps[3].arrive()
        d_pre = collect(dh_got) * silu_slope(pre[...])
        parts = thirds(d_pre)
        feats = ins["feat_all"][...].astype(jnp.bfloat16)
        g_t1[...] = sum(jnp.dot(part, feats, preferred_element_type=jnp.float32) for part in parts)
        ones = jnp.ones((8, lab_all.shape[0]), jnp.bfloat16)
        keep["t1"] = sum(dot_nt(ones, part) for part in parts)
        total = jnp.zeros((1, 1), jnp.float32)
        for ref in (g_cond, g_t1, g_t2, g_cls, ins["done_in"], ins["done_out"]):
            total = total + jnp.sum(ref[...] * ref[...])
        keep["squares"] = total

    def message():
        total = keep["squares"]
        for ref in shards:
            total = total + jnp.sum(ref[...] * ref[...])
        bias_cond = jnp.sum(dm_all[...], 0, keepdims=True)
        blank = jnp.zeros((1, 128 - cols), jnp.float32)
        lines = [jnp.concatenate([keep[name][0:1, :], blank], 1) for name in ("t1", "t2")]
        lines.append(parts_of(total))
        lines.append(parts_of(ins["loss"][0:1, :]))
        lines += [bias_cond[:, 128 * k : 128 * (k + 1)] for k in range(3)]
        lines.append(jnp.zeros((9, 128), jnp.float32))
        note[...] = jnp.concatenate([jnp.sum(small_got[...].astype(jnp.float32), 0)] + lines, 0).astype(jnp.bfloat16)
        swaps[4].start()
        merged[me] = note[...]

    def last():
        swaps[4].arrive()
        for swap in swaps:
            swap.sent()

    return [first, second, third, fourth, message, last]


def dot_nn(left, right):
    return lax.dot_general(left, right, (((1,), (0,)), ((), ())), preferred_element_type=jnp.float32)


def norm_parts(value):
    centered = value - jnp.mean(value, -1, keepdims=True)
    scale = lax.rsqrt(jnp.mean(centered * centered, -1, keepdims=True) + 1e-06)
    return centered * scale, scale


def norm_back(normed, scale, d_normed):
    inner = jnp.mean(d_normed * normed, -1, keepdims=True)
    return scale * (d_normed - jnp.mean(d_normed, -1, keepdims=True) - normed * inner)


GELU_C = math.sqrt(2.0 / math.pi)


def gelu_value(u):
    return 0.5 * u * (1.0 + jnp.tanh(GELU_C * (u + 0.044715 * u * u * u)))


def gelu_slope(u):
    square = u * u
    t = jnp.tanh(GELU_C * u * (1.0 + 0.044715 * square))
    return 0.5 * (1.0 + t) + 0.5 * u * (1.0 - t * t) * (GELU_C * (1.0 + 3 * 0.044715 * square))


def head_masks(shape):
    low_half = lax.broadcasted_iota(jnp.int32, shape, 1) < HEAD_DIM
    return low_half, jnp.logical_not(low_half)


class Weights:
    def __init__(self, hbm, vmem, sems):
        w_in, w_out = hbm
        self.w_in, self.w_out = vmem
        cut = 3 * MODEL_WIDTH
        spans = [
            (w_in.at[pl.ds(0, cut), :], self.w_in.at[pl.ds(0, cut), :]),
            (w_out.at[:, pl.ds(0, MODEL_WIDTH)], self.w_out.at[:, pl.ds(0, MODEL_WIDTH)]),
            (w_in.at[pl.ds(cut, FF), :], self.w_in.at[pl.ds(cut, FF), :]),
            (w_out.at[:, pl.ds(MODEL_WIDTH, FF)], self.w_out.at[:, pl.ds(MODEL_WIDTH, FF)]),
        ]
        self.copies = [pltpu.make_async_copy(src, dst, sems.at[i]) for i, (src, dst) in enumerate(spans)]

    def start(self, order):
        @pl.when(pl.program_id(0) == 0)
        def _():
            for i in order:
                self.copies[i].start()

    def need(self, i):
        @pl.when(pl.program_id(0) == 0)
        def _():
            self.copies[i].wait()


def forward_image(x_ref, mod, weights, b_in, b_out, outs, hook=lambda: None):
    h1, qkv, probs, o, a, x1, h2, u, g, f = outs
    shift1, scale1, gate1, shift2, scale2, gate2 = (mod[0, i : i + 1, :] for i in range(6))
    width = MODEL_WIDTH
    hook()
    x = x_ref[...]
    h1[...] = (norm_parts(x)[0] * (1 + scale1) + shift1).astype(jnp.bfloat16)
    weights.need(0)
    for j in range(3):
        span = slice(j * width, (j + 1) * width)
        qkv[:, span] = (dot_nt(h1[...], weights.w_in[span, :]) + b_in[:, span]).astype(jnp.bfloat16)
    hook()
    for pair in range(HEADS // 2):
        lanes = slice(128 * pair, 128 * (pair + 1))
        q, k, v = (qkv[:, j * width + 128 * pair : j * width + 128 * (pair + 1)] for j in range(3))
        q = q * jnp.bfloat16(HEAD_DIM**-0.5)
        zero = jnp.zeros_like(q)
        mixed = None
        for half, mask in enumerate(head_masks(q.shape)):
            scores = dot_nt(jnp.where(mask, q, zero), k)
            expo = jnp.exp(scores - jnp.max(scores, -1, keepdims=True))
            weight = (expo * pl.reciprocal(jnp.sum(expo, -1, keepdims=True))).astype(jnp.bfloat16)
            probs[0, 2 * pair + half] = weight
            term = dot_nn(weight, jnp.where(mask, v, zero))
            mixed = term if mixed is None else mixed + term
        o[:, lanes] = mixed.astype(jnp.bfloat16)
        hook()
    weights.need(1)
    branch = dot_nt(o[...], weights.w_out[:, :width]) + b_out[:, :width]
    a[...] = branch.astype(jnp.bfloat16)
    x1[...] = x + gate1 * branch
    h2[...] = (norm_parts(x1[...])[0] * (1 + scale2) + shift2).astype(jnp.bfloat16)
    hook()
    weights.need(2)
    weights.need(3)
    total = None
    for j in range(FF // width):
        span = slice(j * width, (j + 1) * width)
        rows = slice((3 + j) * width, (4 + j) * width)
        value = dot_nt(h2[...], weights.w_in[rows, :]) + b_in[:, rows]
        u[:, span] = value.astype(jnp.bfloat16)
        g[:, span] = gelu_value(value).astype(jnp.bfloat16)
        term = dot_nt(g[:, span], weights.w_out[:, (1 + j) * width : (2 + j) * width])
        total = term if total is None else total + term
        hook()
    ffn = total + b_out[:, width:]
    f[...] = ffn.astype(jnp.bfloat16)
    return x1[...] + gate2 * ffn


def head_kernel(scale_out, x, mod, w_in, w_out, b_in, b_out, final, head_t, b_head, targets_t, *refs):
    outs, (dx, d_final, g_head, g_bias, loss), (vm_in, vm_out, sems) = refs[:10], refs[10:15], refs[15:]
    weights = Weights((w_in, w_out), (vm_in, vm_out), sems)
    weights.start((0, 1, 2, 3))
    last = forward_image(x, mod, weights, b_in, b_out, outs)
    normed, scale = norm_parts(last)
    shift_row, scale_row = final[0, 0:1, :], final[0, 1:2, :]
    shaped = (normed * (1 + scale_row) + shift_row).astype(jnp.bfloat16)
    low = head_t[...].astype(jnp.bfloat16)
    error = dot_nt(low, shaped) + b_head[...] - targets_t[0]
    d_out = (error * scale_out).astype(jnp.bfloat16)

    @pl.when(pl.program_id(0) == 0)
    def _():
        g_head[...] = jnp.zeros_like(g_head)
        g_bias[...] = jnp.zeros_like(g_bias)
        loss[...] = jnp.zeros_like(loss)

    g_head[...] += dot_nn(d_out, shaped)
    g_bias[...] += jnp.sum(d_out.astype(jnp.float32), 1, keepdims=True)
    loss[...] += jnp.sum(error * error)
    d_shaped = dot_tn(d_out, low)
    d_final[0, 0:1, :] = jnp.sum(d_shaped, 0, keepdims=True)
    d_final[0, 1:2, :] = jnp.sum(d_shaped * normed, 0, keepdims=True)
    dx[...] = norm_back(normed, scale, d_shaped * (1 + scale_row))


WEIGHT_SCRATCH = [
    pltpu.VMEM((IW, MODEL_WIDTH), jnp.bfloat16),
    pltpu.VMEM((MODEL_WIDTH, OW), jnp.bfloat16),
    pltpu.SemaphoreType.DMA((4,)),
]


def token_block(width):
    return pl.BlockSpec((SEQ, width), lambda i: (i, 0))


def image_block(*dims):
    return pl.BlockSpec((1,) + dims, lambda i: (i,) + (0,) * len(dims))


def whole_block(*dims):
    return pl.BlockSpec(dims, lambda i: (0,) * len(dims))


def kept_shapes(images):
    tokens, width, low, full = images * SEQ, MODEL_WIDTH, jnp.bfloat16, jnp.float32
    shapes = [((tokens, width), low), ((tokens, 3 * width), low), ((images, HEADS, SEQ, SEQ), low), ((tokens, width), low),
              ((tokens, width), low), ((tokens, width), full), ((tokens, width), low), ((tokens, FF), low),
              ((tokens, FF), low), ((tokens, width), low)]
    specs = [token_block(s[1]) if len(s) == 2 else image_block(*s[1:]) for s, _ in shapes]
    return [jax.ShapeDtypeStruct(s, t) for s, t in shapes], specs


def forward_specs():
    any_block = pl.BlockSpec(memory_space=pl.ANY)
    return [token_block(MODEL_WIDTH), image_block(6, MODEL_WIDTH), any_block, any_block, whole_block(1, IW),
            whole_block(1, 2 * MODEL_WIDTH)]


def forward_head(ins, scale_out):
    images = ins[1].shape[0]
    shapes, specs = kept_shapes(images)
    extra = [(images * SEQ, MODEL_WIDTH), (images, 2, MODEL_WIDTH), (PO, MODEL_WIDTH), (PO, 128), (8, 128)]
    return pl.pallas_call(
        functools.partial(head_kernel, scale_out),
        grid=(images,),
        out_shape=shapes + [jax.ShapeDtypeStruct(s, jnp.float32) for s in extra],
        in_specs=forward_specs()
        + [image_block(2, MODEL_WIDTH), whole_block(PO, MODEL_WIDTH), whole_block(PO, 1), image_block(PO, SEQ)],
        out_specs=specs
        + [token_block(MODEL_WIDTH), image_block(2, MODEL_WIDTH), whole_block(PO, MODEL_WIDTH), whole_block(PO, 128),
           whole_block(8, 128)],
        scratch_shapes=WEIGHT_SCRATCH,
        compiler_params=pltpu.CompilerParams(vmem_limit_bytes=56 << 20),
        name="forward_head",
    )(*ins)


def backward_image(refs, mod, weights, outs, hook=lambda: None):
    up_ref, x_ref, x1_ref, probs, qkv, a, f, u = refs
    dx, d_qkv, d_u, d_f, d_a, d_mod, g_bin, g_bout = outs
    width = MODEL_WIDTH
    shift1, scale1, gate1, shift2, scale2, gate2 = (mod[0, i : i + 1, :] for i in range(6))

    @pl.when(pl.program_id(0) == 0)
    def _():
        g_bin[...] = jnp.zeros_like(g_bin)
        g_bout[...] = jnp.zeros_like(g_bout)

    def rows_sum(value):
        return jnp.sum(value.astype(jnp.float32), 0, keepdims=True)

    hook()
    upstream = up_ref[...]
    d_f[...] = (gate2 * upstream).astype(jnp.bfloat16)
    d_mod[0, 5:6, :] = rows_sum(f[...].astype(jnp.float32) * upstream)
    g_bout[:, width:] += rows_sum(d_f[...])
    weights.need(3)
    weights.need(2)
    d_h2 = None
    for j in range(FF // width):
        span = slice(j * width, (j + 1) * width)
        rows = slice((3 + j) * width, (4 + j) * width)
        d_g = dot_nn(d_f[...], weights.w_out[:, (1 + j) * width : (2 + j) * width])
        d_u[:, span] = (d_g * gelu_slope(u[:, span].astype(jnp.float32))).astype(jnp.bfloat16)
        g_bin[:, rows] += rows_sum(d_u[:, span])
        term = dot_nn(d_u[:, span], weights.w_in[rows, :])
        d_h2 = term if d_h2 is None else d_h2 + term
        hook()
    normed, scale = norm_parts(x1_ref[...])
    d_mod[0, 3:4, :] = rows_sum(d_h2)
    d_mod[0, 4:5, :] = rows_sum(d_h2 * normed)
    upstream = upstream + norm_back(normed, scale, d_h2 * (1 + scale2))
    d_mod[0, 2:3, :] = rows_sum(a[...].astype(jnp.float32) * upstream)
    d_a[...] = (gate1 * upstream).astype(jnp.bfloat16)
    g_bout[:, :width] += rows_sum(d_a[...])
    dx[...] = upstream
    weights.need(1)
    d_o = dot_nn(d_a[...], weights.w_out[:, :width]).astype(jnp.bfloat16)
    hook()
    root = HEAD_DIM**-0.5
    for pair in range(HEADS // 2):
        lanes = [slice(j * width + 128 * pair, j * width + 128 * (pair + 1)) for j in range(3)]
        q, k, v = (qkv[:, s] for s in lanes)
        d_mixed = d_o[:, 128 * pair : 128 * (pair + 1)]
        zero = jnp.zeros_like(q)
        sums = [None] * 3
        for half, mask in enumerate(head_masks(q.shape)):
            weight = probs[0, 2 * pair + half]
            full = weight.astype(jnp.float32)
            d_masked = jnp.where(mask, d_mixed, zero)
            d_probs = dot_nt(d_masked, v)
            d_scores = (full * (d_probs - jnp.sum(full * d_probs, -1, keepdims=True))).astype(jnp.bfloat16)
            terms = (
                dot_nn(d_scores, jnp.where(mask, k, zero)),
                dot_tn(d_scores, jnp.where(mask, q, zero)),
                dot_tn(weight, d_masked),
            )
            sums = [t if s is None else s + t for s, t in zip(sums, terms)]
        d_qkv[:, lanes[0]] = (sums[0] * root).astype(jnp.bfloat16)
        d_qkv[:, lanes[1]] = (sums[1] * root).astype(jnp.bfloat16)
        d_qkv[:, lanes[2]] = sums[2].astype(jnp.bfloat16)
        hook()
    weights.need(0)
    d_h1 = None
    for j in range(3):
        span = slice(j * width, (j + 1) * width)
        g_bin[:, span] += rows_sum(d_qkv[:, span])
        term = dot_nn(d_qkv[:, span], weights.w_in[span, :])
        d_h1 = term if d_h1 is None else d_h1 + term
    normed, scale = norm_parts(x_ref[...])
    d_mod[0, 0:1, :] = rows_sum(d_h1)
    d_mod[0, 1:2, :] = rows_sum(d_h1 * normed)
    dx[...] += norm_back(normed, scale, d_h1 * (1 + scale1))
    hook()


def backward_kernel(mod, w_in, w_out, *refs):
    ins, outs, (vm_in, vm_out, sems) = refs[:8], refs[8:16], refs[16:]
    weights = Weights((w_in, w_out), (vm_in, vm_out), sems)
    weights.start((3, 2, 1, 0))
    backward_image(ins, mod, weights, outs)


def backward_block(mods, w_in, w_out, refs):
    images, width, low, full = mods.shape[0], MODEL_WIDTH, jnp.bfloat16, jnp.float32
    tokens = images * SEQ
    any_block = pl.BlockSpec(memory_space=pl.ANY)
    shapes = [((tokens, width), full), ((tokens, 3 * width), low), ((tokens, FF), low), ((tokens, width), low),
              ((tokens, width), low), ((images, 6, width), full), ((1, IW), full), ((1, 2 * width), full)]
    return pl.pallas_call(
        backward_kernel,
        grid=(images,),
        out_shape=[jax.ShapeDtypeStruct(s, t) for s, t in shapes],
        in_specs=[image_block(6, width), any_block, any_block, token_block(width), token_block(width), token_block(width),
                  image_block(HEADS, SEQ, SEQ), token_block(3 * width), token_block(width), token_block(width),
                  token_block(FF)],
        out_specs=[token_block(s[1]) for s, _ in shapes[:5]]
        + [image_block(6, width), whole_block(1, IW), whole_block(1, 2 * width)],
        scratch_shapes=WEIGHT_SCRATCH,
        compiler_params=pltpu.CompilerParams(vmem_limit_bytes=56 << 20),
        name="backward_block",
    )(mods, w_in, w_out, *refs)


def gather_steps(job):
    steps = [job.begin, functools.partial(job.a_step, 0)]
    for dist in (1, 2, 3):
        steps += [functools.partial(job.z_step, dist), functools.partial(job.a_step, dist)]
    for dist in range(4):
        steps += [functools.partial(job.b_step, dist, flip) for flip in range(2)]
    return steps + [job.finish]


class Hooks:
    def __init__(self, steps, slots, points):
        self.points, self.table = points, {}
        for step, slot in zip(steps, slots):
            self.table.setdefault((slot // points, slot % points), []).append(step)
        self.next = 0

    def __call__(self):
        point, self.next = self.next, self.next + 1
        for (turn, where), steps in sorted(self.table.items(), key=lambda item: item[0]):
            if where == point:

                @pl.when(pl.program_id(0) == turn)
                def _():
                    for step in steps:
                        step()


def start_kernel(devices, *refs):
    own, mod_ins, refs = refs[:2], refs[2:10], refs[10:]
    full, mod_outs, refs = refs[:2], refs[2:10], refs[10:]
    part, mod_bufs, mod_sems = refs[:10], refs[10:13], refs[13:]
    greet_all(devices)
    place = Place()
    job = Gather(place, own, part[:2], part[2:4], full, part[4:])
    first, second, third, fourth, last = modulate_steps(devices, mod_ins, mod_outs, mod_bufs, mod_sems)
    moves = gather_steps(job)
    for step in START_ORDER(first, second, third, fourth, last, moves):
        step()


def START_ORDER(first, second, third, fourth, last, moves):
    return [first] + moves[:2] + [second] + moves[2:4] + [third] + moves[4:6] + [fourth] + moves[6:-1] + [last, moves[-1]]


def gather_modulate(pair, ins):
    devices = lax.axis_size(AXIS)
    msg, wt1, wt2, wcls, wcond = ins[:5]
    cols, images = wt1.shape[0], devices * msg.shape[0]
    outs = [
        (devices, msg.shape[0], wcond.shape[0]), (cols, images), (cols, images), (devices * cols, images),
        (devices * cols, images), (images, FREQ), (images, 128), (devices,) + msg.shape,
    ]
    padded = -(-cols // 16) * 16
    vmem = pl.BlockSpec(memory_space=pltpu.VMEM)
    return pl.pallas_call(
        functools.partial(start_kernel, devices),
        out_shape=[jax.ShapeDtypeStruct((devices * a.shape[0], a.shape[1]), jnp.bfloat16) for a in pair]
        + [jax.ShapeDtypeStruct(shape, jnp.float32) for shape in outs],
        in_specs=[vmem] * 10,
        out_specs=[pl.BlockSpec(memory_space=pl.ANY)] * 2 + [vmem] * 8,
        scratch_shapes=gather_scratch(piece_shapes([a.shape for a in pair]))
        + [
            pltpu.VMEM((devices, padded, images), jnp.bfloat16),
            pltpu.VMEM((devices, padded, images), jnp.bfloat16),
            pltpu.VMEM((devices, msg.shape[0], wcond.shape[0]), jnp.float32),
            pltpu.SemaphoreType.DMA((4, devices)),
            pltpu.SemaphoreType.DMA((4, devices)),
        ],
        compiler_params=pltpu.CompilerParams(collective_id=3, has_side_effects=True, vmem_limit_bytes=56 << 20),
        name="gather_modulate",
    )(*pair, *ins)


FORWARD_POINTS = 13


def forward_gather_kernel(slots, x, mod, w_in, w_out, b_in, b_out, own_in, own_out, *refs):
    outs, x_out, full, refs = refs[:10], refs[10], refs[11:13], refs[13:]
    vm_in, vm_out, sems, part = refs[0], refs[1], refs[2], refs[3:]
    place = Place()
    job = Gather(place, (own_in, own_out), part[:2], part[2:4], full, part[4:])
    hooks = Hooks([place.greet] + gather_steps(job), slots, FORWARD_POINTS)
    weights = Weights((w_in, w_out), (vm_in, vm_out), sems)
    weights.start((0, 1, 2, 3))
    x_out[...] = forward_image(x, mod, weights, b_in, b_out, outs, hooks)


GATHER_SLOTS = (0, 0, 13, 15, 26, 28, 39, 41, 50) + (34, 43, 48, 51, 51, 51, 51, 51, 51)


def forward_gather(ins, pair):
    images = ins[1].shape[0]
    devices = lax.axis_size(AXIS)
    shapes, specs = kept_shapes(images)
    any_block = pl.BlockSpec(memory_space=pl.ANY)
    return pl.pallas_call(
        functools.partial(forward_gather_kernel, GATHER_SLOTS),
        grid=(images,),
        out_shape=shapes
        + [jax.ShapeDtypeStruct((images * SEQ, MODEL_WIDTH), jnp.float32)]
        + [jax.ShapeDtypeStruct((devices * a.shape[0], a.shape[1]), jnp.bfloat16) for a in pair],
        in_specs=forward_specs() + [whole_block(*a.shape) for a in pair],
        out_specs=specs + [token_block(MODEL_WIDTH)] + [any_block] * 2,
        scratch_shapes=WEIGHT_SCRATCH + gather_scratch(piece_shapes([a.shape for a in pair])),
        compiler_params=pltpu.CompilerParams(collective_id=1, has_side_effects=True, vmem_limit_bytes=58 << 20),
        name="forward_gather",
    )(*ins, *pair)


GRAD_CUTS = [3 * MODEL_WIDTH // MODEL_WIDTH, FF // MODEL_WIDTH]


class Grads:
    def __init__(self, hbm, bufs, keep_in, keep_out, sems):
        bufs = [bufs[0], bufs[4], *bufs[1:]]
        self.bufs, self.keep_in, self.keep_out = bufs, keep_in, keep_out
        self.copies = [pltpu.make_async_copy(src, dst, sems.at[i]) for i, (src, dst) in enumerate(zip(hbm, bufs))]
        self.here = set()

    def start(self):
        for i in (4, 5, 6, 7, 2, 3, 0):
            self.copies[i].start()

    def need(self, *which):
        for i in which:
            if i not in self.here:
                self.copies[i].wait()
                self.here.add(i)

    def rows_in(self, chunk):
        width = MODEL_WIDTH
        pair = 0 if chunk < 3 else 1
        self.need(2 * pair, 2 * pair + 1)
        left, right = self.bufs[2 * pair], self.bufs[2 * pair + 1]
        at = (chunk - 3 * pair) * width
        self.keep_in[chunk * width : (chunk + 1) * width, :] = dot_tn(left[:, at : at + width], right[...]).astype(
            jnp.bfloat16
        )

    def rows_out(self, part):
        width = MODEL_WIDTH
        rows = slice(part * width // 2, (part + 1) * width // 2)
        self.need(4, 5)
        self.keep_out[rows, :width] = dot_tn(self.bufs[4][:, rows], self.bufs[5][...]).astype(jnp.bfloat16)
        self.need(6, 7)
        for j in range(FF // width):
            span = slice(j * width, (j + 1) * width)
            self.keep_out[rows, (1 + j) * width : (2 + j) * width] = dot_tn(
                self.bufs[6][:, rows], self.bufs[7][:, span]
            ).astype(jnp.bfloat16)
        if part == 0:
            self.copies[1].start()


def grads_out_kernel(*refs):
    ins, g_in, total, refs = refs[:8], refs[8], refs[9:10], refs[10:]
    bufs, keep_in, keep_out, load_sems, store_sem, refs = refs[:7], refs[7], refs[8], refs[9], refs[10], refs[11:]
    place = Place()
    work = Grads(ins, bufs, keep_in, keep_out, load_sems)
    work.start()
    place.greet()
    job = Scatter(place, [keep_out], total, refs[:6], refs[6:])
    work.rows_out(1)
    job.open(3)
    job.open(2)
    work.rows_out(0)
    job.open(0)
    job.open(1)
    moves = job.steps()
    for chunk in range(7):
        moves[chunk]()
        work.rows_in(chunk)
    store = pltpu.make_async_copy(keep_in, g_in, store_sem)
    store.start()
    for move in moves[7:]:
        move()
    store.wait()


def grad_bufs(ins):
    return [pltpu.VMEM(a.shape, a.dtype) for i, a in enumerate(ins) if i != 1] + [
        pltpu.VMEM((IW, MODEL_WIDTH), jnp.bfloat16),
        pltpu.VMEM((MODEL_WIDTH, OW), jnp.bfloat16),
        pltpu.SemaphoreType.DMA((8,)),
    ]


def weight_grads_out(ins, shape):
    any_block = pl.BlockSpec(memory_space=pl.ANY)
    return pl.pallas_call(
        grads_out_kernel,
        out_shape=[jax.ShapeDtypeStruct((IW, MODEL_WIDTH), jnp.bfloat16), jax.ShapeDtypeStruct(shape, jnp.float32)],
        in_specs=[any_block] * 8,
        out_specs=[any_block, pl.BlockSpec(memory_space=pltpu.VMEM)],
        scratch_shapes=grad_bufs(ins) + [pltpu.SemaphoreType.DMA] + scatter_scratch(piece_shapes([shape])),
        compiler_params=pltpu.CompilerParams(collective_id=5, has_side_effects=True, vmem_limit_bytes=58 << 20),
        name="weight_grads_out",
    )(*ins)


BACKWARD_POINTS = 13


def backward_scatter_kernel(slots, mod, w_in, w_out, grad, lat_t, *refs):
    ins, outs, (g_patch, g_pbias, total), refs = refs[:8], refs[8:16], refs[16:19], refs[19:]
    vm_in, vm_out, sems, mine, refs = refs[0], refs[1], refs[2], refs[3], refs[4:]
    place = Place()
    job = Scatter(place, [grad], [total], refs[:6], refs[6:], [mine])
    hooks = Hooks([place.greet, job.open_all] + job.steps(), slots, BACKWARD_POINTS)
    weights = Weights((w_in, w_out), (vm_in, vm_out), sems)
    weights.start((3, 2, 1, 0))
    backward_image(ins, mod, weights, outs, hooks)
    d_patch = outs[0][...].astype(jnp.bfloat16)

    @pl.when(pl.program_id(0) == 0)
    def _():
        g_patch[...] = jnp.zeros_like(g_patch)
        g_pbias[...] = jnp.zeros_like(g_pbias)

    g_patch[...] += dot_nn(lat_t[0], d_patch)
    g_pbias[...] += jnp.sum(d_patch.astype(jnp.float32), 0, keepdims=True)


SCATTER_SLOTS = (0, 0, 3, 6, 10, 14, 18, 22, 26, 29, 33, 37, 41, 45, 49, 51, 51)


def backward_scatter(mods, w_in, w_out, refs, grad, lat_t, shape):
    images, width, low, full = mods.shape[0], MODEL_WIDTH, jnp.bfloat16, jnp.float32
    tokens = images * SEQ
    any_block = pl.BlockSpec(memory_space=pl.ANY)
    shapes = [((tokens, width), full), ((tokens, 3 * width), low), ((tokens, FF), low), ((tokens, width), low),
              ((tokens, width), low), ((images, 6, width), full), ((1, IW), full), ((1, 2 * width), full),
              ((PD, width), full), ((1, width), full), (shape, full)]
    pieces = piece_shapes([shape])
    return pl.pallas_call(
        functools.partial(backward_scatter_kernel, SCATTER_SLOTS),
        grid=(images,),
        out_shape=[jax.ShapeDtypeStruct(s, t) for s, t in shapes],
        in_specs=[image_block(6, width), any_block, any_block, any_block, image_block(PD, SEQ), token_block(width),
                  token_block(width), token_block(width), image_block(HEADS, SEQ, SEQ), token_block(3 * width),
                  token_block(width), token_block(width), token_block(FF)],
        out_specs=[token_block(s[1]) for s, _ in shapes[:5]]
        + [image_block(6, width)] + [whole_block(*s) for s, _ in shapes[6:-1]] + [any_block],
        scratch_shapes=WEIGHT_SCRATCH
        + [pltpu.VMEM((16,) + pieces[0], jnp.bfloat16)] + scatter_scratch(pieces),
        compiler_params=pltpu.CompilerParams(collective_id=6, has_side_effects=True, vmem_limit_bytes=62 << 20),
        name="backward_scatter",
    )(mods, w_in, w_out, grad, lat_t, *refs)


def finish_kernel(devices, *refs):
    count = len(SETTLE_INS)
    ins, set_ins, refs = refs[:8], dict(zip(SETTLE_INS, refs[8 : 8 + count])), refs[8 + count :]
    totals, set_outs, refs = refs[:2], refs[2:7], refs[7:]
    bufs, keep_in, keep_out, load_sems, refs = refs[:7], refs[7], refs[8], refs[9], refs[10:]
    sc_bufs, sc_sems, refs = refs[:12], refs[12:26], refs[26:]
    set_bufs, set_sems = refs[:10], refs[10:]
    work = Grads(ins, bufs, keep_in, keep_out, load_sems)
    work.start()
    greet_all(devices)
    place = Place()
    job = Scatter(place, [keep_in, keep_out], totals, sc_bufs, sc_sems)
    first, second, third, fourth, message, last = settle_steps(devices, set_ins, set_outs, set_bufs, set_sems, totals)
    first()
    work.rows_out(1)
    work.rows_in(5)
    work.rows_in(6)
    job.open(3)
    job.cross_b(3)
    second()
    work.rows_out(0)
    work.rows_in(0)
    work.rows_in(1)
    job.open(0)
    job.cross_b(0)
    job.cross_a(3)
    work.rows_in(3)
    work.rows_in(4)
    job.open(2)
    job.cross_b(2)
    third()
    job.cross_a(0)
    work.rows_in(2)
    job.open(1)
    job.along_z(3)
    job.cross_b(1)
    job.cross_a(2)
    fourth()
    job.along_z(0)
    job.cross_a(1)
    job.along_z(2)
    job.along_z(1)
    job.close()
    job.end()
    message()
    job.finish()
    last()


def finish_grads(ins, shapes, set_ins):
    devices = lax.axis_size(AXIS)
    wcond, d_mods = set_ins["wcond"], set_ins["d_mods"]
    cols, images = set_ins["pre"].shape
    outs = [(wcond.shape[0], devices * cols), (cols, FREQ), (cols, devices * cols), (cols, 1024)]
    vmem = pl.BlockSpec(memory_space=pltpu.VMEM)
    low = jnp.bfloat16
    return pl.pallas_call(
        functools.partial(finish_kernel, devices),
        out_shape=[jax.ShapeDtypeStruct(shape, jnp.float32) for shape in list(shapes) + outs]
        + [jax.ShapeDtypeStruct((devices, 32, 128), low)],
        in_specs=[pl.BlockSpec(memory_space=pl.ANY)] * 8 + [vmem] * len(SETTLE_INS),
        out_specs=[vmem] * 7,
        scratch_shapes=grad_bufs(ins)
        + scatter_scratch(piece_shapes(shapes))
        + [
            pltpu.VMEM(d_mods.shape, jnp.float32),
            pltpu.VMEM((images, 384), jnp.float32),
            pltpu.VMEM((devices * 16, 128), jnp.float32),
            pltpu.VMEM((devices, 16, 128), low),
            pltpu.VMEM((devices, 16, 128), low),
            pltpu.VMEM((devices, 32, images), low),
            pltpu.VMEM((devices, 32, images), low),
            pltpu.VMEM((devices, 32, images), low),
            pltpu.VMEM((devices, 32, images), low),
            pltpu.VMEM((32, 128), low),
            pltpu.SemaphoreType.DMA((5, devices)),
            pltpu.SemaphoreType.DMA((5, devices)),
        ],
        compiler_params=pltpu.CompilerParams(collective_id=4, has_side_effects=True, vmem_limit_bytes=63 << 20),
        name="finish_grads",
    )(*ins, *(set_ins[name] for name in SETTLE_INS))

def code_table():
    quarter = MODEL_WIDTH // 4
    omega = (1.0 / 10000.0 ** (np.arange(quarter, dtype=np.float32) / np.float32(quarter))).astype(np.float32)
    angles = np.arange(GRID, dtype=np.float32)[:, None] * omega
    return np.concatenate([np.sin(angles), np.cos(angles)], 1).astype(np.float32)


def position_sum():
    table = jnp.asarray(code_table())
    half = MODEL_WIDTH // 2
    rows_pos = jnp.broadcast_to(table[:, None, :], (GRID, GRID, half))
    cols_pos = jnp.broadcast_to(table[None, :, :], (GRID, GRID, half))
    return jnp.concatenate([rows_pos, cols_pos], -1).reshape(SEQ, MODEL_WIDTH)


def rows_t(left, right):
    return jnp.einsum("bsd,ed->bse", left, right, preferred_element_type=jnp.float32)


def body(
    latents, targets, timesteps, labels, embed_w, embed_m, embed_v, cond_w, cond_m, cond_v, layer_input_weights, in_m,
    in_v, layer_output_weights, out_m, out_v, head_w, head_m, head_v, biases, bias_m, bias_v,
):
    devices = lax.axis_size("fsdp")
    me = lax.axis_index("fsdp")
    images = latents.shape[0]
    embed_t = embed_w.T
    cond_t = cond_w.T
    in_t = layer_input_weights.transpose(0, 2, 1)
    out_t = layer_output_weights.transpose(0, 2, 1)
    cols, cond_cols = embed_t.shape[0], cond_t.shape[0]
    time_one, time_two, patch_bias, cond_bias, block_input_bias, block_output_bias, head_bias = split_biases(biases)
    features = time_features(timesteps).astype(jnp.bfloat16).astype(jnp.float32)
    label_rows = jnp.broadcast_to(labels.astype(jnp.float32)[:, None], (images, 128))
    own_patch_w = embed_t[:, FREQ + MODEL_WIDTH : FREQ + MODEL_WIDTH + PD].reshape(3, 128)
    note = jnp.concatenate([features, label_rows, jnp.pad(own_patch_w, ((0, images - 3), (0, 0)))], 1)
    w_t1 = embed_t[:, :FREQ]
    w_t2 = embed_t[:, FREQ : FREQ + MODEL_WIDTH]
    w_class = jnp.pad(embed_t[:, FREQ + MODEL_WIDTH + PD :], ((0, 0), (0, 1024 - NCLS)))
    images_all = devices * images

    def own_bias(vector, count):
        part = lax.dynamic_slice(vector, (me * count,), (count,))
        return jnp.broadcast_to(part[:, None], (count, images_all))

    own_cond_bias = lax.dynamic_slice(cond_bias, (me * cond_cols,), (cond_cols,))[None]
    first_in, first_out, mods, pre, cond, hid_all, low_all, feat_all, lab_all, notes = gather_modulate(
        [in_t[0], out_t[0]],
        [note, w_t1, w_t2, w_class, cond_t, own_bias(time_one, cols), own_bias(time_two, cols), own_cond_bias],
    )
    chunks = mods.transpose(1, 0, 2).reshape(images, 6 * LAYERS + 2, MODEL_WIDTH)
    w_patch = notes[:, :3, FREQ + 128 :].reshape(MODEL_WIDTH, PD).astype(jnp.bfloat16)
    x = (rows_t(latents, w_patch) + patch_bias + position_sum()).reshape(images * SEQ, MODEL_WIDTH)
    block_mods = [chunks[:, 6 * i : 6 * (i + 1)] for i in range(LAYERS)]
    head_t = head_w.T
    tokens_all = devices * images * SEQ * PO
    lat_t = latents.transpose(0, 2, 1)
    bias_rows = [(block_input_bias[i][None], block_output_bias[i][None]) for i in range(LAYERS)]
    *kept0, x_mid, last_in, last_out = forward_gather(
        [x, block_mods[0], first_in, first_out, *bias_rows[0]], [in_t[1], out_t[1]]
    )
    *kept1, upstream, d_final, head_grad, head_bias_grad, loss_part = forward_head(
        [x_mid, block_mods[1], last_in, last_out, *bias_rows[1], chunks[:, 6 * LAYERS :], head_t, head_bias[:, None],
         targets.transpose(0, 2, 1)],
        2.0 / tokens_all,
    )
    h1, qkv, probs, o, a, x1, h2, u, g, f = kept1
    upstream, d_qkv, d_u, d_f, d_a, mod_grad1, in_bias1, out_bias1 = backward_block(
        block_mods[1], last_in, last_out, [upstream, x_mid, x1, probs, qkv, a, f, u]
    )
    in_shape, out_shape = in_t.shape[1:], out_t.shape[1:]
    grad_in, out_shard1 = weight_grads_out([d_qkv, h1, d_u, h2, d_a, o, d_f, g], out_shape)
    h1, qkv, probs, o, a, x1, h2, u, g, f = kept0
    (upstream, d_qkv, d_u, d_f, d_a, mod_grad0, in_bias0, out_bias0, patch_grad, patch_bias_grad, in_shard1) = backward_scatter(
        block_mods[0], first_in, first_out, [upstream, x, x1, probs, qkv, a, f, u], grad_in, lat_t, in_shape
    )
    mod_grads, in_bias_grads, out_bias_grads = [mod_grad0, mod_grad1], [in_bias0, in_bias1], [out_bias0, out_bias1]
    d_modulation = jnp.concatenate(mod_grads + [d_final], 1)
    d_mods = d_modulation.reshape(images, devices, cond_cols).transpose(1, 0, 2)
    in_shard0, out_shard0, g_cond, g_t1, g_t2, g_cls, merged = finish_grads(
        [d_qkv, h1, d_u, h2, d_a, o, d_f, g],
        [in_shape, out_shape],
        {
            "d_mods": d_mods, "wt2": w_t2, "wcond": cond_t, "pre": pre, "cond": cond, "hid_all": hid_all, "low_all": low_all,
            "feat_all": feat_all, "lab_all": lab_all, "g_head": head_grad, "g_hbias": head_bias_grad, "loss": loss_part,
            "g_patch": patch_grad, "g_pbias": patch_bias_grad, "bin0": in_bias_grads[0], "bin1": in_bias_grads[1],
            "bout0": out_bias_grads[0], "bout1": out_bias_grads[1], "done_in": in_shard1, "done_out": out_shard1,
        },
    )
    merged = merged.astype(jnp.float32)
    wide = MODEL_WIDTH // 128
    blocks = merged[:, :16]
    patch_total = blocks[:wide].transpose(1, 0, 2).reshape(PD, MODEL_WIDTH)
    head_total = blocks[wide : 3 * wide].reshape(wide, PO, 128).transpose(1, 0, 2).reshape(PO, MODEL_WIDTH)
    flat = blocks[3 * wide :].reshape(-1)
    rest = LAYERS * (IW + 2 * MODEL_WIDTH) + PO
    loss_total = jnp.sum(merged[:, 19, :3])
    bias_total = jnp.concatenate(
        [merged[:, 16, :cols].reshape(-1), merged[:, 17, :cols].reshape(-1), flat[:MODEL_WIDTH],
         merged[:, 20:23].reshape(devices, 384)[:, :cond_cols].reshape(-1), flat[MODEL_WIDTH : MODEL_WIDTH + rest]]
    )
    grad_norm = jnp.sqrt(
        jnp.sum(merged[:, 18, :3])
        + jnp.sum(head_total * head_total)
        + jnp.sum(patch_total * patch_total)
        + jnp.sum(bias_total * bias_total)
    )
    factor = jnp.minimum(1.0, clip_limit / grad_norm)
    own_patch = lax.dynamic_slice(patch_total, (0, me * cols), (PD, cols)).T
    embed_grad = jnp.concatenate([g_t1, g_t2, own_patch, g_cls[:, :NCLS]], 1)
    embed_up = [a.T for a in adam_step(embed_t, embed_m.T, embed_v.T, embed_grad * factor)]
    cond_up = [a.T for a in adam_step(cond_t, cond_m.T, cond_v.T, g_cond * factor)]
    turn = (0, 2, 1)
    in_up = [
        a.transpose(turn)
        for a in adam_step(in_t, in_m.transpose(turn), in_v.transpose(turn), jnp.stack([in_shard0, in_shard1]) * factor)
    ]
    out_up = [
        a.transpose(turn)
        for a in adam_step(out_t, out_m.transpose(turn), out_v.transpose(turn), jnp.stack([out_shard0, out_shard1]) * factor)
    ]
    head_up = [a.T for a in adam_step(head_t, head_m.T, head_v.T, head_total * factor)]
    bias_up = adam_step(biases, bias_m, bias_v, bias_total * factor)
    return (loss_total, grad_norm, *embed_up, *cond_up, *in_up, *out_up, *head_up, *bias_up)


def fits(mesh):
    return mesh.shape["fsdp"] == 32


def solution(mesh):
    in_specs = (
        P("fsdp", None, None),
        P("fsdp", None, None),
        P("fsdp"),
        P("fsdp"),
        P(None, "fsdp"),
        P(None, "fsdp"),
        P(None, "fsdp"),
        P(None, "fsdp"),
        P(None, "fsdp"),
        P(None, "fsdp"),
        P(None, None, "fsdp"),
        P(None, None, "fsdp"),
        P(None, None, "fsdp"),
        P(None, None, "fsdp"),
        P(None, None, "fsdp"),
        P(None, None, "fsdp"),
        P(),
        P(),
        P(),
        P(),
        P(),
        P(),
    )
    out_specs = (
        P(),
        P(),
        P(None, "fsdp"),
        P(None, "fsdp"),
        P(None, "fsdp"),
        P(None, "fsdp"),
        P(None, "fsdp"),
        P(None, "fsdp"),
        P(None, None, "fsdp"),
        P(None, None, "fsdp"),
        P(None, None, "fsdp"),
        P(None, None, "fsdp"),
        P(None, None, "fsdp"),
        P(None, None, "fsdp"),
        P(),
        P(),
        P(),
        P(),
        P(),
        P(),
    )
    chosen = body if fits(mesh) else generic_body
    return jax.shard_map(chosen, mesh=mesh, in_specs=in_specs, out_specs=out_specs, check_vma=False)
```

```python
import functools
import math

import jax
import jax.numpy as jnp
import numpy as np
from jax import lax
from jax.experimental import pallas as pl
from jax.experimental.pallas import tpu as pltpu
from jax.sharding import PartitionSpec as P

MODEL_WIDTH = 768
HEADS = 12
HEAD_DIM = 64
NCLS = 1001
FREQ = 256
PD = 16
PO = 32
GRID = 16
LAYERS = 2
STEP = 10
SEQ = 256
IW = 5376
OW = 3840
FF = 3072
CW = 10752


learn_rate = 0.03
beta_one = 0.9
beta_two = 0.999
adam_eps = 1e-08
decay = 0.01
clip_limit = 0.01
highest = lax.Precision.HIGHEST


def product(left, right):
    return jnp.dot(left, right, preferred_element_type=jnp.float32)


def exact_dot(left, right):
    return jnp.dot(left, right, precision=highest)


def apply_rows(left, right):
    return jnp.einsum("bsd,de->bse", left, right, preferred_element_type=jnp.float32)


def outer_sum(left, right):
    return jnp.einsum("bsd,bse->de", left, right, preferred_element_type=jnp.float32)


def apply_back(left, right):
    return jnp.einsum("bse,de->bsd", left, right, preferred_element_type=jnp.float32)


def column_sum(value):
    return jnp.sum(value.astype(jnp.float32), (0, 1))


def silu(value):
    return value * jax.nn.sigmoid(value)


def gelu(value):
    return jax.nn.gelu(value, approximate=True)


def layer_norm(value):
    centered = value - jnp.mean(value, -1, keepdims=True)
    return centered * lax.rsqrt(jnp.mean(centered * centered, -1, keepdims=True) + 1e-06)


def local_back(func, value, cotangent):
    return jax.vjp(func, value)[1](cotangent)[0]


def position_table():
    quarter = MODEL_WIDTH // 4
    omega = 1.0 / 10000.0 ** (jnp.arange(quarter, dtype=jnp.float32) / quarter)
    places = jnp.arange(GRID * GRID)
    rows_pos = (places // GRID).astype(jnp.float32)[:, None] * omega
    cols_pos = (places % GRID).astype(jnp.float32)[:, None] * omega
    return jnp.concatenate(
        [jnp.sin(rows_pos), jnp.cos(rows_pos), jnp.sin(cols_pos), jnp.cos(cols_pos)], 1
    )


def time_features(timesteps):
    half_freq = FREQ // 2
    rates = jnp.exp(-math.log(10000.0) * jnp.arange(half_freq, dtype=jnp.float32) / half_freq)
    angles = timesteps.astype(jnp.float32)[:, None] * rates
    return jnp.concatenate([jnp.cos(angles), jnp.sin(angles)], 1)


def split_biases(vector):
    lengths = [MODEL_WIDTH, MODEL_WIDTH, MODEL_WIDTH, CW, LAYERS * IW, LAYERS * 2 * MODEL_WIDTH, PO]
    pieces = []
    offset = 0
    for length in lengths:
        pieces.append(vector[offset : offset + length])
        offset += length
    pieces[4] = pieces[4].reshape(LAYERS, IW)
    pieces[5] = pieces[5].reshape(LAYERS, 2 * MODEL_WIDTH)
    return pieces


def split_heads(triple, which):
    n_images, seq_len = (triple.shape[0], triple.shape[1])
    return triple[..., which * MODEL_WIDTH : (which + 1) * MODEL_WIDTH].reshape(
        n_images, seq_len, HEADS, HEAD_DIM
    )


def attend(triple):
    queries, key_part, values = [split_heads(triple, j) for j in range(3)]
    scores = jnp.einsum(
        "bqhd,bkhd->bhqk", queries, key_part, preferred_element_type=jnp.float32
    ) * HEAD_DIM ** (-0.5)
    row_max = jnp.max(scores, -1, keepdims=True)
    expo = jnp.exp(scores - row_max)
    row_sum = jnp.sum(expo, -1, keepdims=True)
    attn_weights = (expo / row_sum).astype(jnp.bfloat16)
    mixed_heads = jnp.einsum(
        "bhqk,bkhd->bqhd", attn_weights, values, preferred_element_type=jnp.float32
    ).astype(jnp.bfloat16)
    return (
        mixed_heads.reshape(triple.shape[0], triple.shape[1], MODEL_WIDTH),
        row_max + jnp.log(row_sum),
    )


def attend_back(triple, log_norm, d_mixed):
    queries, key_part, values = [split_heads(triple, j) for j in range(3)]
    scale = HEAD_DIM ** (-0.5)
    scores = (
        jnp.einsum("bqhd,bkhd->bhqk", queries, key_part, preferred_element_type=jnp.float32) * scale
    )
    probs_full = jnp.exp(scores - log_norm)
    attn_weights = probs_full.astype(jnp.bfloat16)
    d_heads = d_mixed.reshape(queries.shape)
    d_probs = jnp.einsum("bqhd,bkhd->bhqk", d_heads, values, preferred_element_type=jnp.float32)
    d_values = jnp.einsum(
        "bhqk,bqhd->bkhd", attn_weights, d_heads, preferred_element_type=jnp.float32
    )
    d_scores = (probs_full * (d_probs - jnp.sum(probs_full * d_probs, -1, keepdims=True))).astype(
        jnp.bfloat16
    )
    d_queries = (
        jnp.einsum("bhqk,bkhd->bqhd", d_scores, key_part, preferred_element_type=jnp.float32)
        * scale
    )
    d_keys = (
        jnp.einsum("bhqk,bqhd->bkhd", d_scores, queries, preferred_element_type=jnp.float32) * scale
    )
    shape_flat = (triple.shape[0], triple.shape[1], MODEL_WIDTH)
    return jnp.concatenate(
        [d_queries.reshape(shape_flat), d_keys.reshape(shape_flat), d_values.reshape(shape_flat)],
        -1,
    ).astype(jnp.bfloat16)


def block_forward(residual_state, adaptive_modulation, weights_in, weights_out, bias_in, bias_out):
    pieces = [
        adaptive_modulation[:, None, i * MODEL_WIDTH : (i + 1) * MODEL_WIDTH] for i in range(6)
    ]
    shaped_one = (layer_norm(residual_state) * (1 + pieces[1]) + pieces[0]).astype(jnp.bfloat16)
    triple = (
        apply_rows(shaped_one, weights_in[:, : 3 * MODEL_WIDTH]) + bias_in[: 3 * MODEL_WIDTH]
    ).astype(jnp.bfloat16)
    mixed_heads, log_norm = attend(triple)
    branch = apply_rows(mixed_heads, weights_out[:MODEL_WIDTH]) + bias_out[:MODEL_WIDTH]
    middle = residual_state + pieces[2] * branch
    shaped_two = (layer_norm(middle) * (1 + pieces[4]) + pieces[3]).astype(jnp.bfloat16)
    pre_ffn = apply_rows(shaped_two, weights_in[:, 3 * MODEL_WIDTH :]) + bias_in[3 * MODEL_WIDTH :]
    active = gelu(pre_ffn).astype(jnp.bfloat16)
    ffn_out = apply_rows(active, weights_out[MODEL_WIDTH:]) + bias_out[MODEL_WIDTH:]
    kept = (
        residual_state,
        shaped_one,
        triple,
        log_norm,
        mixed_heads,
        branch,
        middle,
        shaped_two,
        pre_ffn,
        active,
        ffn_out,
    )
    return (middle + pieces[5] * ffn_out, kept)


def block_backward(upstream, adaptive_modulation, weights_in, weights_out, kept):
    (
        residual_state,
        shaped_one,
        triple,
        log_norm,
        mixed_heads,
        branch,
        middle,
        shaped_two,
        pre_ffn,
        active,
        ffn_out,
    ) = kept
    pieces = [
        adaptive_modulation[:, None, i * MODEL_WIDTH : (i + 1) * MODEL_WIDTH] for i in range(6)
    ]
    d_ffn = (pieces[5] * upstream).astype(jnp.bfloat16)
    gate_two = jnp.sum(ffn_out * upstream, 1)
    grad_down = outer_sum(active, d_ffn)
    d_active = apply_back(d_ffn, weights_out[MODEL_WIDTH:])
    d_pre = local_back(gelu, pre_ffn, d_active).astype(jnp.bfloat16)
    grad_up = outer_sum(shaped_two, d_pre)
    d_shaped = apply_back(d_pre, weights_in[:, 3 * MODEL_WIDTH :])
    shift_two = jnp.sum(d_shaped, 1)
    scale_two = jnp.sum(d_shaped * layer_norm(middle), 1)
    upstream = upstream + local_back(layer_norm, middle, d_shaped * (1 + pieces[4]))
    gate_one = jnp.sum(branch * upstream, 1)
    d_branch = (pieces[2] * upstream).astype(jnp.bfloat16)
    grad_proj = outer_sum(mixed_heads, d_branch)
    d_mixed = apply_back(d_branch, weights_out[:MODEL_WIDTH]).astype(jnp.bfloat16)
    d_triple = attend_back(triple, log_norm, d_mixed)
    grad_qkv = outer_sum(shaped_one, d_triple)
    d_shaped = apply_back(d_triple, weights_in[:, : 3 * MODEL_WIDTH])
    shift_one = jnp.sum(d_shaped, 1)
    scale_one = jnp.sum(d_shaped * layer_norm(residual_state), 1)
    upstream = upstream + local_back(layer_norm, residual_state, d_shaped * (1 + pieces[1]))
    mod_grad = jnp.concatenate([shift_one, scale_one, gate_one, shift_two, scale_two, gate_two], 1)
    bias_in_grad = jnp.concatenate([column_sum(d_triple), column_sum(d_pre)])
    bias_out_grad = jnp.concatenate([column_sum(d_branch), column_sum(d_ffn)])
    grad_in = jnp.concatenate([grad_qkv, grad_up], 1)
    grad_out = jnp.concatenate([grad_proj, grad_down], 0)
    return (upstream, mod_grad, grad_in, grad_out, bias_in_grad, bias_out_grad)


def fetch_layer(layer_input_weights, layer_output_weights, layer_count):
    return (
        lax.all_gather(
            layer_input_weights[layer_count].astype(jnp.bfloat16), "fsdp", axis=1, tiled=True
        ),
        lax.all_gather(
            layer_output_weights[layer_count].astype(jnp.bfloat16), "fsdp", axis=1, tiled=True
        ),
    )


def adam_step(weight, first, second, gradient):
    first = beta_one * first + (1 - beta_one) * gradient
    second = beta_two * second + (1 - beta_two) * gradient * gradient
    ahead = first / (1 - beta_one**STEP)
    scaled = second / (1 - beta_two**STEP)
    return (
        weight - learn_rate * (ahead / (jnp.sqrt(scaled) + adam_eps) + decay * weight),
        first,
        second,
    )


def generic_body(
    latents,
    targets,
    timesteps,
    labels,
    embed_w,
    embed_m,
    embed_v,
    cond_w,
    cond_m,
    cond_v,
    layer_input_weights,
    in_m,
    in_v,
    layer_output_weights,
    out_m,
    out_v,
    head_w,
    head_m,
    head_v,
    biases,
    bias_m,
    bias_v,
):
    devices = lax.axis_size("fsdp")
    embed_full, cond_full = (
        lax.all_gather(embed_w.astype(jnp.bfloat16), "fsdp", axis=1, tiled=True),
        lax.all_gather(cond_w.astype(jnp.bfloat16), "fsdp", axis=1, tiled=True),
    )
    time_one, time_two, patch_bias, cond_bias, block_input_bias, block_output_bias, head_bias = (
        split_biases(biases)
    )
    head_low = head_w.astype(jnp.bfloat16)
    features = time_features(timesteps).astype(jnp.bfloat16)
    pre_time = product(features, embed_full[:FREQ]) + time_one
    hidden_t = silu(pre_time).astype(jnp.bfloat16)
    time_emb = product(hidden_t, embed_full[FREQ : FREQ + MODEL_WIDTH]) + time_two
    onehot = (labels[:, None] == jnp.arange(NCLS)[None, :]).astype(jnp.bfloat16)
    condition = time_emb + product(onehot, embed_full[FREQ + MODEL_WIDTH + PD :])
    cond_low = silu(condition).astype(jnp.bfloat16)
    adaptive_modulation = product(cond_low, cond_full) + cond_bias
    residual_state = (
        apply_rows(latents, embed_full[FREQ + MODEL_WIDTH : FREQ + MODEL_WIDTH + PD])
        + patch_bias
        + position_table()
    )
    kept_all = []
    for layer_count in range(LAYERS):
        weights_in, weights_out = fetch_layer(
            layer_input_weights, layer_output_weights, layer_count
        )
        residual_state, kept = block_forward(
            residual_state,
            adaptive_modulation[
                :, 6 * MODEL_WIDTH * layer_count : 6 * MODEL_WIDTH * (layer_count + 1)
            ],
            weights_in,
            weights_out,
            block_input_bias[layer_count],
            block_output_bias[layer_count],
        )
        kept_all.append(kept)
    final_mod = adaptive_modulation[:, 6 * MODEL_WIDTH * LAYERS :]
    norm_final = layer_norm(residual_state)
    shaped = (
        norm_final * (1 + final_mod[:, None, MODEL_WIDTH:]) + final_mod[:, None, :MODEL_WIDTH]
    ).astype(jnp.bfloat16)
    output = apply_rows(shaped, head_low) + head_bias
    error_vals = output - targets
    loss_part = jnp.sum(error_vals * error_vals)
    tokens_all = devices * error_vals.shape[0] * SEQ * PO
    d_output = (error_vals * (2.0 / tokens_all)).astype(jnp.bfloat16)
    head_grad = outer_sum(shaped, d_output)
    head_bias_grad = column_sum(d_output)
    d_shaped = apply_back(d_output, head_low)
    d_final = jnp.concatenate([jnp.sum(d_shaped, 1), jnp.sum(d_shaped * norm_final, 1)], 1)
    upstream = local_back(
        layer_norm, residual_state, d_shaped * (1 + final_mod[:, None, MODEL_WIDTH:])
    )
    mod_grads = [None] * LAYERS
    in_shards = [None] * LAYERS
    out_shards = [None] * LAYERS
    in_bias_grads = [None] * LAYERS
    out_bias_grads = [None] * LAYERS
    for layer_count in reversed(range(LAYERS)):
        weights_in, weights_out = (
            lax.all_gather(
                layer_input_weights[layer_count].astype(jnp.bfloat16), "fsdp", axis=1, tiled=True
            ),
            lax.all_gather(
                layer_output_weights[layer_count].astype(jnp.bfloat16), "fsdp", axis=1, tiled=True
            ),
        )
        upstream, mod_grad, grad_in, grad_out, bias_in_grad, bias_out_grad = block_backward(
            upstream,
            adaptive_modulation[
                :, 6 * MODEL_WIDTH * layer_count : 6 * MODEL_WIDTH * (layer_count + 1)
            ],
            weights_in,
            weights_out,
            kept_all[layer_count],
        )
        in_shards[layer_count], out_shards[layer_count] = (
            lax.psum_scatter(grad_in, "fsdp", scatter_dimension=1, tiled=True),
            lax.psum_scatter(grad_out, "fsdp", scatter_dimension=1, tiled=True),
        )
        mod_grads[layer_count] = mod_grad
        in_bias_grads[layer_count] = bias_in_grad
        out_bias_grads[layer_count] = bias_out_grad
    d_patch = upstream.astype(jnp.bfloat16)
    patch_grad = outer_sum(latents, d_patch)
    patch_bias_grad = column_sum(d_patch)
    d_modulation = jnp.concatenate(mod_grads + [d_final], 1)
    d_cond = exact_dot(d_modulation, cond_full.astype(jnp.float32).T)
    d_condition = local_back(silu, condition, d_cond)
    d_hidden = exact_dot(d_condition, embed_full[FREQ : FREQ + MODEL_WIDTH].astype(jnp.float32).T)
    d_pre = local_back(silu, pre_time, d_hidden)
    cond_grad = exact_dot(cond_low.astype(jnp.float32).T, d_modulation)
    class_grad = exact_dot(onehot.astype(jnp.float32).T, d_condition)
    time_two_grad = exact_dot(hidden_t.astype(jnp.float32).T, d_condition)
    time_one_grad = exact_dot(features.astype(jnp.float32).T, d_pre)
    embed_grad = jnp.concatenate([time_one_grad, time_two_grad, patch_grad, class_grad], 0)
    embed_shard, cond_shard = (
        lax.psum_scatter(embed_grad, "fsdp", scatter_dimension=1, tiled=True),
        lax.psum_scatter(cond_grad, "fsdp", scatter_dimension=1, tiled=True),
    )
    bias_grad = jnp.concatenate(
        [jnp.sum(d_pre, 0), jnp.sum(d_condition, 0), patch_bias_grad, jnp.sum(d_modulation, 0)]
        + in_bias_grads
        + out_bias_grads
        + [head_bias_grad]
    )
    head_total, bias_total, loss_total = lax.psum((head_grad, bias_grad, loss_part), "fsdp")
    in_stack = jnp.stack(in_shards, 0)
    out_stack = jnp.stack(out_shards, 0)
    shard_squares = (
        jnp.sum(embed_shard * embed_shard)
        + jnp.sum(cond_shard * cond_shard)
        + jnp.sum(in_stack * in_stack)
        + jnp.sum(out_stack * out_stack)
    )
    square_total = lax.psum(shard_squares, "fsdp")
    grad_norm = jnp.sqrt(
        square_total + jnp.sum(head_total * head_total) + jnp.sum(bias_total * bias_total)
    )
    factor = jnp.minimum(1.0, clip_limit / grad_norm)
    embed_up = adam_step(embed_w, embed_m, embed_v, embed_shard * factor)
    cond_up = adam_step(cond_w, cond_m, cond_v, cond_shard * factor)
    in_up = adam_step(layer_input_weights, in_m, in_v, in_stack * factor)
    out_up = adam_step(layer_output_weights, out_m, out_v, out_stack * factor)
    head_up = adam_step(head_w, head_m, head_v, head_total * factor)
    bias_up = adam_step(biases, bias_m, bias_v, bias_total * factor)
    return (
        loss_total,
        grad_norm,
        embed_up[0],
        embed_up[1],
        embed_up[2],
        cond_up[0],
        cond_up[1],
        cond_up[2],
        in_up[0],
        in_up[1],
        in_up[2],
        out_up[0],
        out_up[1],
        out_up[2],
        head_up[0],
        head_up[1],
        head_up[2],
        bias_up[0],
        bias_up[1],
        bias_up[2],
    )


MESH_ID = pl.DeviceIdType.MESH
AXIS = "fsdp"


class Place:
    def __init__(self):
        me = lax.axis_index(AXIS)
        self.me = me
        self.core = core = me % 2
        x = (me // 2) % 2
        y = (me // 4) % 2
        self.z = me // 8
        self.chip = me // 2
        step_x = 1 - 2 * x
        step_y = 2 - 4 * y
        self.step_a = step_x + core * (step_y - step_x)
        self.step_b = step_y + core * (step_x - step_y)
        self.dev_a = me + 2 * self.step_a
        self.dev_b = me + 2 * self.step_b
        self.sibling = me + 1 - 2 * core

    def other(self, dz, flip_a=0, flip_b=0):
        return self.chip + 4 * dz + flip_a * self.step_a + flip_b * self.step_b

    def valid(self, dz):
        return jnp.logical_and(self.z + dz >= 0, self.z + dz < 4)

    def greet(self):
        barrier = pltpu.get_barrier_semaphore()

        def hello(device):
            pl.semaphore_signal(barrier, inc=1, device_id=(device,), device_id_type=MESH_ID)

        for k in range(1, 8):
            hello(8 * self.z + lax.rem(self.me + k, 8))
        for k in range(1, 4):
            hello(lax.rem(self.me + 8 * k, 32))
        pl.semaphore_wait(barrier, 10)


def remote(src, dst, send_sem, recv_sem, device):
    return pltpu.make_async_remote_copy(
        src_ref=src, dst_ref=dst, send_sem=send_sem, recv_sem=recv_sem, device_id=(device,), device_id_type=MESH_ID
    )


class Gather:
    def __init__(self, place, own, stage, piece, full, sems):
        self.p, self.own, self.stage, self.piece, self.full = place, own, stage, piece, full
        self.xch_send, self.xch_recv, self.local, self.send, self.recv, self.sib_recv = sems
        self.sent = []

    def slot(self, a, chip):
        rows, half = self.piece[a].shape
        return self.full[a].at[
            pl.ds(pl.multiple_of(chip * rows, rows), rows), pl.ds(pl.multiple_of(self.p.core * half, half), half)
        ]

    def push(self, a, k, src, chip, device, sem, cond=None):
        def act(what):
            copy = remote(src(), self.slot(a, chip()), self.send.at[a, k], sem.at[a, chip()], device())
            getattr(copy, what)()

        def guarded(what):
            if cond is None:
                act(what)
            else:
                pl.when(cond())(functools.partial(act, what))

        guarded("start")
        self.sent.append(functools.partial(guarded, "wait_send"))

    def store_own(self, a):
        return pltpu.make_async_copy(self.piece[a], self.slot(a, self.p.chip), self.local.at[a])

    def begin(self):
        core = self.p.core
        copies = []
        for a in range(2):
            rows, half = self.own[a].shape[0], self.piece[a].shape[1]
            dst = self.stage[a].at[pl.ds(pl.multiple_of(core * rows, 8), rows), :]
            away = remote(
                self.own[a].at[:, pl.ds(pl.multiple_of((1 - core) * half, half), half)],
                dst,
                self.xch_send.at[a],
                self.xch_recv.at[a],
                self.p.sibling,
            )
            away.start()
            keep = pltpu.make_async_copy(
                self.own[a].at[:, pl.ds(pl.multiple_of(core * half, half), half)], dst, self.local.at[a]
            )
            keep.start()
            copies.append((away, keep))
        for a in range(2):
            copies[a][0].wait()
            copies[a][1].wait()
            self.piece[a][...] = self.stage[a][...].astype(jnp.bfloat16)
            self.store_own(a).start()
            piece, here = (lambda a=a: self.piece[a]), (lambda: self.p.chip)
            for sign in (-1, 1):
                self.push(
                    a, 0 if sign < 0 else 3, piece, here, lambda sign=sign: self.p.me + 8 * sign, self.recv,
                    lambda sign=sign: self.p.valid(sign),
                )
            self.push(a, 6, piece, here, lambda: self.p.dev_a, self.recv)
            self.push(a, 10, piece, here, lambda: self.p.dev_b, self.recv)
            self.push(a, 18, piece, here, lambda: self.p.sibling, self.sib_recv)

    def arrive(self, a, chip):
        slot = self.slot(a, chip)
        pltpu.make_async_copy(slot, slot, self.recv.at[a, chip]).wait()

    def pass_on(self, dz, flip_a, flip_b, targets):
        def here():
            return self.p.valid(dz)

        def chip():
            return self.p.other(dz, flip_a, flip_b)

        for a in range(2):
            pl.when(here())(lambda a=a: self.arrive(a, chip()))
            for k, device, sem, extra in targets:
                self.push(
                    a, k, lambda a=a: self.slot(a, chip()), chip, device, sem,
                    here if extra is None else lambda extra=extra: jnp.logical_and(here(), self.p.valid(extra)),
                )

    def z_step(self, dist):
        for sign in (-1, 1):
            rel = (sign * dist) % 4
            targets = [
                (6 + rel, lambda: self.p.dev_a, self.recv, None),
                (10 + rel, lambda: self.p.dev_b, self.recv, None),
                (18 + rel, lambda: self.p.sibling, self.sib_recv, None),
            ]
            if dist < 3:
                onward = ((0 if sign > 0 else 3) + dist, lambda sign=sign: self.p.me - 8 * sign, self.recv, -sign)
                targets.insert(0, onward)
            self.pass_on(sign * dist, 0, 0, targets)

    def a_step(self, dist):
        for sign in (-1, 1) if dist else (1,):
            rel = (sign * dist) % 4
            self.pass_on(sign * dist, 1, 0, [
                (14 + rel, lambda: self.p.dev_b, self.recv, None), (22 + rel, lambda: self.p.sibling, self.sib_recv, None)
            ])

    def b_step(self, dist, flip_a):
        for sign in (-1, 1) if dist else (1,):
            rel = (sign * dist) % 4
            self.pass_on(
                sign * dist, flip_a, 1, [(26 + 4 * flip_a + rel, lambda: self.p.sibling, self.sib_recv, None)]
            )

    def finish(self):
        for a in range(2):
            rows, half = self.piece[a].shape

            def take(chip, carry):
                slot = self.full[a].at[
                    pl.ds(pl.multiple_of(chip * rows, rows), rows),
                    pl.ds(pl.multiple_of((1 - self.p.core) * half, half), half),
                ]
                pltpu.make_async_copy(slot, slot, self.sib_recv.at[a, chip]).wait()
                return carry

            lax.fori_loop(0, 16, take, 0)
            self.store_own(a).wait()
        for wait in self.sent:
            wait()


GATHER_SEMS = [
    pltpu.SemaphoreType.DMA((2,)),
    pltpu.SemaphoreType.DMA((2,)),
    pltpu.SemaphoreType.DMA((2,)),
    pltpu.SemaphoreType.DMA((2, 34)),
    pltpu.SemaphoreType.DMA((2, 16)),
    pltpu.SemaphoreType.DMA((2, 16)),
]


def gather_scratch(shapes):
    return (
        [pltpu.VMEM(shape, jnp.float32) for shape in shapes]
        + [pltpu.VMEM(shape, jnp.bfloat16) for shape in shapes]
        + GATHER_SEMS
    )


def piece_shapes(shapes):
    return [(2 * rows, width // 2) for rows, width in shapes]


ORDER = (3, 0, 2, 1)


class Scatter:
    def __init__(self, place, grads, totals, bufs, sems, mine=None):
        self.p, self.grad, self.total, self.mine = place, grads, totals, mine
        count = len(grads)
        self.arrays = range(count)
        self.sib, self.from_b, self.from_a, self.line, self.part, self.last = (
            bufs[count * i : count * i + count] for i in range(6)
        )
        (self.load_sem, self.sib_send, self.sib_recv, self.b_send, self.b_recv, self.a_send, self.a_recv, self.z_send,
         self.z_recv, self.end_send, self.end_recv, self.end_local) = sems

    def rows_of(self, a, chip, core):
        rows, half = self.part[a].shape
        return self.grad[a].at[
            pl.ds(pl.multiple_of(chip * rows, rows), rows), pl.ds(pl.multiple_of(core * half, half), half)
        ]

    def chip_of(self, z, flip_a, flip_b):
        return self.p.other(z - self.p.z, flip_a, flip_b)

    def own(self, a, flip_b, flip_a, z):
        if self.mine is None:
            return self.rows_of(a, self.chip_of(z, flip_a, flip_b), self.p.core)
        return self.mine[a].at[8 * flip_b + 4 * flip_a + z]

    def load(self, a, flip_b, flip_a, z):
        return pltpu.make_async_copy(
            self.rows_of(a, self.chip_of(z, flip_a, flip_b), self.p.core),
            self.own(a, flip_b, flip_a, z),
            self.load_sem.at[a, 8 * flip_b + 4 * flip_a + z],
        )

    def lend(self, a, flip_b, flip_a, z):
        k = 8 * flip_b + 4 * flip_a + z
        return remote(
            self.rows_of(a, self.chip_of(z, flip_b, flip_a), 1 - self.p.core),
            self.sib[a].at[k],
            self.sib_send.at[a, k],
            self.sib_recv.at[a, k],
            self.p.sibling,
        )

    def to_b(self, a, flip_a, z):
        k = 4 * flip_a + z
        return remote(
            self.own(a, 1, flip_a, z), self.from_b[a].at[k], self.b_send.at[a, k], self.b_recv.at[a, k], self.p.dev_b
        )

    def to_a(self, a, z):
        return remote(
            self.own(a, 0, 1, z), self.from_a[a].at[z], self.a_send.at[a, z], self.a_recv.at[a, z], self.p.dev_a
        )

    def to_z(self, a, target, source):
        return remote(
            self.own(a, 0, 0, target),
            self.line[a].at[source],
            self.z_send.at[a, target],
            self.z_recv.at[a, source],
            self.p.me + 8 * (target - self.p.z),
        )

    def open(self, z):
        for flip_b, flip_a in ((1, 1), (1, 0), (0, 1), (0, 0)):
            for a in self.arrays:
                self.lend(a, flip_b, flip_a, z).start()
                if self.mine is not None:
                    self.load(a, flip_b, flip_a, z).start()

    def open_all(self):
        for z in ORDER:
            self.open(z)

    def pair(self, a, flip_b, flip_a, z):
        if self.mine is not None:
            self.load(a, flip_b, flip_a, z).wait()
        self.lend(a, flip_b, flip_a, z).wait_recv()
        k = 8 * flip_b + 4 * flip_a + z
        return self.own(a, flip_b, flip_a, z)[...].astype(jnp.float32) + self.sib[a][k].astype(jnp.float32)

    def cross_b(self, z):
        for flip_a in (1, 0):
            for a in self.arrays:
                self.own(a, 1, flip_a, z)[...] = self.pair(a, 1, flip_a, z).astype(jnp.bfloat16)
                self.to_b(a, flip_a, z).start()

    def cross_a(self, z):
        for a in self.arrays:
            value = self.pair(a, 0, 1, z)
            self.to_b(a, 1, z).wait_recv()
            self.own(a, 0, 1, z)[...] = (value + self.from_b[a][4 + z].astype(jnp.float32)).astype(jnp.bfloat16)
            self.to_a(a, z).start()

    def along_z(self, z):
        place = self.p
        for a in self.arrays:
            value = self.pair(a, 0, 0, z)
            self.to_b(a, 0, z).wait_recv()
            value = value + self.from_b[a][z].astype(jnp.float32)
            self.to_a(a, z).wait_recv()
            self.part[a][...] = value + self.from_a[a][z].astype(jnp.float32)

            @pl.when(place.z != z)
            def _():
                self.own(a, 0, 0, z)[...] = self.part[a][...].astype(jnp.bfloat16)
                self.to_z(a, z, place.z).start()

            @pl.when(place.z == z)
            def _():
                self.last[a][...] = self.part[a][...]

    def end_copies(self, a):
        core = self.p.core
        rows, width = self.total[a].shape
        dst = self.total[a].at[:, pl.ds(pl.multiple_of(core * (width // 2), width // 2), width // 2)]
        away = remote(
            self.last[a].at[pl.ds(pl.multiple_of((1 - core) * rows, 8), rows), :],
            dst,
            self.end_send.at[a],
            self.end_recv.at[a],
            self.p.sibling,
        )
        keep = pltpu.make_async_copy(
            self.last[a].at[pl.ds(pl.multiple_of(core * rows, 8), rows), :], dst, self.end_local.at[a]
        )
        return away, keep

    def close(self):
        for a in self.arrays:

            def add(k, carry):
                source = lax.rem(self.p.z + k, 4)
                self.to_z(a, self.p.z, source).wait_recv()
                self.last[a][...] += self.line[a][source].astype(jnp.float32)
                return carry

            lax.fori_loop(1, 4, add, 0)
            for copy in self.end_copies(a):
                copy.start()

    def end(self):
        for a in self.arrays:
            for copy in self.end_copies(a):
                copy.wait()

    def finish(self):
        def step(z, carry):
            for a in self.arrays:
                for flip_b in range(2):
                    for flip_a in range(2):
                        self.lend(a, flip_b, flip_a, z).wait_send()
                for flip_a in range(2):
                    self.to_b(a, flip_a, z).wait_send()
                self.to_a(a, z).wait_send()

                @pl.when(self.p.z != z)
                def _():
                    self.to_z(a, z, self.p.z).wait_send()

            return carry

        lax.fori_loop(0, 4, step, 0)

    def steps(self):
        z0, z1, z2, z3 = ORDER
        work = [(self.cross_b, z) for z in ORDER]
        work += [(self.cross_a, z0), (self.cross_a, z1), (self.along_z, z0), (self.cross_a, z2), (self.along_z, z1)]
        work += [(self.cross_a, z3), (self.along_z, z2), (self.along_z, z3)]
        return [functools.partial(step, z) for step, z in work] + [self.close, self.end, self.finish]


def scatter_scratch(shapes):
    scratch = []
    for count, kind in ((16, jnp.bfloat16), (8, jnp.bfloat16), (4, jnp.bfloat16), (4, jnp.bfloat16),
                        (0, jnp.float32), (0, jnp.float32)):
        scratch += [pltpu.VMEM(((count,) if count else ()) + shape, kind) for shape in shapes]
    counts = (16, 16, 16, 8, 8, 4, 4, 4, 4)
    several = len(shapes)
    return (
        scratch
        + [pltpu.SemaphoreType.DMA((several, n)) for n in counts]
        + [pltpu.SemaphoreType.DMA((several,))] * 3
    )


def dot_nt(left, right):
    return lax.dot_general(left, right, (((1,), (1,)), ((), ())), preferred_element_type=jnp.float32)


def dot_tn(left, right):
    return lax.dot_general(left, right, (((0,), (0,)), ((), ())), preferred_element_type=jnp.float32)


def thirds(value):
    high = value.astype(jnp.bfloat16)
    rest = value - high.astype(jnp.float32)
    mid = rest.astype(jnp.bfloat16)
    return high, mid, (rest - mid.astype(jnp.float32)).astype(jnp.bfloat16)


def silu_slope(value):
    gate = jax.nn.sigmoid(value)
    return gate * (1 + value * (1 - gate))


PLANE, LINE = 8, 4


class Swap:
    def __init__(self, index, sems, full, away=None, mid=None, reduce=None):
        self.i, self.sems, self.full, self.away, self.mid = index, sems, full, away, mid
        self.second = mid if reduce is None else reduce
        self.me = lax.axis_index(AXIS)
        self.z, self.p = self.me // PLANE, self.me % PLANE
        self.spread = away is None

    def plane(self, peer, slot):
        send, recv = self.sems
        if self.spread:
            src, dst = self.full.at[:, self.p], self.full.at[:, slot]
        else:
            src, dst = self.away.at[:, peer], self.mid.at[:, slot]
        return remote(src, dst, send.at[self.i, peer], recv.at[self.i, slot], self.me + peer - self.p)

    def line(self, peer, slot):
        send, recv = self.sems
        if self.spread:
            src, dst = self.full.at[self.z, self.p], self.full.at[slot, self.p]
        else:
            src, dst = self.second.at[peer], self.full.at[slot]
        return remote(
            src, dst, send.at[self.i, PLANE + peer], recv.at[self.i, PLANE + slot], self.me + PLANE * (peer - self.z)
        )

    def each(self, in_plane, step):
        mine, count = (self.p, PLANE) if in_plane else (self.z, LINE)

        def run(k, carry):
            step(lax.rem(mine + k, count))
            return carry

        lax.fori_loop(1, count, run, 0)

    def hop(self, in_plane):
        make, slot = (self.plane, self.p) if in_plane else (self.line, self.z)
        self.each(in_plane, lambda peer: make(peer, slot).start())

    def come(self, in_plane):
        make = self.plane if in_plane else self.line
        self.each(in_plane, lambda peer: make(peer, peer).wait_recv())

    def start(self):
        if not self.spread:
            for k in range(LINE):
                self.mid[k, self.p] = self.away[k, self.p]
        self.hop(not self.spread)

    def between(self, work=None):
        self.come(not self.spread)
        if work is not None:
            work()
        self.hop(self.spread)
        if not self.spread:
            self.full[self.z] = self.second[self.z]

    def arrive(self):
        self.come(self.spread)

    def sent(self):
        self.each(True, lambda peer: self.plane(peer, self.p).wait_send())
        self.each(False, lambda peer: self.line(peer, self.z).wait_send())


def modulate_steps(devices, ins, outs, bufs, sems):
    msg, wt1, wt2, wcls, wcond, bt1, bt2, bcond = ins
    mods, pre, cond, hid_all, low_all, feat_all, lab_all, got = outs
    hid, low, away, mid = bufs
    me = lax.axis_index(AXIS)
    z, place = me // PLANE, me % PLANE
    images, cols = 4, wt1.shape[0]
    swaps = [Swap(0, sems, got), Swap(1, sems, hid), Swap(2, sems, low), Swap(3, sems, mods, away, mid)]

    def first():
        got[z, place] = msg[...]
        swaps[0].start()

    def second():
        swaps[0].arrive()
        for j in range(devices):
            at = slice(images * j, images * (j + 1))
            block = got[j // PLANE, j % PLANE].astype(jnp.float32)
            feat_all[at, :128] = block[:images]
            feat_all[at, 128:] = block[images : 2 * images]
            digits = block[3 * images : 4 * images]
            lab_all[at, :] = jnp.broadcast_to(32.0 * digits[:, :1] + digits[:, 64:65], (images, 128))
        pre[...] = dot_nt(wt1[...].astype(jnp.bfloat16), feat_all[...].astype(jnp.bfloat16)) + bt1[...]
        hidden = silu(pre[...])
        pad = jnp.zeros((hid.shape[2] - cols, hidden.shape[1]), jnp.float32)
        hid[z, place] = jnp.concatenate([hidden, pad], 0).astype(jnp.bfloat16)
        swaps[1].start()
        classes = lax.broadcasted_iota(jnp.int32, (lab_all.shape[0], wcls.shape[1]), 1).astype(jnp.float32)
        labels = jnp.concatenate([lab_all[...]] * (wcls.shape[1] // 128), 1)
        onehot = (labels == classes).astype(jnp.bfloat16)
        cond[...] = dot_nt(wcls[...].astype(jnp.bfloat16), onehot) + bt2[...]

    def third():
        swaps[1].arrive()
        for j in range(devices):
            hid_all[cols * j : cols * (j + 1), :] = hid[j // PLANE, j % PLANE].astype(jnp.float32)[:cols]
        cond[...] += jnp.dot(
            wt2[...].astype(jnp.bfloat16), hid_all[...].astype(jnp.bfloat16), preferred_element_type=jnp.float32
        )
        value = silu(cond[...])
        pad = jnp.zeros((low.shape[2] - cols, value.shape[1]), jnp.float32)
        low[z, place] = jnp.concatenate([value, pad], 0).astype(jnp.bfloat16)
        swaps[2].start()

    def fourth():
        swaps[2].arrive()
        for j in range(devices):
            low_all[cols * j : cols * (j + 1), :] = low[j // PLANE, j % PLANE].astype(jnp.float32)[:cols]
        rows = dot_nt(low_all[...].T.astype(jnp.bfloat16), wcond[...].astype(jnp.bfloat16)) + bcond[...]
        for j in range(devices):
            away[j // PLANE, j % PLANE] = rows[images * j : images * (j + 1)]
        swaps[3].start()

    def last():
        swaps[3].arrive()
        for swap in swaps:
            swap.sent()

    between = [swap.between for swap in swaps]
    return [first, between[0], second, between[1], third, between[2], fourth, between[3], last]


SETTLE_INS = ("d_mods", "wt2", "wcond", "pre", "cond", "hid_all", "low_all", "feat_all", "lab_all", "g_head", "g_hbias", "loss",
              "g_patch", "g_pbias", "bin0", "bin1", "bout0", "bout1", "done_in", "done_out")


def settle_steps(devices, ins, outs, bufs, sems, shards):
    d_mods, pre, lab_all = ins["d_mods"], ins["pre"], ins["lab_all"]
    g_cond, g_t1, g_t2, g_cls, merged = outs
    dm_mid, dm_got, dm_all, rows, small, small_mid, small_sum, small_got = bufs[:8]
    dc_part, dc_mid, dc_sum, dc_got, dh_part, dh_mid, dh_sum, dh_got = bufs[8:]
    me = lax.axis_index(AXIS)
    images, width = d_mods.shape[2:]
    cols = pre.shape[0]
    swaps = [
        Swap(0, sems, dm_got, d_mods, dm_mid),
        Swap(1, sems, small_got, small, small_mid, small_sum),
        Swap(2, sems, dc_got, dc_part, dc_mid, dc_sum),
        Swap(3, sems, dh_got, dh_part, dh_mid, dh_sum),
        Swap(4, sems, merged),
    ]
    keep = {}

    def share(value, part):
        pad = jnp.zeros((32 - cols, value.shape[1]), jnp.float32)
        for j in range(devices):
            part[j // PLANE, j % PLANE] = jnp.concatenate([value[cols * j : cols * (j + 1)], pad], 0).astype(jnp.bfloat16)

    def add_plane(mid, total):
        for k in range(LINE):
            total[k] = jnp.sum(mid[k].astype(jnp.float32), 0)

    def add_small():
        add_plane(small_mid, small_sum)

    def add_dc():
        add_plane(dc_mid, dc_sum)

    def add_dh():
        add_plane(dh_mid, dh_sum)

    def parts_of(value):
        return sum(
            jnp.where(lax.broadcasted_iota(jnp.int32, (1, 128), 1) == k, part.astype(jnp.float32), 0.0)
            for k, part in enumerate(thirds(value))
        )

    def first():
        swaps[0].start()
        dm_all[...] = jnp.zeros_like(dm_all)
        rows[...] = jnp.zeros_like(rows)
        for k in range(MODEL_WIDTH // 128):
            span = slice(128 * k, 128 * (k + 1))
            rows[16 * k : 16 * (k + 1), :] = ins["g_patch"][:, span]
            rows[96 + 32 * k : 96 + 32 * (k + 1), :] = ins["g_head"][:, span]
        at = 288
        for name in ("g_pbias", "bin0", "bin1", "bout0", "bout1"):
            for k in range(ins[name].shape[1] // 128):
                rows[at : at + 1, :] = ins[name][:, 128 * k : 128 * (k + 1)]
                at += 1
        square = ins["g_hbias"].shape
        diagonal = lax.broadcasted_iota(jnp.int32, square, 0) == lax.broadcasted_iota(jnp.int32, square, 1)
        rows[at : at + 1, :] = jnp.sum(jnp.where(diagonal, ins["g_hbias"][...], 0.0), 0, keepdims=True)
        for j in range(devices):
            small[j // PLANE, j % PLANE] = rows[16 * j : 16 * (j + 1), :].astype(jnp.bfloat16)

    def second():
        swaps[0].arrive()
        for j in range(devices):
            dm_all[images * j : images * (j + 1), :width] = dm_got[j // PLANE, j % PLANE]
        turned = dm_all[...].T[:width]
        parts = thirds(turned)
        weight = ins["wcond"][...].astype(jnp.bfloat16)
        share(sum(dot_tn(weight, part) for part in parts), dc_part)
        swaps[2].start()
        swaps[1].start()
        low = ins["low_all"][...].astype(jnp.bfloat16)
        g_cond[...] = sum(dot_nt(part, low) for part in parts)

    def third():
        swaps[2].arrive()
        d_cond = jnp.sum(dc_got[...], 0)[:cols] * silu_slope(ins["cond"][...])
        parts = thirds(d_cond)
        weight = ins["wt2"][...].astype(jnp.bfloat16)
        share(sum(dot_tn(weight, part) for part in parts), dh_part)
        swaps[3].start()
        classes = lax.broadcasted_iota(jnp.int32, (lab_all.shape[0], g_cls.shape[1]), 1).astype(jnp.float32)
        labels = jnp.concatenate([lab_all[...]] * (g_cls.shape[1] // 128), 1)
        onehot = (labels == classes).astype(jnp.bfloat16)
        g_cls[...] = sum(jnp.dot(part, onehot, preferred_element_type=jnp.float32) for part in parts)
        hidden = ins["hid_all"][...].astype(jnp.bfloat16)
        g_t2[...] = sum(dot_nt(part, hidden) for part in parts)
        ones = jnp.ones((8, lab_all.shape[0]), jnp.bfloat16)
        keep["t2"] = sum(dot_nt(ones, part) for part in parts)

    def fourth():
        swaps[1].arrive()
        swaps[3].arrive()
        d_pre = jnp.sum(dh_got[...], 0)[:cols] * silu_slope(pre[...])
        parts = thirds(d_pre)
        feats = ins["feat_all"][...].astype(jnp.bfloat16)
        g_t1[...] = sum(jnp.dot(part, feats, preferred_element_type=jnp.float32) for part in parts)
        ones = jnp.ones((8, lab_all.shape[0]), jnp.bfloat16)
        keep["t1"] = sum(dot_nt(ones, part) for part in parts)
        total = jnp.zeros((1, 1), jnp.float32)
        for ref in (g_cond, g_t1, g_t2, g_cls, ins["done_in"], ins["done_out"]):
            total = total + jnp.sum(ref[...] * ref[...])
        keep["squares"] = total

    def message():
        total = keep["squares"]
        for ref in shards:
            total = total + jnp.sum(ref[...] * ref[...])
        bias_cond = jnp.sum(dm_all[...], 0, keepdims=True)
        blank = jnp.zeros((1, 128 - cols), jnp.float32)
        lines = [jnp.concatenate([keep[name][0:1, :], blank], 1) for name in ("t1", "t2")]
        lines.append(parts_of(total))
        lines.append(parts_of(ins["loss"][0:1, :]))
        lines += [bias_cond[:, 128 * k : 128 * (k + 1)] for k in range(3)]
        lines.append(jnp.zeros((9, 128), jnp.float32))
        lines.insert(0, jnp.sum(small_got[...], 0))
        merged[me // PLANE, me % PLANE] = jnp.concatenate(lines, 0).astype(jnp.bfloat16)
        swaps[4].start()
        swaps[4].between()

    def last():
        swaps[4].arrive()
        for swap in swaps:
            swap.sent()

    betweens = [
        swaps[0].between,
        functools.partial(swaps[1].between, add_small),
        functools.partial(swaps[2].between, add_dc),
        functools.partial(swaps[3].between, add_dh),
    ]
    return [first, second, third, fourth, message, last], betweens


def dot_nn(left, right):
    return lax.dot_general(left, right, (((1,), (0,)), ((), ())), preferred_element_type=jnp.float32)


def norm_parts(value):
    centered = value - jnp.mean(value, -1, keepdims=True)
    scale = lax.rsqrt(jnp.mean(centered * centered, -1, keepdims=True) + 1e-06)
    return centered * scale, scale


def norm_back(normed, scale, d_normed):
    inner = jnp.mean(d_normed * normed, -1, keepdims=True)
    return scale * (d_normed - jnp.mean(d_normed, -1, keepdims=True) - normed * inner)


GELU_C = math.sqrt(2.0 / math.pi)


def gelu_value(u):
    return 0.5 * u * (1.0 + jnp.tanh(GELU_C * (u + 0.044715 * u * u * u)))


def gelu_slope(u):
    square = u * u
    t = jnp.tanh(GELU_C * u * (1.0 + 0.044715 * square))
    return 0.5 * (1.0 + t) + 0.5 * u * (1.0 - t * t) * (GELU_C * (1.0 + 3 * 0.044715 * square))


def head_masks(shape):
    low_half = lax.broadcasted_iota(jnp.int32, shape, 1) < HEAD_DIM
    return low_half, jnp.logical_not(low_half)


class Weights:
    def __init__(self, hbm, vmem, sems):
        w_in, w_out = hbm
        self.w_in, self.w_out = vmem
        cut = 3 * MODEL_WIDTH
        spans = [
            (w_in.at[pl.ds(0, cut), :], self.w_in.at[pl.ds(0, cut), :]),
            (w_out.at[:, pl.ds(0, MODEL_WIDTH)], self.w_out.at[:, pl.ds(0, MODEL_WIDTH)]),
            (w_in.at[pl.ds(cut, FF), :], self.w_in.at[pl.ds(cut, FF), :]),
            (w_out.at[:, pl.ds(MODEL_WIDTH, FF)], self.w_out.at[:, pl.ds(MODEL_WIDTH, FF)]),
        ]
        self.copies = [pltpu.make_async_copy(src, dst, sems.at[i]) for i, (src, dst) in enumerate(spans)]

    def start(self, order):
        @pl.when(pl.program_id(0) == 0)
        def _():
            for i in order:
                self.copies[i].start()

    def need(self, i):
        @pl.when(pl.program_id(0) == 0)
        def _():
            self.copies[i].wait()


def forward_image(x_ref, mod, weights, b_in, b_out, outs, hook=lambda: None):
    h1, qkv, probs, o, a, x1, h2, u, g, f = outs
    shift1, scale1, gate1, shift2, scale2, gate2 = (mod[0, i : i + 1, :] for i in range(6))
    width = MODEL_WIDTH
    hook()
    x = x_ref[...]
    h1[...] = (norm_parts(x)[0] * (1 + scale1) + shift1).astype(jnp.bfloat16)
    weights.need(0)
    for j in range(3):
        span = slice(j * width, (j + 1) * width)
        qkv[:, span] = (dot_nt(h1[...], weights.w_in[span, :]) + b_in[:, span]).astype(jnp.bfloat16)
    hook()
    for pair in range(HEADS // 2):
        lanes = slice(128 * pair, 128 * (pair + 1))
        q, k, v = (qkv[:, j * width + 128 * pair : j * width + 128 * (pair + 1)] for j in range(3))
        q = q * jnp.bfloat16(HEAD_DIM**-0.5)
        zero = jnp.zeros_like(q)
        mixed = None
        for half, mask in enumerate(head_masks(q.shape)):
            scores = dot_nt(jnp.where(mask, q, zero), k)
            expo = jnp.exp(scores - jnp.max(scores, -1, keepdims=True))
            weight = (expo * pl.reciprocal(jnp.sum(expo, -1, keepdims=True))).astype(jnp.bfloat16)
            probs[0, 2 * pair + half] = weight
            term = dot_nn(weight, jnp.where(mask, v, zero))
            mixed = term if mixed is None else mixed + term
        o[:, lanes] = mixed.astype(jnp.bfloat16)
        hook()
    weights.need(1)
    branch = dot_nt(o[...], weights.w_out[:, :width]) + b_out[:, :width]
    a[...] = branch.astype(jnp.bfloat16)
    x1[...] = x + gate1 * branch
    h2[...] = (norm_parts(x1[...])[0] * (1 + scale2) + shift2).astype(jnp.bfloat16)
    hook()
    weights.need(2)
    weights.need(3)
    total = None
    for j in range(FF // width):
        span = slice(j * width, (j + 1) * width)
        rows = slice((3 + j) * width, (4 + j) * width)
        value = dot_nt(h2[...], weights.w_in[rows, :]) + b_in[:, rows]
        u[:, span] = value.astype(jnp.bfloat16)
        g[:, span] = gelu_value(value).astype(jnp.bfloat16)
        term = dot_nt(g[:, span], weights.w_out[:, (1 + j) * width : (2 + j) * width])
        total = term if total is None else total + term
        hook()
    ffn = total + b_out[:, width:]
    f[...] = ffn.astype(jnp.bfloat16)
    return x1[...] + gate2 * ffn


def head_kernel(scale_out, x, mod, w_in, w_out, b_in, b_out, final, head_t, b_head, targets_t, *refs):
    outs, (dx, d_final, g_head, g_bias, loss), (vm_in, vm_out, sems) = refs[:10], refs[10:15], refs[15:]
    weights = Weights((w_in, w_out), (vm_in, vm_out), sems)
    weights.start((0, 1, 2, 3))
    last = forward_image(x, mod, weights, b_in, b_out, outs)
    normed, scale = norm_parts(last)
    shift_row, scale_row = final[0, 0:1, :], final[0, 1:2, :]
    shaped = (normed * (1 + scale_row) + shift_row).astype(jnp.bfloat16)
    low = head_t[...].astype(jnp.bfloat16)
    error = dot_nt(low, shaped) + b_head[...] - targets_t[0]
    d_out = (error * scale_out).astype(jnp.bfloat16)

    @pl.when(pl.program_id(0) == 0)
    def _():
        g_head[...] = jnp.zeros_like(g_head)
        g_bias[...] = jnp.zeros_like(g_bias)
        loss[...] = jnp.zeros_like(loss)

    g_head[...] += dot_nn(d_out, shaped)
    g_bias[...] += jnp.sum(d_out.astype(jnp.float32), 1, keepdims=True)
    loss[...] += jnp.sum(error * error)
    d_shaped = dot_tn(d_out, low)
    d_final[0, 0:1, :] = jnp.sum(d_shaped, 0, keepdims=True)
    d_final[0, 1:2, :] = jnp.sum(d_shaped * normed, 0, keepdims=True)
    dx[...] = norm_back(normed, scale, d_shaped * (1 + scale_row))


WEIGHT_SCRATCH = [
    pltpu.VMEM((IW, MODEL_WIDTH), jnp.bfloat16),
    pltpu.VMEM((MODEL_WIDTH, OW), jnp.bfloat16),
    pltpu.SemaphoreType.DMA((4,)),
]


def token_block(width):
    return pl.BlockSpec((SEQ, width), lambda i: (i, 0))


def image_block(*dims):
    return pl.BlockSpec((1,) + dims, lambda i: (i,) + (0,) * len(dims))


def whole_block(*dims):
    return pl.BlockSpec(dims, lambda i: (0,) * len(dims))


def kept_shapes(images):
    tokens, width, low, full = images * SEQ, MODEL_WIDTH, jnp.bfloat16, jnp.float32
    shapes = [((tokens, width), low), ((tokens, 3 * width), low), ((images, HEADS, SEQ, SEQ), low), ((tokens, width), low),
              ((tokens, width), low), ((tokens, width), full), ((tokens, width), low), ((tokens, FF), low),
              ((tokens, FF), low), ((tokens, width), low)]
    specs = [token_block(s[1]) if len(s) == 2 else image_block(*s[1:]) for s, _ in shapes]
    return [jax.ShapeDtypeStruct(s, t) for s, t in shapes], specs


def forward_specs():
    any_block = pl.BlockSpec(memory_space=pl.ANY)
    return [token_block(MODEL_WIDTH), image_block(6, MODEL_WIDTH), any_block, any_block, whole_block(1, IW),
            whole_block(1, 2 * MODEL_WIDTH)]


def forward_head(ins, scale_out):
    images = ins[1].shape[0]
    shapes, specs = kept_shapes(images)
    extra = [(images * SEQ, MODEL_WIDTH), (images, 2, MODEL_WIDTH), (PO, MODEL_WIDTH), (PO, 128), (8, 128)]
    return pl.pallas_call(
        functools.partial(head_kernel, scale_out),
        grid=(images,),
        out_shape=shapes + [jax.ShapeDtypeStruct(s, jnp.float32) for s in extra],
        in_specs=forward_specs()
        + [image_block(2, MODEL_WIDTH), whole_block(PO, MODEL_WIDTH), whole_block(PO, 1), image_block(PO, SEQ)],
        out_specs=specs
        + [token_block(MODEL_WIDTH), image_block(2, MODEL_WIDTH), whole_block(PO, MODEL_WIDTH), whole_block(PO, 128),
           whole_block(8, 128)],
        scratch_shapes=WEIGHT_SCRATCH,
        compiler_params=pltpu.CompilerParams(vmem_limit_bytes=56 << 20),
        name="forward_head",
    )(*ins)


def backward_image(refs, mod, weights, outs, hook=lambda: None):
    up_ref, x_ref, x1_ref, probs, qkv, a, f, u = refs
    dx, d_qkv, d_u, d_f, d_a, d_mod, g_bin, g_bout = outs
    width = MODEL_WIDTH
    shift1, scale1, gate1, shift2, scale2, gate2 = (mod[0, i : i + 1, :] for i in range(6))

    @pl.when(pl.program_id(0) == 0)
    def _():
        g_bin[...] = jnp.zeros_like(g_bin)
        g_bout[...] = jnp.zeros_like(g_bout)

    def rows_sum(value):
        return jnp.sum(value.astype(jnp.float32), 0, keepdims=True)

    hook()
    upstream = up_ref[...]
    d_f[...] = (gate2 * upstream).astype(jnp.bfloat16)
    d_mod[0, 5:6, :] = rows_sum(f[...].astype(jnp.float32) * upstream)
    g_bout[:, width:] += rows_sum(d_f[...])
    weights.need(3)
    weights.need(2)
    d_h2 = None
    for j in range(FF // width):
        span = slice(j * width, (j + 1) * width)
        rows = slice((3 + j) * width, (4 + j) * width)
        d_g = dot_nn(d_f[...], weights.w_out[:, (1 + j) * width : (2 + j) * width])
        d_u[:, span] = (d_g * gelu_slope(u[:, span].astype(jnp.float32))).astype(jnp.bfloat16)
        g_bin[:, rows] += rows_sum(d_u[:, span])
        term = dot_nn(d_u[:, span], weights.w_in[rows, :])
        d_h2 = term if d_h2 is None else d_h2 + term
        hook()
    normed, scale = norm_parts(x1_ref[...])
    d_mod[0, 3:4, :] = rows_sum(d_h2)
    d_mod[0, 4:5, :] = rows_sum(d_h2 * normed)
    upstream = upstream + norm_back(normed, scale, d_h2 * (1 + scale2))
    d_mod[0, 2:3, :] = rows_sum(a[...].astype(jnp.float32) * upstream)
    d_a[...] = (gate1 * upstream).astype(jnp.bfloat16)
    g_bout[:, :width] += rows_sum(d_a[...])
    dx[...] = upstream
    weights.need(1)
    d_o = dot_nn(d_a[...], weights.w_out[:, :width]).astype(jnp.bfloat16)
    hook()
    root = HEAD_DIM**-0.5
    for pair in range(HEADS // 2):
        lanes = [slice(j * width + 128 * pair, j * width + 128 * (pair + 1)) for j in range(3)]
        q, k, v = (qkv[:, s] for s in lanes)
        d_mixed = d_o[:, 128 * pair : 128 * (pair + 1)]
        zero = jnp.zeros_like(q)
        sums = [None] * 3
        for half, mask in enumerate(head_masks(q.shape)):
            weight = probs[0, 2 * pair + half]
            full = weight.astype(jnp.float32)
            d_masked = jnp.where(mask, d_mixed, zero)
            d_probs = dot_nt(d_masked, v)
            d_scores = (full * (d_probs - jnp.sum(full * d_probs, -1, keepdims=True))).astype(jnp.bfloat16)
            terms = (
                dot_nn(d_scores, jnp.where(mask, k, zero)),
                dot_tn(d_scores, jnp.where(mask, q, zero)),
                dot_tn(weight, d_masked),
            )
            sums = [t if s is None else s + t for s, t in zip(sums, terms)]
        d_qkv[:, lanes[0]] = (sums[0] * root).astype(jnp.bfloat16)
        d_qkv[:, lanes[1]] = (sums[1] * root).astype(jnp.bfloat16)
        d_qkv[:, lanes[2]] = sums[2].astype(jnp.bfloat16)
        hook()
    weights.need(0)
    d_h1 = None
    for j in range(3):
        span = slice(j * width, (j + 1) * width)
        g_bin[:, span] += rows_sum(d_qkv[:, span])
        term = dot_nn(d_qkv[:, span], weights.w_in[span, :])
        d_h1 = term if d_h1 is None else d_h1 + term
    normed, scale = norm_parts(x_ref[...])
    d_mod[0, 0:1, :] = rows_sum(d_h1)
    d_mod[0, 1:2, :] = rows_sum(d_h1 * normed)
    dx[...] += norm_back(normed, scale, d_h1 * (1 + scale1))
    hook()


def backward_kernel(mod, w_in, w_out, *refs):
    ins, outs, (vm_in, vm_out, sems) = refs[:8], refs[8:16], refs[16:]
    weights = Weights((w_in, w_out), (vm_in, vm_out), sems)
    weights.start((3, 2, 1, 0))
    backward_image(ins, mod, weights, outs)


def backward_block(mods, w_in, w_out, refs):
    images, width, low, full = mods.shape[0], MODEL_WIDTH, jnp.bfloat16, jnp.float32
    tokens = images * SEQ
    any_block = pl.BlockSpec(memory_space=pl.ANY)
    shapes = [((tokens, width), full), ((tokens, 3 * width), low), ((tokens, FF), low), ((tokens, width), low),
              ((tokens, width), low), ((images, 6, width), full), ((1, IW), full), ((1, 2 * width), full)]
    return pl.pallas_call(
        backward_kernel,
        grid=(images,),
        out_shape=[jax.ShapeDtypeStruct(s, t) for s, t in shapes],
        in_specs=[image_block(6, width), any_block, any_block, token_block(width), token_block(width), token_block(width),
                  image_block(HEADS, SEQ, SEQ), token_block(3 * width), token_block(width), token_block(width),
                  token_block(FF)],
        out_specs=[token_block(s[1]) for s, _ in shapes[:5]]
        + [image_block(6, width), whole_block(1, IW), whole_block(1, 2 * width)],
        scratch_shapes=WEIGHT_SCRATCH,
        compiler_params=pltpu.CompilerParams(vmem_limit_bytes=56 << 20),
        name="backward_block",
    )(mods, w_in, w_out, *refs)


def gather_steps(job):
    steps = [job.begin, functools.partial(job.a_step, 0)]
    for dist in (1, 2, 3):
        steps += [functools.partial(job.z_step, dist), functools.partial(job.a_step, dist)]
    for dist in range(4):
        steps += [functools.partial(job.b_step, dist, flip) for flip in range(2)]
    return steps + [job.finish]


class Hooks:
    def __init__(self, steps, slots, points):
        self.points, self.table = points, {}
        for step, slot in zip(steps, slots):
            self.table.setdefault((slot // points, slot % points), []).append(step)
        self.next = 0

    def __call__(self):
        point, self.next = self.next, self.next + 1
        for (turn, where), steps in sorted(self.table.items(), key=lambda item: item[0]):
            if where == point:

                @pl.when(pl.program_id(0) == turn)
                def _():
                    for step in steps:
                        step()


def start_kernel(devices, *refs):
    own, mod_ins, refs = refs[:2], refs[2:10], refs[10:]
    full, mod_outs, refs = refs[:2], refs[2:10], refs[10:]
    part, mod_bufs, mod_sems = refs[:10], refs[10:14], refs[14:]
    place = Place()
    place.greet()
    job = Gather(place, [ref.at[0] for ref in own], part[:2], part[2:4], full, part[4:])
    parts = modulate_steps(devices, mod_ins, mod_outs, mod_bufs, mod_sems)
    moves = gather_steps(job)
    for kind in START_ORDER:
        (parts if kind == "a" else moves).pop(0)()


START_ORDER = "ag" "aa" "gg" "a" "g" "a" "g" "a" "g" "a" "gg" "a" "gggggggg" "a" "g"


def gather_modulate(pair, ins):
    devices = lax.axis_size(AXIS)
    msg, wt1, wt2, wcls, wcond = ins[:5]
    cols, images = wt1.shape[0], ins[5].shape[1]
    outs = [
        (LINE, PLANE, images // devices, wcond.shape[0]), (cols, images), (cols, images), (devices * cols, images),
        (devices * cols, images), (images, FREQ), (images, 128),
    ]
    padded = -(-cols // 16) * 16
    vmem = pl.BlockSpec(memory_space=pltpu.VMEM)
    return pl.pallas_call(
        functools.partial(start_kernel, devices),
        out_shape=[full_shape(a) for a in pair]
        + [jax.ShapeDtypeStruct(shape, jnp.float32) for shape in outs]
        + [jax.ShapeDtypeStruct((LINE, PLANE) + msg.shape, jnp.bfloat16)],
        in_specs=[vmem] * 10,
        out_specs=[pl.BlockSpec(memory_space=pl.ANY)] * 2 + [vmem] * 8,
        scratch_shapes=gather_scratch(piece_shapes([a.shape[1:] for a in pair]))
        + [
            pltpu.VMEM((LINE, PLANE, padded, images), jnp.bfloat16),
            pltpu.VMEM((LINE, PLANE, padded, images), jnp.bfloat16),
            pltpu.VMEM((LINE, PLANE, images // devices, wcond.shape[0]), jnp.float32),
            pltpu.VMEM((LINE, PLANE, images // devices, wcond.shape[0]), jnp.float32),
            pltpu.SemaphoreType.DMA((4, LINE + PLANE)),
            pltpu.SemaphoreType.DMA((4, LINE + PLANE)),
        ],
        compiler_params=pltpu.CompilerParams(collective_id=3, has_side_effects=True, vmem_limit_bytes=56 << 20),
        name="gather_modulate",
    )(*pair, *ins)


FORWARD_POINTS = 13


def forward_gather_kernel(slots, x, mod, w_in, w_out, b_in, b_out, own_in, own_out, *refs):
    outs, x_out, full, refs = refs[:10], refs[10], refs[11:13], refs[13:]
    vm_in, vm_out, sems, part = refs[0], refs[1], refs[2], refs[3:]
    place = Place()
    job = Gather(place, (own_in.at[0], own_out.at[0]), part[:2], part[2:4], full, part[4:])
    hooks = Hooks([place.greet] + gather_steps(job), slots, FORWARD_POINTS)
    weights = Weights((w_in, w_out), (vm_in, vm_out), sems)
    weights.start((0, 1, 2, 3))
    x_out[...] = forward_image(x, mod, weights, b_in, b_out, outs, hooks)


GATHER_SLOTS = (0, 0, 13, 15, 26, 28, 39, 41, 50) + (34, 43, 48, 51, 51, 51, 51, 51, 51)


def layer_block(array, layer):
    return pl.BlockSpec((1,) + array.shape[1:], lambda i: (layer, 0, 0))


def full_shape(array):
    return jax.ShapeDtypeStruct((lax.axis_size(AXIS) * array.shape[1], array.shape[2]), jnp.bfloat16)


def forward_gather(ins, pair, layer):
    images = ins[1].shape[0]
    shapes, specs = kept_shapes(images)
    any_block = pl.BlockSpec(memory_space=pl.ANY)
    return pl.pallas_call(
        functools.partial(forward_gather_kernel, GATHER_SLOTS),
        grid=(images,),
        out_shape=shapes
        + [jax.ShapeDtypeStruct((images * SEQ, MODEL_WIDTH), jnp.float32)]
        + [full_shape(a) for a in pair],
        in_specs=forward_specs() + [layer_block(a, layer) for a in pair],
        out_specs=specs + [token_block(MODEL_WIDTH)] + [any_block] * 2,
        scratch_shapes=WEIGHT_SCRATCH + gather_scratch(piece_shapes([a.shape[1:] for a in pair])),
        compiler_params=pltpu.CompilerParams(collective_id=1, has_side_effects=True, vmem_limit_bytes=58 << 20),
        name="forward_gather",
    )(*ins, *pair)


GRAD_CUTS = [3 * MODEL_WIDTH // MODEL_WIDTH, FF // MODEL_WIDTH]


class Grads:
    def __init__(self, hbm, bufs, keep_in, keep_out, sems):
        bufs = [bufs[0], bufs[4], *bufs[1:]]
        self.bufs, self.keep_in, self.keep_out = bufs, keep_in, keep_out
        self.copies = [pltpu.make_async_copy(src, dst, sems.at[i]) for i, (src, dst) in enumerate(zip(hbm, bufs))]
        self.here = set()

    def start(self):
        for i in (4, 5, 6, 7, 2, 3, 0):
            self.copies[i].start()

    def need(self, *which):
        for i in which:
            if i not in self.here:
                self.copies[i].wait()
                self.here.add(i)

    def rows_in(self, chunk):
        width = MODEL_WIDTH
        pair = 0 if chunk < 3 else 1
        self.need(2 * pair, 2 * pair + 1)
        left, right = self.bufs[2 * pair], self.bufs[2 * pair + 1]
        at = (chunk - 3 * pair) * width
        self.keep_in[chunk * width : (chunk + 1) * width, :] = dot_tn(left[:, at : at + width], right[...]).astype(
            jnp.bfloat16
        )

    def rows_out(self, part):
        width = MODEL_WIDTH
        rows = slice(part * width // 2, (part + 1) * width // 2)
        self.need(4, 5)
        self.keep_out[rows, :width] = dot_tn(self.bufs[4][:, rows], self.bufs[5][...]).astype(jnp.bfloat16)
        self.need(6, 7)
        for j in range(FF // width):
            span = slice(j * width, (j + 1) * width)
            self.keep_out[rows, (1 + j) * width : (2 + j) * width] = dot_tn(
                self.bufs[6][:, rows], self.bufs[7][:, span]
            ).astype(jnp.bfloat16)
        if part == 0:
            self.copies[1].start()


def grads_out_kernel(*refs):
    ins, g_in, total, refs = refs[:8], refs[8], refs[9:10], refs[10:]
    bufs, keep_in, keep_out, load_sems, store_sem, refs = refs[:7], refs[7], refs[8], refs[9], refs[10], refs[11:]
    place = Place()
    work = Grads(ins, bufs, keep_in, keep_out, load_sems)
    work.start()
    place.greet()
    job = Scatter(place, [keep_out], total, refs[:6], refs[6:])
    work.rows_out(1)
    job.open(3)
    job.open(2)
    work.rows_out(0)
    job.open(0)
    job.open(1)
    moves = job.steps()
    for chunk in range(7):
        moves[chunk]()
        work.rows_in(chunk)
    store = pltpu.make_async_copy(keep_in, g_in, store_sem)
    store.start()
    for move in moves[7:]:
        move()
    store.wait()


def grad_bufs(ins):
    return [pltpu.VMEM(a.shape, a.dtype) for i, a in enumerate(ins) if i != 1] + [
        pltpu.VMEM((IW, MODEL_WIDTH), jnp.bfloat16),
        pltpu.VMEM((MODEL_WIDTH, OW), jnp.bfloat16),
        pltpu.SemaphoreType.DMA((8,)),
    ]


def weight_grads_out(ins, shape):
    any_block = pl.BlockSpec(memory_space=pl.ANY)
    return pl.pallas_call(
        grads_out_kernel,
        out_shape=[jax.ShapeDtypeStruct((IW, MODEL_WIDTH), jnp.bfloat16), jax.ShapeDtypeStruct(shape, jnp.float32)],
        in_specs=[any_block] * 8,
        out_specs=[any_block, pl.BlockSpec(memory_space=pltpu.VMEM)],
        scratch_shapes=grad_bufs(ins) + [pltpu.SemaphoreType.DMA] + scatter_scratch(piece_shapes([shape])),
        compiler_params=pltpu.CompilerParams(collective_id=5, has_side_effects=True, vmem_limit_bytes=58 << 20),
        name="weight_grads_out",
    )(*ins)


BACKWARD_POINTS = 13


def backward_scatter_kernel(slots, mod, w_in, w_out, grad, lat_t, *refs):
    ins, outs, (g_patch, g_pbias, total), refs = refs[:8], refs[8:16], refs[16:19], refs[19:]
    vm_in, vm_out, sems, mine, refs = refs[0], refs[1], refs[2], refs[3], refs[4:]
    place = Place()
    job = Scatter(place, [grad], [total], refs[:6], refs[6:], [mine])
    hooks = Hooks([place.greet, job.open_all] + job.steps(), slots, BACKWARD_POINTS)
    weights = Weights((w_in, w_out), (vm_in, vm_out), sems)
    weights.start((3, 2, 1, 0))
    backward_image(ins, mod, weights, outs, hooks)
    d_patch = outs[0][...].astype(jnp.bfloat16)

    @pl.when(pl.program_id(0) == 0)
    def _():
        g_patch[...] = jnp.zeros_like(g_patch)
        g_pbias[...] = jnp.zeros_like(g_pbias)

    g_patch[...] += dot_nn(lat_t[0], d_patch)
    g_pbias[...] += jnp.sum(d_patch.astype(jnp.float32), 0, keepdims=True)


SCATTER_SLOTS = (0, 0, 3, 6, 10, 13, 18, 25, 27, 32, 34, 38, 42, 51, 51, 51, 51)


def backward_scatter(mods, w_in, w_out, refs, grad, lat_t, shape):
    images, width, low, full = mods.shape[0], MODEL_WIDTH, jnp.bfloat16, jnp.float32
    tokens = images * SEQ
    any_block = pl.BlockSpec(memory_space=pl.ANY)
    shapes = [((tokens, width), full), ((tokens, 3 * width), low), ((tokens, FF), low), ((tokens, width), low),
              ((tokens, width), low), ((images, 6, width), full), ((1, IW), full), ((1, 2 * width), full),
              ((PD, width), full), ((1, width), full), (shape, full)]
    pieces = piece_shapes([shape])
    return pl.pallas_call(
        functools.partial(backward_scatter_kernel, SCATTER_SLOTS),
        grid=(images,),
        out_shape=[jax.ShapeDtypeStruct(s, t) for s, t in shapes],
        in_specs=[image_block(6, width), any_block, any_block, any_block, image_block(PD, SEQ), token_block(width),
                  token_block(width), token_block(width), image_block(HEADS, SEQ, SEQ), token_block(3 * width),
                  token_block(width), token_block(width), token_block(FF)],
        out_specs=[token_block(s[1]) for s, _ in shapes[:5]]
        + [image_block(6, width)] + [whole_block(*s) for s, _ in shapes[6:-1]] + [any_block],
        scratch_shapes=WEIGHT_SCRATCH
        + [pltpu.VMEM((16,) + pieces[0], jnp.bfloat16)] + scatter_scratch(pieces),
        compiler_params=pltpu.CompilerParams(collective_id=6, has_side_effects=True, vmem_limit_bytes=62 << 20),
        name="backward_scatter",
    )(mods, w_in, w_out, grad, lat_t, *refs)


def finish_kernel(devices, *refs):
    count = len(SETTLE_INS)
    ins, set_ins, refs = refs[:8], dict(zip(SETTLE_INS, refs[8 : 8 + count])), refs[8 + count :]
    totals, set_outs, refs = refs[:2], refs[2:7], refs[7:]
    bufs, keep_in, keep_out, load_sems, refs = refs[:7], refs[7], refs[8], refs[9], refs[10:]
    sc_bufs, sc_sems, refs = refs[:12], refs[12:24], refs[24:]
    set_bufs, set_sems = refs[:16], refs[16:]
    work = Grads(ins, bufs, keep_in, keep_out, load_sems)
    work.start()
    place = Place()
    place.greet()
    job = Scatter(place, [keep_in, keep_out], totals, sc_bufs, sc_sems)
    (first, second, third, fourth, message, last), betweens = settle_steps(
        devices, set_ins, set_outs, set_bufs, set_sems, totals
    )
    first()
    work.rows_out(1)
    betweens[0]()
    work.rows_in(5)
    work.rows_in(6)
    second()
    job.open(3)
    work.rows_out(0)
    betweens[2]()
    job.cross_b(3)
    work.rows_in(0)
    work.rows_in(1)
    job.open(0)
    third()
    work.rows_in(3)
    job.cross_b(0)
    work.rows_in(4)
    job.open(2)
    job.cross_a(3)
    work.rows_in(2)
    job.cross_b(2)
    job.open(1)
    job.cross_a(0)
    job.along_z(3)
    job.cross_b(1)
    betweens[1]()
    betweens[3]()
    job.cross_a(2)
    job.along_z(0)
    job.cross_a(1)
    job.along_z(2)
    fourth()
    job.along_z(1)
    job.close()
    job.end()
    message()
    job.finish()
    last()


def finish_grads(ins, shapes, set_ins):
    devices = lax.axis_size(AXIS)
    wcond, d_mods = set_ins["wcond"], set_ins["d_mods"]
    cols, images = set_ins["pre"].shape
    outs = [(wcond.shape[0], devices * cols), (cols, FREQ), (cols, devices * cols), (cols, 1024)]
    vmem = pl.BlockSpec(memory_space=pltpu.VMEM)
    low = jnp.bfloat16
    return pl.pallas_call(
        functools.partial(finish_kernel, devices),
        out_shape=[jax.ShapeDtypeStruct(shape, jnp.float32) for shape in list(shapes) + outs]
        + [jax.ShapeDtypeStruct((LINE, PLANE, 32, 128), low)],
        in_specs=[pl.BlockSpec(memory_space=pl.ANY)] * 8 + [vmem] * len(SETTLE_INS),
        out_specs=[vmem] * 7,
        scratch_shapes=grad_bufs(ins)
        + scatter_scratch(piece_shapes(shapes))
        + [
            pltpu.VMEM(d_mods.shape, jnp.float32),
            pltpu.VMEM(d_mods.shape, jnp.float32),
            pltpu.VMEM((images, 384), jnp.float32),
            pltpu.VMEM((devices * 16, 128), jnp.float32),
            pltpu.VMEM((LINE, PLANE, 16, 128), low),
            pltpu.VMEM((LINE, PLANE, 16, 128), low),
            pltpu.VMEM((LINE, 16, 128), jnp.float32),
            pltpu.VMEM((LINE, 16, 128), jnp.float32),
        ]
        + [
            pltpu.VMEM((LINE, PLANE, 32, images), low),
            pltpu.VMEM((LINE, PLANE, 32, images), low),
            pltpu.VMEM((LINE, 32, images), jnp.float32),
            pltpu.VMEM((LINE, 32, images), jnp.float32),
        ]
        * 2
        + [
            pltpu.SemaphoreType.DMA((5, LINE + PLANE)),
            pltpu.SemaphoreType.DMA((5, LINE + PLANE)),
        ],
        compiler_params=pltpu.CompilerParams(collective_id=4, has_side_effects=True, vmem_limit_bytes=63 << 20),
        name="finish_grads",
    )(*ins, *(set_ins[name] for name in SETTLE_INS))

def code_table():
    quarter = MODEL_WIDTH // 4
    omega = (1.0 / 10000.0 ** (np.arange(quarter, dtype=np.float32) / np.float32(quarter))).astype(np.float32)
    angles = np.arange(GRID, dtype=np.float32)[:, None] * omega
    return np.concatenate([np.sin(angles), np.cos(angles)], 1).astype(np.float32)


def position_sum():
    table = jnp.asarray(code_table())
    half = MODEL_WIDTH // 2
    rows_pos = jnp.broadcast_to(table[:, None, :], (GRID, GRID, half))
    cols_pos = jnp.broadcast_to(table[None, :, :], (GRID, GRID, half))
    return jnp.concatenate([rows_pos, cols_pos], -1).reshape(SEQ, MODEL_WIDTH)


def rows_t(left, right):
    return jnp.einsum("bsd,ed->bse", left, right, preferred_element_type=jnp.float32)


def body(
    latents, targets, timesteps, labels, embed_w, embed_m, embed_v, cond_w, cond_m, cond_v, layer_input_weights, in_m,
    in_v, layer_output_weights, out_m, out_v, head_w, head_m, head_v, biases, bias_m, bias_v,
):
    devices = lax.axis_size("fsdp")
    me = lax.axis_index("fsdp")
    images = latents.shape[0]
    embed_t = embed_w.T
    cond_t = cond_w.T
    in_t = layer_input_weights.transpose(0, 2, 1)
    out_t = layer_output_weights.transpose(0, 2, 1)
    cols, cond_cols = embed_t.shape[0], cond_t.shape[0]
    time_one, time_two, patch_bias, cond_bias, block_input_bias, block_output_bias, head_bias = split_biases(biases)
    features = time_features(timesteps)
    own_patch_w = jnp.pad(embed_t[:, FREQ + MODEL_WIDTH : FREQ + MODEL_WIDTH + PD].reshape(3, 128), ((0, 1), (0, 0)))
    digits = jnp.stack([labels // 32, labels % 32], 1).astype(jnp.float32)
    digits = jnp.broadcast_to(digits[:, :, None], (images, 2, 64)).reshape(images, 128)
    note = jnp.concatenate([features[:, :128], features[:, 128:], own_patch_w, digits], 0).astype(jnp.bfloat16)
    w_t1 = embed_t[:, :FREQ]
    w_t2 = embed_t[:, FREQ : FREQ + MODEL_WIDTH]
    w_class = jnp.pad(embed_t[:, FREQ + MODEL_WIDTH + PD :], ((0, 0), (0, 1024 - NCLS)))
    images_all = devices * images

    def own_bias(vector, count):
        part = lax.dynamic_slice(vector, (me * count,), (count,))
        return jnp.broadcast_to(part[:, None], (count, images_all))

    own_cond_bias = lax.dynamic_slice(cond_bias, (me * cond_cols,), (cond_cols,))[None]
    first_in, first_out, mods, pre, cond, hid_all, low_all, feat_all, lab_all, notes = gather_modulate(
        [in_t, out_t],
        [note, w_t1, w_t2, w_class, cond_t, own_bias(time_one, cols), own_bias(time_two, cols), own_cond_bias],
    )
    chunks = mods.reshape(devices, images, cond_cols).transpose(1, 0, 2).reshape(images, 6 * LAYERS + 2, MODEL_WIDTH)
    w_patch = notes[:, :, 8:11].reshape(MODEL_WIDTH, PD)
    x = (rows_t(latents, w_patch) + patch_bias + position_sum()).reshape(images * SEQ, MODEL_WIDTH)
    block_mods = [chunks[:, 6 * i : 6 * (i + 1)] for i in range(LAYERS)]
    head_t = head_w.T
    tokens_all = devices * images * SEQ * PO
    lat_t = latents.transpose(0, 2, 1)
    bias_rows = [(block_input_bias[i][None], block_output_bias[i][None]) for i in range(LAYERS)]
    *kept0, x_mid, last_in, last_out = forward_gather(
        [x, block_mods[0], first_in, first_out, *bias_rows[0]], [in_t, out_t], 1
    )
    *kept1, upstream, d_final, head_grad, head_bias_grad, loss_part = forward_head(
        [x_mid, block_mods[1], last_in, last_out, *bias_rows[1], chunks[:, 6 * LAYERS :], head_t, head_bias[:, None],
         targets.transpose(0, 2, 1)],
        2.0 / tokens_all,
    )
    h1, qkv, probs, o, a, x1, h2, u, g, f = kept1
    upstream, d_qkv, d_u, d_f, d_a, mod_grad1, in_bias1, out_bias1 = backward_block(
        block_mods[1], last_in, last_out, [upstream, x_mid, x1, probs, qkv, a, f, u]
    )
    in_shape, out_shape = in_t.shape[1:], out_t.shape[1:]
    grad_in, out_shard1 = weight_grads_out([d_qkv, h1, d_u, h2, d_a, o, d_f, g], out_shape)
    h1, qkv, probs, o, a, x1, h2, u, g, f = kept0
    (upstream, d_qkv, d_u, d_f, d_a, mod_grad0, in_bias0, out_bias0, patch_grad, patch_bias_grad, in_shard1) = backward_scatter(
        block_mods[0], first_in, first_out, [upstream, x, x1, probs, qkv, a, f, u], grad_in, lat_t, in_shape
    )
    mod_grads, in_bias_grads, out_bias_grads = [mod_grad0, mod_grad1], [in_bias0, in_bias1], [out_bias0, out_bias1]
    d_modulation = jnp.concatenate(mod_grads + [d_final], 1)
    d_mods = d_modulation.reshape(images, devices, cond_cols).transpose(1, 0, 2)
    d_mods = d_mods.reshape(LINE, PLANE, images, cond_cols)
    in_shard0, out_shard0, g_cond, g_t1, g_t2, g_cls, merged = finish_grads(
        [d_qkv, h1, d_u, h2, d_a, o, d_f, g],
        [in_shape, out_shape],
        {
            "d_mods": d_mods, "wt2": w_t2, "wcond": cond_t, "pre": pre, "cond": cond, "hid_all": hid_all, "low_all": low_all,
            "feat_all": feat_all, "lab_all": lab_all, "g_head": head_grad, "g_hbias": head_bias_grad, "loss": loss_part,
            "g_patch": patch_grad, "g_pbias": patch_bias_grad, "bin0": in_bias_grads[0], "bin1": in_bias_grads[1],
            "bout0": out_bias_grads[0], "bout1": out_bias_grads[1], "done_in": in_shard1, "done_out": out_shard1,
        },
    )
    merged = merged.astype(jnp.float32).reshape(devices, 32, 128)
    wide = MODEL_WIDTH // 128
    blocks = merged[:, :16]
    patch_total = blocks[:wide].transpose(1, 0, 2).reshape(PD, MODEL_WIDTH)
    head_total = blocks[wide : 3 * wide].reshape(wide, PO, 128).transpose(1, 0, 2).reshape(PO, MODEL_WIDTH)
    flat = blocks[3 * wide :].reshape(-1)
    rest = LAYERS * (IW + 2 * MODEL_WIDTH) + PO
    loss_total = jnp.sum(merged[:, 19, :3])
    bias_total = jnp.concatenate(
        [merged[:, 16, :cols].reshape(-1), merged[:, 17, :cols].reshape(-1), flat[:MODEL_WIDTH],
         merged[:, 20:23].reshape(devices, 384)[:, :cond_cols].reshape(-1), flat[MODEL_WIDTH : MODEL_WIDTH + rest]]
    )
    grad_norm = jnp.sqrt(
        jnp.sum(merged[:, 18, :3])
        + jnp.sum(head_total * head_total)
        + jnp.sum(patch_total * patch_total)
        + jnp.sum(bias_total * bias_total)
    )
    factor = jnp.minimum(1.0, clip_limit / grad_norm)
    own_patch = lax.dynamic_slice(patch_total, (0, me * cols), (PD, cols)).T
    embed_grad = jnp.concatenate([g_t1, g_t2, own_patch, g_cls[:, :NCLS]], 1)
    embed_up = [a.T for a in adam_step(embed_t, embed_m.T, embed_v.T, embed_grad * factor)]
    cond_up = [a.T for a in adam_step(cond_t, cond_m.T, cond_v.T, g_cond * factor)]
    turn = (0, 2, 1)
    in_up = [
        a.transpose(turn)
        for a in adam_step(in_t, in_m.transpose(turn), in_v.transpose(turn), jnp.stack([in_shard0, in_shard1]) * factor)
    ]
    out_up = [
        a.transpose(turn)
        for a in adam_step(out_t, out_m.transpose(turn), out_v.transpose(turn), jnp.stack([out_shard0, out_shard1]) * factor)
    ]
    head_up = [a.T for a in adam_step(head_t, head_m.T, head_v.T, head_total * factor)]
    bias_up = adam_step(biases, bias_m, bias_v, bias_total * factor)
    return (loss_total, grad_norm, *embed_up, *cond_up, *in_up, *out_up, *head_up, *bias_up)


def fits(mesh):
    return mesh.shape["fsdp"] == 32


def solution(mesh):
    in_specs = (
        P("fsdp", None, None),
        P("fsdp", None, None),
        P("fsdp"),
        P("fsdp"),
        P(None, "fsdp"),
        P(None, "fsdp"),
        P(None, "fsdp"),
        P(None, "fsdp"),
        P(None, "fsdp"),
        P(None, "fsdp"),
        P(None, None, "fsdp"),
        P(None, None, "fsdp"),
        P(None, None, "fsdp"),
        P(None, None, "fsdp"),
        P(None, None, "fsdp"),
        P(None, None, "fsdp"),
        P(),
        P(),
        P(),
        P(),
        P(),
        P(),
    )
    out_specs = (
        P(),
        P(),
        P(None, "fsdp"),
        P(None, "fsdp"),
        P(None, "fsdp"),
        P(None, "fsdp"),
        P(None, "fsdp"),
        P(None, "fsdp"),
        P(None, None, "fsdp"),
        P(None, None, "fsdp"),
        P(None, None, "fsdp"),
        P(None, None, "fsdp"),
        P(None, None, "fsdp"),
        P(None, None, "fsdp"),
        P(),
        P(),
        P(),
        P(),
        P(),
        P(),
    )
    chosen = body if fits(mesh) else generic_body
    return jax.shard_map(chosen, mesh=mesh, in_specs=in_specs, out_specs=out_specs, check_vma=False)
```

```python
import functools
import math

import jax
import jax.numpy as jnp
import numpy as np
from jax import lax
from jax.experimental import pallas as pl
from jax.experimental.pallas import tpu as pltpu
from jax.sharding import PartitionSpec as P

MODEL_WIDTH = 768
HEADS = 12
HEAD_DIM = 64
NCLS = 1001
FREQ = 256
PD = 16
PO = 32
GRID = 16
LAYERS = 2
STEP = 10
SEQ = 256
IW = 5376
OW = 3840
FF = 3072
CW = 10752


learn_rate = 0.03
beta_one = 0.9
beta_two = 0.999
adam_eps = 1e-08
decay = 0.01
clip_limit = 0.01
highest = lax.Precision.HIGHEST


def product(left, right):
    return jnp.dot(left, right, preferred_element_type=jnp.float32)


def exact_dot(left, right):
    return jnp.dot(left, right, precision=highest)


def apply_rows(left, right):
    return jnp.einsum("bsd,de->bse", left, right, preferred_element_type=jnp.float32)


def outer_sum(left, right):
    return jnp.einsum("bsd,bse->de", left, right, preferred_element_type=jnp.float32)


def apply_back(left, right):
    return jnp.einsum("bse,de->bsd", left, right, preferred_element_type=jnp.float32)


def column_sum(value):
    return jnp.sum(value.astype(jnp.float32), (0, 1))


def silu(value):
    return value * jax.nn.sigmoid(value)


def gelu(value):
    return jax.nn.gelu(value, approximate=True)


def layer_norm(value):
    centered = value - jnp.mean(value, -1, keepdims=True)
    return centered * lax.rsqrt(jnp.mean(centered * centered, -1, keepdims=True) + 1e-06)


def local_back(func, value, cotangent):
    return jax.vjp(func, value)[1](cotangent)[0]


def position_table():
    quarter = MODEL_WIDTH // 4
    omega = 1.0 / 10000.0 ** (jnp.arange(quarter, dtype=jnp.float32) / quarter)
    places = jnp.arange(GRID * GRID)
    rows_pos = (places // GRID).astype(jnp.float32)[:, None] * omega
    cols_pos = (places % GRID).astype(jnp.float32)[:, None] * omega
    return jnp.concatenate(
        [jnp.sin(rows_pos), jnp.cos(rows_pos), jnp.sin(cols_pos), jnp.cos(cols_pos)], 1
    )


def time_features(timesteps):
    half_freq = FREQ // 2
    rates = jnp.exp(-math.log(10000.0) * jnp.arange(half_freq, dtype=jnp.float32) / half_freq)
    angles = timesteps.astype(jnp.float32)[:, None] * rates
    return jnp.concatenate([jnp.cos(angles), jnp.sin(angles)], 1)


def split_biases(vector):
    lengths = [MODEL_WIDTH, MODEL_WIDTH, MODEL_WIDTH, CW, LAYERS * IW, LAYERS * 2 * MODEL_WIDTH, PO]
    pieces = []
    offset = 0
    for length in lengths:
        pieces.append(vector[offset : offset + length])
        offset += length
    pieces[4] = pieces[4].reshape(LAYERS, IW)
    pieces[5] = pieces[5].reshape(LAYERS, 2 * MODEL_WIDTH)
    return pieces


def split_heads(triple, which):
    n_images, seq_len = (triple.shape[0], triple.shape[1])
    return triple[..., which * MODEL_WIDTH : (which + 1) * MODEL_WIDTH].reshape(
        n_images, seq_len, HEADS, HEAD_DIM
    )


def attend(triple):
    queries, key_part, values = [split_heads(triple, j) for j in range(3)]
    scores = jnp.einsum(
        "bqhd,bkhd->bhqk", queries, key_part, preferred_element_type=jnp.float32
    ) * HEAD_DIM ** (-0.5)
    row_max = jnp.max(scores, -1, keepdims=True)
    expo = jnp.exp(scores - row_max)
    row_sum = jnp.sum(expo, -1, keepdims=True)
    attn_weights = (expo / row_sum).astype(jnp.bfloat16)
    mixed_heads = jnp.einsum(
        "bhqk,bkhd->bqhd", attn_weights, values, preferred_element_type=jnp.float32
    ).astype(jnp.bfloat16)
    return (
        mixed_heads.reshape(triple.shape[0], triple.shape[1], MODEL_WIDTH),
        row_max + jnp.log(row_sum),
    )


def attend_back(triple, log_norm, d_mixed):
    queries, key_part, values = [split_heads(triple, j) for j in range(3)]
    scale = HEAD_DIM ** (-0.5)
    scores = (
        jnp.einsum("bqhd,bkhd->bhqk", queries, key_part, preferred_element_type=jnp.float32) * scale
    )
    probs_full = jnp.exp(scores - log_norm)
    attn_weights = probs_full.astype(jnp.bfloat16)
    d_heads = d_mixed.reshape(queries.shape)
    d_probs = jnp.einsum("bqhd,bkhd->bhqk", d_heads, values, preferred_element_type=jnp.float32)
    d_values = jnp.einsum(
        "bhqk,bqhd->bkhd", attn_weights, d_heads, preferred_element_type=jnp.float32
    )
    d_scores = (probs_full * (d_probs - jnp.sum(probs_full * d_probs, -1, keepdims=True))).astype(
        jnp.bfloat16
    )
    d_queries = (
        jnp.einsum("bhqk,bkhd->bqhd", d_scores, key_part, preferred_element_type=jnp.float32)
        * scale
    )
    d_keys = (
        jnp.einsum("bhqk,bqhd->bkhd", d_scores, queries, preferred_element_type=jnp.float32) * scale
    )
    shape_flat = (triple.shape[0], triple.shape[1], MODEL_WIDTH)
    return jnp.concatenate(
        [d_queries.reshape(shape_flat), d_keys.reshape(shape_flat), d_values.reshape(shape_flat)],
        -1,
    ).astype(jnp.bfloat16)


def block_forward(residual_state, adaptive_modulation, weights_in, weights_out, bias_in, bias_out):
    pieces = [
        adaptive_modulation[:, None, i * MODEL_WIDTH : (i + 1) * MODEL_WIDTH] for i in range(6)
    ]
    shaped_one = (layer_norm(residual_state) * (1 + pieces[1]) + pieces[0]).astype(jnp.bfloat16)
    triple = (
        apply_rows(shaped_one, weights_in[:, : 3 * MODEL_WIDTH]) + bias_in[: 3 * MODEL_WIDTH]
    ).astype(jnp.bfloat16)
    mixed_heads, log_norm = attend(triple)
    branch = apply_rows(mixed_heads, weights_out[:MODEL_WIDTH]) + bias_out[:MODEL_WIDTH]
    middle = residual_state + pieces[2] * branch
    shaped_two = (layer_norm(middle) * (1 + pieces[4]) + pieces[3]).astype(jnp.bfloat16)
    pre_ffn = apply_rows(shaped_two, weights_in[:, 3 * MODEL_WIDTH :]) + bias_in[3 * MODEL_WIDTH :]
    active = gelu(pre_ffn).astype(jnp.bfloat16)
    ffn_out = apply_rows(active, weights_out[MODEL_WIDTH:]) + bias_out[MODEL_WIDTH:]
    kept = (
        residual_state,
        shaped_one,
        triple,
        log_norm,
        mixed_heads,
        branch,
        middle,
        shaped_two,
        pre_ffn,
        active,
        ffn_out,
    )
    return (middle + pieces[5] * ffn_out, kept)


def block_backward(upstream, adaptive_modulation, weights_in, weights_out, kept):
    (
        residual_state,
        shaped_one,
        triple,
        log_norm,
        mixed_heads,
        branch,
        middle,
        shaped_two,
        pre_ffn,
        active,
        ffn_out,
    ) = kept
    pieces = [
        adaptive_modulation[:, None, i * MODEL_WIDTH : (i + 1) * MODEL_WIDTH] for i in range(6)
    ]
    d_ffn = (pieces[5] * upstream).astype(jnp.bfloat16)
    gate_two = jnp.sum(ffn_out * upstream, 1)
    grad_down = outer_sum(active, d_ffn)
    d_active = apply_back(d_ffn, weights_out[MODEL_WIDTH:])
    d_pre = local_back(gelu, pre_ffn, d_active).astype(jnp.bfloat16)
    grad_up = outer_sum(shaped_two, d_pre)
    d_shaped = apply_back(d_pre, weights_in[:, 3 * MODEL_WIDTH :])
    shift_two = jnp.sum(d_shaped, 1)
    scale_two = jnp.sum(d_shaped * layer_norm(middle), 1)
    upstream = upstream + local_back(layer_norm, middle, d_shaped * (1 + pieces[4]))
    gate_one = jnp.sum(branch * upstream, 1)
    d_branch = (pieces[2] * upstream).astype(jnp.bfloat16)
    grad_proj = outer_sum(mixed_heads, d_branch)
    d_mixed = apply_back(d_branch, weights_out[:MODEL_WIDTH]).astype(jnp.bfloat16)
    d_triple = attend_back(triple, log_norm, d_mixed)
    grad_qkv = outer_sum(shaped_one, d_triple)
    d_shaped = apply_back(d_triple, weights_in[:, : 3 * MODEL_WIDTH])
    shift_one = jnp.sum(d_shaped, 1)
    scale_one = jnp.sum(d_shaped * layer_norm(residual_state), 1)
    upstream = upstream + local_back(layer_norm, residual_state, d_shaped * (1 + pieces[1]))
    mod_grad = jnp.concatenate([shift_one, scale_one, gate_one, shift_two, scale_two, gate_two], 1)
    bias_in_grad = jnp.concatenate([column_sum(d_triple), column_sum(d_pre)])
    bias_out_grad = jnp.concatenate([column_sum(d_branch), column_sum(d_ffn)])
    grad_in = jnp.concatenate([grad_qkv, grad_up], 1)
    grad_out = jnp.concatenate([grad_proj, grad_down], 0)
    return (upstream, mod_grad, grad_in, grad_out, bias_in_grad, bias_out_grad)


def fetch_layer(layer_input_weights, layer_output_weights, layer_count):
    return (
        lax.all_gather(
            layer_input_weights[layer_count].astype(jnp.bfloat16), "fsdp", axis=1, tiled=True
        ),
        lax.all_gather(
            layer_output_weights[layer_count].astype(jnp.bfloat16), "fsdp", axis=1, tiled=True
        ),
    )


def adam_step(weight, first, second, gradient):
    first = beta_one * first + (1 - beta_one) * gradient
    second = beta_two * second + (1 - beta_two) * gradient * gradient
    ahead = first / (1 - beta_one**STEP)
    scaled = second / (1 - beta_two**STEP)
    return (
        weight - learn_rate * (ahead / (jnp.sqrt(scaled) + adam_eps) + decay * weight),
        first,
        second,
    )


def generic_body(
    latents,
    targets,
    timesteps,
    labels,
    embed_w,
    embed_m,
    embed_v,
    cond_w,
    cond_m,
    cond_v,
    layer_input_weights,
    in_m,
    in_v,
    layer_output_weights,
    out_m,
    out_v,
    head_w,
    head_m,
    head_v,
    biases,
    bias_m,
    bias_v,
):
    devices = lax.axis_size("fsdp")
    embed_full, cond_full = (
        lax.all_gather(embed_w.astype(jnp.bfloat16), "fsdp", axis=1, tiled=True),
        lax.all_gather(cond_w.astype(jnp.bfloat16), "fsdp", axis=1, tiled=True),
    )
    time_one, time_two, patch_bias, cond_bias, block_input_bias, block_output_bias, head_bias = (
        split_biases(biases)
    )
    head_low = head_w.astype(jnp.bfloat16)
    features = time_features(timesteps).astype(jnp.bfloat16)
    pre_time = product(features, embed_full[:FREQ]) + time_one
    hidden_t = silu(pre_time).astype(jnp.bfloat16)
    time_emb = product(hidden_t, embed_full[FREQ : FREQ + MODEL_WIDTH]) + time_two
    onehot = (labels[:, None] == jnp.arange(NCLS)[None, :]).astype(jnp.bfloat16)
    condition = time_emb + product(onehot, embed_full[FREQ + MODEL_WIDTH + PD :])
    cond_low = silu(condition).astype(jnp.bfloat16)
    adaptive_modulation = product(cond_low, cond_full) + cond_bias
    residual_state = (
        apply_rows(latents, embed_full[FREQ + MODEL_WIDTH : FREQ + MODEL_WIDTH + PD])
        + patch_bias
        + position_table()
    )
    kept_all = []
    for layer_count in range(LAYERS):
        weights_in, weights_out = fetch_layer(
            layer_input_weights, layer_output_weights, layer_count
        )
        residual_state, kept = block_forward(
            residual_state,
            adaptive_modulation[
                :, 6 * MODEL_WIDTH * layer_count : 6 * MODEL_WIDTH * (layer_count + 1)
            ],
            weights_in,
            weights_out,
            block_input_bias[layer_count],
            block_output_bias[layer_count],
        )
        kept_all.append(kept)
    final_mod = adaptive_modulation[:, 6 * MODEL_WIDTH * LAYERS :]
    norm_final = layer_norm(residual_state)
    shaped = (
        norm_final * (1 + final_mod[:, None, MODEL_WIDTH:]) + final_mod[:, None, :MODEL_WIDTH]
    ).astype(jnp.bfloat16)
    output = apply_rows(shaped, head_low) + head_bias
    error_vals = output - targets
    loss_part = jnp.sum(error_vals * error_vals)
    tokens_all = devices * error_vals.shape[0] * SEQ * PO
    d_output = (error_vals * (2.0 / tokens_all)).astype(jnp.bfloat16)
    head_grad = outer_sum(shaped, d_output)
    head_bias_grad = column_sum(d_output)
    d_shaped = apply_back(d_output, head_low)
    d_final = jnp.concatenate([jnp.sum(d_shaped, 1), jnp.sum(d_shaped * norm_final, 1)], 1)
    upstream = local_back(
        layer_norm, residual_state, d_shaped * (1 + final_mod[:, None, MODEL_WIDTH:])
    )
    mod_grads = [None] * LAYERS
    in_shards = [None] * LAYERS
    out_shards = [None] * LAYERS
    in_bias_grads = [None] * LAYERS
    out_bias_grads = [None] * LAYERS
    for layer_count in reversed(range(LAYERS)):
        weights_in, weights_out = (
            lax.all_gather(
                layer_input_weights[layer_count].astype(jnp.bfloat16), "fsdp", axis=1, tiled=True
            ),
            lax.all_gather(
                layer_output_weights[layer_count].astype(jnp.bfloat16), "fsdp", axis=1, tiled=True
            ),
        )
        upstream, mod_grad, grad_in, grad_out, bias_in_grad, bias_out_grad = block_backward(
            upstream,
            adaptive_modulation[
                :, 6 * MODEL_WIDTH * layer_count : 6 * MODEL_WIDTH * (layer_count + 1)
            ],
            weights_in,
            weights_out,
            kept_all[layer_count],
        )
        in_shards[layer_count], out_shards[layer_count] = (
            lax.psum_scatter(grad_in, "fsdp", scatter_dimension=1, tiled=True),
            lax.psum_scatter(grad_out, "fsdp", scatter_dimension=1, tiled=True),
        )
        mod_grads[layer_count] = mod_grad
        in_bias_grads[layer_count] = bias_in_grad
        out_bias_grads[layer_count] = bias_out_grad
    d_patch = upstream.astype(jnp.bfloat16)
    patch_grad = outer_sum(latents, d_patch)
    patch_bias_grad = column_sum(d_patch)
    d_modulation = jnp.concatenate(mod_grads + [d_final], 1)
    d_cond = exact_dot(d_modulation, cond_full.astype(jnp.float32).T)
    d_condition = local_back(silu, condition, d_cond)
    d_hidden = exact_dot(d_condition, embed_full[FREQ : FREQ + MODEL_WIDTH].astype(jnp.float32).T)
    d_pre = local_back(silu, pre_time, d_hidden)
    cond_grad = exact_dot(cond_low.astype(jnp.float32).T, d_modulation)
    class_grad = exact_dot(onehot.astype(jnp.float32).T, d_condition)
    time_two_grad = exact_dot(hidden_t.astype(jnp.float32).T, d_condition)
    time_one_grad = exact_dot(features.astype(jnp.float32).T, d_pre)
    embed_grad = jnp.concatenate([time_one_grad, time_two_grad, patch_grad, class_grad], 0)
    embed_shard, cond_shard = (
        lax.psum_scatter(embed_grad, "fsdp", scatter_dimension=1, tiled=True),
        lax.psum_scatter(cond_grad, "fsdp", scatter_dimension=1, tiled=True),
    )
    bias_grad = jnp.concatenate(
        [jnp.sum(d_pre, 0), jnp.sum(d_condition, 0), patch_bias_grad, jnp.sum(d_modulation, 0)]
        + in_bias_grads
        + out_bias_grads
        + [head_bias_grad]
    )
    head_total, bias_total, loss_total = lax.psum((head_grad, bias_grad, loss_part), "fsdp")
    in_stack = jnp.stack(in_shards, 0)
    out_stack = jnp.stack(out_shards, 0)
    shard_squares = (
        jnp.sum(embed_shard * embed_shard)
        + jnp.sum(cond_shard * cond_shard)
        + jnp.sum(in_stack * in_stack)
        + jnp.sum(out_stack * out_stack)
    )
    square_total = lax.psum(shard_squares, "fsdp")
    grad_norm = jnp.sqrt(
        square_total + jnp.sum(head_total * head_total) + jnp.sum(bias_total * bias_total)
    )
    factor = jnp.minimum(1.0, clip_limit / grad_norm)
    embed_up = adam_step(embed_w, embed_m, embed_v, embed_shard * factor)
    cond_up = adam_step(cond_w, cond_m, cond_v, cond_shard * factor)
    in_up = adam_step(layer_input_weights, in_m, in_v, in_stack * factor)
    out_up = adam_step(layer_output_weights, out_m, out_v, out_stack * factor)
    head_up = adam_step(head_w, head_m, head_v, head_total * factor)
    bias_up = adam_step(biases, bias_m, bias_v, bias_total * factor)
    return (
        loss_total,
        grad_norm,
        embed_up[0],
        embed_up[1],
        embed_up[2],
        cond_up[0],
        cond_up[1],
        cond_up[2],
        in_up[0],
        in_up[1],
        in_up[2],
        out_up[0],
        out_up[1],
        out_up[2],
        head_up[0],
        head_up[1],
        head_up[2],
        bias_up[0],
        bias_up[1],
        bias_up[2],
    )


MESH_ID = pl.DeviceIdType.MESH
AXIS = "fsdp"


class Place:
    def __init__(self):
        me = lax.axis_index(AXIS)
        self.me = me
        self.core = core = me % 2
        x = (me // 2) % 2
        y = (me // 4) % 2
        self.z = me // 8
        self.chip = me // 2
        step_x = 1 - 2 * x
        step_y = 2 - 4 * y
        self.step_a = step_x + core * (step_y - step_x)
        self.step_b = step_y + core * (step_x - step_y)
        self.dev_a = me + 2 * self.step_a
        self.dev_b = me + 2 * self.step_b
        self.sibling = me + 1 - 2 * core

    def other(self, dz, flip_a=0, flip_b=0):
        return self.chip + 4 * dz + flip_a * self.step_a + flip_b * self.step_b

    def valid(self, dz):
        return jnp.logical_and(self.z + dz >= 0, self.z + dz < 4)

    def greet(self):
        barrier = pltpu.get_barrier_semaphore()

        def hello(device):
            pl.semaphore_signal(barrier, inc=1, device_id=(device,), device_id_type=MESH_ID)

        for k in range(1, 8):
            hello(8 * self.z + lax.rem(self.me + k, 8))
        for k in range(1, 4):
            hello(lax.rem(self.me + 8 * k, 32))
        pl.semaphore_wait(barrier, 10)


def remote(src, dst, send_sem, recv_sem, device):
    return pltpu.make_async_remote_copy(
        src_ref=src, dst_ref=dst, send_sem=send_sem, recv_sem=recv_sem, device_id=(device,), device_id_type=MESH_ID
    )


class Gather:
    def __init__(self, place, own, stage, piece, full, sems):
        self.p, self.own, self.stage, self.piece, self.full = place, own, stage, piece, full
        self.xch_send, self.xch_recv, self.local, self.send, self.recv, self.sib_recv = sems
        self.sent = []

    def slot(self, a, chip):
        rows, half = self.piece[a].shape
        return self.full[a].at[
            pl.ds(pl.multiple_of(chip * rows, rows), rows), pl.ds(pl.multiple_of(self.p.core * half, half), half)
        ]

    def push(self, a, k, src, chip, device, sem, cond=None):
        def act(what):
            copy = remote(src(), self.slot(a, chip()), self.send.at[a, k], sem.at[a, chip()], device())
            getattr(copy, what)()

        def guarded(what):
            if cond is None:
                act(what)
            else:
                pl.when(cond())(functools.partial(act, what))

        guarded("start")
        self.sent.append(functools.partial(guarded, "wait_send"))

    def store_own(self, a):
        return pltpu.make_async_copy(self.piece[a], self.slot(a, self.p.chip), self.local.at[a])

    def begin(self):
        core = self.p.core
        copies = []
        for a in range(2):
            rows, half = self.own[a].shape[0], self.piece[a].shape[1]
            dst = self.stage[a].at[pl.ds(pl.multiple_of(core * rows, 8), rows), :]
            away = remote(
                self.own[a].at[:, pl.ds(pl.multiple_of((1 - core) * half, half), half)],
                dst,
                self.xch_send.at[a],
                self.xch_recv.at[a],
                self.p.sibling,
            )
            away.start()
            keep = pltpu.make_async_copy(
                self.own[a].at[:, pl.ds(pl.multiple_of(core * half, half), half)], dst, self.local.at[a]
            )
            keep.start()
            copies.append((away, keep))
        for a in range(2):
            copies[a][0].wait()
            copies[a][1].wait()
            self.piece[a][...] = self.stage[a][...].astype(jnp.bfloat16)
            self.store_own(a).start()
            piece, here = (lambda a=a: self.piece[a]), (lambda: self.p.chip)
            for sign in (-1, 1):
                self.push(
                    a, 0 if sign < 0 else 3, piece, here, lambda sign=sign: self.p.me + 8 * sign, self.recv,
                    lambda sign=sign: self.p.valid(sign),
                )
            self.push(a, 6, piece, here, lambda: self.p.dev_a, self.recv)
            self.push(a, 10, piece, here, lambda: self.p.dev_b, self.recv)
            self.push(a, 18, piece, here, lambda: self.p.sibling, self.sib_recv)

    def arrive(self, a, chip):
        slot = self.slot(a, chip)
        pltpu.make_async_copy(slot, slot, self.recv.at[a, chip]).wait()

    def pass_on(self, dz, flip_a, flip_b, targets):
        def here():
            return self.p.valid(dz)

        def chip():
            return self.p.other(dz, flip_a, flip_b)

        for a in range(2):
            pl.when(here())(lambda a=a: self.arrive(a, chip()))
            for k, device, sem, extra in targets:
                self.push(
                    a, k, lambda a=a: self.slot(a, chip()), chip, device, sem,
                    here if extra is None else lambda extra=extra: jnp.logical_and(here(), self.p.valid(extra)),
                )

    def z_step(self, dist):
        for sign in (-1, 1):
            rel = (sign * dist) % 4
            targets = [
                (6 + rel, lambda: self.p.dev_a, self.recv, None),
                (10 + rel, lambda: self.p.dev_b, self.recv, None),
                (18 + rel, lambda: self.p.sibling, self.sib_recv, None),
            ]
            if dist < 3:
                onward = ((0 if sign > 0 else 3) + dist, lambda sign=sign: self.p.me - 8 * sign, self.recv, -sign)
                targets.insert(0, onward)
            self.pass_on(sign * dist, 0, 0, targets)

    def a_step(self, dist):
        for sign in (-1, 1) if dist else (1,):
            rel = (sign * dist) % 4
            self.pass_on(sign * dist, 1, 0, [
                (14 + rel, lambda: self.p.dev_b, self.recv, None), (22 + rel, lambda: self.p.sibling, self.sib_recv, None)
            ])

    def b_step(self, dist, flip_a):
        for sign in (-1, 1) if dist else (1,):
            rel = (sign * dist) % 4
            self.pass_on(
                sign * dist, flip_a, 1, [(26 + 4 * flip_a + rel, lambda: self.p.sibling, self.sib_recv, None)]
            )

    def finish(self):
        for a in range(2):
            rows, half = self.piece[a].shape

            def take(chip, carry):
                slot = self.full[a].at[
                    pl.ds(pl.multiple_of(chip * rows, rows), rows),
                    pl.ds(pl.multiple_of((1 - self.p.core) * half, half), half),
                ]
                pltpu.make_async_copy(slot, slot, self.sib_recv.at[a, chip]).wait()
                return carry

            lax.fori_loop(0, 16, take, 0)
            self.store_own(a).wait()
        for wait in self.sent:
            wait()


GATHER_SEMS = [
    pltpu.SemaphoreType.DMA((2,)),
    pltpu.SemaphoreType.DMA((2,)),
    pltpu.SemaphoreType.DMA((2,)),
    pltpu.SemaphoreType.DMA((2, 34)),
    pltpu.SemaphoreType.DMA((2, 16)),
    pltpu.SemaphoreType.DMA((2, 16)),
]


def gather_scratch(shapes):
    return (
        [pltpu.VMEM(shape, jnp.float32) for shape in shapes]
        + [pltpu.VMEM(shape, jnp.bfloat16) for shape in shapes]
        + GATHER_SEMS
    )


def piece_shapes(shapes):
    return [(2 * rows, width // 2) for rows, width in shapes]


ORDER = (3, 0, 2, 1)


class Scatter:
    def __init__(self, place, grads, totals, bufs, sems, mine=None):
        self.p, self.grad, self.total, self.mine = place, grads, totals, mine
        count = len(grads)
        self.arrays = range(count)
        self.sib, self.from_b, self.from_a, self.line, self.part, self.last = (
            bufs[count * i : count * i + count] for i in range(6)
        )
        (self.load_sem, self.sib_send, self.sib_recv, self.b_send, self.b_recv, self.a_send, self.a_recv, self.z_send,
         self.z_recv, self.end_send, self.end_recv, self.end_local) = sems

    def rows_of(self, a, chip, core):
        rows, half = self.part[a].shape
        return self.grad[a].at[
            pl.ds(pl.multiple_of(chip * rows, rows), rows), pl.ds(pl.multiple_of(core * half, half), half)
        ]

    def chip_of(self, z, flip_a, flip_b):
        return self.p.other(z - self.p.z, flip_a, flip_b)

    def own(self, a, flip_b, flip_a, z):
        if self.mine is None:
            return self.rows_of(a, self.chip_of(z, flip_a, flip_b), self.p.core)
        return self.mine[a].at[8 * flip_b + 4 * flip_a + z]

    def load(self, a, flip_b, flip_a, z):
        return pltpu.make_async_copy(
            self.rows_of(a, self.chip_of(z, flip_a, flip_b), self.p.core),
            self.own(a, flip_b, flip_a, z),
            self.load_sem.at[a, 8 * flip_b + 4 * flip_a + z],
        )

    def lend(self, a, flip_b, flip_a, z):
        k = 8 * flip_b + 4 * flip_a + z
        return remote(
            self.rows_of(a, self.chip_of(z, flip_b, flip_a), 1 - self.p.core),
            self.sib[a].at[k],
            self.sib_send.at[a, k],
            self.sib_recv.at[a, k],
            self.p.sibling,
        )

    def to_b(self, a, flip_a, z):
        k = 4 * flip_a + z
        return remote(
            self.own(a, 1, flip_a, z), self.from_b[a].at[k], self.b_send.at[a, k], self.b_recv.at[a, k], self.p.dev_b
        )

    def to_a(self, a, z):
        return remote(
            self.own(a, 0, 1, z), self.from_a[a].at[z], self.a_send.at[a, z], self.a_recv.at[a, z], self.p.dev_a
        )

    def to_z(self, a, target, source):
        return remote(
            self.own(a, 0, 0, target),
            self.line[a].at[source],
            self.z_send.at[a, target],
            self.z_recv.at[a, source],
            self.p.me + 8 * (target - self.p.z),
        )

    def open(self, z):
        for flip_b, flip_a in ((1, 1), (1, 0), (0, 1), (0, 0)):
            for a in self.arrays:
                self.lend(a, flip_b, flip_a, z).start()
                if self.mine is not None:
                    self.load(a, flip_b, flip_a, z).start()

    def open_all(self):
        for z in ORDER:
            self.open(z)

    def pair(self, a, flip_b, flip_a, z):
        if self.mine is not None:
            self.load(a, flip_b, flip_a, z).wait()
        self.lend(a, flip_b, flip_a, z).wait_recv()
        k = 8 * flip_b + 4 * flip_a + z
        return self.own(a, flip_b, flip_a, z)[...].astype(jnp.float32) + self.sib[a][k].astype(jnp.float32)

    def cross_b(self, z):
        for flip_a in (1, 0):
            for a in self.arrays:
                self.own(a, 1, flip_a, z)[...] = self.pair(a, 1, flip_a, z).astype(jnp.bfloat16)
                self.to_b(a, flip_a, z).start()

    def cross_a(self, z):
        for a in self.arrays:
            value = self.pair(a, 0, 1, z)
            self.to_b(a, 1, z).wait_recv()
            self.own(a, 0, 1, z)[...] = (value + self.from_b[a][4 + z].astype(jnp.float32)).astype(jnp.bfloat16)
            self.to_a(a, z).start()

    def along_z(self, z):
        place = self.p
        for a in self.arrays:
            value = self.pair(a, 0, 0, z)
            self.to_b(a, 0, z).wait_recv()
            value = value + self.from_b[a][z].astype(jnp.float32)
            self.to_a(a, z).wait_recv()
            self.part[a][...] = value + self.from_a[a][z].astype(jnp.float32)

            @pl.when(place.z != z)
            def _():
                self.own(a, 0, 0, z)[...] = self.part[a][...].astype(jnp.bfloat16)
                self.to_z(a, z, place.z).start()

            @pl.when(place.z == z)
            def _():
                self.last[a][...] = self.part[a][...]

    def end_copies(self, a):
        core = self.p.core
        rows, width = self.total[a].shape
        dst = self.total[a].at[:, pl.ds(pl.multiple_of(core * (width // 2), width // 2), width // 2)]
        away = remote(
            self.last[a].at[pl.ds(pl.multiple_of((1 - core) * rows, 8), rows), :],
            dst,
            self.end_send.at[a],
            self.end_recv.at[a],
            self.p.sibling,
        )
        keep = pltpu.make_async_copy(
            self.last[a].at[pl.ds(pl.multiple_of(core * rows, 8), rows), :], dst, self.end_local.at[a]
        )
        return away, keep

    def close(self):
        for a in self.arrays:

            def add(k, carry):
                source = lax.rem(self.p.z + k, 4)
                self.to_z(a, self.p.z, source).wait_recv()
                self.last[a][...] += self.line[a][source].astype(jnp.float32)
                return carry

            lax.fori_loop(1, 4, add, 0)
            for copy in self.end_copies(a):
                copy.start()

    def end(self):
        for a in self.arrays:
            for copy in self.end_copies(a):
                copy.wait()

    def finish(self):
        def step(z, carry):
            for a in self.arrays:
                for flip_b in range(2):
                    for flip_a in range(2):
                        self.lend(a, flip_b, flip_a, z).wait_send()
                for flip_a in range(2):
                    self.to_b(a, flip_a, z).wait_send()
                self.to_a(a, z).wait_send()

                @pl.when(self.p.z != z)
                def _():
                    self.to_z(a, z, self.p.z).wait_send()

            return carry

        lax.fori_loop(0, 4, step, 0)

    def steps(self):
        z0, z1, z2, z3 = ORDER
        work = [(self.cross_b, z) for z in ORDER]
        work += [(self.cross_a, z0), (self.cross_a, z1), (self.along_z, z0), (self.cross_a, z2), (self.along_z, z1)]
        work += [(self.cross_a, z3), (self.along_z, z2), (self.along_z, z3)]
        return [functools.partial(step, z) for step, z in work] + [self.close, self.end, self.finish]


def scatter_scratch(shapes):
    scratch = []
    for count, kind in ((16, jnp.bfloat16), (8, jnp.bfloat16), (4, jnp.bfloat16), (4, jnp.bfloat16),
                        (0, jnp.float32), (0, jnp.float32)):
        scratch += [pltpu.VMEM(((count,) if count else ()) + shape, kind) for shape in shapes]
    counts = (16, 16, 16, 8, 8, 4, 4, 4, 4)
    several = len(shapes)
    return (
        scratch
        + [pltpu.SemaphoreType.DMA((several, n)) for n in counts]
        + [pltpu.SemaphoreType.DMA((several,))] * 3
    )


def dot_nt(left, right):
    return lax.dot_general(left, right, (((1,), (1,)), ((), ())), preferred_element_type=jnp.float32)


def dot_tn(left, right):
    return lax.dot_general(left, right, (((0,), (0,)), ((), ())), preferred_element_type=jnp.float32)


def thirds(value):
    high = value.astype(jnp.bfloat16)
    rest = value - high.astype(jnp.float32)
    mid = rest.astype(jnp.bfloat16)
    return high, mid, (rest - mid.astype(jnp.float32)).astype(jnp.bfloat16)


def silu_slope(value):
    gate = jax.nn.sigmoid(value)
    return gate * (1 + value * (1 - gate))


PLANE, LINE = 8, 4


class Swap:
    def __init__(self, index, sems, full, away=None, mid=None, reduce=None):
        self.i, self.sems, self.full, self.away, self.mid = index, sems, full, away, mid
        self.second = mid if reduce is None else reduce
        self.me = lax.axis_index(AXIS)
        self.z, self.p = self.me // PLANE, self.me % PLANE
        self.spread = away is None

    def plane(self, peer, slot):
        send, recv = self.sems
        if self.spread:
            src, dst = self.full.at[:, self.p], self.full.at[:, slot]
        else:
            src, dst = self.away.at[:, peer], self.mid.at[:, slot]
        return remote(src, dst, send.at[self.i, peer], recv.at[self.i, slot], self.me + peer - self.p)

    def line(self, peer, slot):
        send, recv = self.sems
        if self.spread:
            src, dst = self.full.at[self.z, self.p], self.full.at[slot, self.p]
        else:
            src, dst = self.second.at[peer], self.full.at[slot]
        return remote(
            src, dst, send.at[self.i, PLANE + peer], recv.at[self.i, PLANE + slot], self.me + PLANE * (peer - self.z)
        )

    def each(self, in_plane, step):
        mine, count = (self.p, PLANE) if in_plane else (self.z, LINE)

        def run(k, carry):
            step(lax.rem(mine + k, count))
            return carry

        lax.fori_loop(1, count, run, 0)

    def hop(self, in_plane):
        make, slot = (self.plane, self.p) if in_plane else (self.line, self.z)
        self.each(in_plane, lambda peer: make(peer, slot).start())

    def come(self, in_plane):
        make = self.plane if in_plane else self.line
        self.each(in_plane, lambda peer: make(peer, peer).wait_recv())

    def start(self):
        if not self.spread:
            for k in range(LINE):
                self.mid[k, self.p] = self.away[k, self.p]
        self.hop(not self.spread)

    def between(self, work=None):
        self.come(not self.spread)
        if work is not None:
            work()
        self.hop(self.spread)
        if not self.spread:
            self.full[self.z] = self.second[self.z]

    def arrive(self):
        self.come(self.spread)

    def sent(self):
        self.each(True, lambda peer: self.plane(peer, self.p).wait_send())
        self.each(False, lambda peer: self.line(peer, self.z).wait_send())


def modulate_steps(devices, ins, outs, bufs, sems):
    msg, emb, wcond, bt1, bt2, bcond = ins
    mods, pre, cond, hid_all, low_all, feat_all, lab_all, got = outs
    hid, low, away, mid, wcls = bufs
    me = lax.axis_index(AXIS)
    z, place = me // PLANE, me % PLANE
    images, cols = 4, emb.shape[0]
    wt1, wt2 = emb.at[:, :FREQ], emb.at[:, FREQ : FREQ + MODEL_WIDTH]
    swaps = [Swap(0, sems, got), Swap(1, sems, hid), Swap(2, sems, low), Swap(3, sems, mods, away, mid)]

    def first():
        got[z, place] = msg[...]
        wcls[...] = jnp.zeros_like(wcls)
        wcls[:, : emb.shape[1] - FREQ - MODEL_WIDTH] = emb[:, FREQ + MODEL_WIDTH :]
        swaps[0].start()

    def second():
        swaps[0].arrive()
        for j in range(devices):
            at = slice(images * j, images * (j + 1))
            block = got[j // PLANE, j % PLANE].astype(jnp.float32)
            feat_all[at, :128] = block[:images]
            feat_all[at, 128:] = block[images : 2 * images]
            digits = block[3 * images : 4 * images]
            lab_all[at, :] = jnp.broadcast_to(32.0 * digits[:, :1] + digits[:, 64:65], (images, 128))
        pre[...] = dot_nt(wt1[...].astype(jnp.bfloat16), feat_all[...].astype(jnp.bfloat16)) + bt1[...]
        hidden = silu(pre[...])
        pad = jnp.zeros((hid.shape[2] - cols, hidden.shape[1]), jnp.float32)
        hid[z, place] = jnp.concatenate([hidden, pad], 0).astype(jnp.bfloat16)
        swaps[1].start()
        classes = lax.broadcasted_iota(jnp.int32, (lab_all.shape[0], wcls.shape[1]), 1).astype(jnp.float32)
        labels = jnp.concatenate([lab_all[...] + PD] * (wcls.shape[1] // 128), 1)
        onehot = (labels == classes).astype(jnp.bfloat16)
        cond[...] = dot_nt(wcls[...].astype(jnp.bfloat16), onehot) + bt2[...]

    def third():
        swaps[1].arrive()
        for j in range(devices):
            hid_all[cols * j : cols * (j + 1), :] = hid[j // PLANE, j % PLANE].astype(jnp.float32)[:cols]
        cond[...] += jnp.dot(
            wt2[...].astype(jnp.bfloat16), hid_all[...].astype(jnp.bfloat16), preferred_element_type=jnp.float32
        )
        value = silu(cond[...])
        pad = jnp.zeros((low.shape[2] - cols, value.shape[1]), jnp.float32)
        low[z, place] = jnp.concatenate([value, pad], 0).astype(jnp.bfloat16)
        swaps[2].start()

    def fourth():
        swaps[2].arrive()
        for j in range(devices):
            low_all[cols * j : cols * (j + 1), :] = low[j // PLANE, j % PLANE].astype(jnp.float32)[:cols]
        rows = dot_nt(low_all[...].T.astype(jnp.bfloat16), wcond[...].astype(jnp.bfloat16)) + bcond[...]
        for j in range(devices):
            away[j // PLANE, j % PLANE] = rows[images * j : images * (j + 1)]
        swaps[3].start()

    def last():
        swaps[3].arrive()
        for swap in swaps:
            swap.sent()

    between = [swap.between for swap in swaps]
    return [first, between[0], second, between[1], third, between[2], fourth, between[3], last]


SETTLE_INS = ("d_mods", "emb", "wcond", "pre", "cond", "hid_all", "low_all", "feat_all", "lab_all", "g_head", "g_hbias", "loss",
              "g_patch", "g_pbias", "bin0", "bin1", "bout0", "bout1", "done_in", "done_out")


def settle_steps(devices, ins, outs, bufs, sems, shards):
    d_mods, pre, lab_all = ins["d_mods"], ins["pre"], ins["lab_all"]
    g_cond, g_t1, g_t2, g_cls, merged = outs
    dm_mid, dm_got, dm_all, rows, small, small_mid, small_sum, small_got = bufs[:8]
    dc_part, dc_mid, dc_sum, dc_got, dh_part, dh_mid, dh_sum, dh_got = bufs[8:]
    me = lax.axis_index(AXIS)
    images, width = d_mods.shape[2:]
    cols = pre.shape[0]
    swaps = [
        Swap(0, sems, dm_got, d_mods, dm_mid),
        Swap(1, sems, small_got, small, small_mid, small_sum),
        Swap(2, sems, dc_got, dc_part, dc_mid, dc_sum),
        Swap(3, sems, dh_got, dh_part, dh_mid, dh_sum),
        Swap(4, sems, merged),
    ]
    keep = {}

    def share(value, part):
        pad = jnp.zeros((32 - cols, value.shape[1]), jnp.float32)
        for j in range(devices):
            part[j // PLANE, j % PLANE] = jnp.concatenate([value[cols * j : cols * (j + 1)], pad], 0).astype(jnp.bfloat16)

    def add_plane(mid, total):
        for k in range(LINE):
            total[k] = jnp.sum(mid[k].astype(jnp.float32), 0)

    def add_small():
        add_plane(small_mid, small_sum)

    def add_dc():
        add_plane(dc_mid, dc_sum)

    def add_dh():
        add_plane(dh_mid, dh_sum)

    def parts_of(value):
        return sum(
            jnp.where(lax.broadcasted_iota(jnp.int32, (1, 128), 1) == k, part.astype(jnp.float32), 0.0)
            for k, part in enumerate(thirds(value))
        )

    def first():
        swaps[0].start()
        dm_all[...] = jnp.zeros_like(dm_all)
        rows[...] = jnp.zeros_like(rows)
        for k in range(MODEL_WIDTH // 128):
            span = slice(128 * k, 128 * (k + 1))
            rows[16 * k : 16 * (k + 1), :] = ins["g_patch"][:, span]
            rows[96 + 32 * k : 96 + 32 * (k + 1), :] = ins["g_head"][:, span]
        at = 288
        for name in ("g_pbias", "bin0", "bin1", "bout0", "bout1"):
            for k in range(ins[name].shape[1] // 128):
                rows[at : at + 1, :] = ins[name][:, 128 * k : 128 * (k + 1)]
                at += 1
        square = ins["g_hbias"].shape
        diagonal = lax.broadcasted_iota(jnp.int32, square, 0) == lax.broadcasted_iota(jnp.int32, square, 1)
        rows[at : at + 1, :] = jnp.sum(jnp.where(diagonal, ins["g_hbias"][...], 0.0), 0, keepdims=True)
        for j in range(devices):
            small[j // PLANE, j % PLANE] = rows[16 * j : 16 * (j + 1), :].astype(jnp.bfloat16)

    def second():
        swaps[0].arrive()
        for j in range(devices):
            dm_all[images * j : images * (j + 1), :width] = dm_got[j // PLANE, j % PLANE]
        turned = dm_all[...].T[:width]
        parts = thirds(turned)
        weight = ins["wcond"][...].astype(jnp.bfloat16)
        share(sum(dot_tn(weight, part) for part in parts), dc_part)
        swaps[2].start()
        swaps[1].start()
        low = ins["low_all"][...].astype(jnp.bfloat16)
        g_cond[...] = sum(dot_nt(part, low) for part in parts)

    def third():
        swaps[2].arrive()
        d_cond = jnp.sum(dc_got[...], 0)[:cols] * silu_slope(ins["cond"][...])
        parts = thirds(d_cond)
        weight = ins["emb"][:, FREQ : FREQ + MODEL_WIDTH].astype(jnp.bfloat16)
        share(sum(dot_tn(weight, part) for part in parts), dh_part)
        swaps[3].start()
        classes = lax.broadcasted_iota(jnp.int32, (lab_all.shape[0], g_cls.shape[1]), 1).astype(jnp.float32)
        labels = jnp.concatenate([lab_all[...] + PD] * (g_cls.shape[1] // 128), 1)
        onehot = (labels == classes).astype(jnp.bfloat16)
        g_cls[...] = sum(jnp.dot(part, onehot, preferred_element_type=jnp.float32) for part in parts)
        hidden = ins["hid_all"][...].astype(jnp.bfloat16)
        g_t2[...] = sum(dot_nt(part, hidden) for part in parts)
        ones = jnp.ones((8, lab_all.shape[0]), jnp.bfloat16)
        keep["t2"] = sum(dot_nt(ones, part) for part in parts)

    def fourth():
        swaps[1].arrive()
        swaps[3].arrive()
        d_pre = jnp.sum(dh_got[...], 0)[:cols] * silu_slope(pre[...])
        parts = thirds(d_pre)
        feats = ins["feat_all"][...].astype(jnp.bfloat16)
        g_t1[...] = sum(jnp.dot(part, feats, preferred_element_type=jnp.float32) for part in parts)
        ones = jnp.ones((8, lab_all.shape[0]), jnp.bfloat16)
        keep["t1"] = sum(dot_nt(ones, part) for part in parts)
        total = jnp.zeros((1, 1), jnp.float32)
        for ref in (g_cond, g_t1, g_t2, g_cls, ins["done_in"], ins["done_out"]):
            total = total + jnp.sum(ref[...] * ref[...])
        keep["squares"] = total

    def message():
        total = keep["squares"]
        for ref in shards:
            total = total + jnp.sum(ref[...] * ref[...])
        bias_cond = jnp.sum(dm_all[...], 0, keepdims=True)
        blank = jnp.zeros((1, 128 - cols), jnp.float32)
        lines = [jnp.concatenate([keep[name][0:1, :], blank], 1) for name in ("t1", "t2")]
        lines.append(parts_of(total))
        lines.append(parts_of(ins["loss"][0:1, :]))
        lines += [bias_cond[:, 128 * k : 128 * (k + 1)] for k in range(3)]
        lines.append(jnp.zeros((9, 128), jnp.float32))
        lines.insert(0, jnp.sum(small_got[...], 0))
        merged[me // PLANE, me % PLANE] = jnp.concatenate(lines, 0).astype(jnp.bfloat16)
        swaps[4].start()
        swaps[4].between()

    def last():
        swaps[4].arrive()
        for swap in swaps:
            swap.sent()

    betweens = [
        swaps[0].between,
        functools.partial(swaps[1].between, add_small),
        functools.partial(swaps[2].between, add_dc),
        functools.partial(swaps[3].between, add_dh),
    ]
    return [first, second, third, fourth, message, last], betweens


def dot_nn(left, right):
    return lax.dot_general(left, right, (((1,), (0,)), ((), ())), preferred_element_type=jnp.float32)


def norm_parts(value):
    centered = value - jnp.mean(value, -1, keepdims=True)
    scale = lax.rsqrt(jnp.mean(centered * centered, -1, keepdims=True) + 1e-06)
    return centered * scale, scale


def norm_back(normed, scale, d_normed):
    inner = jnp.mean(d_normed * normed, -1, keepdims=True)
    return scale * (d_normed - jnp.mean(d_normed, -1, keepdims=True) - normed * inner)


GELU_C = math.sqrt(2.0 / math.pi)


def gelu_value(u):
    return 0.5 * u * (1.0 + jnp.tanh(GELU_C * (u + 0.044715 * u * u * u)))


def gelu_slope(u):
    square = u * u
    t = jnp.tanh(GELU_C * u * (1.0 + 0.044715 * square))
    return 0.5 * (1.0 + t) + 0.5 * u * (1.0 - t * t) * (GELU_C * (1.0 + 3 * 0.044715 * square))


def head_masks(shape):
    low_half = lax.broadcasted_iota(jnp.int32, shape, 1) < HEAD_DIM
    return low_half, jnp.logical_not(low_half)


class Weights:
    def __init__(self, hbm, vmem, sems):
        w_in, w_out = hbm
        self.w_in, self.w_out = vmem
        cut = 3 * MODEL_WIDTH
        spans = [
            (w_in.at[pl.ds(0, cut), :], self.w_in.at[pl.ds(0, cut), :]),
            (w_out.at[:, pl.ds(0, MODEL_WIDTH)], self.w_out.at[:, pl.ds(0, MODEL_WIDTH)]),
            (w_in.at[pl.ds(cut, FF), :], self.w_in.at[pl.ds(cut, FF), :]),
            (w_out.at[:, pl.ds(MODEL_WIDTH, FF)], self.w_out.at[:, pl.ds(MODEL_WIDTH, FF)]),
        ]
        self.copies = [pltpu.make_async_copy(src, dst, sems.at[i]) for i, (src, dst) in enumerate(spans)]

    def start(self, order):
        @pl.when(pl.program_id(0) == 0)
        def _():
            for i in order:
                self.copies[i].start()

    def need(self, i):
        @pl.when(pl.program_id(0) == 0)
        def _():
            self.copies[i].wait()


def forward_image(x_ref, mod, weights, b_in, b_out, outs, hook=lambda: None):
    h1, qkv, probs, o, a, x1, h2, u, g, f = outs
    shift1, scale1, gate1, shift2, scale2, gate2 = (mod[0, i : i + 1, :] for i in range(6))
    width = MODEL_WIDTH
    hook()
    x = x_ref[...]
    h1[...] = (norm_parts(x)[0] * (1 + scale1) + shift1).astype(jnp.bfloat16)
    weights.need(0)
    for j in range(3):
        span = slice(j * width, (j + 1) * width)
        qkv[:, span] = (dot_nt(h1[...], weights.w_in[span, :]) + b_in[:, span]).astype(jnp.bfloat16)
    hook()
    def scores_of(pair):
        q, k = (qkv[:, j * width + 128 * pair : j * width + 128 * (pair + 1)] for j in range(2))
        q = q * jnp.bfloat16(HEAD_DIM**-0.5)
        zero = jnp.zeros_like(q)
        return dot_nt(jnp.concatenate([jnp.where(mask, q, zero) for mask in head_masks(q.shape)], 0), k)

    ahead = scores_of(0)
    for pair in range(HEADS // 2):
        scores, ahead = ahead, scores_of(pair + 1) if pair + 1 < HEADS // 2 else None
        v = qkv[:, 2 * width + 128 * pair : 2 * width + 128 * (pair + 1)]
        expo = jnp.exp(scores - jnp.max(scores, -1, keepdims=True))
        weight = (expo * pl.reciprocal(jnp.sum(expo, -1, keepdims=True))).astype(jnp.bfloat16)
        probs[0, 2 * pair] = weight[:SEQ]
        probs[0, 2 * pair + 1] = weight[SEQ:]
        both = dot_nn(weight, v)
        mixed = jnp.where(head_masks(v.shape)[0], both[:SEQ], both[SEQ:])
        o[:, 128 * pair : 128 * (pair + 1)] = mixed.astype(jnp.bfloat16)
        hook()
    weights.need(1)
    branch = dot_nt(o[...], weights.w_out[:, :width]) + b_out[:, :width]
    a[...] = branch.astype(jnp.bfloat16)
    x1[...] = x + gate1 * branch
    h2[...] = (norm_parts(x1[...])[0] * (1 + scale2) + shift2).astype(jnp.bfloat16)
    hook()
    weights.need(2)
    weights.need(3)
    def up_part(j):
        rows = slice((3 + j) * width, (4 + j) * width)
        return dot_nt(h2[...], weights.w_in[rows, :]) + b_in[:, rows]

    total, ahead = None, up_part(0)
    for j in range(FF // width):
        span = slice(j * width, (j + 1) * width)
        value, ahead = ahead, up_part(j + 1) if j + 1 < FF // width else None
        u[:, span] = value.astype(jnp.bfloat16)
        active = gelu_value(value).astype(jnp.bfloat16)
        g[:, span] = active
        term = dot_nt(active, weights.w_out[:, (1 + j) * width : (2 + j) * width])
        total = term if total is None else total + term
        hook()
    ffn = total + b_out[:, width:]
    f[...] = ffn.astype(jnp.bfloat16)
    return x1[...] + gate2 * ffn


def head_kernel(scale_out, x, mod, w_in, w_out, b_in, b_out, final, head_t, b_head, targets_t, *refs):
    outs, (dx, d_final, g_head, g_bias, loss), (vm_in, vm_out, sems) = refs[:10], refs[10:15], refs[15:]
    weights = Weights((w_in, w_out), (vm_in, vm_out), sems)
    weights.start((0, 1, 2, 3))
    last = forward_image(x, mod, weights, b_in, b_out, outs)
    normed, scale = norm_parts(last)
    shift_row, scale_row = final[0, 0:1, :], final[0, 1:2, :]
    shaped = (normed * (1 + scale_row) + shift_row).astype(jnp.bfloat16)
    low = head_t[...].astype(jnp.bfloat16)
    error = dot_nt(low, shaped) + b_head[...] - targets_t[0]
    d_out = (error * scale_out).astype(jnp.bfloat16)

    @pl.when(pl.program_id(0) == 0)
    def _():
        g_head[...] = jnp.zeros_like(g_head)
        g_bias[...] = jnp.zeros_like(g_bias)
        loss[...] = jnp.zeros_like(loss)

    g_head[...] += dot_nn(d_out, shaped)
    g_bias[...] += jnp.sum(d_out.astype(jnp.float32), 1, keepdims=True)
    loss[...] += jnp.sum(error * error)
    d_shaped = dot_tn(d_out, low)
    d_final[0, 0:1, :] = jnp.sum(d_shaped, 0, keepdims=True)
    d_final[0, 1:2, :] = jnp.sum(d_shaped * normed, 0, keepdims=True)
    dx[...] = norm_back(normed, scale, d_shaped * (1 + scale_row))


WEIGHT_SCRATCH = [
    pltpu.VMEM((IW, MODEL_WIDTH), jnp.bfloat16),
    pltpu.VMEM((MODEL_WIDTH, OW), jnp.bfloat16),
    pltpu.SemaphoreType.DMA((4,)),
]


def token_block(width):
    return pl.BlockSpec((SEQ, width), lambda i: (i, 0))


def image_block(*dims):
    return pl.BlockSpec((1,) + dims, lambda i: (i,) + (0,) * len(dims))


def whole_block(*dims):
    return pl.BlockSpec(dims, lambda i: (0,) * len(dims))


def kept_shapes(images):
    tokens, width, low, full = images * SEQ, MODEL_WIDTH, jnp.bfloat16, jnp.float32
    shapes = [((tokens, width), low), ((tokens, 3 * width), low), ((images, HEADS, SEQ, SEQ), low), ((tokens, width), low),
              ((tokens, width), low), ((tokens, width), full), ((tokens, width), low), ((tokens, FF), low),
              ((tokens, FF), low), ((tokens, width), low)]
    specs = [token_block(s[1]) if len(s) == 2 else image_block(*s[1:]) for s, _ in shapes]
    return [jax.ShapeDtypeStruct(s, t) for s, t in shapes], specs


def forward_specs():
    any_block = pl.BlockSpec(memory_space=pl.ANY)
    return [token_block(MODEL_WIDTH), image_block(6, MODEL_WIDTH), any_block, any_block, whole_block(1, IW),
            whole_block(1, 2 * MODEL_WIDTH)]


def forward_head(ins, scale_out):
    images = ins[1].shape[0]
    shapes, specs = kept_shapes(images)
    extra = [(images * SEQ, MODEL_WIDTH), (images, 2, MODEL_WIDTH), (PO, MODEL_WIDTH), (PO, 128), (8, 128)]
    return pl.pallas_call(
        functools.partial(head_kernel, scale_out),
        grid=(images,),
        out_shape=shapes + [jax.ShapeDtypeStruct(s, jnp.float32) for s in extra],
        in_specs=forward_specs()
        + [image_block(2, MODEL_WIDTH), whole_block(PO, MODEL_WIDTH), whole_block(PO, 1), image_block(PO, SEQ)],
        out_specs=specs
        + [token_block(MODEL_WIDTH), image_block(2, MODEL_WIDTH), whole_block(PO, MODEL_WIDTH), whole_block(PO, 128),
           whole_block(8, 128)],
        scratch_shapes=WEIGHT_SCRATCH,
        compiler_params=pltpu.CompilerParams(vmem_limit_bytes=56 << 20),
        name="forward_head",
    )(*ins)


def backward_image(refs, mod, weights, outs, hook=lambda: None):
    up_ref, x_ref, x1_ref, probs, qkv, a, f, u = refs
    dx, d_qkv, d_u, d_f, d_a, d_mod, g_bin, g_bout = outs
    width = MODEL_WIDTH
    shift1, scale1, gate1, shift2, scale2, gate2 = (mod[0, i : i + 1, :] for i in range(6))

    @pl.when(pl.program_id(0) == 0)
    def _():
        g_bin[...] = jnp.zeros_like(g_bin)
        g_bout[...] = jnp.zeros_like(g_bout)

    def rows_sum(value):
        return jnp.sum(value.astype(jnp.float32), 0, keepdims=True)

    hook()
    upstream = up_ref[...]
    d_f[...] = (gate2 * upstream).astype(jnp.bfloat16)
    d_mod[0, 5:6, :] = rows_sum(f[...].astype(jnp.float32) * upstream)
    g_bout[:, width:] += rows_sum(d_f[...])
    weights.need(3)
    weights.need(2)
    d_h2 = None
    for j in range(FF // width):
        span = slice(j * width, (j + 1) * width)
        rows = slice((3 + j) * width, (4 + j) * width)
        d_g = dot_nn(d_f[...], weights.w_out[:, (1 + j) * width : (2 + j) * width])
        d_u[:, span] = (d_g * gelu_slope(u[:, span].astype(jnp.float32))).astype(jnp.bfloat16)
        g_bin[:, rows] += rows_sum(d_u[:, span])
        term = dot_nn(d_u[:, span], weights.w_in[rows, :])
        d_h2 = term if d_h2 is None else d_h2 + term
        hook()
    normed, scale = norm_parts(x1_ref[...])
    d_mod[0, 3:4, :] = rows_sum(d_h2)
    d_mod[0, 4:5, :] = rows_sum(d_h2 * normed)
    upstream = upstream + norm_back(normed, scale, d_h2 * (1 + scale2))
    d_mod[0, 2:3, :] = rows_sum(a[...].astype(jnp.float32) * upstream)
    d_a[...] = (gate1 * upstream).astype(jnp.bfloat16)
    g_bout[:, :width] += rows_sum(d_a[...])
    dx[...] = upstream
    weights.need(1)
    d_o = dot_nn(d_a[...], weights.w_out[:, :width]).astype(jnp.bfloat16)
    hook()
    root = HEAD_DIM**-0.5

    def probs_back(pair):
        d_mixed = d_o[:, 128 * pair : 128 * (pair + 1)]
        zero = jnp.zeros_like(d_mixed)
        both = jnp.concatenate([jnp.where(mask, d_mixed, zero) for mask in head_masks(d_mixed.shape)], 0)
        return both, dot_nt(both, qkv[:, 2 * width + 128 * pair : 2 * width + 128 * (pair + 1)])

    for pair in range(HEADS // 2):
        lanes = [slice(j * width + 128 * pair, j * width + 128 * (pair + 1)) for j in range(3)]
        d_masked, d_probs = probs_back(pair)
        q, k = qkv[:, lanes[0]], qkv[:, lanes[1]]
        zero = jnp.zeros_like(q)
        masks = head_masks(q.shape)
        weight = probs[0, 2 * pair : 2 * pair + 2].reshape(2 * SEQ, SEQ)
        full = weight.astype(jnp.float32)
        d_scores = (full * (d_probs - jnp.sum(full * d_probs, -1, keepdims=True))).astype(jnp.bfloat16)
        both = dot_nn(d_scores, k)
        d_q = jnp.where(masks[0], both[:SEQ], both[SEQ:])
        d_k = dot_tn(d_scores, jnp.concatenate([jnp.where(mask, q, zero) for mask in masks], 0))
        d_qkv[:, lanes[0]] = (d_q * root).astype(jnp.bfloat16)
        d_qkv[:, lanes[1]] = (d_k * root).astype(jnp.bfloat16)
        d_qkv[:, lanes[2]] = dot_tn(weight, d_masked).astype(jnp.bfloat16)
        hook()
    weights.need(0)
    d_h1 = None
    for j in range(3):
        span = slice(j * width, (j + 1) * width)
        g_bin[:, span] += rows_sum(d_qkv[:, span])
        term = dot_nn(d_qkv[:, span], weights.w_in[span, :])
        d_h1 = term if d_h1 is None else d_h1 + term
    normed, scale = norm_parts(x_ref[...])
    d_mod[0, 0:1, :] = rows_sum(d_h1)
    d_mod[0, 1:2, :] = rows_sum(d_h1 * normed)
    dx[...] += norm_back(normed, scale, d_h1 * (1 + scale1))
    hook()


def backward_kernel(mod, w_in, w_out, *refs):
    ins, outs, (vm_in, vm_out, sems) = refs[:8], refs[8:16], refs[16:]
    weights = Weights((w_in, w_out), (vm_in, vm_out), sems)
    weights.start((3, 2, 1, 0))
    backward_image(ins, mod, weights, outs)


def backward_block(mods, w_in, w_out, refs):
    images, width, low, full = mods.shape[0], MODEL_WIDTH, jnp.bfloat16, jnp.float32
    tokens = images * SEQ
    any_block = pl.BlockSpec(memory_space=pl.ANY)
    shapes = [((tokens, width), full), ((tokens, 3 * width), low), ((tokens, FF), low), ((tokens, width), low),
              ((tokens, width), low), ((images, 6, width), full), ((1, IW), full), ((1, 2 * width), full)]
    return pl.pallas_call(
        backward_kernel,
        grid=(images,),
        out_shape=[jax.ShapeDtypeStruct(s, t) for s, t in shapes],
        in_specs=[image_block(6, width), any_block, any_block, token_block(width), token_block(width), token_block(width),
                  image_block(HEADS, SEQ, SEQ), token_block(3 * width), token_block(width), token_block(width),
                  token_block(FF)],
        out_specs=[token_block(s[1]) for s, _ in shapes[:5]]
        + [image_block(6, width), whole_block(1, IW), whole_block(1, 2 * width)],
        scratch_shapes=WEIGHT_SCRATCH,
        compiler_params=pltpu.CompilerParams(vmem_limit_bytes=56 << 20),
        name="backward_block",
    )(mods, w_in, w_out, *refs)


def gather_steps(job):
    steps = [job.begin, functools.partial(job.a_step, 0)]
    for dist in (1, 2, 3):
        steps += [functools.partial(job.z_step, dist), functools.partial(job.a_step, dist)]
    for dist in range(4):
        steps += [functools.partial(job.b_step, dist, flip) for flip in range(2)]
    return steps + [job.finish]


class Hooks:
    def __init__(self, steps, slots, points):
        self.points, self.table = points, {}
        for step, slot in zip(steps, slots):
            self.table.setdefault((slot // points, slot % points), []).append(step)
        self.next = 0

    def __call__(self):
        point, self.next = self.next, self.next + 1
        for (turn, where), steps in sorted(self.table.items(), key=lambda item: item[0]):
            if where == point:

                @pl.when(pl.program_id(0) == turn)
                def _():
                    for step in steps:
                        step()


def start_kernel(devices, *refs):
    own, mod_ins, refs = refs[:2], refs[2:8], refs[8:]
    full, mod_outs, refs = refs[:2], refs[2:10], refs[10:]
    part, mod_bufs, mod_sems = refs[:10], refs[10:15], refs[15:]
    place = Place()
    place.greet()
    job = Gather(place, [ref.at[0] for ref in own], part[:2], part[2:4], full, part[4:])
    parts = modulate_steps(devices, mod_ins, mod_outs, mod_bufs, mod_sems)
    moves = gather_steps(job)
    for kind in START_ORDER:
        (parts if kind == "a" else moves).pop(0)()


START_ORDER = "ag" "aa" "gg" "a" "g" "a" "g" "a" "g" "a" "gg" "a" "gggggggg" "a" "g"


def gather_modulate(pair, ins):
    devices = lax.axis_size(AXIS)
    msg, _, wcond, rows = ins[:4]
    cols, images = rows.shape
    outs = [
        (LINE, PLANE, images // devices, wcond.shape[0]), (cols, images), (cols, images), (devices * cols, images),
        (devices * cols, images), (images, FREQ), (images, 128),
    ]
    padded = -(-cols // 16) * 16
    vmem = pl.BlockSpec(memory_space=pltpu.VMEM)
    return pl.pallas_call(
        functools.partial(start_kernel, devices),
        out_shape=[full_shape(a) for a in pair]
        + [jax.ShapeDtypeStruct(shape, jnp.float32) for shape in outs]
        + [jax.ShapeDtypeStruct((LINE, PLANE) + msg.shape, jnp.bfloat16)],
        in_specs=[vmem] * 8,
        out_specs=[pl.BlockSpec(memory_space=pl.ANY)] * 2 + [vmem] * 8,
        scratch_shapes=gather_scratch(piece_shapes([a.shape[1:] for a in pair]))
        + [
            pltpu.VMEM((LINE, PLANE, padded, images), jnp.bfloat16),
            pltpu.VMEM((LINE, PLANE, padded, images), jnp.bfloat16),
            pltpu.VMEM((LINE, PLANE, images // devices, wcond.shape[0]), jnp.float32),
            pltpu.VMEM((LINE, PLANE, images // devices, wcond.shape[0]), jnp.float32),
            pltpu.VMEM((cols, 1024), jnp.float32),
            pltpu.SemaphoreType.DMA((4, LINE + PLANE)),
            pltpu.SemaphoreType.DMA((4, LINE + PLANE)),
        ],
        compiler_params=pltpu.CompilerParams(collective_id=3, has_side_effects=True, vmem_limit_bytes=56 << 20),
        name="gather_modulate",
    )(*pair, *ins)


FORWARD_POINTS = 13


def forward_gather_kernel(slots, x, mod, w_in, w_out, b_in, b_out, own_in, own_out, *refs):
    outs, x_out, full, refs = refs[:10], refs[10], refs[11:13], refs[13:]
    vm_in, vm_out, sems, part = refs[0], refs[1], refs[2], refs[3:]
    place = Place()
    job = Gather(place, (own_in.at[0], own_out.at[0]), part[:2], part[2:4], full, part[4:])
    hooks = Hooks([place.greet] + gather_steps(job), slots, FORWARD_POINTS)
    weights = Weights((w_in, w_out), (vm_in, vm_out), sems)
    weights.start((0, 1, 2, 3))
    x_out[...] = forward_image(x, mod, weights, b_in, b_out, outs, hooks)


GATHER_SLOTS = (0, 0, 13, 15, 26, 28, 39, 41, 50) + (34, 43, 48, 51, 51, 51, 51, 51, 51)


def layer_block(array, layer):
    return pl.BlockSpec((1,) + array.shape[1:], lambda i: (layer, 0, 0))


def full_shape(array):
    return jax.ShapeDtypeStruct((lax.axis_size(AXIS) * array.shape[1], array.shape[2]), jnp.bfloat16)


def forward_gather(ins, pair, layer):
    images = ins[1].shape[0]
    shapes, specs = kept_shapes(images)
    any_block = pl.BlockSpec(memory_space=pl.ANY)
    return pl.pallas_call(
        functools.partial(forward_gather_kernel, GATHER_SLOTS),
        grid=(images,),
        out_shape=shapes
        + [jax.ShapeDtypeStruct((images * SEQ, MODEL_WIDTH), jnp.float32)]
        + [full_shape(a) for a in pair],
        in_specs=forward_specs() + [layer_block(a, layer) for a in pair],
        out_specs=specs + [token_block(MODEL_WIDTH)] + [any_block] * 2,
        scratch_shapes=WEIGHT_SCRATCH + gather_scratch(piece_shapes([a.shape[1:] for a in pair])),
        compiler_params=pltpu.CompilerParams(collective_id=1, has_side_effects=True, vmem_limit_bytes=58 << 20),
        name="forward_gather",
    )(*ins, *pair)


GRAD_CUTS = [3 * MODEL_WIDTH // MODEL_WIDTH, FF // MODEL_WIDTH]


class Grads:
    def __init__(self, hbm, bufs, keep_in, keep_out, sems):
        bufs = [bufs[0], bufs[4], *bufs[1:]]
        self.bufs, self.keep_in, self.keep_out = bufs, keep_in, keep_out
        self.copies = [pltpu.make_async_copy(src, dst, sems.at[i]) for i, (src, dst) in enumerate(zip(hbm, bufs))]
        self.here = set()

    def start(self):
        for i in (4, 5, 6, 7, 2, 3, 0):
            self.copies[i].start()

    def need(self, *which):
        for i in which:
            if i not in self.here:
                self.copies[i].wait()
                self.here.add(i)

    def rows_in(self, chunk):
        width = MODEL_WIDTH
        pair = 0 if chunk < 3 else 1
        self.need(2 * pair, 2 * pair + 1)
        left, right = self.bufs[2 * pair], self.bufs[2 * pair + 1]
        at = (chunk - 3 * pair) * width
        self.keep_in[chunk * width : (chunk + 1) * width, :] = dot_tn(left[:, at : at + width], right[...]).astype(
            jnp.bfloat16
        )

    def rows_out(self, part):
        width = MODEL_WIDTH
        rows = slice(part * width // 2, (part + 1) * width // 2)
        self.need(4, 5)
        self.keep_out[rows, :width] = dot_tn(self.bufs[4][:, rows], self.bufs[5][...]).astype(jnp.bfloat16)
        self.need(6, 7)
        for j in range(FF // width):
            span = slice(j * width, (j + 1) * width)
            self.keep_out[rows, (1 + j) * width : (2 + j) * width] = dot_tn(
                self.bufs[6][:, rows], self.bufs[7][:, span]
            ).astype(jnp.bfloat16)
        if part == 0:
            self.copies[1].start()


def grads_out_kernel(*refs):
    ins, g_in, total, refs = refs[:8], refs[8], refs[9:10], refs[10:]
    bufs, keep_in, keep_out, load_sems, store_sem, refs = refs[:7], refs[7], refs[8], refs[9], refs[10], refs[11:]
    place = Place()
    work = Grads(ins, bufs, keep_in, keep_out, load_sems)
    work.start()
    place.greet()
    job = Scatter(place, [keep_out], total, refs[:6], refs[6:])
    work.rows_out(1)
    job.open(3)
    job.open(2)
    work.rows_out(0)
    job.open(0)
    job.open(1)
    moves = job.steps()
    for chunk in range(7):
        moves[chunk]()
        work.rows_in(chunk)
    store = pltpu.make_async_copy(keep_in, g_in, store_sem)
    store.start()
    for move in moves[7:]:
        move()
    store.wait()


def grad_bufs(ins):
    return [pltpu.VMEM(a.shape, a.dtype) for i, a in enumerate(ins) if i != 1] + [
        pltpu.VMEM((IW, MODEL_WIDTH), jnp.bfloat16),
        pltpu.VMEM((MODEL_WIDTH, OW), jnp.bfloat16),
        pltpu.SemaphoreType.DMA((8,)),
    ]


def weight_grads_out(ins, shape):
    any_block = pl.BlockSpec(memory_space=pl.ANY)
    return pl.pallas_call(
        grads_out_kernel,
        out_shape=[jax.ShapeDtypeStruct((IW, MODEL_WIDTH), jnp.bfloat16), jax.ShapeDtypeStruct(shape, jnp.float32)],
        in_specs=[any_block] * 8,
        out_specs=[any_block, pl.BlockSpec(memory_space=pltpu.VMEM)],
        scratch_shapes=grad_bufs(ins) + [pltpu.SemaphoreType.DMA] + scatter_scratch(piece_shapes([shape])),
        compiler_params=pltpu.CompilerParams(collective_id=5, has_side_effects=True, vmem_limit_bytes=58 << 20),
        name="weight_grads_out",
    )(*ins)


BACKWARD_POINTS = 13


def backward_scatter_kernel(slots, mod, w_in, w_out, grad, lat_t, *refs):
    ins, outs, (g_patch, g_pbias, total), refs = refs[:8], refs[8:16], refs[16:19], refs[19:]
    vm_in, vm_out, sems, mine, refs = refs[0], refs[1], refs[2], refs[3], refs[4:]
    place = Place()
    job = Scatter(place, [grad], [total], refs[:6], refs[6:], [mine])
    hooks = Hooks([place.greet, job.open_all] + job.steps(), slots, BACKWARD_POINTS)
    weights = Weights((w_in, w_out), (vm_in, vm_out), sems)
    weights.start((3, 2, 1, 0))
    backward_image(ins, mod, weights, outs, hooks)
    d_patch = outs[0][...].astype(jnp.bfloat16)

    @pl.when(pl.program_id(0) == 0)
    def _():
        g_patch[...] = jnp.zeros_like(g_patch)
        g_pbias[...] = jnp.zeros_like(g_pbias)

    g_patch[...] += dot_nn(lat_t[0], d_patch)
    g_pbias[...] += jnp.sum(d_patch.astype(jnp.float32), 0, keepdims=True)


SCATTER_SLOTS = (0, 0, 3, 6, 10, 13, 18, 25, 27, 32, 34, 38, 42, 51, 51, 51, 51)


def backward_scatter(mods, w_in, w_out, refs, grad, lat_t, shape):
    images, width, low, full = mods.shape[0], MODEL_WIDTH, jnp.bfloat16, jnp.float32
    tokens = images * SEQ
    any_block = pl.BlockSpec(memory_space=pl.ANY)
    shapes = [((tokens, width), full), ((tokens, 3 * width), low), ((tokens, FF), low), ((tokens, width), low),
              ((tokens, width), low), ((images, 6, width), full), ((1, IW), full), ((1, 2 * width), full),
              ((PD, width), full), ((1, width), full), (shape, full)]
    pieces = piece_shapes([shape])
    return pl.pallas_call(
        functools.partial(backward_scatter_kernel, SCATTER_SLOTS),
        grid=(images,),
        out_shape=[jax.ShapeDtypeStruct(s, t) for s, t in shapes],
        in_specs=[image_block(6, width), any_block, any_block, any_block, image_block(PD, SEQ), token_block(width),
                  token_block(width), token_block(width), image_block(HEADS, SEQ, SEQ), token_block(3 * width),
                  token_block(width), token_block(width), token_block(FF)],
        out_specs=[token_block(s[1]) for s, _ in shapes[:5]]
        + [image_block(6, width)] + [whole_block(*s) for s, _ in shapes[6:-1]] + [any_block],
        scratch_shapes=WEIGHT_SCRATCH
        + [pltpu.VMEM((16,) + pieces[0], jnp.bfloat16)] + scatter_scratch(pieces),
        compiler_params=pltpu.CompilerParams(collective_id=6, has_side_effects=True, vmem_limit_bytes=62 << 20),
        name="backward_scatter",
    )(mods, w_in, w_out, grad, lat_t, *refs)


def finish_kernel(devices, *refs):
    count = len(SETTLE_INS)
    ins, set_ins, refs = refs[:8], dict(zip(SETTLE_INS, refs[8 : 8 + count])), refs[8 + count :]
    totals, set_outs, refs = refs[:2], refs[2:7], refs[7:]
    bufs, keep_in, keep_out, load_sems, refs = refs[:7], refs[7], refs[8], refs[9], refs[10:]
    sc_bufs, sc_sems, refs = refs[:12], refs[12:24], refs[24:]
    set_bufs, set_sems = refs[:16], refs[16:]
    work = Grads(ins, bufs, keep_in, keep_out, load_sems)
    work.start()
    place = Place()
    place.greet()
    job = Scatter(place, [keep_in, keep_out], totals, sc_bufs, sc_sems)
    (first, second, third, fourth, message, last), betweens = settle_steps(
        devices, set_ins, set_outs, set_bufs, set_sems, totals
    )
    first()
    work.rows_out(1)
    betweens[0]()
    work.rows_in(5)
    work.rows_in(6)
    second()
    job.open(3)
    work.rows_out(0)
    betweens[2]()
    job.cross_b(3)
    work.rows_in(0)
    work.rows_in(1)
    job.open(0)
    third()
    work.rows_in(3)
    job.cross_b(0)
    work.rows_in(4)
    job.open(2)
    job.cross_a(3)
    work.rows_in(2)
    job.cross_b(2)
    job.open(1)
    job.cross_a(0)
    job.along_z(3)
    job.cross_b(1)
    betweens[1]()
    betweens[3]()
    job.cross_a(2)
    job.along_z(0)
    job.cross_a(1)
    job.along_z(2)
    fourth()
    job.along_z(1)
    job.close()
    job.end()
    message()
    job.finish()
    last()


def finish_grads(ins, shapes, set_ins):
    devices = lax.axis_size(AXIS)
    wcond, d_mods = set_ins["wcond"], set_ins["d_mods"]
    cols, images = set_ins["pre"].shape
    outs = [(wcond.shape[0], devices * cols), (cols, FREQ), (cols, devices * cols), (cols, 1024)]
    vmem = pl.BlockSpec(memory_space=pltpu.VMEM)
    low = jnp.bfloat16
    return pl.pallas_call(
        functools.partial(finish_kernel, devices),
        out_shape=[jax.ShapeDtypeStruct(shape, jnp.float32) for shape in list(shapes) + outs]
        + [jax.ShapeDtypeStruct((LINE, PLANE, 32, 128), low)],
        in_specs=[pl.BlockSpec(memory_space=pl.ANY)] * 8 + [vmem] * len(SETTLE_INS),
        out_specs=[vmem] * 7,
        scratch_shapes=grad_bufs(ins)
        + scatter_scratch(piece_shapes(shapes))
        + [
            pltpu.VMEM(d_mods.shape, jnp.float32),
            pltpu.VMEM(d_mods.shape, jnp.float32),
            pltpu.VMEM((images, 384), jnp.float32),
            pltpu.VMEM((devices * 16, 128), jnp.float32),
            pltpu.VMEM((LINE, PLANE, 16, 128), low),
            pltpu.VMEM((LINE, PLANE, 16, 128), low),
            pltpu.VMEM((LINE, 16, 128), jnp.float32),
            pltpu.VMEM((LINE, 16, 128), jnp.float32),
        ]
        + [
            pltpu.VMEM((LINE, PLANE, 32, images), low),
            pltpu.VMEM((LINE, PLANE, 32, images), low),
            pltpu.VMEM((LINE, 32, images), jnp.float32),
            pltpu.VMEM((LINE, 32, images), jnp.float32),
        ]
        * 2
        + [
            pltpu.SemaphoreType.DMA((5, LINE + PLANE)),
            pltpu.SemaphoreType.DMA((5, LINE + PLANE)),
        ],
        compiler_params=pltpu.CompilerParams(collective_id=4, has_side_effects=True, vmem_limit_bytes=63 << 20),
        name="finish_grads",
    )(*ins, *(set_ins[name] for name in SETTLE_INS))

def code_table():
    quarter = MODEL_WIDTH // 4
    omega = (1.0 / 10000.0 ** (np.arange(quarter, dtype=np.float32) / np.float32(quarter))).astype(np.float32)
    angles = np.arange(GRID, dtype=np.float32)[:, None] * omega
    return np.concatenate([np.sin(angles), np.cos(angles)], 1).astype(np.float32)


def position_sum():
    table = jnp.asarray(code_table())
    half = MODEL_WIDTH // 2
    rows_pos = jnp.broadcast_to(table[:, None, :], (GRID, GRID, half))
    cols_pos = jnp.broadcast_to(table[None, :, :], (GRID, GRID, half))
    return jnp.concatenate([rows_pos, cols_pos], -1).reshape(SEQ, MODEL_WIDTH)


def rows_t(left, right):
    return jnp.einsum("bsd,ed->bse", left, right, preferred_element_type=jnp.float32)


def body(
    latents, targets, timesteps, labels, embed_w, embed_m, embed_v, cond_w, cond_m, cond_v, layer_input_weights, in_m,
    in_v, layer_output_weights, out_m, out_v, head_w, head_m, head_v, biases, bias_m, bias_v,
):
    devices = lax.axis_size("fsdp")
    me = lax.axis_index("fsdp")
    images = latents.shape[0]
    embed_t = embed_w.T
    cond_t = cond_w.T
    in_t = layer_input_weights.transpose(0, 2, 1)
    out_t = layer_output_weights.transpose(0, 2, 1)
    cols, cond_cols = embed_t.shape[0], cond_t.shape[0]
    time_one, time_two, patch_bias, cond_bias, block_input_bias, block_output_bias, head_bias = split_biases(biases)
    features = time_features(timesteps)
    own_patch_w = jnp.pad(embed_t[:, FREQ + MODEL_WIDTH : FREQ + MODEL_WIDTH + PD].reshape(3, 128), ((0, 1), (0, 0)))
    digits = jnp.stack([labels // 32, labels % 32], 1).astype(jnp.float32)
    digits = jnp.broadcast_to(digits[:, :, None], (images, 2, 64)).reshape(images, 128)
    note = jnp.concatenate([features[:, :128], features[:, 128:], own_patch_w, digits], 0).astype(jnp.bfloat16)
    images_all = devices * images

    def own_bias(vector, count):
        part = lax.dynamic_slice(vector, (me * count,), (count,))
        return jnp.broadcast_to(part[:, None], (count, images_all))

    own_cond_bias = lax.dynamic_slice(cond_bias, (me * cond_cols,), (cond_cols,))[None]
    first_in, first_out, mods, pre, cond, hid_all, low_all, feat_all, lab_all, notes = gather_modulate(
        [in_t, out_t],
        [note, embed_t, cond_t, own_bias(time_one, cols), own_bias(time_two, cols), own_cond_bias],
    )
    chunks = mods.reshape(devices, images, cond_cols).transpose(1, 0, 2).reshape(images, 6 * LAYERS + 2, MODEL_WIDTH)
    w_patch = notes[:, :, 8:11].reshape(MODEL_WIDTH, PD)
    x = (rows_t(latents, w_patch) + patch_bias + position_sum()).reshape(images * SEQ, MODEL_WIDTH)
    block_mods = [chunks[:, 6 * i : 6 * (i + 1)] for i in range(LAYERS)]
    head_t = head_w.T
    tokens_all = devices * images * SEQ * PO
    lat_t = latents.transpose(0, 2, 1)
    bias_rows = [(block_input_bias[i][None], block_output_bias[i][None]) for i in range(LAYERS)]
    *kept0, x_mid, last_in, last_out = forward_gather(
        [x, block_mods[0], first_in, first_out, *bias_rows[0]], [in_t, out_t], 1
    )
    *kept1, upstream, d_final, head_grad, head_bias_grad, loss_part = forward_head(
        [x_mid, block_mods[1], last_in, last_out, *bias_rows[1], chunks[:, 6 * LAYERS :], head_t, head_bias[:, None],
         targets.transpose(0, 2, 1)],
        2.0 / tokens_all,
    )
    h1, qkv, probs, o, a, x1, h2, u, g, f = kept1
    upstream, d_qkv, d_u, d_f, d_a, mod_grad1, in_bias1, out_bias1 = backward_block(
        block_mods[1], last_in, last_out, [upstream, x_mid, x1, probs, qkv, a, f, u]
    )
    in_shape, out_shape = in_t.shape[1:], out_t.shape[1:]
    grad_in, out_shard1 = weight_grads_out([d_qkv, h1, d_u, h2, d_a, o, d_f, g], out_shape)
    h1, qkv, probs, o, a, x1, h2, u, g, f = kept0
    (upstream, d_qkv, d_u, d_f, d_a, mod_grad0, in_bias0, out_bias0, patch_grad, patch_bias_grad, in_shard1) = backward_scatter(
        block_mods[0], first_in, first_out, [upstream, x, x1, probs, qkv, a, f, u], grad_in, lat_t, in_shape
    )
    mod_grads, in_bias_grads, out_bias_grads = [mod_grad0, mod_grad1], [in_bias0, in_bias1], [out_bias0, out_bias1]
    d_modulation = jnp.concatenate(mod_grads + [d_final], 1)
    d_mods = d_modulation.reshape(images, devices, cond_cols).transpose(1, 0, 2)
    d_mods = d_mods.reshape(LINE, PLANE, images, cond_cols)
    in_shard0, out_shard0, g_cond, g_t1, g_t2, g_cls, merged = finish_grads(
        [d_qkv, h1, d_u, h2, d_a, o, d_f, g],
        [in_shape, out_shape],
        {
            "d_mods": d_mods, "emb": embed_t, "wcond": cond_t, "pre": pre, "cond": cond, "hid_all": hid_all, "low_all": low_all,
            "feat_all": feat_all, "lab_all": lab_all, "g_head": head_grad, "g_hbias": head_bias_grad, "loss": loss_part,
            "g_patch": patch_grad, "g_pbias": patch_bias_grad, "bin0": in_bias_grads[0], "bin1": in_bias_grads[1],
            "bout0": out_bias_grads[0], "bout1": out_bias_grads[1], "done_in": in_shard1, "done_out": out_shard1,
        },
    )
    merged = merged.astype(jnp.float32).reshape(devices, 32, 128)
    wide = MODEL_WIDTH // 128
    blocks = merged[:, :16]
    patch_total = blocks[:wide].transpose(1, 0, 2).reshape(PD, MODEL_WIDTH)
    head_total = blocks[wide : 3 * wide].reshape(wide, PO, 128).transpose(1, 0, 2).reshape(PO, MODEL_WIDTH)
    flat = blocks[3 * wide :].reshape(-1)
    rest = LAYERS * (IW + 2 * MODEL_WIDTH) + PO
    loss_total = jnp.sum(merged[:, 19, :3])
    bias_total = jnp.concatenate(
        [merged[:, 16, :cols].reshape(-1), merged[:, 17, :cols].reshape(-1), flat[:MODEL_WIDTH],
         merged[:, 20:23].reshape(devices, 384)[:, :cond_cols].reshape(-1), flat[MODEL_WIDTH : MODEL_WIDTH + rest]]
    )
    grad_norm = jnp.sqrt(
        jnp.sum(merged[:, 18, :3])
        + jnp.sum(head_total * head_total)
        + jnp.sum(patch_total * patch_total)
        + jnp.sum(bias_total * bias_total)
    )
    factor = jnp.minimum(1.0, clip_limit / grad_norm)
    own_patch = lax.dynamic_slice(patch_total, (0, me * cols), (PD, cols)).T
    embed_grad = jnp.concatenate([g_t1, g_t2, own_patch, g_cls[:, PD : PD + NCLS]], 1)
    embed_up = [a.T for a in adam_step(embed_t, embed_m.T, embed_v.T, embed_grad * factor)]
    cond_up = [a.T for a in adam_step(cond_t, cond_m.T, cond_v.T, g_cond * factor)]
    turn = (0, 2, 1)
    in_up = [
        a.transpose(turn)
        for a in adam_step(in_t, in_m.transpose(turn), in_v.transpose(turn), jnp.stack([in_shard0, in_shard1]) * factor)
    ]
    out_up = [
        a.transpose(turn)
        for a in adam_step(out_t, out_m.transpose(turn), out_v.transpose(turn), jnp.stack([out_shard0, out_shard1]) * factor)
    ]
    head_up = [a.T for a in adam_step(head_t, head_m.T, head_v.T, head_total * factor)]
    bias_up = adam_step(biases, bias_m, bias_v, bias_total * factor)
    return (loss_total, grad_norm, *embed_up, *cond_up, *in_up, *out_up, *head_up, *bias_up)


def fits(mesh):
    return mesh.shape["fsdp"] == 32


def solution(mesh):
    in_specs = (
        P("fsdp", None, None),
        P("fsdp", None, None),
        P("fsdp"),
        P("fsdp"),
        P(None, "fsdp"),
        P(None, "fsdp"),
        P(None, "fsdp"),
        P(None, "fsdp"),
        P(None, "fsdp"),
        P(None, "fsdp"),
        P(None, None, "fsdp"),
        P(None, None, "fsdp"),
        P(None, None, "fsdp"),
        P(None, None, "fsdp"),
        P(None, None, "fsdp"),
        P(None, None, "fsdp"),
        P(),
        P(),
        P(),
        P(),
        P(),
        P(),
    )
    out_specs = (
        P(),
        P(),
        P(None, "fsdp"),
        P(None, "fsdp"),
        P(None, "fsdp"),
        P(None, "fsdp"),
        P(None, "fsdp"),
        P(None, "fsdp"),
        P(None, None, "fsdp"),
        P(None, None, "fsdp"),
        P(None, None, "fsdp"),
        P(None, None, "fsdp"),
        P(None, None, "fsdp"),
        P(None, None, "fsdp"),
        P(),
        P(),
        P(),
        P(),
        P(),
        P(),
    )
    chosen = body if fits(mesh) else generic_body
    return jax.shard_map(chosen, mesh=mesh, in_specs=in_specs, out_specs=out_specs, check_vma=False)
```

```python
import functools
import math

import jax
import jax.numpy as jnp
import numpy as np
from jax import lax
from jax.experimental import pallas as pl
from jax.experimental.pallas import tpu as pltpu
from jax.sharding import PartitionSpec as P

MODEL_WIDTH = 768
HEADS = 12
HEAD_DIM = 64
NCLS = 1001
FREQ = 256
PD = 16
PO = 32
GRID = 16
LAYERS = 2
STEP = 10
SEQ = 256
IW = 5376
OW = 3840
FF = 3072
CW = 10752


learn_rate = 0.03
beta_one = 0.9
beta_two = 0.999
adam_eps = 1e-08
decay = 0.01
clip_limit = 0.01
highest = lax.Precision.HIGHEST


def product(left, right):
    return jnp.dot(left, right, preferred_element_type=jnp.float32)


def exact_dot(left, right):
    return jnp.dot(left, right, precision=highest)


def apply_rows(left, right):
    return jnp.einsum("bsd,de->bse", left, right, preferred_element_type=jnp.float32)


def outer_sum(left, right):
    return jnp.einsum("bsd,bse->de", left, right, preferred_element_type=jnp.float32)


def apply_back(left, right):
    return jnp.einsum("bse,de->bsd", left, right, preferred_element_type=jnp.float32)


def column_sum(value):
    return jnp.sum(value.astype(jnp.float32), (0, 1))


def silu(value):
    return value * jax.nn.sigmoid(value)


def gelu(value):
    return jax.nn.gelu(value, approximate=True)


def layer_norm(value):
    centered = value - jnp.mean(value, -1, keepdims=True)
    return centered * lax.rsqrt(jnp.mean(centered * centered, -1, keepdims=True) + 1e-06)


def local_back(func, value, cotangent):
    return jax.vjp(func, value)[1](cotangent)[0]


def position_table():
    quarter = MODEL_WIDTH // 4
    omega = 1.0 / 10000.0 ** (jnp.arange(quarter, dtype=jnp.float32) / quarter)
    places = jnp.arange(GRID * GRID)
    rows_pos = (places // GRID).astype(jnp.float32)[:, None] * omega
    cols_pos = (places % GRID).astype(jnp.float32)[:, None] * omega
    return jnp.concatenate(
        [jnp.sin(rows_pos), jnp.cos(rows_pos), jnp.sin(cols_pos), jnp.cos(cols_pos)], 1
    )


def time_features(timesteps):
    half_freq = FREQ // 2
    rates = jnp.exp(-math.log(10000.0) * jnp.arange(half_freq, dtype=jnp.float32) / half_freq)
    angles = timesteps.astype(jnp.float32)[:, None] * rates
    return jnp.concatenate([jnp.cos(angles), jnp.sin(angles)], 1)


def split_biases(vector):
    lengths = [MODEL_WIDTH, MODEL_WIDTH, MODEL_WIDTH, CW, LAYERS * IW, LAYERS * 2 * MODEL_WIDTH, PO]
    pieces = []
    offset = 0
    for length in lengths:
        pieces.append(vector[offset : offset + length])
        offset += length
    pieces[4] = pieces[4].reshape(LAYERS, IW)
    pieces[5] = pieces[5].reshape(LAYERS, 2 * MODEL_WIDTH)
    return pieces


def split_heads(triple, which):
    n_images, seq_len = (triple.shape[0], triple.shape[1])
    return triple[..., which * MODEL_WIDTH : (which + 1) * MODEL_WIDTH].reshape(
        n_images, seq_len, HEADS, HEAD_DIM
    )


def attend(triple):
    queries, key_part, values = [split_heads(triple, j) for j in range(3)]
    scores = jnp.einsum(
        "bqhd,bkhd->bhqk", queries, key_part, preferred_element_type=jnp.float32
    ) * HEAD_DIM ** (-0.5)
    row_max = jnp.max(scores, -1, keepdims=True)
    expo = jnp.exp(scores - row_max)
    row_sum = jnp.sum(expo, -1, keepdims=True)
    attn_weights = (expo / row_sum).astype(jnp.bfloat16)
    mixed_heads = jnp.einsum(
        "bhqk,bkhd->bqhd", attn_weights, values, preferred_element_type=jnp.float32
    ).astype(jnp.bfloat16)
    return (
        mixed_heads.reshape(triple.shape[0], triple.shape[1], MODEL_WIDTH),
        row_max + jnp.log(row_sum),
    )


def attend_back(triple, log_norm, d_mixed):
    queries, key_part, values = [split_heads(triple, j) for j in range(3)]
    scale = HEAD_DIM ** (-0.5)
    scores = (
        jnp.einsum("bqhd,bkhd->bhqk", queries, key_part, preferred_element_type=jnp.float32) * scale
    )
    probs_full = jnp.exp(scores - log_norm)
    attn_weights = probs_full.astype(jnp.bfloat16)
    d_heads = d_mixed.reshape(queries.shape)
    d_probs = jnp.einsum("bqhd,bkhd->bhqk", d_heads, values, preferred_element_type=jnp.float32)
    d_values = jnp.einsum(
        "bhqk,bqhd->bkhd", attn_weights, d_heads, preferred_element_type=jnp.float32
    )
    d_scores = (probs_full * (d_probs - jnp.sum(probs_full * d_probs, -1, keepdims=True))).astype(
        jnp.bfloat16
    )
    d_queries = (
        jnp.einsum("bhqk,bkhd->bqhd", d_scores, key_part, preferred_element_type=jnp.float32)
        * scale
    )
    d_keys = (
        jnp.einsum("bhqk,bqhd->bkhd", d_scores, queries, preferred_element_type=jnp.float32) * scale
    )
    shape_flat = (triple.shape[0], triple.shape[1], MODEL_WIDTH)
    return jnp.concatenate(
        [d_queries.reshape(shape_flat), d_keys.reshape(shape_flat), d_values.reshape(shape_flat)],
        -1,
    ).astype(jnp.bfloat16)


def block_forward(residual_state, adaptive_modulation, weights_in, weights_out, bias_in, bias_out):
    pieces = [
        adaptive_modulation[:, None, i * MODEL_WIDTH : (i + 1) * MODEL_WIDTH] for i in range(6)
    ]
    shaped_one = (layer_norm(residual_state) * (1 + pieces[1]) + pieces[0]).astype(jnp.bfloat16)
    triple = (
        apply_rows(shaped_one, weights_in[:, : 3 * MODEL_WIDTH]) + bias_in[: 3 * MODEL_WIDTH]
    ).astype(jnp.bfloat16)
    mixed_heads, log_norm = attend(triple)
    branch = apply_rows(mixed_heads, weights_out[:MODEL_WIDTH]) + bias_out[:MODEL_WIDTH]
    middle = residual_state + pieces[2] * branch
    shaped_two = (layer_norm(middle) * (1 + pieces[4]) + pieces[3]).astype(jnp.bfloat16)
    pre_ffn = apply_rows(shaped_two, weights_in[:, 3 * MODEL_WIDTH :]) + bias_in[3 * MODEL_WIDTH :]
    active = gelu(pre_ffn).astype(jnp.bfloat16)
    ffn_out = apply_rows(active, weights_out[MODEL_WIDTH:]) + bias_out[MODEL_WIDTH:]
    kept = (
        residual_state,
        shaped_one,
        triple,
        log_norm,
        mixed_heads,
        branch,
        middle,
        shaped_two,
        pre_ffn,
        active,
        ffn_out,
    )
    return (middle + pieces[5] * ffn_out, kept)


def block_backward(upstream, adaptive_modulation, weights_in, weights_out, kept):
    (
        residual_state,
        shaped_one,
        triple,
        log_norm,
        mixed_heads,
        branch,
        middle,
        shaped_two,
        pre_ffn,
        active,
        ffn_out,
    ) = kept
    pieces = [
        adaptive_modulation[:, None, i * MODEL_WIDTH : (i + 1) * MODEL_WIDTH] for i in range(6)
    ]
    d_ffn = (pieces[5] * upstream).astype(jnp.bfloat16)
    gate_two = jnp.sum(ffn_out * upstream, 1)
    grad_down = outer_sum(active, d_ffn)
    d_active = apply_back(d_ffn, weights_out[MODEL_WIDTH:])
    d_pre = local_back(gelu, pre_ffn, d_active).astype(jnp.bfloat16)
    grad_up = outer_sum(shaped_two, d_pre)
    d_shaped = apply_back(d_pre, weights_in[:, 3 * MODEL_WIDTH :])
    shift_two = jnp.sum(d_shaped, 1)
    scale_two = jnp.sum(d_shaped * layer_norm(middle), 1)
    upstream = upstream + local_back(layer_norm, middle, d_shaped * (1 + pieces[4]))
    gate_one = jnp.sum(branch * upstream, 1)
    d_branch = (pieces[2] * upstream).astype(jnp.bfloat16)
    grad_proj = outer_sum(mixed_heads, d_branch)
    d_mixed = apply_back(d_branch, weights_out[:MODEL_WIDTH]).astype(jnp.bfloat16)
    d_triple = attend_back(triple, log_norm, d_mixed)
    grad_qkv = outer_sum(shaped_one, d_triple)
    d_shaped = apply_back(d_triple, weights_in[:, : 3 * MODEL_WIDTH])
    shift_one = jnp.sum(d_shaped, 1)
    scale_one = jnp.sum(d_shaped * layer_norm(residual_state), 1)
    upstream = upstream + local_back(layer_norm, residual_state, d_shaped * (1 + pieces[1]))
    mod_grad = jnp.concatenate([shift_one, scale_one, gate_one, shift_two, scale_two, gate_two], 1)
    bias_in_grad = jnp.concatenate([column_sum(d_triple), column_sum(d_pre)])
    bias_out_grad = jnp.concatenate([column_sum(d_branch), column_sum(d_ffn)])
    grad_in = jnp.concatenate([grad_qkv, grad_up], 1)
    grad_out = jnp.concatenate([grad_proj, grad_down], 0)
    return (upstream, mod_grad, grad_in, grad_out, bias_in_grad, bias_out_grad)


def fetch_layer(layer_input_weights, layer_output_weights, layer_count):
    return (
        lax.all_gather(
            layer_input_weights[layer_count].astype(jnp.bfloat16), "fsdp", axis=1, tiled=True
        ),
        lax.all_gather(
            layer_output_weights[layer_count].astype(jnp.bfloat16), "fsdp", axis=1, tiled=True
        ),
    )


def adam_step(weight, first, second, gradient):
    first = beta_one * first + (1 - beta_one) * gradient
    second = beta_two * second + (1 - beta_two) * gradient * gradient
    ahead = first / (1 - beta_one**STEP)
    scaled = second / (1 - beta_two**STEP)
    return (
        weight - learn_rate * (ahead / (jnp.sqrt(scaled) + adam_eps) + decay * weight),
        first,
        second,
    )


def generic_body(
    latents,
    targets,
    timesteps,
    labels,
    embed_w,
    embed_m,
    embed_v,
    cond_w,
    cond_m,
    cond_v,
    layer_input_weights,
    in_m,
    in_v,
    layer_output_weights,
    out_m,
    out_v,
    head_w,
    head_m,
    head_v,
    biases,
    bias_m,
    bias_v,
):
    devices = lax.axis_size("fsdp")
    embed_full, cond_full = (
        lax.all_gather(embed_w.astype(jnp.bfloat16), "fsdp", axis=1, tiled=True),
        lax.all_gather(cond_w.astype(jnp.bfloat16), "fsdp", axis=1, tiled=True),
    )
    time_one, time_two, patch_bias, cond_bias, block_input_bias, block_output_bias, head_bias = (
        split_biases(biases)
    )
    head_low = head_w.astype(jnp.bfloat16)
    features = time_features(timesteps).astype(jnp.bfloat16)
    pre_time = product(features, embed_full[:FREQ]) + time_one
    hidden_t = silu(pre_time).astype(jnp.bfloat16)
    time_emb = product(hidden_t, embed_full[FREQ : FREQ + MODEL_WIDTH]) + time_two
    onehot = (labels[:, None] == jnp.arange(NCLS)[None, :]).astype(jnp.bfloat16)
    condition = time_emb + product(onehot, embed_full[FREQ + MODEL_WIDTH + PD :])
    cond_low = silu(condition).astype(jnp.bfloat16)
    adaptive_modulation = product(cond_low, cond_full) + cond_bias
    residual_state = (
        apply_rows(latents, embed_full[FREQ + MODEL_WIDTH : FREQ + MODEL_WIDTH + PD])
        + patch_bias
        + position_table()
    )
    kept_all = []
    for layer_count in range(LAYERS):
        weights_in, weights_out = fetch_layer(
            layer_input_weights, layer_output_weights, layer_count
        )
        residual_state, kept = block_forward(
            residual_state,
            adaptive_modulation[
                :, 6 * MODEL_WIDTH * layer_count : 6 * MODEL_WIDTH * (layer_count + 1)
            ],
            weights_in,
            weights_out,
            block_input_bias[layer_count],
            block_output_bias[layer_count],
        )
        kept_all.append(kept)
    final_mod = adaptive_modulation[:, 6 * MODEL_WIDTH * LAYERS :]
    norm_final = layer_norm(residual_state)
    shaped = (
        norm_final * (1 + final_mod[:, None, MODEL_WIDTH:]) + final_mod[:, None, :MODEL_WIDTH]
    ).astype(jnp.bfloat16)
    output = apply_rows(shaped, head_low) + head_bias
    error_vals = output - targets
    loss_part = jnp.sum(error_vals * error_vals)
    tokens_all = devices * error_vals.shape[0] * SEQ * PO
    d_output = (error_vals * (2.0 / tokens_all)).astype(jnp.bfloat16)
    head_grad = outer_sum(shaped, d_output)
    head_bias_grad = column_sum(d_output)
    d_shaped = apply_back(d_output, head_low)
    d_final = jnp.concatenate([jnp.sum(d_shaped, 1), jnp.sum(d_shaped * norm_final, 1)], 1)
    upstream = local_back(
        layer_norm, residual_state, d_shaped * (1 + final_mod[:, None, MODEL_WIDTH:])
    )
    mod_grads = [None] * LAYERS
    in_shards = [None] * LAYERS
    out_shards = [None] * LAYERS
    in_bias_grads = [None] * LAYERS
    out_bias_grads = [None] * LAYERS
    for layer_count in reversed(range(LAYERS)):
        weights_in, weights_out = (
            lax.all_gather(
                layer_input_weights[layer_count].astype(jnp.bfloat16), "fsdp", axis=1, tiled=True
            ),
            lax.all_gather(
                layer_output_weights[layer_count].astype(jnp.bfloat16), "fsdp", axis=1, tiled=True
            ),
        )
        upstream, mod_grad, grad_in, grad_out, bias_in_grad, bias_out_grad = block_backward(
            upstream,
            adaptive_modulation[
                :, 6 * MODEL_WIDTH * layer_count : 6 * MODEL_WIDTH * (layer_count + 1)
            ],
            weights_in,
            weights_out,
            kept_all[layer_count],
        )
        in_shards[layer_count], out_shards[layer_count] = (
            lax.psum_scatter(grad_in, "fsdp", scatter_dimension=1, tiled=True),
            lax.psum_scatter(grad_out, "fsdp", scatter_dimension=1, tiled=True),
        )
        mod_grads[layer_count] = mod_grad
        in_bias_grads[layer_count] = bias_in_grad
        out_bias_grads[layer_count] = bias_out_grad
    d_patch = upstream.astype(jnp.bfloat16)
    patch_grad = outer_sum(latents, d_patch)
    patch_bias_grad = column_sum(d_patch)
    d_modulation = jnp.concatenate(mod_grads + [d_final], 1)
    d_cond = exact_dot(d_modulation, cond_full.astype(jnp.float32).T)
    d_condition = local_back(silu, condition, d_cond)
    d_hidden = exact_dot(d_condition, embed_full[FREQ : FREQ + MODEL_WIDTH].astype(jnp.float32).T)
    d_pre = local_back(silu, pre_time, d_hidden)
    cond_grad = exact_dot(cond_low.astype(jnp.float32).T, d_modulation)
    class_grad = exact_dot(onehot.astype(jnp.float32).T, d_condition)
    time_two_grad = exact_dot(hidden_t.astype(jnp.float32).T, d_condition)
    time_one_grad = exact_dot(features.astype(jnp.float32).T, d_pre)
    embed_grad = jnp.concatenate([time_one_grad, time_two_grad, patch_grad, class_grad], 0)
    embed_shard, cond_shard = (
        lax.psum_scatter(embed_grad, "fsdp", scatter_dimension=1, tiled=True),
        lax.psum_scatter(cond_grad, "fsdp", scatter_dimension=1, tiled=True),
    )
    bias_grad = jnp.concatenate(
        [jnp.sum(d_pre, 0), jnp.sum(d_condition, 0), patch_bias_grad, jnp.sum(d_modulation, 0)]
        + in_bias_grads
        + out_bias_grads
        + [head_bias_grad]
    )
    head_total, bias_total, loss_total = lax.psum((head_grad, bias_grad, loss_part), "fsdp")
    in_stack = jnp.stack(in_shards, 0)
    out_stack = jnp.stack(out_shards, 0)
    shard_squares = (
        jnp.sum(embed_shard * embed_shard)
        + jnp.sum(cond_shard * cond_shard)
        + jnp.sum(in_stack * in_stack)
        + jnp.sum(out_stack * out_stack)
    )
    square_total = lax.psum(shard_squares, "fsdp")
    grad_norm = jnp.sqrt(
        square_total + jnp.sum(head_total * head_total) + jnp.sum(bias_total * bias_total)
    )
    factor = jnp.minimum(1.0, clip_limit / grad_norm)
    embed_up = adam_step(embed_w, embed_m, embed_v, embed_shard * factor)
    cond_up = adam_step(cond_w, cond_m, cond_v, cond_shard * factor)
    in_up = adam_step(layer_input_weights, in_m, in_v, in_stack * factor)
    out_up = adam_step(layer_output_weights, out_m, out_v, out_stack * factor)
    head_up = adam_step(head_w, head_m, head_v, head_total * factor)
    bias_up = adam_step(biases, bias_m, bias_v, bias_total * factor)
    return (
        loss_total,
        grad_norm,
        embed_up[0],
        embed_up[1],
        embed_up[2],
        cond_up[0],
        cond_up[1],
        cond_up[2],
        in_up[0],
        in_up[1],
        in_up[2],
        out_up[0],
        out_up[1],
        out_up[2],
        head_up[0],
        head_up[1],
        head_up[2],
        bias_up[0],
        bias_up[1],
        bias_up[2],
    )


MESH_ID = pl.DeviceIdType.MESH
AXIS = "fsdp"


class Place:
    def __init__(self):
        me = lax.axis_index(AXIS)
        self.me = me
        self.core = core = me % 2
        x = (me // 2) % 2
        y = (me // 4) % 2
        self.z = me // 8
        self.chip = me // 2
        step_x = 1 - 2 * x
        step_y = 2 - 4 * y
        self.step_a = step_x + core * (step_y - step_x)
        self.step_b = step_y + core * (step_x - step_y)
        self.dev_a = me + 2 * self.step_a
        self.dev_b = me + 2 * self.step_b
        self.sibling = me + 1 - 2 * core

    def other(self, dz, flip_a=0, flip_b=0):
        return self.chip + 4 * dz + flip_a * self.step_a + flip_b * self.step_b

    def valid(self, dz):
        return jnp.logical_and(self.z + dz >= 0, self.z + dz < 4)

    def greet(self):
        barrier = pltpu.get_barrier_semaphore()

        def hello(device):
            pl.semaphore_signal(barrier, inc=1, device_id=(device,), device_id_type=MESH_ID)

        for k in range(1, 8):
            hello(8 * self.z + lax.rem(self.me + k, 8))
        for k in range(1, 4):
            hello(lax.rem(self.me + 8 * k, 32))
        pl.semaphore_wait(barrier, 10)


def remote(src, dst, send_sem, recv_sem, device):
    return pltpu.make_async_remote_copy(
        src_ref=src, dst_ref=dst, send_sem=send_sem, recv_sem=recv_sem, device_id=(device,), device_id_type=MESH_ID
    )


class Gather:
    def __init__(self, place, own, stage, piece, full, sems):
        self.p, self.own, self.stage, self.piece, self.full = place, own, stage, piece, full
        self.xch_send, self.xch_recv, self.local, self.send, self.recv, self.sib_recv = sems
        self.sent = []

    def slot(self, a, chip):
        rows, half = self.piece[a].shape
        return self.full[a].at[
            pl.ds(pl.multiple_of(chip * rows, rows), rows), pl.ds(pl.multiple_of(self.p.core * half, half), half)
        ]

    def push(self, a, k, src, chip, device, sem, cond=None):
        def act(what):
            copy = remote(src(), self.slot(a, chip()), self.send.at[a, k], sem.at[a, chip()], device())
            getattr(copy, what)()

        def guarded(what):
            if cond is None:
                act(what)
            else:
                pl.when(cond())(functools.partial(act, what))

        guarded("start")
        self.sent.append(functools.partial(guarded, "wait_send"))

    def store_own(self, a):
        return pltpu.make_async_copy(self.piece[a], self.slot(a, self.p.chip), self.local.at[a])

    def begin(self):
        core = self.p.core
        copies = []
        for a in range(2):
            rows, half = self.own[a].shape[0], self.piece[a].shape[1]
            dst = self.stage[a].at[pl.ds(pl.multiple_of(core * rows, 8), rows), :]
            away = remote(
                self.own[a].at[:, pl.ds(pl.multiple_of((1 - core) * half, half), half)],
                dst,
                self.xch_send.at[a],
                self.xch_recv.at[a],
                self.p.sibling,
            )
            away.start()
            keep = pltpu.make_async_copy(
                self.own[a].at[:, pl.ds(pl.multiple_of(core * half, half), half)], dst, self.local.at[a]
            )
            keep.start()
            copies.append((away, keep))
        for a in range(2):
            copies[a][0].wait()
            copies[a][1].wait()
            self.piece[a][...] = self.stage[a][...].astype(jnp.bfloat16)
            self.store_own(a).start()
            piece, here = (lambda a=a: self.piece[a]), (lambda: self.p.chip)
            for sign in (-1, 1):
                self.push(
                    a, 0 if sign < 0 else 3, piece, here, lambda sign=sign: self.p.me + 8 * sign, self.recv,
                    lambda sign=sign: self.p.valid(sign),
                )
            self.push(a, 6, piece, here, lambda: self.p.dev_a, self.recv)
            self.push(a, 10, piece, here, lambda: self.p.dev_b, self.recv)
            self.push(a, 18, piece, here, lambda: self.p.sibling, self.sib_recv)

    def arrive(self, a, chip):
        slot = self.slot(a, chip)
        pltpu.make_async_copy(slot, slot, self.recv.at[a, chip]).wait()

    def pass_on(self, dz, flip_a, flip_b, targets):
        def here():
            return self.p.valid(dz)

        def chip():
            return self.p.other(dz, flip_a, flip_b)

        for a in range(2):
            pl.when(here())(lambda a=a: self.arrive(a, chip()))
            for k, device, sem, extra in targets:
                self.push(
                    a, k, lambda a=a: self.slot(a, chip()), chip, device, sem,
                    here if extra is None else lambda extra=extra: jnp.logical_and(here(), self.p.valid(extra)),
                )

    def z_step(self, dist):
        for sign in (-1, 1):
            rel = (sign * dist) % 4
            targets = [
                (6 + rel, lambda: self.p.dev_a, self.recv, None),
                (10 + rel, lambda: self.p.dev_b, self.recv, None),
                (18 + rel, lambda: self.p.sibling, self.sib_recv, None),
            ]
            if dist < 3:
                onward = ((0 if sign > 0 else 3) + dist, lambda sign=sign: self.p.me - 8 * sign, self.recv, -sign)
                targets.insert(0, onward)
            self.pass_on(sign * dist, 0, 0, targets)

    def a_step(self, dist):
        for sign in (-1, 1) if dist else (1,):
            rel = (sign * dist) % 4
            self.pass_on(sign * dist, 1, 0, [
                (14 + rel, lambda: self.p.dev_b, self.recv, None), (22 + rel, lambda: self.p.sibling, self.sib_recv, None)
            ])

    def b_step(self, dist, flip_a):
        for sign in (-1, 1) if dist else (1,):
            rel = (sign * dist) % 4
            self.pass_on(
                sign * dist, flip_a, 1, [(26 + 4 * flip_a + rel, lambda: self.p.sibling, self.sib_recv, None)]
            )

    def finish(self):
        for a in range(2):
            rows, half = self.piece[a].shape

            def take(chip, carry):
                slot = self.full[a].at[
                    pl.ds(pl.multiple_of(chip * rows, rows), rows),
                    pl.ds(pl.multiple_of((1 - self.p.core) * half, half), half),
                ]
                pltpu.make_async_copy(slot, slot, self.sib_recv.at[a, chip]).wait()
                return carry

            lax.fori_loop(0, 16, take, 0)
            self.store_own(a).wait()
        for wait in self.sent:
            wait()


GATHER_SEMS = [
    pltpu.SemaphoreType.DMA((2,)),
    pltpu.SemaphoreType.DMA((2,)),
    pltpu.SemaphoreType.DMA((2,)),
    pltpu.SemaphoreType.DMA((2, 34)),
    pltpu.SemaphoreType.DMA((2, 16)),
    pltpu.SemaphoreType.DMA((2, 16)),
]


def gather_scratch(shapes):
    return (
        [pltpu.VMEM(shape, jnp.float32) for shape in shapes]
        + [pltpu.VMEM(shape, jnp.bfloat16) for shape in shapes]
        + GATHER_SEMS
    )


def piece_shapes(shapes):
    return [(2 * rows, width // 2) for rows, width in shapes]


ORDER = (3, 0, 2, 1)


class Scatter:
    def __init__(self, place, grads, totals, bufs, sems, mine=None):
        self.p, self.grad, self.total, self.mine = place, grads, totals, mine
        count = len(grads)
        self.arrays = range(count)
        self.sib, self.from_b, self.from_a, self.line, self.part, self.last = (
            bufs[count * i : count * i + count] for i in range(6)
        )
        (self.load_sem, self.sib_send, self.sib_recv, self.b_send, self.b_recv, self.a_send, self.a_recv, self.z_send,
         self.z_recv, self.end_send, self.end_recv, self.end_local) = sems

    def rows_of(self, a, chip, core):
        rows, half = self.part[a].shape
        return self.grad[a].at[
            pl.ds(pl.multiple_of(chip * rows, rows), rows), pl.ds(pl.multiple_of(core * half, half), half)
        ]

    def chip_of(self, z, flip_a, flip_b):
        return self.p.other(z - self.p.z, flip_a, flip_b)

    def own(self, a, flip_b, flip_a, z):
        if self.mine is None:
            return self.rows_of(a, self.chip_of(z, flip_a, flip_b), self.p.core)
        return self.mine[a].at[8 * flip_b + 4 * flip_a + z]

    def load(self, a, flip_b, flip_a, z):
        return pltpu.make_async_copy(
            self.rows_of(a, self.chip_of(z, flip_a, flip_b), self.p.core),
            self.own(a, flip_b, flip_a, z),
            self.load_sem.at[a, 8 * flip_b + 4 * flip_a + z],
        )

    def lend(self, a, flip_b, flip_a, z):
        k = 8 * flip_b + 4 * flip_a + z
        return remote(
            self.rows_of(a, self.chip_of(z, flip_b, flip_a), 1 - self.p.core),
            self.sib[a].at[k],
            self.sib_send.at[a, k],
            self.sib_recv.at[a, k],
            self.p.sibling,
        )

    def to_b(self, a, flip_a, z):
        k = 4 * flip_a + z
        return remote(
            self.own(a, 1, flip_a, z), self.from_b[a].at[k], self.b_send.at[a, k], self.b_recv.at[a, k], self.p.dev_b
        )

    def to_a(self, a, z):
        return remote(
            self.own(a, 0, 1, z), self.from_a[a].at[z], self.a_send.at[a, z], self.a_recv.at[a, z], self.p.dev_a
        )

    def to_z(self, a, target, source):
        return remote(
            self.own(a, 0, 0, target),
            self.line[a].at[source],
            self.z_send.at[a, target],
            self.z_recv.at[a, source],
            self.p.me + 8 * (target - self.p.z),
        )

    def open(self, z):
        for flip_b, flip_a in ((1, 1), (1, 0), (0, 1), (0, 0)):
            for a in self.arrays:
                self.lend(a, flip_b, flip_a, z).start()
                if self.mine is not None:
                    self.load(a, flip_b, flip_a, z).start()

    def open_all(self):
        for z in ORDER:
            self.open(z)

    def pair(self, a, flip_b, flip_a, z):
        if self.mine is not None:
            self.load(a, flip_b, flip_a, z).wait()
        self.lend(a, flip_b, flip_a, z).wait_recv()
        k = 8 * flip_b + 4 * flip_a + z
        return self.own(a, flip_b, flip_a, z)[...].astype(jnp.float32) + self.sib[a][k].astype(jnp.float32)

    def cross_b(self, z):
        for flip_a in (1, 0):
            for a in self.arrays:
                self.own(a, 1, flip_a, z)[...] = self.pair(a, 1, flip_a, z).astype(jnp.bfloat16)
                self.to_b(a, flip_a, z).start()

    def cross_a(self, z):
        for a in self.arrays:
            value = self.pair(a, 0, 1, z)
            self.to_b(a, 1, z).wait_recv()
            self.own(a, 0, 1, z)[...] = (value + self.from_b[a][4 + z].astype(jnp.float32)).astype(jnp.bfloat16)
            self.to_a(a, z).start()

    def along_z(self, z):
        place = self.p
        for a in self.arrays:
            value = self.pair(a, 0, 0, z)
            self.to_b(a, 0, z).wait_recv()
            value = value + self.from_b[a][z].astype(jnp.float32)
            self.to_a(a, z).wait_recv()
            self.part[a][...] = value + self.from_a[a][z].astype(jnp.float32)

            @pl.when(place.z != z)
            def _():
                self.own(a, 0, 0, z)[...] = self.part[a][...].astype(jnp.bfloat16)
                self.to_z(a, z, place.z).start()

            @pl.when(place.z == z)
            def _():
                self.last[a][...] = self.part[a][...]

    def end_copies(self, a):
        core = self.p.core
        rows, width = self.total[a].shape
        dst = self.total[a].at[:, pl.ds(pl.multiple_of(core * (width // 2), width // 2), width // 2)]
        away = remote(
            self.last[a].at[pl.ds(pl.multiple_of((1 - core) * rows, 8), rows), :],
            dst,
            self.end_send.at[a],
            self.end_recv.at[a],
            self.p.sibling,
        )
        keep = pltpu.make_async_copy(
            self.last[a].at[pl.ds(pl.multiple_of(core * rows, 8), rows), :], dst, self.end_local.at[a]
        )
        return away, keep

    def close(self):
        for a in self.arrays:

            def add(k, carry):
                source = lax.rem(self.p.z + k, 4)
                self.to_z(a, self.p.z, source).wait_recv()
                self.last[a][...] += self.line[a][source].astype(jnp.float32)
                return carry

            lax.fori_loop(1, 4, add, 0)
            for copy in self.end_copies(a):
                copy.start()

    def end(self):
        for a in self.arrays:
            for copy in self.end_copies(a):
                copy.wait()

    def finish(self):
        def step(z, carry):
            for a in self.arrays:
                for flip_b in range(2):
                    for flip_a in range(2):
                        self.lend(a, flip_b, flip_a, z).wait_send()
                for flip_a in range(2):
                    self.to_b(a, flip_a, z).wait_send()
                self.to_a(a, z).wait_send()

                @pl.when(self.p.z != z)
                def _():
                    self.to_z(a, z, self.p.z).wait_send()

            return carry

        lax.fori_loop(0, 4, step, 0)

    def steps(self):
        z0, z1, z2, z3 = ORDER
        work = [(self.cross_b, z) for z in ORDER]
        work += [(self.cross_a, z0), (self.cross_a, z1), (self.along_z, z0), (self.cross_a, z2), (self.along_z, z1)]
        work += [(self.cross_a, z3), (self.along_z, z2), (self.along_z, z3)]
        return [functools.partial(step, z) for step, z in work] + [self.close, self.end, self.finish]


def scatter_scratch(shapes):
    scratch = []
    for count, kind in ((16, jnp.bfloat16), (8, jnp.bfloat16), (4, jnp.bfloat16), (4, jnp.bfloat16),
                        (0, jnp.float32), (0, jnp.float32)):
        scratch += [pltpu.VMEM(((count,) if count else ()) + shape, kind) for shape in shapes]
    counts = (16, 16, 16, 8, 8, 4, 4, 4, 4)
    several = len(shapes)
    return (
        scratch
        + [pltpu.SemaphoreType.DMA((several, n)) for n in counts]
        + [pltpu.SemaphoreType.DMA((several,))] * 3
    )


def dot_nt(left, right):
    return lax.dot_general(left, right, (((1,), (1,)), ((), ())), preferred_element_type=jnp.float32)


def dot_tn(left, right):
    return lax.dot_general(left, right, (((0,), (0,)), ((), ())), preferred_element_type=jnp.float32)


def thirds(value):
    high = value.astype(jnp.bfloat16)
    rest = value - high.astype(jnp.float32)
    mid = rest.astype(jnp.bfloat16)
    return high, mid, (rest - mid.astype(jnp.float32)).astype(jnp.bfloat16)


def silu_slope(value):
    gate = jax.nn.sigmoid(value)
    return gate * (1 + value * (1 - gate))


PLANE, LINE = 8, 4


class Swap:
    def __init__(self, index, sems, full, away=None, mid=None, reduce=None):
        self.i, self.sems, self.full, self.away, self.mid = index, sems, full, away, mid
        self.second = mid if reduce is None else reduce
        self.me = lax.axis_index(AXIS)
        self.z, self.p = self.me // PLANE, self.me % PLANE
        self.spread = away is None

    def plane(self, peer, slot):
        send, recv = self.sems
        if self.spread:
            src, dst = self.full.at[:, self.p], self.full.at[:, slot]
        else:
            src, dst = self.away.at[:, peer], self.mid.at[:, slot]
        return remote(src, dst, send.at[self.i, peer], recv.at[self.i, slot], self.me + peer - self.p)

    def line(self, peer, slot):
        send, recv = self.sems
        if self.spread:
            src, dst = self.full.at[self.z, self.p], self.full.at[slot, self.p]
        else:
            src, dst = self.second.at[peer], self.full.at[slot]
        return remote(
            src, dst, send.at[self.i, PLANE + peer], recv.at[self.i, PLANE + slot], self.me + PLANE * (peer - self.z)
        )

    def each(self, in_plane, step):
        mine, count = (self.p, PLANE) if in_plane else (self.z, LINE)

        def run(k, carry):
            step(lax.rem(mine + k, count))
            return carry

        lax.fori_loop(1, count, run, 0)

    def hop(self, in_plane):
        make, slot = (self.plane, self.p) if in_plane else (self.line, self.z)
        self.each(in_plane, lambda peer: make(peer, slot).start())

    def come(self, in_plane):
        make = self.plane if in_plane else self.line
        self.each(in_plane, lambda peer: make(peer, peer).wait_recv())

    def start(self):
        if not self.spread:
            for k in range(LINE):
                self.mid[k, self.p] = self.away[k, self.p]
        self.hop(not self.spread)

    def between(self, work=None):
        self.come(not self.spread)
        if work is not None:
            work()
        self.hop(self.spread)
        if not self.spread:
            self.full[self.z] = self.second[self.z]

    def arrive(self):
        self.come(self.spread)

    def sent(self):
        self.each(True, lambda peer: self.plane(peer, self.p).wait_send())
        self.each(False, lambda peer: self.line(peer, self.z).wait_send())


def modulate_steps(devices, ins, outs, bufs, sems):
    msg, emb, wcond, bt1, bt2, bcond = ins
    mods, pre, cond, hid_all, low_all, feat_all, lab_all, got = outs
    hid, low, away, mid, wcls = bufs
    me = lax.axis_index(AXIS)
    z, place = me // PLANE, me % PLANE
    images, cols = 4, emb.shape[0]
    wt1, wt2 = emb.at[:, :FREQ], emb.at[:, FREQ : FREQ + MODEL_WIDTH]
    swaps = [Swap(0, sems, got), Swap(1, sems, hid), Swap(2, sems, low), Swap(3, sems, mods, away, mid)]

    def first():
        got[z, place] = msg[...]
        wcls[...] = jnp.zeros_like(wcls)
        wcls[:, : emb.shape[1] - FREQ - MODEL_WIDTH] = emb[:, FREQ + MODEL_WIDTH :]
        swaps[0].start()

    def second():
        swaps[0].arrive()
        for j in range(devices):
            at = slice(images * j, images * (j + 1))
            block = got[j // PLANE, j % PLANE].astype(jnp.float32)
            feat_all[at, :128] = block[:images]
            feat_all[at, 128:] = block[images : 2 * images]
            digits = block[3 * images : 4 * images]
            lab_all[at, :] = jnp.broadcast_to(32.0 * digits[:, :1] + digits[:, 64:65], (images, 128))
        pre[...] = dot_nt(wt1[...].astype(jnp.bfloat16), feat_all[...].astype(jnp.bfloat16)) + bt1[...]
        hidden = silu(pre[...])
        pad = jnp.zeros((hid.shape[2] - cols, hidden.shape[1]), jnp.float32)
        hid[z, place] = jnp.concatenate([hidden, pad], 0).astype(jnp.bfloat16)
        swaps[1].start()
        classes = lax.broadcasted_iota(jnp.int32, (lab_all.shape[0], wcls.shape[1]), 1).astype(jnp.float32)
        labels = jnp.concatenate([lab_all[...] + PD] * (wcls.shape[1] // 128), 1)
        onehot = (labels == classes).astype(jnp.bfloat16)
        cond[...] = dot_nt(wcls[...].astype(jnp.bfloat16), onehot) + bt2[...]

    def third():
        swaps[1].arrive()
        for j in range(devices):
            hid_all[cols * j : cols * (j + 1), :] = hid[j // PLANE, j % PLANE].astype(jnp.float32)[:cols]
        cond[...] += jnp.dot(
            wt2[...].astype(jnp.bfloat16), hid_all[...].astype(jnp.bfloat16), preferred_element_type=jnp.float32
        )
        value = silu(cond[...])
        pad = jnp.zeros((low.shape[2] - cols, value.shape[1]), jnp.float32)
        low[z, place] = jnp.concatenate([value, pad], 0).astype(jnp.bfloat16)
        swaps[2].start()

    def fourth():
        swaps[2].arrive()
        for j in range(devices):
            low_all[cols * j : cols * (j + 1), :] = low[j // PLANE, j % PLANE].astype(jnp.float32)[:cols]
        rows = dot_nt(low_all[...].T.astype(jnp.bfloat16), wcond[...].astype(jnp.bfloat16)) + bcond[...]
        for j in range(devices):
            away[j // PLANE, j % PLANE] = rows[images * j : images * (j + 1)]
        swaps[3].start()

    def last():
        swaps[3].arrive()
        for swap in swaps:
            swap.sent()

    between = [swap.between for swap in swaps]
    return [first, between[0], second, between[1], third, between[2], fourth, between[3], last]


SETTLE_INS = ("d_mods", "emb", "wcond", "pre", "cond", "hid_all", "low_all", "feat_all", "lab_all", "g_head", "g_hbias", "loss",
              "g_patch", "g_pbias", "bin0", "bin1", "bout0", "bout1", "done_in", "done_out")


def settle_steps(devices, ins, outs, bufs, sems, shards):
    d_mods, pre, lab_all = ins["d_mods"], ins["pre"], ins["lab_all"]
    g_cond, g_t1, g_t2, g_cls, merged = outs
    dm_mid, dm_got, dm_all, rows, small, small_mid, small_sum, small_got = bufs[:8]
    dc_part, dc_mid, dc_sum, dc_got, dh_part, dh_mid, dh_sum, dh_got = bufs[8:]
    me = lax.axis_index(AXIS)
    images, width = d_mods.shape[2:]
    cols = pre.shape[0]
    swaps = [
        Swap(0, sems, dm_got, d_mods, dm_mid),
        Swap(1, sems, small_got, small, small_mid, small_sum),
        Swap(2, sems, dc_got, dc_part, dc_mid, dc_sum),
        Swap(3, sems, dh_got, dh_part, dh_mid, dh_sum),
        Swap(4, sems, merged),
    ]
    keep = {}

    def share(value, part):
        pad = jnp.zeros((32 - cols, value.shape[1]), jnp.float32)
        for j in range(devices):
            part[j // PLANE, j % PLANE] = jnp.concatenate([value[cols * j : cols * (j + 1)], pad], 0).astype(jnp.bfloat16)

    def add_plane(mid, total):
        for k in range(LINE):
            total[k] = jnp.sum(mid[k].astype(jnp.float32), 0)

    def add_small():
        add_plane(small_mid, small_sum)

    def add_dc():
        add_plane(dc_mid, dc_sum)

    def add_dh():
        add_plane(dh_mid, dh_sum)

    def parts_of(value):
        return sum(
            jnp.where(lax.broadcasted_iota(jnp.int32, (1, 128), 1) == k, part.astype(jnp.float32), 0.0)
            for k, part in enumerate(thirds(value))
        )

    def first():
        swaps[0].start()
        dm_all[...] = jnp.zeros_like(dm_all)
        rows[...] = jnp.zeros_like(rows)
        for k in range(MODEL_WIDTH // 128):
            span = slice(128 * k, 128 * (k + 1))
            rows[16 * k : 16 * (k + 1), :] = ins["g_patch"][:, span]
            rows[96 + 32 * k : 96 + 32 * (k + 1), :] = ins["g_head"][:, span]
        at = 288
        for name in ("g_pbias", "bin0", "bin1", "bout0", "bout1"):
            for k in range(ins[name].shape[1] // 128):
                rows[at : at + 1, :] = ins[name][:, 128 * k : 128 * (k + 1)]
                at += 1
        square = ins["g_hbias"].shape
        diagonal = lax.broadcasted_iota(jnp.int32, square, 0) == lax.broadcasted_iota(jnp.int32, square, 1)
        rows[at : at + 1, :] = jnp.sum(jnp.where(diagonal, ins["g_hbias"][...], 0.0), 0, keepdims=True)
        for j in range(devices):
            small[j // PLANE, j % PLANE] = rows[16 * j : 16 * (j + 1), :].astype(jnp.bfloat16)

    def second():
        swaps[0].arrive()
        for j in range(devices):
            dm_all[images * j : images * (j + 1), :width] = dm_got[j // PLANE, j % PLANE]
        turned = dm_all[...].T[:width]
        parts = thirds(turned)
        weight = ins["wcond"][...].astype(jnp.bfloat16)
        share(sum(dot_tn(weight, part) for part in parts), dc_part)
        swaps[2].start()
        swaps[1].start()
        low = ins["low_all"][...].astype(jnp.bfloat16)
        g_cond[...] = sum(dot_nt(part, low) for part in parts)

    def third():
        swaps[2].arrive()
        d_cond = jnp.sum(dc_got[...], 0)[:cols] * silu_slope(ins["cond"][...])
        parts = thirds(d_cond)
        weight = ins["emb"][:, FREQ : FREQ + MODEL_WIDTH].astype(jnp.bfloat16)
        share(sum(dot_tn(weight, part) for part in parts), dh_part)
        swaps[3].start()
        classes = lax.broadcasted_iota(jnp.int32, (lab_all.shape[0], g_cls.shape[1]), 1).astype(jnp.float32)
        labels = jnp.concatenate([lab_all[...] + PD] * (g_cls.shape[1] // 128), 1)
        onehot = (labels == classes).astype(jnp.bfloat16)
        g_cls[...] = sum(jnp.dot(part, onehot, preferred_element_type=jnp.float32) for part in parts)
        hidden = ins["hid_all"][...].astype(jnp.bfloat16)
        g_t2[...] = sum(dot_nt(part, hidden) for part in parts)
        ones = jnp.ones((8, lab_all.shape[0]), jnp.bfloat16)
        keep["t2"] = sum(dot_nt(ones, part) for part in parts)

    def fourth():
        swaps[1].arrive()
        swaps[3].arrive()
        d_pre = jnp.sum(dh_got[...], 0)[:cols] * silu_slope(pre[...])
        parts = thirds(d_pre)
        feats = ins["feat_all"][...].astype(jnp.bfloat16)
        g_t1[...] = sum(jnp.dot(part, feats, preferred_element_type=jnp.float32) for part in parts)
        ones = jnp.ones((8, lab_all.shape[0]), jnp.bfloat16)
        keep["t1"] = sum(dot_nt(ones, part) for part in parts)
        total = jnp.zeros((1, 1), jnp.float32)
        for ref in (g_cond, g_t1, g_t2, g_cls, ins["done_in"], ins["done_out"]):
            total = total + jnp.sum(ref[...] * ref[...])
        keep["squares"] = total

    def message():
        total = keep["squares"]
        for ref in shards:
            total = total + jnp.sum(ref[...] * ref[...])
        bias_cond = jnp.sum(dm_all[...], 0, keepdims=True)
        blank = jnp.zeros((1, 128 - cols), jnp.float32)
        lines = [jnp.concatenate([keep[name][0:1, :], blank], 1) for name in ("t1", "t2")]
        lines.append(parts_of(total))
        lines.append(parts_of(ins["loss"][0:1, :]))
        lines += [bias_cond[:, 128 * k : 128 * (k + 1)] for k in range(3)]
        lines.append(jnp.zeros((9, 128), jnp.float32))
        lines.insert(0, jnp.sum(small_got[...], 0))
        merged[me // PLANE, me % PLANE] = jnp.concatenate(lines, 0).astype(jnp.bfloat16)
        swaps[4].start()
        swaps[4].between()

    def last():
        swaps[4].arrive()
        for swap in swaps:
            swap.sent()

    betweens = [
        swaps[0].between,
        functools.partial(swaps[1].between, add_small),
        functools.partial(swaps[2].between, add_dc),
        functools.partial(swaps[3].between, add_dh),
    ]
    return [first, second, third, fourth, message, last], betweens


def dot_nn(left, right):
    return lax.dot_general(left, right, (((1,), (0,)), ((), ())), preferred_element_type=jnp.float32)


def norm_parts(value):
    centered = value - jnp.mean(value, -1, keepdims=True)
    scale = lax.rsqrt(jnp.mean(centered * centered, -1, keepdims=True) + 1e-06)
    return centered * scale, scale


def norm_back(normed, scale, d_normed):
    inner = jnp.mean(d_normed * normed, -1, keepdims=True)
    return scale * (d_normed - jnp.mean(d_normed, -1, keepdims=True) - normed * inner)


GELU_C = math.sqrt(2.0 / math.pi)


def gelu_value(u):
    return 0.5 * u * (1.0 + jnp.tanh(GELU_C * (u + 0.044715 * u * u * u)))


def gelu_slope(u):
    square = u * u
    t = jnp.tanh(GELU_C * u * (1.0 + 0.044715 * square))
    return 0.5 * (1.0 + t) + 0.5 * u * (1.0 - t * t) * (GELU_C * (1.0 + 3 * 0.044715 * square))


def head_masks(shape):
    low_half = lax.broadcasted_iota(jnp.int32, shape, 1) < HEAD_DIM
    return low_half, jnp.logical_not(low_half)


class Weights:
    def __init__(self, hbm, vmem, sems):
        w_in, w_out = hbm
        self.w_in, self.w_out = vmem
        cut = 3 * MODEL_WIDTH
        spans = [
            (w_in.at[pl.ds(0, cut), :], self.w_in.at[pl.ds(0, cut), :]),
            (w_out.at[:, pl.ds(0, MODEL_WIDTH)], self.w_out.at[:, pl.ds(0, MODEL_WIDTH)]),
            (w_in.at[pl.ds(cut, FF), :], self.w_in.at[pl.ds(cut, FF), :]),
            (w_out.at[:, pl.ds(MODEL_WIDTH, FF)], self.w_out.at[:, pl.ds(MODEL_WIDTH, FF)]),
        ]
        self.copies = [pltpu.make_async_copy(src, dst, sems.at[i]) for i, (src, dst) in enumerate(spans)]

    def start(self, order):
        @pl.when(pl.program_id(0) == 0)
        def _():
            for i in order:
                self.copies[i].start()

    def need(self, i):
        @pl.when(pl.program_id(0) == 0)
        def _():
            self.copies[i].wait()


def forward_image(x_ref, mod, base, weights, b_in, b_out, outs, hook=lambda: None):
    h1, qkv, probs, o, a, x1, h2, u, g, f = outs
    shift1, scale1, gate1, shift2, scale2, gate2 = (mod[0, base + i : base + i + 1, :] for i in range(6))
    width = MODEL_WIDTH
    hook()
    x = x_ref[...]
    h1[...] = (norm_parts(x)[0] * (1 + scale1) + shift1).astype(jnp.bfloat16)
    weights.need(0)
    for j in range(3):
        span = slice(j * width, (j + 1) * width)
        qkv[:, span] = (dot_nt(h1[...], weights.w_in[span, :]) + b_in[:, span]).astype(jnp.bfloat16)
    hook()
    def scores_of(pair):
        q, k = (qkv[:, j * width + 128 * pair : j * width + 128 * (pair + 1)] for j in range(2))
        q = q * jnp.bfloat16(HEAD_DIM**-0.5)
        zero = jnp.zeros_like(q)
        return dot_nt(jnp.concatenate([jnp.where(mask, q, zero) for mask in head_masks(q.shape)], 0), k)

    ahead = scores_of(0)
    for pair in range(HEADS // 2):
        scores, ahead = ahead, scores_of(pair + 1) if pair + 1 < HEADS // 2 else None
        v = qkv[:, 2 * width + 128 * pair : 2 * width + 128 * (pair + 1)]
        expo = jnp.exp(scores - jnp.max(scores, -1, keepdims=True))
        weight = (expo * pl.reciprocal(jnp.sum(expo, -1, keepdims=True))).astype(jnp.bfloat16)
        probs[0, 2 * pair] = weight[:SEQ]
        probs[0, 2 * pair + 1] = weight[SEQ:]
        both = dot_nn(weight, v)
        mixed = jnp.where(head_masks(v.shape)[0], both[:SEQ], both[SEQ:])
        o[:, 128 * pair : 128 * (pair + 1)] = mixed.astype(jnp.bfloat16)
        hook()
    weights.need(1)
    branch = dot_nt(o[...], weights.w_out[:, :width]) + b_out[:, :width]
    a[...] = branch.astype(jnp.bfloat16)
    x1[...] = x + gate1 * branch
    h2[...] = (norm_parts(x1[...])[0] * (1 + scale2) + shift2).astype(jnp.bfloat16)
    hook()
    weights.need(2)
    weights.need(3)
    def up_part(j):
        rows = slice((3 + j) * width, (4 + j) * width)
        return dot_nt(h2[...], weights.w_in[rows, :]) + b_in[:, rows]

    total, ahead = None, up_part(0)
    for j in range(FF // width):
        span = slice(j * width, (j + 1) * width)
        value, ahead = ahead, up_part(j + 1) if j + 1 < FF // width else None
        u[:, span] = value.astype(jnp.bfloat16)
        active = gelu_value(value).astype(jnp.bfloat16)
        g[:, span] = active
        term = dot_nt(active, weights.w_out[:, (1 + j) * width : (2 + j) * width])
        total = term if total is None else total + term
        hook()
    ffn = total + b_out[:, width:]
    f[...] = ffn.astype(jnp.bfloat16)
    return x1[...] + gate2 * ffn


def head_kernel(scale_out, x, mod, w_in, w_out, b_in, b_out, head_t, b_head, targets_t, *refs):
    outs, (dx, d_final, g_head, g_bias, loss), (vm_in, vm_out, sems) = refs[:10], refs[10:15], refs[15:]
    weights = Weights((w_in, w_out), (vm_in, vm_out), sems)
    weights.start((0, 1, 2, 3))
    last = forward_image(x, mod, 6 * (LAYERS - 1), weights, b_in.at[0], b_out.at[0], outs)
    normed, scale = norm_parts(last)
    shift_row, scale_row = mod[0, 6 * LAYERS : 6 * LAYERS + 1, :], mod[0, 6 * LAYERS + 1 :, :]
    shaped = (normed * (1 + scale_row) + shift_row).astype(jnp.bfloat16)
    low = head_t[...].astype(jnp.bfloat16)
    error = dot_nt(low, shaped) + b_head[...] - targets_t[0]
    d_out = (error * scale_out).astype(jnp.bfloat16)

    @pl.when(pl.program_id(0) == 0)
    def _():
        g_head[...] = jnp.zeros_like(g_head)
        g_bias[...] = jnp.zeros_like(g_bias)
        loss[...] = jnp.zeros_like(loss)

    g_head[...] += dot_nn(d_out, shaped)
    g_bias[...] += jnp.sum(d_out.astype(jnp.float32), 1, keepdims=True)
    loss[...] += jnp.sum(error * error)
    d_shaped = dot_tn(d_out, low)
    d_final[0, 0:1, :] = jnp.sum(d_shaped, 0, keepdims=True)
    d_final[0, 1:2, :] = jnp.sum(d_shaped * normed, 0, keepdims=True)
    dx[...] = norm_back(normed, scale, d_shaped * (1 + scale_row))


WEIGHT_SCRATCH = [
    pltpu.VMEM((IW, MODEL_WIDTH), jnp.bfloat16),
    pltpu.VMEM((MODEL_WIDTH, OW), jnp.bfloat16),
    pltpu.SemaphoreType.DMA((4,)),
]


def token_block(width):
    return pl.BlockSpec((SEQ, width), lambda i: (i, 0))


def image_block(*dims):
    return pl.BlockSpec((1,) + dims, lambda i: (i,) + (0,) * len(dims))


def whole_block(*dims):
    return pl.BlockSpec(dims, lambda i: (0,) * len(dims))


def kept_shapes(images):
    tokens, width, low, full = images * SEQ, MODEL_WIDTH, jnp.bfloat16, jnp.float32
    shapes = [((tokens, width), low), ((tokens, 3 * width), low), ((images, HEADS, SEQ, SEQ), low), ((tokens, width), low),
              ((tokens, width), low), ((tokens, width), full), ((tokens, width), low), ((tokens, FF), low),
              ((tokens, FF), low), ((tokens, width), low)]
    specs = [token_block(s[1]) if len(s) == 2 else image_block(*s[1:]) for s, _ in shapes]
    return [jax.ShapeDtypeStruct(s, t) for s, t in shapes], specs


def layer_block(array, layer):
    return pl.BlockSpec((1,) + array.shape[1:], lambda i: (layer, 0, 0))


def forward_specs(ins, layer):
    any_block = pl.BlockSpec(memory_space=pl.ANY)
    return [token_block(MODEL_WIDTH), image_block(*ins[1].shape[1:]), any_block, any_block, layer_block(ins[4], layer),
            layer_block(ins[5], layer)]


def forward_head(ins, scale_out):
    images = ins[1].shape[0]
    shapes, specs = kept_shapes(images)
    extra = [(images * SEQ, MODEL_WIDTH), (images, 2, MODEL_WIDTH), (PO, MODEL_WIDTH), (PO, 128), (8, 128)]
    return pl.pallas_call(
        functools.partial(head_kernel, scale_out),
        grid=(images,),
        out_shape=shapes + [jax.ShapeDtypeStruct(s, jnp.float32) for s in extra],
        in_specs=forward_specs(ins, LAYERS - 1)
        + [whole_block(PO, MODEL_WIDTH), whole_block(PO, 1), image_block(PO, SEQ)],
        out_specs=specs
        + [token_block(MODEL_WIDTH), image_block(2, MODEL_WIDTH), whole_block(PO, MODEL_WIDTH), whole_block(PO, 128),
           whole_block(8, 128)],
        scratch_shapes=WEIGHT_SCRATCH,
        compiler_params=pltpu.CompilerParams(vmem_limit_bytes=56 << 20),
        name="forward_head",
    )(*ins)


def backward_image(refs, mod, base, weights, outs, hook=lambda: None):
    up_ref, x_ref, x1_ref, probs, qkv, a, f, u = refs
    dx, d_qkv, d_u, d_f, d_a, d_mod, g_bin, g_bout = outs
    width = MODEL_WIDTH
    shift1, scale1, gate1, shift2, scale2, gate2 = (mod[0, base + i : base + i + 1, :] for i in range(6))

    @pl.when(pl.program_id(0) == 0)
    def _():
        g_bin[...] = jnp.zeros_like(g_bin)
        g_bout[...] = jnp.zeros_like(g_bout)

    def rows_sum(value):
        return jnp.sum(value.astype(jnp.float32), 0, keepdims=True)

    hook()
    upstream = up_ref[...]
    d_f[...] = (gate2 * upstream).astype(jnp.bfloat16)
    d_mod[0, 5:6, :] = rows_sum(f[...].astype(jnp.float32) * upstream)
    g_bout[:, width:] += rows_sum(d_f[...])
    weights.need(3)
    weights.need(2)
    d_h2 = None
    for j in range(FF // width):
        span = slice(j * width, (j + 1) * width)
        rows = slice((3 + j) * width, (4 + j) * width)
        d_g = dot_nn(d_f[...], weights.w_out[:, (1 + j) * width : (2 + j) * width])
        d_u[:, span] = (d_g * gelu_slope(u[:, span].astype(jnp.float32))).astype(jnp.bfloat16)
        g_bin[:, rows] += rows_sum(d_u[:, span])
        term = dot_nn(d_u[:, span], weights.w_in[rows, :])
        d_h2 = term if d_h2 is None else d_h2 + term
        hook()
    normed, scale = norm_parts(x1_ref[...])
    d_mod[0, 3:4, :] = rows_sum(d_h2)
    d_mod[0, 4:5, :] = rows_sum(d_h2 * normed)
    upstream = upstream + norm_back(normed, scale, d_h2 * (1 + scale2))
    d_mod[0, 2:3, :] = rows_sum(a[...].astype(jnp.float32) * upstream)
    d_a[...] = (gate1 * upstream).astype(jnp.bfloat16)
    g_bout[:, :width] += rows_sum(d_a[...])
    dx[...] = upstream
    weights.need(1)
    d_o = dot_nn(d_a[...], weights.w_out[:, :width]).astype(jnp.bfloat16)
    hook()
    root = HEAD_DIM**-0.5

    def probs_back(pair):
        d_mixed = d_o[:, 128 * pair : 128 * (pair + 1)]
        zero = jnp.zeros_like(d_mixed)
        both = jnp.concatenate([jnp.where(mask, d_mixed, zero) for mask in head_masks(d_mixed.shape)], 0)
        return both, dot_nt(both, qkv[:, 2 * width + 128 * pair : 2 * width + 128 * (pair + 1)])

    for pair in range(HEADS // 2):
        lanes = [slice(j * width + 128 * pair, j * width + 128 * (pair + 1)) for j in range(3)]
        d_masked, d_probs = probs_back(pair)
        q, k = qkv[:, lanes[0]], qkv[:, lanes[1]]
        zero = jnp.zeros_like(q)
        masks = head_masks(q.shape)
        weight = probs[0, 2 * pair : 2 * pair + 2].reshape(2 * SEQ, SEQ)
        full = weight.astype(jnp.float32)
        d_scores = (full * (d_probs - jnp.sum(full * d_probs, -1, keepdims=True))).astype(jnp.bfloat16)
        both = dot_nn(d_scores, k)
        d_q = jnp.where(masks[0], both[:SEQ], both[SEQ:])
        d_k = dot_tn(d_scores, jnp.concatenate([jnp.where(mask, q, zero) for mask in masks], 0))
        d_qkv[:, lanes[0]] = (d_q * root).astype(jnp.bfloat16)
        d_qkv[:, lanes[1]] = (d_k * root).astype(jnp.bfloat16)
        d_qkv[:, lanes[2]] = dot_tn(weight, d_masked).astype(jnp.bfloat16)
        hook()
    weights.need(0)
    d_h1 = None
    for j in range(3):
        span = slice(j * width, (j + 1) * width)
        g_bin[:, span] += rows_sum(d_qkv[:, span])
        term = dot_nn(d_qkv[:, span], weights.w_in[span, :])
        d_h1 = term if d_h1 is None else d_h1 + term
    normed, scale = norm_parts(x_ref[...])
    d_mod[0, 0:1, :] = rows_sum(d_h1)
    d_mod[0, 1:2, :] = rows_sum(d_h1 * normed)
    dx[...] += norm_back(normed, scale, d_h1 * (1 + scale1))
    hook()


def backward_kernel(mod, w_in, w_out, *refs):
    ins, outs, (vm_in, vm_out, sems) = refs[:8], refs[8:16], refs[16:]
    weights = Weights((w_in, w_out), (vm_in, vm_out), sems)
    weights.start((3, 2, 1, 0))
    backward_image(ins, mod, 6 * (LAYERS - 1), weights, outs)


def backward_block(mods, w_in, w_out, refs):
    images, width, low, full = mods.shape[0], MODEL_WIDTH, jnp.bfloat16, jnp.float32
    tokens = images * SEQ
    any_block = pl.BlockSpec(memory_space=pl.ANY)
    shapes = [((tokens, width), full), ((tokens, 3 * width), low), ((tokens, FF), low), ((tokens, width), low),
              ((tokens, width), low), ((images, 6, width), full), ((1, IW), full), ((1, 2 * width), full)]
    return pl.pallas_call(
        backward_kernel,
        grid=(images,),
        out_shape=[jax.ShapeDtypeStruct(s, t) for s, t in shapes],
        in_specs=[image_block(*mods.shape[1:]), any_block, any_block, token_block(width), token_block(width), token_block(width),
                  image_block(HEADS, SEQ, SEQ), token_block(3 * width), token_block(width), token_block(width),
                  token_block(FF)],
        out_specs=[token_block(s[1]) for s, _ in shapes[:5]]
        + [image_block(6, width), whole_block(1, IW), whole_block(1, 2 * width)],
        scratch_shapes=WEIGHT_SCRATCH,
        compiler_params=pltpu.CompilerParams(vmem_limit_bytes=56 << 20),
        name="backward_block",
    )(mods, w_in, w_out, *refs)


def gather_steps(job):
    steps = [job.begin, functools.partial(job.a_step, 0)]
    for dist in (1, 2, 3):
        steps += [functools.partial(job.z_step, dist), functools.partial(job.a_step, dist)]
    for dist in range(4):
        steps += [functools.partial(job.b_step, dist, flip) for flip in range(2)]
    return steps + [job.finish]


class Hooks:
    def __init__(self, steps, slots, points):
        self.points, self.table = points, {}
        for step, slot in zip(steps, slots):
            self.table.setdefault((slot // points, slot % points), []).append(step)
        self.next = 0

    def __call__(self):
        point, self.next = self.next, self.next + 1
        for (turn, where), steps in sorted(self.table.items(), key=lambda item: item[0]):
            if where == point:

                @pl.when(pl.program_id(0) == turn)
                def _():
                    for step in steps:
                        step()


def start_kernel(devices, *refs):
    own, mod_ins, refs = refs[:2], refs[2:8], refs[8:]
    full, mod_outs, refs = refs[:2], refs[2:10], refs[10:]
    part, mod_bufs, mod_sems = refs[:10], refs[10:15], refs[15:]
    place = Place()
    place.greet()
    job = Gather(place, [ref.at[0] for ref in own], part[:2], part[2:4], full, part[4:])
    parts = modulate_steps(devices, mod_ins, mod_outs, mod_bufs, mod_sems)
    moves = gather_steps(job)
    for kind in START_ORDER:
        (parts if kind == "a" else moves).pop(0)()


START_ORDER = "ag" "aa" "gg" "a" "g" "a" "g" "a" "g" "a" "gg" "a" "gggggggg" "a" "g"


def gather_modulate(pair, ins):
    devices = lax.axis_size(AXIS)
    msg, _, wcond, rows = ins[:4]
    cols, images = rows.shape
    outs = [
        (LINE, PLANE, images // devices, wcond.shape[0]), (cols, images), (cols, images), (devices * cols, images),
        (devices * cols, images), (images, FREQ), (images, 128),
    ]
    padded = -(-cols // 16) * 16
    vmem = pl.BlockSpec(memory_space=pltpu.VMEM)
    return pl.pallas_call(
        functools.partial(start_kernel, devices),
        out_shape=[full_shape(a) for a in pair]
        + [jax.ShapeDtypeStruct(shape, jnp.float32) for shape in outs]
        + [jax.ShapeDtypeStruct((LINE, PLANE) + msg.shape, jnp.bfloat16)],
        in_specs=[vmem] * 8,
        out_specs=[pl.BlockSpec(memory_space=pl.ANY)] * 2 + [vmem] * 8,
        scratch_shapes=gather_scratch(piece_shapes([a.shape[1:] for a in pair]))
        + [
            pltpu.VMEM((LINE, PLANE, padded, images), jnp.bfloat16),
            pltpu.VMEM((LINE, PLANE, padded, images), jnp.bfloat16),
            pltpu.VMEM((LINE, PLANE, images // devices, wcond.shape[0]), jnp.float32),
            pltpu.VMEM((LINE, PLANE, images // devices, wcond.shape[0]), jnp.float32),
            pltpu.VMEM((cols, 1024), jnp.float32),
            pltpu.SemaphoreType.DMA((4, LINE + PLANE)),
            pltpu.SemaphoreType.DMA((4, LINE + PLANE)),
        ],
        compiler_params=pltpu.CompilerParams(collective_id=3, has_side_effects=True, vmem_limit_bytes=56 << 20),
        name="gather_modulate",
    )(*pair, *ins)


FORWARD_POINTS = 13


def forward_gather_kernel(slots, lat_t, mod, w_in, w_out, b_in, b_out, w_patch, b_patch, table, own_in, own_out, *refs):
    outs, x_out, full, x, refs = refs[:10], refs[10], refs[11:13], refs[13], refs[14:]
    pos, vm_in, vm_out, sems, part = refs[0], refs[1], refs[2], refs[3], refs[4:]
    place = Place()
    job = Gather(place, (own_in.at[0], own_out.at[0]), part[:2], part[2:4], full, part[4:])
    hooks = Hooks([place.greet] + gather_steps(job), slots, FORWARD_POINTS)
    weights = Weights((w_in, w_out), (vm_in, vm_out), sems)
    weights.start((0, 1, 2, 3))

    @pl.when(pl.program_id(0) == 0)
    def _():
        half = table.shape[1]
        for row in range(GRID):
            at = slice(GRID * row, GRID * (row + 1))
            pos[at, :half] = jnp.broadcast_to(table[row : row + 1, :], (GRID, half))
            pos[at, half:] = table[...]

    latents = lat_t[0].astype(jnp.float32).T.astype(jnp.bfloat16)
    x[...] = dot_nt(latents, w_patch[...]) + b_patch[...] + pos[...]
    x_out[...] = forward_image(x, mod, 0, weights, b_in.at[0], b_out.at[0], outs, hooks)


GATHER_SLOTS = (0, 0, 13, 15, 26, 28, 39, 41, 50) + (34, 43, 48, 51, 51, 51, 51, 51, 51)


def full_shape(array):
    return jax.ShapeDtypeStruct((lax.axis_size(AXIS) * array.shape[1], array.shape[2]), jnp.bfloat16)


def forward_gather(ins, patch, pair, layer):
    images = ins[1].shape[0]
    shapes, specs = kept_shapes(images)
    tokens = jax.ShapeDtypeStruct((images * SEQ, MODEL_WIDTH), jnp.float32)
    any_block = pl.BlockSpec(memory_space=pl.ANY)
    return pl.pallas_call(
        functools.partial(forward_gather_kernel, GATHER_SLOTS),
        grid=(images,),
        out_shape=shapes + [tokens] + [full_shape(a) for a in pair] + [tokens],
        in_specs=[image_block(PD, SEQ)]
        + forward_specs(ins, 0)[1:]
        + [whole_block(*a.shape) for a in patch]
        + [layer_block(a, layer) for a in pair],
        out_specs=specs + [token_block(MODEL_WIDTH)] + [any_block] * 2 + [token_block(MODEL_WIDTH)],
        scratch_shapes=[pltpu.VMEM((SEQ, MODEL_WIDTH), jnp.float32)]
        + WEIGHT_SCRATCH
        + gather_scratch(piece_shapes([a.shape[1:] for a in pair])),
        compiler_params=pltpu.CompilerParams(collective_id=1, has_side_effects=True, vmem_limit_bytes=58 << 20),
        name="forward_gather",
    )(*ins, *patch, *pair)


GRAD_CUTS = [3 * MODEL_WIDTH // MODEL_WIDTH, FF // MODEL_WIDTH]


class Grads:
    def __init__(self, hbm, bufs, keep_in, keep_out, sems):
        bufs = [bufs[0], bufs[4], *bufs[1:]]
        self.bufs, self.keep_in, self.keep_out = bufs, keep_in, keep_out
        self.copies = [pltpu.make_async_copy(src, dst, sems.at[i]) for i, (src, dst) in enumerate(zip(hbm, bufs))]
        self.here = set()

    def start(self):
        for i in (4, 5, 6, 7, 2, 3, 0):
            self.copies[i].start()

    def need(self, *which):
        for i in which:
            if i not in self.here:
                self.copies[i].wait()
                self.here.add(i)

    def rows_in(self, chunk):
        width = MODEL_WIDTH
        pair = 0 if chunk < 3 else 1
        self.need(2 * pair, 2 * pair + 1)
        left, right = self.bufs[2 * pair], self.bufs[2 * pair + 1]
        at = (chunk - 3 * pair) * width
        self.keep_in[chunk * width : (chunk + 1) * width, :] = dot_tn(left[:, at : at + width], right[...]).astype(
            jnp.bfloat16
        )

    def rows_out(self, part):
        width = MODEL_WIDTH
        rows = slice(part * width // 2, (part + 1) * width // 2)
        self.need(4, 5)
        self.keep_out[rows, :width] = dot_tn(self.bufs[4][:, rows], self.bufs[5][...]).astype(jnp.bfloat16)
        self.need(6, 7)
        for j in range(FF // width):
            span = slice(j * width, (j + 1) * width)
            self.keep_out[rows, (1 + j) * width : (2 + j) * width] = dot_tn(
                self.bufs[6][:, rows], self.bufs[7][:, span]
            ).astype(jnp.bfloat16)
        if part == 0:
            self.copies[1].start()


def grads_out_kernel(*refs):
    ins, g_in, total, refs = refs[:8], refs[8], refs[9:10], refs[10:]
    bufs, keep_in, keep_out, load_sems, store_sem, refs = refs[:7], refs[7], refs[8], refs[9], refs[10], refs[11:]
    place = Place()
    work = Grads(ins, bufs, keep_in, keep_out, load_sems)
    work.start()
    place.greet()
    job = Scatter(place, [keep_out], total, refs[:6], refs[6:])
    work.rows_out(1)
    job.open(3)
    job.open(2)
    work.rows_out(0)
    job.open(0)
    job.open(1)
    moves = job.steps()
    for chunk in range(7):
        moves[chunk]()
        work.rows_in(chunk)
    store = pltpu.make_async_copy(keep_in, g_in, store_sem)
    store.start()
    for move in moves[7:]:
        move()
    store.wait()


def grad_bufs(ins):
    return [pltpu.VMEM(a.shape, a.dtype) for i, a in enumerate(ins) if i != 1] + [
        pltpu.VMEM((IW, MODEL_WIDTH), jnp.bfloat16),
        pltpu.VMEM((MODEL_WIDTH, OW), jnp.bfloat16),
        pltpu.SemaphoreType.DMA((8,)),
    ]


def weight_grads_out(ins, shape):
    any_block = pl.BlockSpec(memory_space=pl.ANY)
    return pl.pallas_call(
        grads_out_kernel,
        out_shape=[jax.ShapeDtypeStruct((IW, MODEL_WIDTH), jnp.bfloat16), jax.ShapeDtypeStruct(shape, jnp.float32)],
        in_specs=[any_block] * 8,
        out_specs=[any_block, pl.BlockSpec(memory_space=pltpu.VMEM)],
        scratch_shapes=grad_bufs(ins) + [pltpu.SemaphoreType.DMA] + scatter_scratch(piece_shapes([shape])),
        compiler_params=pltpu.CompilerParams(collective_id=5, has_side_effects=True, vmem_limit_bytes=58 << 20),
        name="weight_grads_out",
    )(*ins)


BACKWARD_POINTS = 13


def backward_scatter_kernel(slots, mod, w_in, w_out, grad, lat_t, *refs):
    ins, outs, (g_patch, g_pbias, total), refs = refs[:8], refs[8:16], refs[16:19], refs[19:]
    vm_in, vm_out, sems, mine, refs = refs[0], refs[1], refs[2], refs[3], refs[4:]
    place = Place()
    job = Scatter(place, [grad], [total], refs[:6], refs[6:], [mine])
    hooks = Hooks([place.greet, job.open_all] + job.steps(), slots, BACKWARD_POINTS)
    weights = Weights((w_in, w_out), (vm_in, vm_out), sems)
    weights.start((3, 2, 1, 0))
    backward_image(ins, mod, 0, weights, outs, hooks)
    d_patch = outs[0][...].astype(jnp.bfloat16)

    @pl.when(pl.program_id(0) == 0)
    def _():
        g_patch[...] = jnp.zeros_like(g_patch)
        g_pbias[...] = jnp.zeros_like(g_pbias)

    g_patch[...] += dot_nn(lat_t[0], d_patch)
    g_pbias[...] += jnp.sum(d_patch.astype(jnp.float32), 0, keepdims=True)


SCATTER_SLOTS = (0, 0, 3, 6, 10, 13, 18, 25, 27, 32, 34, 38, 42, 51, 51, 51, 51)


def backward_scatter(mods, w_in, w_out, refs, grad, lat_t, shape):
    images, width, low, full = mods.shape[0], MODEL_WIDTH, jnp.bfloat16, jnp.float32
    tokens = images * SEQ
    any_block = pl.BlockSpec(memory_space=pl.ANY)
    shapes = [((tokens, width), full), ((tokens, 3 * width), low), ((tokens, FF), low), ((tokens, width), low),
              ((tokens, width), low), ((images, 6, width), full), ((1, IW), full), ((1, 2 * width), full),
              ((PD, width), full), ((1, width), full), (shape, full)]
    pieces = piece_shapes([shape])
    return pl.pallas_call(
        functools.partial(backward_scatter_kernel, SCATTER_SLOTS),
        grid=(images,),
        out_shape=[jax.ShapeDtypeStruct(s, t) for s, t in shapes],
        in_specs=[image_block(*mods.shape[1:]), any_block, any_block, any_block, image_block(PD, SEQ), token_block(width),
                  token_block(width), token_block(width), image_block(HEADS, SEQ, SEQ), token_block(3 * width),
                  token_block(width), token_block(width), token_block(FF)],
        out_specs=[token_block(s[1]) for s, _ in shapes[:5]]
        + [image_block(6, width)] + [whole_block(*s) for s, _ in shapes[6:-1]] + [any_block],
        scratch_shapes=WEIGHT_SCRATCH
        + [pltpu.VMEM((16,) + pieces[0], jnp.bfloat16)] + scatter_scratch(pieces),
        compiler_params=pltpu.CompilerParams(collective_id=6, has_side_effects=True, vmem_limit_bytes=62 << 20),
        name="backward_scatter",
    )(mods, w_in, w_out, grad, lat_t, *refs)


def finish_kernel(devices, *refs):
    count = len(SETTLE_INS)
    ins, set_ins, refs = refs[:8], dict(zip(SETTLE_INS, refs[8 : 8 + count])), refs[8 + count :]
    totals, set_outs, refs = refs[:2], refs[2:7], refs[7:]
    bufs, keep_in, keep_out, load_sems, refs = refs[:7], refs[7], refs[8], refs[9], refs[10:]
    sc_bufs, sc_sems, refs = refs[:12], refs[12:24], refs[24:]
    set_bufs, set_sems = refs[:16], refs[16:]
    work = Grads(ins, bufs, keep_in, keep_out, load_sems)
    work.start()
    place = Place()
    place.greet()
    job = Scatter(place, [keep_in, keep_out], totals, sc_bufs, sc_sems)
    (first, second, third, fourth, message, last), betweens = settle_steps(
        devices, set_ins, set_outs, set_bufs, set_sems, totals
    )
    first()
    work.rows_out(1)
    betweens[0]()
    work.rows_in(5)
    work.rows_in(6)
    second()
    job.open(3)
    work.rows_out(0)
    betweens[2]()
    job.cross_b(3)
    work.rows_in(0)
    work.rows_in(1)
    job.open(0)
    third()
    work.rows_in(3)
    job.cross_b(0)
    work.rows_in(4)
    job.open(2)
    job.cross_a(3)
    work.rows_in(2)
    job.cross_b(2)
    job.open(1)
    job.cross_a(0)
    job.along_z(3)
    job.cross_b(1)
    betweens[1]()
    betweens[3]()
    job.cross_a(2)
    job.along_z(0)
    job.cross_a(1)
    job.along_z(2)
    fourth()
    job.along_z(1)
    job.close()
    job.end()
    message()
    job.finish()
    last()


def finish_grads(ins, shapes, set_ins):
    devices = lax.axis_size(AXIS)
    wcond, d_mods = set_ins["wcond"], set_ins["d_mods"]
    cols, images = set_ins["pre"].shape
    outs = [(wcond.shape[0], devices * cols), (cols, FREQ), (cols, devices * cols), (cols, 1024)]
    vmem = pl.BlockSpec(memory_space=pltpu.VMEM)
    low = jnp.bfloat16
    return pl.pallas_call(
        functools.partial(finish_kernel, devices),
        out_shape=[jax.ShapeDtypeStruct(shape, jnp.float32) for shape in list(shapes) + outs]
        + [jax.ShapeDtypeStruct((LINE, PLANE, 32, 128), low)],
        in_specs=[pl.BlockSpec(memory_space=pl.ANY)] * 8 + [vmem] * len(SETTLE_INS),
        out_specs=[vmem] * 7,
        scratch_shapes=grad_bufs(ins)
        + scatter_scratch(piece_shapes(shapes))
        + [
            pltpu.VMEM(d_mods.shape, jnp.float32),
            pltpu.VMEM(d_mods.shape, jnp.float32),
            pltpu.VMEM((images, 384), jnp.float32),
            pltpu.VMEM((devices * 16, 128), jnp.float32),
            pltpu.VMEM((LINE, PLANE, 16, 128), low),
            pltpu.VMEM((LINE, PLANE, 16, 128), low),
            pltpu.VMEM((LINE, 16, 128), jnp.float32),
            pltpu.VMEM((LINE, 16, 128), jnp.float32),
        ]
        + [
            pltpu.VMEM((LINE, PLANE, 32, images), low),
            pltpu.VMEM((LINE, PLANE, 32, images), low),
            pltpu.VMEM((LINE, 32, images), jnp.float32),
            pltpu.VMEM((LINE, 32, images), jnp.float32),
        ]
        * 2
        + [
            pltpu.SemaphoreType.DMA((5, LINE + PLANE)),
            pltpu.SemaphoreType.DMA((5, LINE + PLANE)),
        ],
        compiler_params=pltpu.CompilerParams(collective_id=4, has_side_effects=True, vmem_limit_bytes=63 << 20),
        name="finish_grads",
    )(*ins, *(set_ins[name] for name in SETTLE_INS))

def code_table():
    quarter = MODEL_WIDTH // 4
    omega = (1.0 / 10000.0 ** (np.arange(quarter, dtype=np.float32) / np.float32(quarter))).astype(np.float32)
    angles = np.arange(GRID, dtype=np.float32)[:, None] * omega
    return np.concatenate([np.sin(angles), np.cos(angles)], 1).astype(np.float32)


def body(
    latents, targets, timesteps, labels, embed_w, embed_m, embed_v, cond_w, cond_m, cond_v, layer_input_weights, in_m,
    in_v, layer_output_weights, out_m, out_v, head_w, head_m, head_v, biases, bias_m, bias_v,
):
    devices = lax.axis_size("fsdp")
    me = lax.axis_index("fsdp")
    images = latents.shape[0]
    embed_t = embed_w.T
    cond_t = cond_w.T
    in_t = layer_input_weights.transpose(0, 2, 1)
    out_t = layer_output_weights.transpose(0, 2, 1)
    cols, cond_cols = embed_t.shape[0], cond_t.shape[0]
    time_one, time_two, patch_bias, cond_bias, block_input_bias, block_output_bias, head_bias = split_biases(biases)
    features = time_features(timesteps)
    own_patch_w = jnp.pad(embed_t[:, FREQ + MODEL_WIDTH : FREQ + MODEL_WIDTH + PD].reshape(3, 128), ((0, 1), (0, 0)))
    digits = jnp.stack([labels // 32, labels % 32], 1).astype(jnp.float32)
    digits = jnp.broadcast_to(digits[:, :, None], (images, 2, 64)).reshape(images, 128)
    note = jnp.concatenate([features[:, :128], features[:, 128:], own_patch_w, digits], 0).astype(jnp.bfloat16)
    images_all = devices * images

    def own_bias(vector, count):
        part = lax.dynamic_slice(vector, (me * count,), (count,))
        return jnp.broadcast_to(part[:, None], (count, images_all))

    own_cond_bias = lax.dynamic_slice(cond_bias, (me * cond_cols,), (cond_cols,))[None]
    first_in, first_out, mods, pre, cond, hid_all, low_all, feat_all, lab_all, notes = gather_modulate(
        [in_t, out_t],
        [note, embed_t, cond_t, own_bias(time_one, cols), own_bias(time_two, cols), own_cond_bias],
    )
    chunks = mods.reshape(devices, images, cond_cols).transpose(1, 0, 2).reshape(images, 6 * LAYERS + 2, MODEL_WIDTH)
    w_patch = notes[:, :, 8:11].reshape(MODEL_WIDTH, PD)
    head_t = head_w.T
    tokens_all = devices * images * SEQ * PO
    lat_t = latents.transpose(0, 2, 1)
    bias_rows = [block_input_bias[:, None], block_output_bias[:, None]]
    *kept0, x_mid, last_in, last_out, x = forward_gather(
        [lat_t, chunks, first_in, first_out, *bias_rows],
        [w_patch, patch_bias[None], jnp.asarray(code_table())],
        [in_t, out_t],
        1,
    )
    *kept1, upstream, d_final, head_grad, head_bias_grad, loss_part = forward_head(
        [x_mid, chunks, last_in, last_out, *bias_rows, head_t, head_bias[:, None],
         targets.transpose(0, 2, 1)],
        2.0 / tokens_all,
    )
    h1, qkv, probs, o, a, x1, h2, u, g, f = kept1
    upstream, d_qkv, d_u, d_f, d_a, mod_grad1, in_bias1, out_bias1 = backward_block(
        chunks, last_in, last_out, [upstream, x_mid, x1, probs, qkv, a, f, u]
    )
    in_shape, out_shape = in_t.shape[1:], out_t.shape[1:]
    grad_in, out_shard1 = weight_grads_out([d_qkv, h1, d_u, h2, d_a, o, d_f, g], out_shape)
    h1, qkv, probs, o, a, x1, h2, u, g, f = kept0
    (upstream, d_qkv, d_u, d_f, d_a, mod_grad0, in_bias0, out_bias0, patch_grad, patch_bias_grad, in_shard1) = backward_scatter(
        chunks, first_in, first_out, [upstream, x, x1, probs, qkv, a, f, u], grad_in, lat_t, in_shape
    )
    mod_grads, in_bias_grads, out_bias_grads = [mod_grad0, mod_grad1], [in_bias0, in_bias1], [out_bias0, out_bias1]
    d_modulation = jnp.concatenate(mod_grads + [d_final], 1)
    d_mods = d_modulation.reshape(images, devices, cond_cols).transpose(1, 0, 2)
    d_mods = d_mods.reshape(LINE, PLANE, images, cond_cols)
    in_shard0, out_shard0, g_cond, g_t1, g_t2, g_cls, merged = finish_grads(
        [d_qkv, h1, d_u, h2, d_a, o, d_f, g],
        [in_shape, out_shape],
        {
            "d_mods": d_mods, "emb": embed_t, "wcond": cond_t, "pre": pre, "cond": cond, "hid_all": hid_all, "low_all": low_all,
            "feat_all": feat_all, "lab_all": lab_all, "g_head": head_grad, "g_hbias": head_bias_grad, "loss": loss_part,
            "g_patch": patch_grad, "g_pbias": patch_bias_grad, "bin0": in_bias_grads[0], "bin1": in_bias_grads[1],
            "bout0": out_bias_grads[0], "bout1": out_bias_grads[1], "done_in": in_shard1, "done_out": out_shard1,
        },
    )
    merged = merged.astype(jnp.float32).reshape(devices, 32, 128)
    wide = MODEL_WIDTH // 128
    blocks = merged[:, :16]
    patch_total = blocks[:wide].transpose(1, 0, 2).reshape(PD, MODEL_WIDTH)
    head_total = blocks[wide : 3 * wide].reshape(wide, PO, 128).transpose(1, 0, 2).reshape(PO, MODEL_WIDTH)
    flat = blocks[3 * wide :].reshape(-1)
    rest = LAYERS * (IW + 2 * MODEL_WIDTH) + PO
    loss_total = jnp.sum(merged[:, 19, :3])
    bias_total = jnp.concatenate(
        [merged[:, 16, :cols].reshape(-1), merged[:, 17, :cols].reshape(-1), flat[:MODEL_WIDTH],
         merged[:, 20:23].reshape(devices, 384)[:, :cond_cols].reshape(-1), flat[MODEL_WIDTH : MODEL_WIDTH + rest]]
    )
    grad_norm = jnp.sqrt(
        jnp.sum(merged[:, 18, :3])
        + jnp.sum(head_total * head_total)
        + jnp.sum(patch_total * patch_total)
        + jnp.sum(bias_total * bias_total)
    )
    factor = jnp.minimum(1.0, clip_limit / grad_norm)
    own_patch = lax.dynamic_slice(patch_total, (0, me * cols), (PD, cols)).T
    embed_grad = jnp.concatenate([g_t1, g_t2, own_patch, g_cls[:, PD : PD + NCLS]], 1)
    embed_up = [a.T for a in adam_step(embed_t, embed_m.T, embed_v.T, embed_grad * factor)]
    cond_up = [a.T for a in adam_step(cond_t, cond_m.T, cond_v.T, g_cond * factor)]
    turn = (0, 2, 1)
    in_up = [
        a.transpose(turn)
        for a in adam_step(in_t, in_m.transpose(turn), in_v.transpose(turn), jnp.stack([in_shard0, in_shard1]) * factor)
    ]
    out_up = [
        a.transpose(turn)
        for a in adam_step(out_t, out_m.transpose(turn), out_v.transpose(turn), jnp.stack([out_shard0, out_shard1]) * factor)
    ]
    head_up = [a.T for a in adam_step(head_t, head_m.T, head_v.T, head_total * factor)]
    bias_up = adam_step(biases, bias_m, bias_v, bias_total * factor)
    return (loss_total, grad_norm, *embed_up, *cond_up, *in_up, *out_up, *head_up, *bias_up)


def fits(mesh):
    return mesh.shape["fsdp"] == 32


def solution(mesh):
    in_specs = (
        P("fsdp", None, None),
        P("fsdp", None, None),
        P("fsdp"),
        P("fsdp"),
        P(None, "fsdp"),
        P(None, "fsdp"),
        P(None, "fsdp"),
        P(None, "fsdp"),
        P(None, "fsdp"),
        P(None, "fsdp"),
        P(None, None, "fsdp"),
        P(None, None, "fsdp"),
        P(None, None, "fsdp"),
        P(None, None, "fsdp"),
        P(None, None, "fsdp"),
        P(None, None, "fsdp"),
        P(),
        P(),
        P(),
        P(),
        P(),
        P(),
    )
    out_specs = (
        P(),
        P(),
        P(None, "fsdp"),
        P(None, "fsdp"),
        P(None, "fsdp"),
        P(None, "fsdp"),
        P(None, "fsdp"),
        P(None, "fsdp"),
        P(None, None, "fsdp"),
        P(None, None, "fsdp"),
        P(None, None, "fsdp"),
        P(None, None, "fsdp"),
        P(None, None, "fsdp"),
        P(None, None, "fsdp"),
        P(),
        P(),
        P(),
        P(),
        P(),
        P(),
    )
    chosen = body if fits(mesh) else generic_body
    return jax.shard_map(chosen, mesh=mesh, in_specs=in_specs, out_specs=out_specs, check_vma=False)
```

```python
import functools
import math

import jax
import jax.numpy as jnp
import numpy as np
from jax import lax
from jax.experimental import pallas as pl
from jax.experimental.pallas import tpu as pltpu
from jax.sharding import PartitionSpec as P

MODEL_WIDTH = 768
HEADS = 12
HEAD_DIM = 64
NCLS = 1001
FREQ = 256
PD = 16
PO = 32
GRID = 16
LAYERS = 2
STEP = 10
SEQ = 256
IW = 5376
OW = 3840
FF = 3072
CW = 10752


learn_rate = 0.03
beta_one = 0.9
beta_two = 0.999
adam_eps = 1e-08
decay = 0.01
clip_limit = 0.01
highest = lax.Precision.HIGHEST


def product(left, right):
    return jnp.dot(left, right, preferred_element_type=jnp.float32)


def exact_dot(left, right):
    return jnp.dot(left, right, precision=highest)


def apply_rows(left, right):
    return jnp.einsum("bsd,de->bse", left, right, preferred_element_type=jnp.float32)


def outer_sum(left, right):
    return jnp.einsum("bsd,bse->de", left, right, preferred_element_type=jnp.float32)


def apply_back(left, right):
    return jnp.einsum("bse,de->bsd", left, right, preferred_element_type=jnp.float32)


def column_sum(value):
    return jnp.sum(value.astype(jnp.float32), (0, 1))


def silu(value):
    return value * jax.nn.sigmoid(value)


def gelu(value):
    return jax.nn.gelu(value, approximate=True)


def layer_norm(value):
    centered = value - jnp.mean(value, -1, keepdims=True)
    return centered * lax.rsqrt(jnp.mean(centered * centered, -1, keepdims=True) + 1e-06)


def local_back(func, value, cotangent):
    return jax.vjp(func, value)[1](cotangent)[0]


def position_table():
    quarter = MODEL_WIDTH // 4
    omega = 1.0 / 10000.0 ** (jnp.arange(quarter, dtype=jnp.float32) / quarter)
    places = jnp.arange(GRID * GRID)
    rows_pos = (places // GRID).astype(jnp.float32)[:, None] * omega
    cols_pos = (places % GRID).astype(jnp.float32)[:, None] * omega
    return jnp.concatenate(
        [jnp.sin(rows_pos), jnp.cos(rows_pos), jnp.sin(cols_pos), jnp.cos(cols_pos)], 1
    )


def time_features(timesteps):
    half_freq = FREQ // 2
    rates = jnp.exp(-math.log(10000.0) * jnp.arange(half_freq, dtype=jnp.float32) / half_freq)
    angles = timesteps.astype(jnp.float32)[:, None] * rates
    return jnp.concatenate([jnp.cos(angles), jnp.sin(angles)], 1)


def split_biases(vector):
    lengths = [MODEL_WIDTH, MODEL_WIDTH, MODEL_WIDTH, CW, LAYERS * IW, LAYERS * 2 * MODEL_WIDTH, PO]
    pieces = []
    offset = 0
    for length in lengths:
        pieces.append(vector[offset : offset + length])
        offset += length
    pieces[4] = pieces[4].reshape(LAYERS, IW)
    pieces[5] = pieces[5].reshape(LAYERS, 2 * MODEL_WIDTH)
    return pieces


def split_heads(triple, which):
    n_images, seq_len = (triple.shape[0], triple.shape[1])
    return triple[..., which * MODEL_WIDTH : (which + 1) * MODEL_WIDTH].reshape(
        n_images, seq_len, HEADS, HEAD_DIM
    )


def attend(triple):
    queries, key_part, values = [split_heads(triple, j) for j in range(3)]
    scores = jnp.einsum(
        "bqhd,bkhd->bhqk", queries, key_part, preferred_element_type=jnp.float32
    ) * HEAD_DIM ** (-0.5)
    row_max = jnp.max(scores, -1, keepdims=True)
    expo = jnp.exp(scores - row_max)
    row_sum = jnp.sum(expo, -1, keepdims=True)
    attn_weights = (expo / row_sum).astype(jnp.bfloat16)
    mixed_heads = jnp.einsum(
        "bhqk,bkhd->bqhd", attn_weights, values, preferred_element_type=jnp.float32
    ).astype(jnp.bfloat16)
    return (
        mixed_heads.reshape(triple.shape[0], triple.shape[1], MODEL_WIDTH),
        row_max + jnp.log(row_sum),
    )


def attend_back(triple, log_norm, d_mixed):
    queries, key_part, values = [split_heads(triple, j) for j in range(3)]
    scale = HEAD_DIM ** (-0.5)
    scores = (
        jnp.einsum("bqhd,bkhd->bhqk", queries, key_part, preferred_element_type=jnp.float32) * scale
    )
    probs_full = jnp.exp(scores - log_norm)
    attn_weights = probs_full.astype(jnp.bfloat16)
    d_heads = d_mixed.reshape(queries.shape)
    d_probs = jnp.einsum("bqhd,bkhd->bhqk", d_heads, values, preferred_element_type=jnp.float32)
    d_values = jnp.einsum(
        "bhqk,bqhd->bkhd", attn_weights, d_heads, preferred_element_type=jnp.float32
    )
    d_scores = (probs_full * (d_probs - jnp.sum(probs_full * d_probs, -1, keepdims=True))).astype(
        jnp.bfloat16
    )
    d_queries = (
        jnp.einsum("bhqk,bkhd->bqhd", d_scores, key_part, preferred_element_type=jnp.float32)
        * scale
    )
    d_keys = (
        jnp.einsum("bhqk,bqhd->bkhd", d_scores, queries, preferred_element_type=jnp.float32) * scale
    )
    shape_flat = (triple.shape[0], triple.shape[1], MODEL_WIDTH)
    return jnp.concatenate(
        [d_queries.reshape(shape_flat), d_keys.reshape(shape_flat), d_values.reshape(shape_flat)],
        -1,
    ).astype(jnp.bfloat16)


def block_forward(residual_state, adaptive_modulation, weights_in, weights_out, bias_in, bias_out):
    pieces = [
        adaptive_modulation[:, None, i * MODEL_WIDTH : (i + 1) * MODEL_WIDTH] for i in range(6)
    ]
    shaped_one = (layer_norm(residual_state) * (1 + pieces[1]) + pieces[0]).astype(jnp.bfloat16)
    triple = (
        apply_rows(shaped_one, weights_in[:, : 3 * MODEL_WIDTH]) + bias_in[: 3 * MODEL_WIDTH]
    ).astype(jnp.bfloat16)
    mixed_heads, log_norm = attend(triple)
    branch = apply_rows(mixed_heads, weights_out[:MODEL_WIDTH]) + bias_out[:MODEL_WIDTH]
    middle = residual_state + pieces[2] * branch
    shaped_two = (layer_norm(middle) * (1 + pieces[4]) + pieces[3]).astype(jnp.bfloat16)
    pre_ffn = apply_rows(shaped_two, weights_in[:, 3 * MODEL_WIDTH :]) + bias_in[3 * MODEL_WIDTH :]
    active = gelu(pre_ffn).astype(jnp.bfloat16)
    ffn_out = apply_rows(active, weights_out[MODEL_WIDTH:]) + bias_out[MODEL_WIDTH:]
    kept = (
        residual_state,
        shaped_one,
        triple,
        log_norm,
        mixed_heads,
        branch,
        middle,
        shaped_two,
        pre_ffn,
        active,
        ffn_out,
    )
    return (middle + pieces[5] * ffn_out, kept)


def block_backward(upstream, adaptive_modulation, weights_in, weights_out, kept):
    (
        residual_state,
        shaped_one,
        triple,
        log_norm,
        mixed_heads,
        branch,
        middle,
        shaped_two,
        pre_ffn,
        active,
        ffn_out,
    ) = kept
    pieces = [
        adaptive_modulation[:, None, i * MODEL_WIDTH : (i + 1) * MODEL_WIDTH] for i in range(6)
    ]
    d_ffn = (pieces[5] * upstream).astype(jnp.bfloat16)
    gate_two = jnp.sum(ffn_out * upstream, 1)
    grad_down = outer_sum(active, d_ffn)
    d_active = apply_back(d_ffn, weights_out[MODEL_WIDTH:])
    d_pre = local_back(gelu, pre_ffn, d_active).astype(jnp.bfloat16)
    grad_up = outer_sum(shaped_two, d_pre)
    d_shaped = apply_back(d_pre, weights_in[:, 3 * MODEL_WIDTH :])
    shift_two = jnp.sum(d_shaped, 1)
    scale_two = jnp.sum(d_shaped * layer_norm(middle), 1)
    upstream = upstream + local_back(layer_norm, middle, d_shaped * (1 + pieces[4]))
    gate_one = jnp.sum(branch * upstream, 1)
    d_branch = (pieces[2] * upstream).astype(jnp.bfloat16)
    grad_proj = outer_sum(mixed_heads, d_branch)
    d_mixed = apply_back(d_branch, weights_out[:MODEL_WIDTH]).astype(jnp.bfloat16)
    d_triple = attend_back(triple, log_norm, d_mixed)
    grad_qkv = outer_sum(shaped_one, d_triple)
    d_shaped = apply_back(d_triple, weights_in[:, : 3 * MODEL_WIDTH])
    shift_one = jnp.sum(d_shaped, 1)
    scale_one = jnp.sum(d_shaped * layer_norm(residual_state), 1)
    upstream = upstream + local_back(layer_norm, residual_state, d_shaped * (1 + pieces[1]))
    mod_grad = jnp.concatenate([shift_one, scale_one, gate_one, shift_two, scale_two, gate_two], 1)
    bias_in_grad = jnp.concatenate([column_sum(d_triple), column_sum(d_pre)])
    bias_out_grad = jnp.concatenate([column_sum(d_branch), column_sum(d_ffn)])
    grad_in = jnp.concatenate([grad_qkv, grad_up], 1)
    grad_out = jnp.concatenate([grad_proj, grad_down], 0)
    return (upstream, mod_grad, grad_in, grad_out, bias_in_grad, bias_out_grad)


def fetch_layer(layer_input_weights, layer_output_weights, layer_count):
    return (
        lax.all_gather(
            layer_input_weights[layer_count].astype(jnp.bfloat16), "fsdp", axis=1, tiled=True
        ),
        lax.all_gather(
            layer_output_weights[layer_count].astype(jnp.bfloat16), "fsdp", axis=1, tiled=True
        ),
    )


def adam_step(weight, first, second, gradient):
    first = beta_one * first + (1 - beta_one) * gradient
    second = beta_two * second + (1 - beta_two) * gradient * gradient
    ahead = first / (1 - beta_one**STEP)
    scaled = second / (1 - beta_two**STEP)
    return (
        weight - learn_rate * (ahead / (jnp.sqrt(scaled) + adam_eps) + decay * weight),
        first,
        second,
    )


def generic_body(
    latents,
    targets,
    timesteps,
    labels,
    embed_w,
    embed_m,
    embed_v,
    cond_w,
    cond_m,
    cond_v,
    layer_input_weights,
    in_m,
    in_v,
    layer_output_weights,
    out_m,
    out_v,
    head_w,
    head_m,
    head_v,
    biases,
    bias_m,
    bias_v,
):
    devices = lax.axis_size("fsdp")
    embed_full, cond_full = (
        lax.all_gather(embed_w.astype(jnp.bfloat16), "fsdp", axis=1, tiled=True),
        lax.all_gather(cond_w.astype(jnp.bfloat16), "fsdp", axis=1, tiled=True),
    )
    time_one, time_two, patch_bias, cond_bias, block_input_bias, block_output_bias, head_bias = (
        split_biases(biases)
    )
    head_low = head_w.astype(jnp.bfloat16)
    features = time_features(timesteps).astype(jnp.bfloat16)
    pre_time = product(features, embed_full[:FREQ]) + time_one
    hidden_t = silu(pre_time).astype(jnp.bfloat16)
    time_emb = product(hidden_t, embed_full[FREQ : FREQ + MODEL_WIDTH]) + time_two
    onehot = (labels[:, None] == jnp.arange(NCLS)[None, :]).astype(jnp.bfloat16)
    condition = time_emb + product(onehot, embed_full[FREQ + MODEL_WIDTH + PD :])
    cond_low = silu(condition).astype(jnp.bfloat16)
    adaptive_modulation = product(cond_low, cond_full) + cond_bias
    residual_state = (
        apply_rows(latents, embed_full[FREQ + MODEL_WIDTH : FREQ + MODEL_WIDTH + PD])
        + patch_bias
        + position_table()
    )
    kept_all = []
    for layer_count in range(LAYERS):
        weights_in, weights_out = fetch_layer(
            layer_input_weights, layer_output_weights, layer_count
        )
        residual_state, kept = block_forward(
            residual_state,
            adaptive_modulation[
                :, 6 * MODEL_WIDTH * layer_count : 6 * MODEL_WIDTH * (layer_count + 1)
            ],
            weights_in,
            weights_out,
            block_input_bias[layer_count],
            block_output_bias[layer_count],
        )
        kept_all.append(kept)
    final_mod = adaptive_modulation[:, 6 * MODEL_WIDTH * LAYERS :]
    norm_final = layer_norm(residual_state)
    shaped = (
        norm_final * (1 + final_mod[:, None, MODEL_WIDTH:]) + final_mod[:, None, :MODEL_WIDTH]
    ).astype(jnp.bfloat16)
    output = apply_rows(shaped, head_low) + head_bias
    error_vals = output - targets
    loss_part = jnp.sum(error_vals * error_vals)
    tokens_all = devices * error_vals.shape[0] * SEQ * PO
    d_output = (error_vals * (2.0 / tokens_all)).astype(jnp.bfloat16)
    head_grad = outer_sum(shaped, d_output)
    head_bias_grad = column_sum(d_output)
    d_shaped = apply_back(d_output, head_low)
    d_final = jnp.concatenate([jnp.sum(d_shaped, 1), jnp.sum(d_shaped * norm_final, 1)], 1)
    upstream = local_back(
        layer_norm, residual_state, d_shaped * (1 + final_mod[:, None, MODEL_WIDTH:])
    )
    mod_grads = [None] * LAYERS
    in_shards = [None] * LAYERS
    out_shards = [None] * LAYERS
    in_bias_grads = [None] * LAYERS
    out_bias_grads = [None] * LAYERS
    for layer_count in reversed(range(LAYERS)):
        weights_in, weights_out = (
            lax.all_gather(
                layer_input_weights[layer_count].astype(jnp.bfloat16), "fsdp", axis=1, tiled=True
            ),
            lax.all_gather(
                layer_output_weights[layer_count].astype(jnp.bfloat16), "fsdp", axis=1, tiled=True
            ),
        )
        upstream, mod_grad, grad_in, grad_out, bias_in_grad, bias_out_grad = block_backward(
            upstream,
            adaptive_modulation[
                :, 6 * MODEL_WIDTH * layer_count : 6 * MODEL_WIDTH * (layer_count + 1)
            ],
            weights_in,
            weights_out,
            kept_all[layer_count],
        )
        in_shards[layer_count], out_shards[layer_count] = (
            lax.psum_scatter(grad_in, "fsdp", scatter_dimension=1, tiled=True),
            lax.psum_scatter(grad_out, "fsdp", scatter_dimension=1, tiled=True),
        )
        mod_grads[layer_count] = mod_grad
        in_bias_grads[layer_count] = bias_in_grad
        out_bias_grads[layer_count] = bias_out_grad
    d_patch = upstream.astype(jnp.bfloat16)
    patch_grad = outer_sum(latents, d_patch)
    patch_bias_grad = column_sum(d_patch)
    d_modulation = jnp.concatenate(mod_grads + [d_final], 1)
    d_cond = exact_dot(d_modulation, cond_full.astype(jnp.float32).T)
    d_condition = local_back(silu, condition, d_cond)
    d_hidden = exact_dot(d_condition, embed_full[FREQ : FREQ + MODEL_WIDTH].astype(jnp.float32).T)
    d_pre = local_back(silu, pre_time, d_hidden)
    cond_grad = exact_dot(cond_low.astype(jnp.float32).T, d_modulation)
    class_grad = exact_dot(onehot.astype(jnp.float32).T, d_condition)
    time_two_grad = exact_dot(hidden_t.astype(jnp.float32).T, d_condition)
    time_one_grad = exact_dot(features.astype(jnp.float32).T, d_pre)
    embed_grad = jnp.concatenate([time_one_grad, time_two_grad, patch_grad, class_grad], 0)
    embed_shard, cond_shard = (
        lax.psum_scatter(embed_grad, "fsdp", scatter_dimension=1, tiled=True),
        lax.psum_scatter(cond_grad, "fsdp", scatter_dimension=1, tiled=True),
    )
    bias_grad = jnp.concatenate(
        [jnp.sum(d_pre, 0), jnp.sum(d_condition, 0), patch_bias_grad, jnp.sum(d_modulation, 0)]
        + in_bias_grads
        + out_bias_grads
        + [head_bias_grad]
    )
    head_total, bias_total, loss_total = lax.psum((head_grad, bias_grad, loss_part), "fsdp")
    in_stack = jnp.stack(in_shards, 0)
    out_stack = jnp.stack(out_shards, 0)
    shard_squares = (
        jnp.sum(embed_shard * embed_shard)
        + jnp.sum(cond_shard * cond_shard)
        + jnp.sum(in_stack * in_stack)
        + jnp.sum(out_stack * out_stack)
    )
    square_total = lax.psum(shard_squares, "fsdp")
    grad_norm = jnp.sqrt(
        square_total + jnp.sum(head_total * head_total) + jnp.sum(bias_total * bias_total)
    )
    factor = jnp.minimum(1.0, clip_limit / grad_norm)
    embed_up = adam_step(embed_w, embed_m, embed_v, embed_shard * factor)
    cond_up = adam_step(cond_w, cond_m, cond_v, cond_shard * factor)
    in_up = adam_step(layer_input_weights, in_m, in_v, in_stack * factor)
    out_up = adam_step(layer_output_weights, out_m, out_v, out_stack * factor)
    head_up = adam_step(head_w, head_m, head_v, head_total * factor)
    bias_up = adam_step(biases, bias_m, bias_v, bias_total * factor)
    return (
        loss_total,
        grad_norm,
        embed_up[0],
        embed_up[1],
        embed_up[2],
        cond_up[0],
        cond_up[1],
        cond_up[2],
        in_up[0],
        in_up[1],
        in_up[2],
        out_up[0],
        out_up[1],
        out_up[2],
        head_up[0],
        head_up[1],
        head_up[2],
        bias_up[0],
        bias_up[1],
        bias_up[2],
    )


MESH_ID = pl.DeviceIdType.MESH
AXIS = "fsdp"


class Place:
    def __init__(self):
        me = lax.axis_index(AXIS)
        self.me = me
        self.core = core = me % 2
        x = (me // 2) % 2
        y = (me // 4) % 2
        self.z = me // 8
        self.chip = me // 2
        step_x = 1 - 2 * x
        step_y = 2 - 4 * y
        self.step_a = step_x + core * (step_y - step_x)
        self.step_b = step_y + core * (step_x - step_y)
        self.dev_a = me + 2 * self.step_a
        self.dev_b = me + 2 * self.step_b
        self.sibling = me + 1 - 2 * core

    def other(self, dz, flip_a=0, flip_b=0):
        return self.chip + 4 * dz + flip_a * self.step_a + flip_b * self.step_b

    def valid(self, dz):
        return jnp.logical_and(self.z + dz >= 0, self.z + dz < 4)

    def greet(self):
        barrier = pltpu.get_barrier_semaphore()

        def hello(device):
            pl.semaphore_signal(barrier, inc=1, device_id=(device,), device_id_type=MESH_ID)

        for k in range(1, 8):
            hello(8 * self.z + lax.rem(self.me + k, 8))
        for k in range(1, 4):
            hello(lax.rem(self.me + 8 * k, 32))
        pl.semaphore_wait(barrier, 10)


def remote(src, dst, send_sem, recv_sem, device):
    return pltpu.make_async_remote_copy(
        src_ref=src, dst_ref=dst, send_sem=send_sem, recv_sem=recv_sem, device_id=(device,), device_id_type=MESH_ID
    )


class Gather:
    def __init__(self, place, own, stage, piece, full, sems):
        self.p, self.own, self.stage, self.piece, self.full = place, own, stage, piece, full
        self.xch_send, self.xch_recv, self.local, self.send, self.recv, self.sib_recv = sems
        self.sent = []

    def slot(self, a, chip):
        rows, half = self.piece[a].shape
        return self.full[a].at[
            pl.ds(pl.multiple_of(chip * rows, rows), rows), pl.ds(pl.multiple_of(self.p.core * half, half), half)
        ]

    def push(self, a, k, src, chip, device, sem, cond=None):
        def act(what):
            copy = remote(src(), self.slot(a, chip()), self.send.at[a, k], sem.at[a, chip()], device())
            getattr(copy, what)()

        def guarded(what):
            if cond is None:
                act(what)
            else:
                pl.when(cond())(functools.partial(act, what))

        guarded("start")
        self.sent.append(functools.partial(guarded, "wait_send"))

    def store_own(self, a):
        return pltpu.make_async_copy(self.piece[a], self.slot(a, self.p.chip), self.local.at[a])

    def begin(self):
        core = self.p.core
        copies = []
        for a in range(2):
            rows, half = self.own[a].shape[0], self.piece[a].shape[1]
            dst = self.stage[a].at[pl.ds(pl.multiple_of(core * rows, 8), rows), :]
            away = remote(
                self.own[a].at[:, pl.ds(pl.multiple_of((1 - core) * half, half), half)],
                dst,
                self.xch_send.at[a],
                self.xch_recv.at[a],
                self.p.sibling,
            )
            away.start()
            keep = pltpu.make_async_copy(
                self.own[a].at[:, pl.ds(pl.multiple_of(core * half, half), half)], dst, self.local.at[a]
            )
            keep.start()
            copies.append((away, keep))
        for a in range(2):
            copies[a][0].wait()
            copies[a][1].wait()
            self.piece[a][...] = self.stage[a][...].astype(jnp.bfloat16)
            self.store_own(a).start()
            piece, here = (lambda a=a: self.piece[a]), (lambda: self.p.chip)
            for sign in (-1, 1):
                self.push(
                    a, 0 if sign < 0 else 3, piece, here, lambda sign=sign: self.p.me + 8 * sign, self.recv,
                    lambda sign=sign: self.p.valid(sign),
                )
            self.push(a, 6, piece, here, lambda: self.p.dev_a, self.recv)
            self.push(a, 10, piece, here, lambda: self.p.dev_b, self.recv)
            self.push(a, 18, piece, here, lambda: self.p.sibling, self.sib_recv)

    def arrive(self, a, chip):
        slot = self.slot(a, chip)
        pltpu.make_async_copy(slot, slot, self.recv.at[a, chip]).wait()

    def pass_on(self, dz, flip_a, flip_b, targets):
        def here():
            return self.p.valid(dz)

        def chip():
            return self.p.other(dz, flip_a, flip_b)

        for a in range(2):
            pl.when(here())(lambda a=a: self.arrive(a, chip()))
            for k, device, sem, extra in targets:
                self.push(
                    a, k, lambda a=a: self.slot(a, chip()), chip, device, sem,
                    here if extra is None else lambda extra=extra: jnp.logical_and(here(), self.p.valid(extra)),
                )

    def z_step(self, dist):
        for sign in (-1, 1):
            rel = (sign * dist) % 4
            targets = [
                (6 + rel, lambda: self.p.dev_a, self.recv, None),
                (10 + rel, lambda: self.p.dev_b, self.recv, None),
                (18 + rel, lambda: self.p.sibling, self.sib_recv, None),
            ]
            if dist < 3:
                onward = ((0 if sign > 0 else 3) + dist, lambda sign=sign: self.p.me - 8 * sign, self.recv, -sign)
                targets.insert(0, onward)
            self.pass_on(sign * dist, 0, 0, targets)

    def a_step(self, dist):
        for sign in (-1, 1) if dist else (1,):
            rel = (sign * dist) % 4
            self.pass_on(sign * dist, 1, 0, [
                (14 + rel, lambda: self.p.dev_b, self.recv, None), (22 + rel, lambda: self.p.sibling, self.sib_recv, None)
            ])

    def b_step(self, dist, flip_a):
        for sign in (-1, 1) if dist else (1,):
            rel = (sign * dist) % 4
            self.pass_on(
                sign * dist, flip_a, 1, [(26 + 4 * flip_a + rel, lambda: self.p.sibling, self.sib_recv, None)]
            )

    def finish(self):
        for a in range(2):
            rows, half = self.piece[a].shape

            def take(chip, carry):
                slot = self.full[a].at[
                    pl.ds(pl.multiple_of(chip * rows, rows), rows),
                    pl.ds(pl.multiple_of((1 - self.p.core) * half, half), half),
                ]
                pltpu.make_async_copy(slot, slot, self.sib_recv.at[a, chip]).wait()
                return carry

            lax.fori_loop(0, 16, take, 0)
            self.store_own(a).wait()
        for wait in self.sent:
            wait()


GATHER_SEMS = [
    pltpu.SemaphoreType.DMA((2,)),
    pltpu.SemaphoreType.DMA((2,)),
    pltpu.SemaphoreType.DMA((2,)),
    pltpu.SemaphoreType.DMA((2, 34)),
    pltpu.SemaphoreType.DMA((2, 16)),
    pltpu.SemaphoreType.DMA((2, 16)),
]


def gather_scratch(shapes):
    return (
        [pltpu.VMEM(shape, jnp.float32) for shape in shapes]
        + [pltpu.VMEM(shape, jnp.bfloat16) for shape in shapes]
        + GATHER_SEMS
    )


def piece_shapes(shapes):
    return [(2 * rows, width // 2) for rows, width in shapes]


ORDER = (3, 0, 2, 1)


class Scatter:
    def __init__(self, place, grads, totals, bufs, sems, mine=None):
        self.p, self.grad, self.total, self.mine = place, grads, totals, mine
        count = len(grads)
        self.arrays = range(count)
        self.sib, self.from_b, self.from_a, self.line, self.part, self.last = (
            bufs[count * i : count * i + count] for i in range(6)
        )
        (self.load_sem, self.sib_send, self.sib_recv, self.b_send, self.b_recv, self.a_send, self.a_recv, self.z_send,
         self.z_recv, self.end_send, self.end_recv, self.end_local) = sems

    def rows_of(self, a, chip, core):
        rows, half = self.part[a].shape
        return self.grad[a].at[
            pl.ds(pl.multiple_of(chip * rows, rows), rows), pl.ds(pl.multiple_of(core * half, half), half)
        ]

    def chip_of(self, z, flip_a, flip_b):
        return self.p.other(z - self.p.z, flip_a, flip_b)

    def own(self, a, flip_b, flip_a, z):
        if self.mine is None:
            return self.rows_of(a, self.chip_of(z, flip_a, flip_b), self.p.core)
        return self.mine[a].at[8 * flip_b + 4 * flip_a + z]

    def load(self, a, flip_b, flip_a, z):
        return pltpu.make_async_copy(
            self.rows_of(a, self.chip_of(z, flip_a, flip_b), self.p.core),
            self.own(a, flip_b, flip_a, z),
            self.load_sem.at[a, 8 * flip_b + 4 * flip_a + z],
        )

    def lend(self, a, flip_b, flip_a, z):
        k = 8 * flip_b + 4 * flip_a + z
        return remote(
            self.rows_of(a, self.chip_of(z, flip_b, flip_a), 1 - self.p.core),
            self.sib[a].at[k],
            self.sib_send.at[a, k],
            self.sib_recv.at[a, k],
            self.p.sibling,
        )

    def to_b(self, a, flip_a, z):
        k = 4 * flip_a + z
        return remote(
            self.own(a, 1, flip_a, z), self.from_b[a].at[k], self.b_send.at[a, k], self.b_recv.at[a, k], self.p.dev_b
        )

    def to_a(self, a, z):
        return remote(
            self.own(a, 0, 1, z), self.from_a[a].at[z], self.a_send.at[a, z], self.a_recv.at[a, z], self.p.dev_a
        )

    def to_z(self, a, target, source):
        return remote(
            self.own(a, 0, 0, target),
            self.line[a].at[source],
            self.z_send.at[a, target],
            self.z_recv.at[a, source],
            self.p.me + 8 * (target - self.p.z),
        )

    def open(self, z):
        for flip_b, flip_a in ((1, 1), (1, 0), (0, 1), (0, 0)):
            for a in self.arrays:
                self.lend(a, flip_b, flip_a, z).start()
                if self.mine is not None:
                    self.load(a, flip_b, flip_a, z).start()

    def open_all(self):
        for z in ORDER:
            self.open(z)

    def pair(self, a, flip_b, flip_a, z):
        if self.mine is not None:
            self.load(a, flip_b, flip_a, z).wait()
        self.lend(a, flip_b, flip_a, z).wait_recv()
        k = 8 * flip_b + 4 * flip_a + z
        return self.own(a, flip_b, flip_a, z)[...].astype(jnp.float32) + self.sib[a][k].astype(jnp.float32)

    def cross_b(self, z):
        for flip_a in (1, 0):
            for a in self.arrays:
                self.own(a, 1, flip_a, z)[...] = self.pair(a, 1, flip_a, z).astype(jnp.bfloat16)
                self.to_b(a, flip_a, z).start()

    def cross_a(self, z):
        for a in self.arrays:
            value = self.pair(a, 0, 1, z)
            self.to_b(a, 1, z).wait_recv()
            self.own(a, 0, 1, z)[...] = (value + self.from_b[a][4 + z].astype(jnp.float32)).astype(jnp.bfloat16)
            self.to_a(a, z).start()

    def along_z(self, z):
        place = self.p
        for a in self.arrays:
            value = self.pair(a, 0, 0, z)
            self.to_b(a, 0, z).wait_recv()
            value = value + self.from_b[a][z].astype(jnp.float32)
            self.to_a(a, z).wait_recv()
            self.part[a][...] = value + self.from_a[a][z].astype(jnp.float32)

            @pl.when(place.z != z)
            def _():
                self.own(a, 0, 0, z)[...] = self.part[a][...].astype(jnp.bfloat16)
                self.to_z(a, z, place.z).start()

            @pl.when(place.z == z)
            def _():
                self.last[a][...] = self.part[a][...]

    def end_copies(self, a):
        core = self.p.core
        rows, width = self.total[a].shape
        dst = self.total[a].at[:, pl.ds(pl.multiple_of(core * (width // 2), width // 2), width // 2)]
        away = remote(
            self.last[a].at[pl.ds(pl.multiple_of((1 - core) * rows, 8), rows), :],
            dst,
            self.end_send.at[a],
            self.end_recv.at[a],
            self.p.sibling,
        )
        keep = pltpu.make_async_copy(
            self.last[a].at[pl.ds(pl.multiple_of(core * rows, 8), rows), :], dst, self.end_local.at[a]
        )
        return away, keep

    def close(self):
        for a in self.arrays:

            def add(k, carry):
                source = lax.rem(self.p.z + k, 4)
                self.to_z(a, self.p.z, source).wait_recv()
                self.last[a][...] += self.line[a][source].astype(jnp.float32)
                return carry

            lax.fori_loop(1, 4, add, 0)
            for copy in self.end_copies(a):
                copy.start()

    def end(self):
        for a in self.arrays:
            for copy in self.end_copies(a):
                copy.wait()

    def finish(self):
        def step(z, carry):
            for a in self.arrays:
                for flip_b in range(2):
                    for flip_a in range(2):
                        self.lend(a, flip_b, flip_a, z).wait_send()
                for flip_a in range(2):
                    self.to_b(a, flip_a, z).wait_send()
                self.to_a(a, z).wait_send()

                @pl.when(self.p.z != z)
                def _():
                    self.to_z(a, z, self.p.z).wait_send()

            return carry

        lax.fori_loop(0, 4, step, 0)

    def steps(self):
        z0, z1, z2, z3 = ORDER
        work = [(self.cross_b, z) for z in ORDER]
        work += [(self.cross_a, z0), (self.cross_a, z1), (self.along_z, z0), (self.cross_a, z2), (self.along_z, z1)]
        work += [(self.cross_a, z3), (self.along_z, z2), (self.along_z, z3)]
        return [functools.partial(step, z) for step, z in work] + [self.close, self.end, self.finish]


def scatter_scratch(shapes):
    scratch = []
    for count, kind in ((16, jnp.bfloat16), (8, jnp.bfloat16), (4, jnp.bfloat16), (4, jnp.bfloat16),
                        (0, jnp.float32), (0, jnp.float32)):
        scratch += [pltpu.VMEM(((count,) if count else ()) + shape, kind) for shape in shapes]
    counts = (16, 16, 16, 8, 8, 4, 4, 4, 4)
    several = len(shapes)
    return (
        scratch
        + [pltpu.SemaphoreType.DMA((several, n)) for n in counts]
        + [pltpu.SemaphoreType.DMA((several,))] * 3
    )


def dot_nt(left, right):
    return lax.dot_general(left, right, (((1,), (1,)), ((), ())), preferred_element_type=jnp.float32)


def dot_tn(left, right):
    return lax.dot_general(left, right, (((0,), (0,)), ((), ())), preferred_element_type=jnp.float32)


def thirds(value):
    high = value.astype(jnp.bfloat16)
    rest = value - high.astype(jnp.float32)
    mid = rest.astype(jnp.bfloat16)
    return high, mid, (rest - mid.astype(jnp.float32)).astype(jnp.bfloat16)


def silu_slope(value):
    gate = jax.nn.sigmoid(value)
    return gate * (1 + value * (1 - gate))


PLANE, LINE = 8, 4


class Swap:
    def __init__(self, index, sems, full, away=None, mid=None, reduce=None):
        self.i, self.sems, self.full, self.away, self.mid = index, sems, full, away, mid
        self.second = mid if reduce is None else reduce
        self.me = lax.axis_index(AXIS)
        self.z, self.p = self.me // PLANE, self.me % PLANE
        self.spread = away is None

    def plane(self, peer, slot):
        send, recv = self.sems
        if self.spread:
            src, dst = self.full.at[:, self.p], self.full.at[:, slot]
        else:
            src, dst = self.away.at[:, peer], self.mid.at[:, slot]
        return remote(src, dst, send.at[self.i, peer], recv.at[self.i, slot], self.me + peer - self.p)

    def line(self, peer, slot):
        send, recv = self.sems
        if self.spread:
            src, dst = self.full.at[self.z, self.p], self.full.at[slot, self.p]
        else:
            src, dst = self.second.at[peer], self.full.at[slot]
        return remote(
            src, dst, send.at[self.i, PLANE + peer], recv.at[self.i, PLANE + slot], self.me + PLANE * (peer - self.z)
        )

    def each(self, in_plane, step):
        mine, count = (self.p, PLANE) if in_plane else (self.z, LINE)

        def run(k, carry):
            step(lax.rem(mine + k, count))
            return carry

        lax.fori_loop(1, count, run, 0)

    def hop(self, in_plane):
        make, slot = (self.plane, self.p) if in_plane else (self.line, self.z)
        self.each(in_plane, lambda peer: make(peer, slot).start())

    def come(self, in_plane):
        make = self.plane if in_plane else self.line
        self.each(in_plane, lambda peer: make(peer, peer).wait_recv())

    def start(self):
        if not self.spread:
            for k in range(LINE):
                self.mid[k, self.p] = self.away[k, self.p]
        self.hop(not self.spread)

    def between(self, work=None):
        self.come(not self.spread)
        if work is not None:
            work()
        self.hop(self.spread)
        if not self.spread:
            self.full[self.z] = self.second[self.z]

    def arrive(self):
        self.come(self.spread)

    def sent(self):
        self.each(True, lambda peer: self.plane(peer, self.p).wait_send())
        self.each(False, lambda peer: self.line(peer, self.z).wait_send())


def modulate_steps(devices, ins, outs, bufs, sems):
    msg, emb, wcond, bt1, bt2, bcond = ins
    mods, pre, cond, hid_all, low_all, feat_all, lab_all, got = outs
    hid, low, away, mid, wcls = bufs
    me = lax.axis_index(AXIS)
    z, place = me // PLANE, me % PLANE
    images, cols = 4, emb.shape[0]
    wt1, wt2 = emb.at[:, :FREQ], emb.at[:, FREQ : FREQ + MODEL_WIDTH]
    swaps = [Swap(0, sems, got), Swap(1, sems, hid), Swap(2, sems, low), Swap(3, sems, mods, away, mid)]

    def first():
        got[z, place] = msg[...]
        wcls[...] = jnp.zeros_like(wcls)
        wcls[:, : emb.shape[1] - FREQ - MODEL_WIDTH] = emb[:, FREQ + MODEL_WIDTH :]
        swaps[0].start()

    def second():
        swaps[0].arrive()
        for j in range(devices):
            at = slice(images * j, images * (j + 1))
            block = got[j // PLANE, j % PLANE].astype(jnp.float32)
            feat_all[at, :128] = block[:images]
            feat_all[at, 128:] = block[images : 2 * images]
            digits = block[3 * images : 4 * images]
            lab_all[at, :] = jnp.broadcast_to(32.0 * digits[:, :1] + digits[:, 64:65], (images, 128))
        pre[...] = dot_nt(wt1[...].astype(jnp.bfloat16), feat_all[...].astype(jnp.bfloat16)) + bt1[...]
        hidden = silu(pre[...])
        pad = jnp.zeros((hid.shape[2] - cols, hidden.shape[1]), jnp.float32)
        hid[z, place] = jnp.concatenate([hidden, pad], 0).astype(jnp.bfloat16)
        swaps[1].start()
        classes = lax.broadcasted_iota(jnp.int32, (lab_all.shape[0], wcls.shape[1]), 1).astype(jnp.float32)
        labels = jnp.concatenate([lab_all[...] + PD] * (wcls.shape[1] // 128), 1)
        onehot = (labels == classes).astype(jnp.bfloat16)
        cond[...] = dot_nt(wcls[...].astype(jnp.bfloat16), onehot) + bt2[...]

    def third():
        swaps[1].arrive()
        for j in range(devices):
            hid_all[cols * j : cols * (j + 1), :] = hid[j // PLANE, j % PLANE].astype(jnp.float32)[:cols]
        cond[...] += jnp.dot(
            wt2[...].astype(jnp.bfloat16), hid_all[...].astype(jnp.bfloat16), preferred_element_type=jnp.float32
        )
        value = silu(cond[...])
        pad = jnp.zeros((low.shape[2] - cols, value.shape[1]), jnp.float32)
        low[z, place] = jnp.concatenate([value, pad], 0).astype(jnp.bfloat16)
        swaps[2].start()

    def fourth():
        swaps[2].arrive()
        for j in range(devices):
            low_all[cols * j : cols * (j + 1), :] = low[j // PLANE, j % PLANE].astype(jnp.float32)[:cols]
        rows = dot_nt(low_all[...].T.astype(jnp.bfloat16), wcond[...].astype(jnp.bfloat16)) + bcond[...]
        for j in range(devices):
            away[j // PLANE, j % PLANE] = rows[images * j : images * (j + 1)]
        swaps[3].start()

    def last():
        swaps[3].arrive()
        for swap in swaps:
            swap.sent()

    between = [swap.between for swap in swaps]
    return [first, between[0], second, between[1], third, between[2], fourth, between[3], last]


SETTLE_INS = ("d_mods", "emb", "wcond", "pre", "cond", "hid_all", "low_all", "feat_all", "lab_all", "g_head", "g_hbias", "loss",
              "g_patch", "g_pbias", "bin0", "bin1", "bout0", "bout1", "done_in", "done_out")


def settle_steps(devices, ins, outs, bufs, sems, shards):
    d_mods, pre, lab_all = ins["d_mods"], ins["pre"], ins["lab_all"]
    g_cond, g_t1, g_t2, g_cls, merged = outs
    dm_mid, dm_got, dm_all, rows, small, small_mid, small_sum, small_got = bufs[:8]
    dc_part, dc_mid, dc_sum, dc_got, dh_part, dh_mid, dh_sum, dh_got = bufs[8:]
    me = lax.axis_index(AXIS)
    images, width = d_mods.shape[2:]
    cols = pre.shape[0]
    swaps = [
        Swap(0, sems, dm_got, d_mods, dm_mid),
        Swap(1, sems, small_got, small, small_mid, small_sum),
        Swap(2, sems, dc_got, dc_part, dc_mid, dc_sum),
        Swap(3, sems, dh_got, dh_part, dh_mid, dh_sum),
        Swap(4, sems, merged),
    ]
    keep = {}

    def share(value, part):
        pad = jnp.zeros((32 - cols, value.shape[1]), jnp.float32)
        for j in range(devices):
            part[j // PLANE, j % PLANE] = jnp.concatenate([value[cols * j : cols * (j + 1)], pad], 0).astype(jnp.bfloat16)

    def add_plane(mid, total):
        for k in range(LINE):
            total[k] = jnp.sum(mid[k].astype(jnp.float32), 0)

    def add_small():
        add_plane(small_mid, small_sum)

    def add_dc():
        add_plane(dc_mid, dc_sum)

    def add_dh():
        add_plane(dh_mid, dh_sum)

    def parts_of(value):
        return sum(
            jnp.where(lax.broadcasted_iota(jnp.int32, (1, 128), 1) == k, part.astype(jnp.float32), 0.0)
            for k, part in enumerate(thirds(value))
        )

    def first():
        swaps[0].start()
        dm_all[...] = jnp.zeros_like(dm_all)
        rows[...] = jnp.zeros_like(rows)
        for k in range(MODEL_WIDTH // 128):
            span = slice(128 * k, 128 * (k + 1))
            rows[16 * k : 16 * (k + 1), :] = ins["g_patch"][:, span]
            rows[96 + 32 * k : 96 + 32 * (k + 1), :] = ins["g_head"][:, span]
        at = 288
        for name in ("g_pbias", "bin0", "bin1", "bout0", "bout1"):
            for k in range(ins[name].shape[1] // 128):
                rows[at : at + 1, :] = ins[name][:, 128 * k : 128 * (k + 1)]
                at += 1
        square = ins["g_hbias"].shape
        diagonal = lax.broadcasted_iota(jnp.int32, square, 0) == lax.broadcasted_iota(jnp.int32, square, 1)
        rows[at : at + 1, :] = jnp.sum(jnp.where(diagonal, ins["g_hbias"][...], 0.0), 0, keepdims=True)
        for j in range(devices):
            small[j // PLANE, j % PLANE] = rows[16 * j : 16 * (j + 1), :].astype(jnp.bfloat16)

    def second():
        swaps[0].arrive()
        for j in range(devices):
            dm_all[images * j : images * (j + 1), :width] = dm_got[j // PLANE, j % PLANE]
        turned = dm_all[...].T[:width]
        parts = thirds(turned)
        weight = ins["wcond"][...].astype(jnp.bfloat16)
        share(sum(dot_tn(weight, part) for part in parts), dc_part)
        swaps[2].start()
        swaps[1].start()
        low = ins["low_all"][...].astype(jnp.bfloat16)
        g_cond[...] = sum(dot_nt(part, low) for part in parts)

    def third():
        swaps[2].arrive()
        d_cond = jnp.sum(dc_got[...], 0)[:cols] * silu_slope(ins["cond"][...])
        parts = thirds(d_cond)
        weight = ins["emb"][:, FREQ : FREQ + MODEL_WIDTH].astype(jnp.bfloat16)
        share(sum(dot_tn(weight, part) for part in parts), dh_part)
        swaps[3].start()
        classes = lax.broadcasted_iota(jnp.int32, (lab_all.shape[0], g_cls.shape[1]), 1).astype(jnp.float32)
        labels = jnp.concatenate([lab_all[...] + PD] * (g_cls.shape[1] // 128), 1)
        onehot = (labels == classes).astype(jnp.bfloat16)
        g_cls[...] = sum(jnp.dot(part, onehot, preferred_element_type=jnp.float32) for part in parts)
        hidden = ins["hid_all"][...].astype(jnp.bfloat16)
        g_t2[...] = sum(dot_nt(part, hidden) for part in parts)
        ones = jnp.ones((8, lab_all.shape[0]), jnp.bfloat16)
        keep["t2"] = sum(dot_nt(ones, part) for part in parts)

    def fourth():
        swaps[1].arrive()
        swaps[3].arrive()
        d_pre = jnp.sum(dh_got[...], 0)[:cols] * silu_slope(pre[...])
        parts = thirds(d_pre)
        feats = ins["feat_all"][...].astype(jnp.bfloat16)
        g_t1[...] = sum(jnp.dot(part, feats, preferred_element_type=jnp.float32) for part in parts)
        ones = jnp.ones((8, lab_all.shape[0]), jnp.bfloat16)
        keep["t1"] = sum(dot_nt(ones, part) for part in parts)
        total = jnp.zeros((1, 1), jnp.float32)
        for ref in (g_cond, g_t1, g_t2, g_cls, ins["done_in"], ins["done_out"]):
            total = total + jnp.sum(ref[...] * ref[...])
        keep["squares"] = total

    def message():
        total = keep["squares"]
        for ref in shards:
            total = total + jnp.sum(ref[...] * ref[...])
        bias_cond = jnp.sum(dm_all[...], 0, keepdims=True)
        blank = jnp.zeros((1, 128 - cols), jnp.float32)
        lines = [jnp.concatenate([keep[name][0:1, :], blank], 1) for name in ("t1", "t2")]
        lines.append(parts_of(total))
        lines.append(parts_of(ins["loss"][0:1, :]))
        lines += [bias_cond[:, 128 * k : 128 * (k + 1)] for k in range(3)]
        lines.append(jnp.zeros((9, 128), jnp.float32))
        lines.insert(0, jnp.sum(small_got[...], 0))
        merged[me // PLANE, me % PLANE] = jnp.concatenate(lines, 0).astype(jnp.bfloat16)
        swaps[4].start()
        swaps[4].between()

    def last():
        swaps[4].arrive()
        for swap in swaps:
            swap.sent()

    betweens = [
        swaps[0].between,
        functools.partial(swaps[1].between, add_small),
        functools.partial(swaps[2].between, add_dc),
        functools.partial(swaps[3].between, add_dh),
    ]
    return [first, second, third, fourth, message, last], betweens


def dot_nn(left, right):
    return lax.dot_general(left, right, (((1,), (0,)), ((), ())), preferred_element_type=jnp.float32)


def norm_parts(value):
    centered = value - jnp.mean(value, -1, keepdims=True)
    scale = lax.rsqrt(jnp.mean(centered * centered, -1, keepdims=True) + 1e-06)
    return centered * scale, scale


def norm_back(normed, scale, d_normed):
    inner = jnp.mean(d_normed * normed, -1, keepdims=True)
    return scale * (d_normed - jnp.mean(d_normed, -1, keepdims=True) - normed * inner)


GELU_C = math.sqrt(2.0 / math.pi)


def gelu_value(u):
    return 0.5 * u * (1.0 + jnp.tanh(GELU_C * (u + 0.044715 * u * u * u)))


def gelu_slope(u):
    square = u * u
    t = jnp.tanh(GELU_C * u * (1.0 + 0.044715 * square))
    return 0.5 * (1.0 + t) + 0.5 * u * (1.0 - t * t) * (GELU_C * (1.0 + 3 * 0.044715 * square))


def head_masks(shape):
    low_half = lax.broadcasted_iota(jnp.int32, shape, 1) < HEAD_DIM
    return low_half, jnp.logical_not(low_half)


class Weights:
    def __init__(self, hbm, vmem, sems):
        w_in, w_out = hbm
        self.w_in, self.w_out = vmem
        cut = 3 * MODEL_WIDTH
        spans = [
            (w_in.at[pl.ds(0, cut), :], self.w_in.at[pl.ds(0, cut), :]),
            (w_out.at[:, pl.ds(0, MODEL_WIDTH)], self.w_out.at[:, pl.ds(0, MODEL_WIDTH)]),
            (w_in.at[pl.ds(cut, FF), :], self.w_in.at[pl.ds(cut, FF), :]),
            (w_out.at[:, pl.ds(MODEL_WIDTH, FF)], self.w_out.at[:, pl.ds(MODEL_WIDTH, FF)]),
        ]
        self.copies = [pltpu.make_async_copy(src, dst, sems.at[i]) for i, (src, dst) in enumerate(spans)]

    def start(self, order):
        @pl.when(pl.program_id(0) == 0)
        def _():
            for i in order:
                self.copies[i].start()

    def need(self, i):
        @pl.when(pl.program_id(0) == 0)
        def _():
            self.copies[i].wait()


def forward_image(x_ref, mod, base, weights, b_in, b_out, outs, hook=lambda: None):
    h1, qkv, probs, o, a, x1, h2, u, g, f = outs
    shift1, scale1, gate1, shift2, scale2, gate2 = (mod[0, base + i : base + i + 1, :] for i in range(6))
    width = MODEL_WIDTH
    hook()
    x = x_ref[...]
    h1[...] = (norm_parts(x)[0] * (1 + scale1) + shift1).astype(jnp.bfloat16)
    weights.need(0)
    for j in range(3):
        span = slice(j * width, (j + 1) * width)
        qkv[:, span] = (dot_nt(h1[...], weights.w_in[span, :]) + b_in[:, span]).astype(jnp.bfloat16)
    hook()
    def scores_of(pair):
        q, k = (qkv[:, j * width + 128 * pair : j * width + 128 * (pair + 1)] for j in range(2))
        q = q * jnp.bfloat16(HEAD_DIM**-0.5)
        zero = jnp.zeros_like(q)
        return dot_nt(jnp.concatenate([jnp.where(mask, q, zero) for mask in head_masks(q.shape)], 0), k)

    ahead = scores_of(0)
    for pair in range(HEADS // 2):
        scores, ahead = ahead, scores_of(pair + 1) if pair + 1 < HEADS // 2 else None
        v = qkv[:, 2 * width + 128 * pair : 2 * width + 128 * (pair + 1)]
        expo = jnp.exp(scores - jnp.max(scores, -1, keepdims=True))
        weight = (expo * pl.reciprocal(jnp.sum(expo, -1, keepdims=True))).astype(jnp.bfloat16)
        probs[0, 2 * pair] = weight[:SEQ]
        probs[0, 2 * pair + 1] = weight[SEQ:]
        both = dot_nn(weight, v)
        mixed = jnp.where(head_masks(v.shape)[0], both[:SEQ], both[SEQ:])
        o[:, 128 * pair : 128 * (pair + 1)] = mixed.astype(jnp.bfloat16)
        hook()
    weights.need(1)
    branch = dot_nt(o[...], weights.w_out[:, :width]) + b_out[:, :width]
    a[...] = branch.astype(jnp.bfloat16)
    x1[...] = x + gate1 * branch
    h2[...] = (norm_parts(x1[...])[0] * (1 + scale2) + shift2).astype(jnp.bfloat16)
    hook()
    weights.need(2)
    weights.need(3)
    def up_part(j):
        rows = slice((3 + j) * width, (4 + j) * width)
        return dot_nt(h2[...], weights.w_in[rows, :]) + b_in[:, rows]

    total, ahead = None, up_part(0)
    for j in range(FF // width):
        span = slice(j * width, (j + 1) * width)
        value, ahead = ahead, up_part(j + 1) if j + 1 < FF // width else None
        u[:, span] = value.astype(jnp.bfloat16)
        active = gelu_value(value).astype(jnp.bfloat16)
        g[:, span] = active
        term = dot_nt(active, weights.w_out[:, (1 + j) * width : (2 + j) * width])
        total = term if total is None else total + term
        hook()
    ffn = total + b_out[:, width:]
    f[...] = ffn.astype(jnp.bfloat16)
    return x1[...] + gate2 * ffn


def head_kernel(scale_out, x, mod, w_in, w_out, b_in, b_out, head_t, b_head, targets_t, *refs):
    outs, (dx, d_final, g_head, g_bias, loss), (vm_in, vm_out, sems) = refs[:10], refs[10:15], refs[15:]
    weights = Weights((w_in, w_out), (vm_in, vm_out), sems)
    weights.start((0, 1, 2, 3))
    last = forward_image(x, mod, 6 * (LAYERS - 1), weights, b_in.at[0], b_out.at[0], outs)
    normed, scale = norm_parts(last)
    shift_row, scale_row = mod[0, 6 * LAYERS : 6 * LAYERS + 1, :], mod[0, 6 * LAYERS + 1 :, :]
    shaped = (normed * (1 + scale_row) + shift_row).astype(jnp.bfloat16)
    low = head_t[...].astype(jnp.bfloat16)
    error = dot_nt(low, shaped) + b_head[...] - targets_t[0]
    d_out = (error * scale_out).astype(jnp.bfloat16)

    @pl.when(pl.program_id(0) == 0)
    def _():
        g_head[...] = jnp.zeros_like(g_head)
        g_bias[...] = jnp.zeros_like(g_bias)
        loss[...] = jnp.zeros_like(loss)

    g_head[...] += dot_nn(d_out, shaped)
    g_bias[...] += jnp.sum(d_out.astype(jnp.float32), 1, keepdims=True)
    loss[...] += jnp.sum(error * error)
    d_shaped = dot_tn(d_out, low)
    d_final[0, 0:1, :] = jnp.sum(d_shaped, 0, keepdims=True)
    d_final[0, 1:2, :] = jnp.sum(d_shaped * normed, 0, keepdims=True)
    dx[...] = norm_back(normed, scale, d_shaped * (1 + scale_row))


WEIGHT_SCRATCH = [
    pltpu.VMEM((IW, MODEL_WIDTH), jnp.bfloat16),
    pltpu.VMEM((MODEL_WIDTH, OW), jnp.bfloat16),
    pltpu.SemaphoreType.DMA((4,)),
]


def token_block(width):
    return pl.BlockSpec((SEQ, width), lambda i: (i, 0))


def image_block(*dims):
    return pl.BlockSpec((1,) + dims, lambda i: (i,) + (0,) * len(dims))


def whole_block(*dims):
    return pl.BlockSpec(dims, lambda i: (0,) * len(dims))


def kept_shapes(images):
    tokens, width, low, full = images * SEQ, MODEL_WIDTH, jnp.bfloat16, jnp.float32
    shapes = [((tokens, width), low), ((tokens, 3 * width), low), ((images, HEADS, SEQ, SEQ), low), ((tokens, width), low),
              ((tokens, width), low), ((tokens, width), full), ((tokens, width), low), ((tokens, FF), low),
              ((tokens, FF), low), ((tokens, width), low)]
    specs = [token_block(s[1]) if len(s) == 2 else image_block(*s[1:]) for s, _ in shapes]
    return [jax.ShapeDtypeStruct(s, t) for s, t in shapes], specs


def layer_block(array, layer):
    return pl.BlockSpec((1,) + array.shape[1:], lambda i: (layer, 0, 0))


def forward_specs(ins, layer):
    any_block = pl.BlockSpec(memory_space=pl.ANY)
    return [token_block(MODEL_WIDTH), image_block(*ins[1].shape[1:]), any_block, any_block, layer_block(ins[4], layer),
            layer_block(ins[5], layer)]


def forward_head(ins, scale_out):
    images = ins[1].shape[0]
    shapes, specs = kept_shapes(images)
    extra = [(images * SEQ, MODEL_WIDTH), (images, 2, MODEL_WIDTH), (PO, MODEL_WIDTH), (PO, 128), (8, 128)]
    return pl.pallas_call(
        functools.partial(head_kernel, scale_out),
        grid=(images,),
        out_shape=shapes + [jax.ShapeDtypeStruct(s, jnp.float32) for s in extra],
        in_specs=forward_specs(ins, LAYERS - 1)
        + [whole_block(PO, MODEL_WIDTH), whole_block(PO, 1), image_block(PO, SEQ)],
        out_specs=specs
        + [token_block(MODEL_WIDTH), image_block(2, MODEL_WIDTH), whole_block(PO, MODEL_WIDTH), whole_block(PO, 128),
           whole_block(8, 128)],
        scratch_shapes=WEIGHT_SCRATCH,
        compiler_params=pltpu.CompilerParams(vmem_limit_bytes=56 << 20),
        name="forward_head",
    )(*ins)


def backward_image(refs, mod, base, weights, outs, hook=lambda: None, early=False):
    up_ref, x_ref, x1_ref, probs, qkv, a, f, u = refs
    dx, d_qkv, d_u, d_f, d_a, d_mod, g_bin, g_bout = outs
    width = MODEL_WIDTH
    shift1, scale1, gate1, shift2, scale2, gate2 = (mod[0, base + i : base + i + 1, :] for i in range(6))

    @pl.when(pl.program_id(0) == 0)
    def _():
        g_bin[...] = jnp.zeros_like(g_bin)
        g_bout[...] = jnp.zeros_like(g_bout)

    def rows_sum(value):
        return jnp.sum(value.astype(jnp.float32), 0, keepdims=True)

    hook()
    upstream = up_ref[...]
    d_f[...] = (gate2 * upstream).astype(jnp.bfloat16)
    d_mod[0, 5:6, :] = rows_sum(f[...].astype(jnp.float32) * upstream)
    g_bout[:, width:] += rows_sum(d_f[...])
    weights.need(3)
    weights.need(2)
    d_h2 = None
    for j in range(FF // width):
        span = slice(j * width, (j + 1) * width)
        rows = slice((3 + j) * width, (4 + j) * width)
        d_g = dot_nn(d_f[...], weights.w_out[:, (1 + j) * width : (2 + j) * width])
        d_u[:, span] = (d_g * gelu_slope(u[:, span].astype(jnp.float32))).astype(jnp.bfloat16)
        g_bin[:, rows] += rows_sum(d_u[:, span])
        term = dot_nn(d_u[:, span], weights.w_in[rows, :])
        d_h2 = term if d_h2 is None else d_h2 + term
        hook()
    normed, scale = norm_parts(x1_ref[...])
    d_mod[0, 3:4, :] = rows_sum(d_h2)
    d_mod[0, 4:5, :] = rows_sum(d_h2 * normed)
    upstream = upstream + norm_back(normed, scale, d_h2 * (1 + scale2))
    d_mod[0, 2:3, :] = rows_sum(a[...].astype(jnp.float32) * upstream)
    d_a[...] = (gate1 * upstream).astype(jnp.bfloat16)
    g_bout[:, :width] += rows_sum(d_a[...])
    dx[...] = upstream
    weights.need(1)
    d_o = dot_nn(d_a[...], weights.w_out[:, :width]).astype(jnp.bfloat16)
    hook()
    root = HEAD_DIM**-0.5

    def probs_back(pair):
        d_mixed = d_o[:, 128 * pair : 128 * (pair + 1)]
        zero = jnp.zeros_like(d_mixed)
        both = jnp.concatenate([jnp.where(mask, d_mixed, zero) for mask in head_masks(d_mixed.shape)], 0)
        return both, dot_nt(both, qkv[:, 2 * width + 128 * pair : 2 * width + 128 * (pair + 1)])

    ahead = probs_back(0) if early else None
    for pair in range(HEADS // 2):
        lanes = [slice(j * width + 128 * pair, j * width + 128 * (pair + 1)) for j in range(3)]
        if early:
            (d_masked, d_probs), ahead = ahead, probs_back(pair + 1) if pair + 1 < HEADS // 2 else None
        else:
            d_masked, d_probs = probs_back(pair)
        q, k = qkv[:, lanes[0]], qkv[:, lanes[1]]
        zero = jnp.zeros_like(q)
        masks = head_masks(q.shape)
        weight = probs[0, 2 * pair : 2 * pair + 2].reshape(2 * SEQ, SEQ)
        full = weight.astype(jnp.float32)
        d_scores = (full * (d_probs - jnp.sum(full * d_probs, -1, keepdims=True))).astype(jnp.bfloat16)
        both = dot_nn(d_scores, k)
        d_q = jnp.where(masks[0], both[:SEQ], both[SEQ:])
        d_k = dot_tn(d_scores, jnp.concatenate([jnp.where(mask, q, zero) for mask in masks], 0))
        d_qkv[:, lanes[0]] = (d_q * root).astype(jnp.bfloat16)
        d_qkv[:, lanes[1]] = (d_k * root).astype(jnp.bfloat16)
        d_qkv[:, lanes[2]] = dot_tn(weight, d_masked).astype(jnp.bfloat16)
        hook()
    weights.need(0)
    d_h1 = None
    for j in range(3):
        span = slice(j * width, (j + 1) * width)
        g_bin[:, span] += rows_sum(d_qkv[:, span])
        term = dot_nn(d_qkv[:, span], weights.w_in[span, :])
        d_h1 = term if d_h1 is None else d_h1 + term
    normed, scale = norm_parts(x_ref[...])
    d_mod[0, 0:1, :] = rows_sum(d_h1)
    d_mod[0, 1:2, :] = rows_sum(d_h1 * normed)
    dx[...] += norm_back(normed, scale, d_h1 * (1 + scale1))
    hook()


def backward_kernel(mod, w_in, w_out, *refs):
    ins, outs, (vm_in, vm_out, sems) = refs[:8], refs[8:16], refs[16:]
    weights = Weights((w_in, w_out), (vm_in, vm_out), sems)
    weights.start((3, 2, 1, 0))
    backward_image(ins, mod, 6 * (LAYERS - 1), weights, outs)


def backward_block(mods, w_in, w_out, refs):
    images, width, low, full = mods.shape[0], MODEL_WIDTH, jnp.bfloat16, jnp.float32
    tokens = images * SEQ
    any_block = pl.BlockSpec(memory_space=pl.ANY)
    shapes = [((tokens, width), full), ((tokens, 3 * width), low), ((tokens, FF), low), ((tokens, width), low),
              ((tokens, width), low), ((images, 6, width), full), ((1, IW), full), ((1, 2 * width), full)]
    return pl.pallas_call(
        backward_kernel,
        grid=(images,),
        out_shape=[jax.ShapeDtypeStruct(s, t) for s, t in shapes],
        in_specs=[image_block(*mods.shape[1:]), any_block, any_block, token_block(width), token_block(width), token_block(width),
                  image_block(HEADS, SEQ, SEQ), token_block(3 * width), token_block(width), token_block(width),
                  token_block(FF)],
        out_specs=[token_block(s[1]) for s, _ in shapes[:5]]
        + [image_block(6, width), whole_block(1, IW), whole_block(1, 2 * width)],
        scratch_shapes=WEIGHT_SCRATCH,
        compiler_params=pltpu.CompilerParams(vmem_limit_bytes=56 << 20),
        name="backward_block",
    )(mods, w_in, w_out, *refs)


def gather_steps(job):
    steps = [job.begin, functools.partial(job.a_step, 0)]
    for dist in (1, 2, 3):
        steps += [functools.partial(job.z_step, dist), functools.partial(job.a_step, dist)]
    for dist in range(4):
        steps += [functools.partial(job.b_step, dist, flip) for flip in range(2)]
    return steps + [job.finish]


class Hooks:
    def __init__(self, steps, slots, points):
        self.points, self.table = points, {}
        for step, slot in zip(steps, slots):
            self.table.setdefault((slot // points, slot % points), []).append(step)
        self.next = 0

    def __call__(self):
        point, self.next = self.next, self.next + 1
        for (turn, where), steps in sorted(self.table.items(), key=lambda item: item[0]):
            if where == point:

                @pl.when(pl.program_id(0) == turn)
                def _():
                    for step in steps:
                        step()


def start_kernel(devices, *refs):
    own, mod_ins, refs = refs[:2], refs[2:8], refs[8:]
    full, mod_outs, refs = refs[:2], refs[2:10], refs[10:]
    part, mod_bufs, mod_sems = refs[:10], refs[10:15], refs[15:]
    place = Place()
    place.greet()
    job = Gather(place, [ref.at[0] for ref in own], part[:2], part[2:4], full, part[4:])
    parts = modulate_steps(devices, mod_ins, mod_outs, mod_bufs, mod_sems)
    moves = gather_steps(job)
    for kind in START_ORDER:
        (parts if kind == "a" else moves).pop(0)()


START_ORDER = "ag" "aa" "gg" "a" "g" "a" "g" "a" "g" "a" "gg" "a" "gggggggg" "a" "g"


def gather_modulate(pair, ins):
    devices = lax.axis_size(AXIS)
    msg, _, wcond, rows = ins[:4]
    cols, images = rows.shape
    outs = [
        (LINE, PLANE, images // devices, wcond.shape[0]), (cols, images), (cols, images), (devices * cols, images),
        (devices * cols, images), (images, FREQ), (images, 128),
    ]
    padded = -(-cols // 16) * 16
    vmem = pl.BlockSpec(memory_space=pltpu.VMEM)
    return pl.pallas_call(
        functools.partial(start_kernel, devices),
        out_shape=[full_shape(a) for a in pair]
        + [jax.ShapeDtypeStruct(shape, jnp.float32) for shape in outs]
        + [jax.ShapeDtypeStruct((LINE, PLANE) + msg.shape, jnp.bfloat16)],
        in_specs=[vmem] * 8,
        out_specs=[pl.BlockSpec(memory_space=pl.ANY)] * 2 + [vmem] * 8,
        scratch_shapes=gather_scratch(piece_shapes([a.shape[1:] for a in pair]))
        + [
            pltpu.VMEM((LINE, PLANE, padded, images), jnp.bfloat16),
            pltpu.VMEM((LINE, PLANE, padded, images), jnp.bfloat16),
            pltpu.VMEM((LINE, PLANE, images // devices, wcond.shape[0]), jnp.float32),
            pltpu.VMEM((LINE, PLANE, images // devices, wcond.shape[0]), jnp.float32),
            pltpu.VMEM((cols, 1024), jnp.float32),
            pltpu.SemaphoreType.DMA((4, LINE + PLANE)),
            pltpu.SemaphoreType.DMA((4, LINE + PLANE)),
        ],
        compiler_params=pltpu.CompilerParams(collective_id=3, has_side_effects=True, vmem_limit_bytes=56 << 20),
        name="gather_modulate",
    )(*pair, *ins)


FORWARD_POINTS = 13


def forward_gather_kernel(slots, lat_t, mod, w_in, w_out, b_in, b_out, w_patch, b_patch, table, own_in, own_out, *refs):
    outs, x_out, full, x, refs = refs[:10], refs[10], refs[11:13], refs[13], refs[14:]
    pos, vm_in, vm_out, sems, part = refs[0], refs[1], refs[2], refs[3], refs[4:]
    place = Place()
    job = Gather(place, (own_in.at[0], own_out.at[0]), part[:2], part[2:4], full, part[4:])
    hooks = Hooks([place.greet] + gather_steps(job), slots, FORWARD_POINTS)
    weights = Weights((w_in, w_out), (vm_in, vm_out), sems)
    weights.start((0, 1, 2, 3))

    @pl.when(pl.program_id(0) == 0)
    def _():
        half = table.shape[1]
        for row in range(GRID):
            at = slice(GRID * row, GRID * (row + 1))
            pos[at, :half] = jnp.broadcast_to(table[row : row + 1, :], (GRID, half))
            pos[at, half:] = table[...]

    latents = lat_t[0].astype(jnp.float32).T.astype(jnp.bfloat16)
    x[...] = dot_nt(latents, w_patch[...]) + b_patch[...] + pos[...]
    x_out[...] = forward_image(x, mod, 0, weights, b_in.at[0], b_out.at[0], outs, hooks)


GATHER_SLOTS = (0, 0, 13, 15, 26, 28, 39, 41, 50) + (34, 43, 48, 51, 51, 51, 51, 51, 51)


def full_shape(array):
    return jax.ShapeDtypeStruct((lax.axis_size(AXIS) * array.shape[1], array.shape[2]), jnp.bfloat16)


def forward_gather(ins, patch, pair, layer):
    images = ins[1].shape[0]
    shapes, specs = kept_shapes(images)
    tokens = jax.ShapeDtypeStruct((images * SEQ, MODEL_WIDTH), jnp.float32)
    any_block = pl.BlockSpec(memory_space=pl.ANY)
    return pl.pallas_call(
        functools.partial(forward_gather_kernel, GATHER_SLOTS),
        grid=(images,),
        out_shape=shapes + [tokens] + [full_shape(a) for a in pair] + [tokens],
        in_specs=[image_block(PD, SEQ)]
        + forward_specs(ins, 0)[1:]
        + [whole_block(*a.shape) for a in patch]
        + [layer_block(a, layer) for a in pair],
        out_specs=specs + [token_block(MODEL_WIDTH)] + [any_block] * 2 + [token_block(MODEL_WIDTH)],
        scratch_shapes=[pltpu.VMEM((SEQ, MODEL_WIDTH), jnp.float32)]
        + WEIGHT_SCRATCH
        + gather_scratch(piece_shapes([a.shape[1:] for a in pair])),
        compiler_params=pltpu.CompilerParams(collective_id=1, has_side_effects=True, vmem_limit_bytes=58 << 20),
        name="forward_gather",
    )(*ins, *patch, *pair)


GRAD_CUTS = [3 * MODEL_WIDTH // MODEL_WIDTH, FF // MODEL_WIDTH]


class Grads:
    def __init__(self, hbm, bufs, keep_in, keep_out, sems):
        bufs = [bufs[0], bufs[4], *bufs[1:]]
        self.bufs, self.keep_in, self.keep_out = bufs, keep_in, keep_out
        self.copies = [pltpu.make_async_copy(src, dst, sems.at[i]) for i, (src, dst) in enumerate(zip(hbm, bufs))]
        self.here = set()

    def start(self):
        for i in (4, 5, 6, 7, 2, 3, 0):
            self.copies[i].start()

    def need(self, *which):
        for i in which:
            if i not in self.here:
                self.copies[i].wait()
                self.here.add(i)

    def rows_in(self, chunk):
        width = MODEL_WIDTH
        pair = 0 if chunk < 3 else 1
        self.need(2 * pair, 2 * pair + 1)
        left, right = self.bufs[2 * pair], self.bufs[2 * pair + 1]
        at = (chunk - 3 * pair) * width
        self.keep_in[chunk * width : (chunk + 1) * width, :] = dot_tn(left[:, at : at + width], right[...]).astype(
            jnp.bfloat16
        )

    def rows_out(self, part):
        width = MODEL_WIDTH
        rows = slice(part * width // 2, (part + 1) * width // 2)
        self.need(4, 5)
        self.keep_out[rows, :width] = dot_tn(self.bufs[4][:, rows], self.bufs[5][...]).astype(jnp.bfloat16)
        self.need(6, 7)
        for j in range(FF // width):
            span = slice(j * width, (j + 1) * width)
            self.keep_out[rows, (1 + j) * width : (2 + j) * width] = dot_tn(
                self.bufs[6][:, rows], self.bufs[7][:, span]
            ).astype(jnp.bfloat16)
        if part == 0:
            self.copies[1].start()


def grads_out_kernel(*refs):
    ins, g_in, total, refs = refs[:8], refs[8], refs[9:10], refs[10:]
    bufs, keep_in, keep_out, load_sems, store_sem, refs = refs[:7], refs[7], refs[8], refs[9], refs[10], refs[11:]
    place = Place()
    work = Grads(ins, bufs, keep_in, keep_out, load_sems)
    work.start()
    place.greet()
    job = Scatter(place, [keep_out], total, refs[:6], refs[6:])
    work.rows_out(1)
    job.open(3)
    job.open(2)
    work.rows_out(0)
    job.open(0)
    job.open(1)
    moves = job.steps()
    for chunk in range(7):
        moves[chunk]()
        work.rows_in(chunk)
    store = pltpu.make_async_copy(keep_in, g_in, store_sem)
    store.start()
    for move in moves[7:]:
        move()
    store.wait()


def grad_bufs(ins):
    return [pltpu.VMEM(a.shape, a.dtype) for i, a in enumerate(ins) if i != 1] + [
        pltpu.VMEM((IW, MODEL_WIDTH), jnp.bfloat16),
        pltpu.VMEM((MODEL_WIDTH, OW), jnp.bfloat16),
        pltpu.SemaphoreType.DMA((8,)),
    ]


def weight_grads_out(ins, shape):
    any_block = pl.BlockSpec(memory_space=pl.ANY)
    return pl.pallas_call(
        grads_out_kernel,
        out_shape=[jax.ShapeDtypeStruct((IW, MODEL_WIDTH), jnp.bfloat16), jax.ShapeDtypeStruct(shape, jnp.float32)],
        in_specs=[any_block] * 8,
        out_specs=[any_block, pl.BlockSpec(memory_space=pltpu.VMEM)],
        scratch_shapes=grad_bufs(ins) + [pltpu.SemaphoreType.DMA] + scatter_scratch(piece_shapes([shape])),
        compiler_params=pltpu.CompilerParams(collective_id=5, has_side_effects=True, vmem_limit_bytes=58 << 20),
        name="weight_grads_out",
    )(*ins)


BACKWARD_POINTS = 13


def backward_scatter_kernel(slots, mod, w_in, w_out, grad, lat_t, *refs):
    ins, outs, (g_patch, g_pbias, total), refs = refs[:8], refs[8:16], refs[16:19], refs[19:]
    vm_in, vm_out, sems, mine, refs = refs[0], refs[1], refs[2], refs[3], refs[4:]
    place = Place()
    job = Scatter(place, [grad], [total], refs[:6], refs[6:], [mine])
    hooks = Hooks([place.greet, job.open_all] + job.steps(), slots, BACKWARD_POINTS)
    weights = Weights((w_in, w_out), (vm_in, vm_out), sems)
    weights.start((3, 2, 1, 0))
    backward_image(ins, mod, 0, weights, outs, hooks, True)
    d_patch = outs[0][...].astype(jnp.bfloat16)

    @pl.when(pl.program_id(0) == 0)
    def _():
        g_patch[...] = jnp.zeros_like(g_patch)
        g_pbias[...] = jnp.zeros_like(g_pbias)

    g_patch[...] += dot_nn(lat_t[0], d_patch)
    g_pbias[...] += jnp.sum(d_patch.astype(jnp.float32), 0, keepdims=True)


SCATTER_SLOTS = (0, 0, 3, 6, 10, 13, 18, 25, 27, 32, 34, 38, 42, 51, 51, 51, 51)


def backward_scatter(mods, w_in, w_out, refs, grad, lat_t, shape):
    images, width, low, full = mods.shape[0], MODEL_WIDTH, jnp.bfloat16, jnp.float32
    tokens = images * SEQ
    any_block = pl.BlockSpec(memory_space=pl.ANY)
    shapes = [((tokens, width), full), ((tokens, 3 * width), low), ((tokens, FF), low), ((tokens, width), low),
              ((tokens, width), low), ((images, 6, width), full), ((1, IW), full), ((1, 2 * width), full),
              ((PD, width), full), ((1, width), full), (shape, full)]
    pieces = piece_shapes([shape])
    return pl.pallas_call(
        functools.partial(backward_scatter_kernel, SCATTER_SLOTS),
        grid=(images,),
        out_shape=[jax.ShapeDtypeStruct(s, t) for s, t in shapes],
        in_specs=[image_block(*mods.shape[1:]), any_block, any_block, any_block, image_block(PD, SEQ), token_block(width),
                  token_block(width), token_block(width), image_block(HEADS, SEQ, SEQ), token_block(3 * width),
                  token_block(width), token_block(width), token_block(FF)],
        out_specs=[token_block(s[1]) for s, _ in shapes[:5]]
        + [image_block(6, width)] + [whole_block(*s) for s, _ in shapes[6:-1]] + [any_block],
        scratch_shapes=WEIGHT_SCRATCH
        + [pltpu.VMEM((16,) + pieces[0], jnp.bfloat16)] + scatter_scratch(pieces),
        compiler_params=pltpu.CompilerParams(collective_id=6, has_side_effects=True, vmem_limit_bytes=62 << 20),
        name="backward_scatter",
    )(mods, w_in, w_out, grad, lat_t, *refs)


def finish_kernel(devices, *refs):
    count = len(SETTLE_INS)
    ins, set_ins, refs = refs[:8], dict(zip(SETTLE_INS, refs[8 : 8 + count])), refs[8 + count :]
    totals, set_outs, refs = refs[:2], refs[2:7], refs[7:]
    bufs, keep_in, keep_out, load_sems, refs = refs[:7], refs[7], refs[8], refs[9], refs[10:]
    sc_bufs, sc_sems, refs = refs[:12], refs[12:24], refs[24:]
    set_bufs, set_sems = refs[:16], refs[16:]
    work = Grads(ins, bufs, keep_in, keep_out, load_sems)
    work.start()
    place = Place()
    place.greet()
    job = Scatter(place, [keep_in, keep_out], totals, sc_bufs, sc_sems)
    (first, second, third, fourth, message, last), betweens = settle_steps(
        devices, set_ins, set_outs, set_bufs, set_sems, totals
    )
    first()
    work.rows_out(1)
    betweens[0]()
    work.rows_in(5)
    work.rows_in(6)
    second()
    job.open(3)
    work.rows_out(0)
    betweens[2]()
    job.cross_b(3)
    work.rows_in(0)
    work.rows_in(1)
    job.open(0)
    third()
    work.rows_in(3)
    job.cross_b(0)
    work.rows_in(4)
    job.open(2)
    job.cross_a(3)
    work.rows_in(2)
    job.cross_b(2)
    job.open(1)
    job.cross_a(0)
    job.along_z(3)
    job.cross_b(1)
    betweens[1]()
    betweens[3]()
    job.cross_a(2)
    job.along_z(0)
    job.cross_a(1)
    job.along_z(2)
    fourth()
    job.along_z(1)
    job.close()
    job.end()
    message()
    job.finish()
    last()


def finish_grads(ins, shapes, set_ins):
    devices = lax.axis_size(AXIS)
    wcond, d_mods = set_ins["wcond"], set_ins["d_mods"]
    cols, images = set_ins["pre"].shape
    outs = [(wcond.shape[0], devices * cols), (cols, FREQ), (cols, devices * cols), (cols, 1024)]
    vmem = pl.BlockSpec(memory_space=pltpu.VMEM)
    low = jnp.bfloat16
    return pl.pallas_call(
        functools.partial(finish_kernel, devices),
        out_shape=[jax.ShapeDtypeStruct(shape, jnp.float32) for shape in list(shapes) + outs]
        + [jax.ShapeDtypeStruct((LINE, PLANE, 32, 128), low)],
        in_specs=[pl.BlockSpec(memory_space=pl.ANY)] * 8 + [vmem] * len(SETTLE_INS),
        out_specs=[vmem] * 7,
        scratch_shapes=grad_bufs(ins)
        + scatter_scratch(piece_shapes(shapes))
        + [
            pltpu.VMEM(d_mods.shape, jnp.float32),
            pltpu.VMEM(d_mods.shape, jnp.float32),
            pltpu.VMEM((images, 384), jnp.float32),
            pltpu.VMEM((devices * 16, 128), jnp.float32),
            pltpu.VMEM((LINE, PLANE, 16, 128), low),
            pltpu.VMEM((LINE, PLANE, 16, 128), low),
            pltpu.VMEM((LINE, 16, 128), jnp.float32),
            pltpu.VMEM((LINE, 16, 128), jnp.float32),
        ]
        + [
            pltpu.VMEM((LINE, PLANE, 32, images), low),
            pltpu.VMEM((LINE, PLANE, 32, images), low),
            pltpu.VMEM((LINE, 32, images), jnp.float32),
            pltpu.VMEM((LINE, 32, images), jnp.float32),
        ]
        * 2
        + [
            pltpu.SemaphoreType.DMA((5, LINE + PLANE)),
            pltpu.SemaphoreType.DMA((5, LINE + PLANE)),
        ],
        compiler_params=pltpu.CompilerParams(collective_id=4, has_side_effects=True, vmem_limit_bytes=63 << 20),
        name="finish_grads",
    )(*ins, *(set_ins[name] for name in SETTLE_INS))

def code_table():
    quarter = MODEL_WIDTH // 4
    omega = (1.0 / 10000.0 ** (np.arange(quarter, dtype=np.float32) / np.float32(quarter))).astype(np.float32)
    angles = np.arange(GRID, dtype=np.float32)[:, None] * omega
    return np.concatenate([np.sin(angles), np.cos(angles)], 1).astype(np.float32)


def body(
    latents, targets, timesteps, labels, embed_w, embed_m, embed_v, cond_w, cond_m, cond_v, layer_input_weights, in_m,
    in_v, layer_output_weights, out_m, out_v, head_w, head_m, head_v, biases, bias_m, bias_v,
):
    devices = lax.axis_size("fsdp")
    me = lax.axis_index("fsdp")
    images = latents.shape[0]
    embed_t = embed_w.T
    cond_t = cond_w.T
    in_t = layer_input_weights.transpose(0, 2, 1)
    out_t = layer_output_weights.transpose(0, 2, 1)
    cols, cond_cols = embed_t.shape[0], cond_t.shape[0]
    time_one, time_two, patch_bias, cond_bias, block_input_bias, block_output_bias, head_bias = split_biases(biases)
    features = time_features(timesteps)
    own_patch_w = jnp.pad(embed_t[:, FREQ + MODEL_WIDTH : FREQ + MODEL_WIDTH + PD].reshape(3, 128), ((0, 1), (0, 0)))
    digits = jnp.stack([labels // 32, labels % 32], 1).astype(jnp.float32)
    digits = jnp.broadcast_to(digits[:, :, None], (images, 2, 64)).reshape(images, 128)
    note = jnp.concatenate([features[:, :128], features[:, 128:], own_patch_w, digits], 0).astype(jnp.bfloat16)
    images_all = devices * images

    def own_bias(vector, count):
        part = lax.dynamic_slice(vector, (me * count,), (count,))
        return jnp.broadcast_to(part[:, None], (count, images_all))

    own_cond_bias = lax.dynamic_slice(cond_bias, (me * cond_cols,), (cond_cols,))[None]
    first_in, first_out, mods, pre, cond, hid_all, low_all, feat_all, lab_all, notes = gather_modulate(
        [in_t, out_t],
        [note, embed_t, cond_t, own_bias(time_one, cols), own_bias(time_two, cols), own_cond_bias],
    )
    chunks = mods.reshape(devices, images, cond_cols).transpose(1, 0, 2).reshape(images, 6 * LAYERS + 2, MODEL_WIDTH)
    w_patch = notes[:, :, 8:11].reshape(MODEL_WIDTH, PD)
    head_t = head_w.T
    tokens_all = devices * images * SEQ * PO
    lat_t = latents.transpose(0, 2, 1)
    bias_rows = [block_input_bias[:, None], block_output_bias[:, None]]
    *kept0, x_mid, last_in, last_out, x = forward_gather(
        [lat_t, chunks, first_in, first_out, *bias_rows],
        [w_patch, patch_bias[None], jnp.asarray(code_table())],
        [in_t, out_t],
        1,
    )
    *kept1, upstream, d_final, head_grad, head_bias_grad, loss_part = forward_head(
        [x_mid, chunks, last_in, last_out, *bias_rows, head_t, head_bias[:, None],
         targets.transpose(0, 2, 1)],
        2.0 / tokens_all,
    )
    h1, qkv, probs, o, a, x1, h2, u, g, f = kept1
    upstream, d_qkv, d_u, d_f, d_a, mod_grad1, in_bias1, out_bias1 = backward_block(
        chunks, last_in, last_out, [upstream, x_mid, x1, probs, qkv, a, f, u]
    )
    in_shape, out_shape = in_t.shape[1:], out_t.shape[1:]
    grad_in, out_shard1 = weight_grads_out([d_qkv, h1, d_u, h2, d_a, o, d_f, g], out_shape)
    h1, qkv, probs, o, a, x1, h2, u, g, f = kept0
    (upstream, d_qkv, d_u, d_f, d_a, mod_grad0, in_bias0, out_bias0, patch_grad, patch_bias_grad, in_shard1) = backward_scatter(
        chunks, first_in, first_out, [upstream, x, x1, probs, qkv, a, f, u], grad_in, lat_t, in_shape
    )
    mod_grads, in_bias_grads, out_bias_grads = [mod_grad0, mod_grad1], [in_bias0, in_bias1], [out_bias0, out_bias1]
    d_modulation = jnp.concatenate(mod_grads + [d_final], 1)
    d_mods = d_modulation.reshape(images, devices, cond_cols).transpose(1, 0, 2)
    d_mods = d_mods.reshape(LINE, PLANE, images, cond_cols)
    in_shard0, out_shard0, g_cond, g_t1, g_t2, g_cls, merged = finish_grads(
        [d_qkv, h1, d_u, h2, d_a, o, d_f, g],
        [in_shape, out_shape],
        {
            "d_mods": d_mods, "emb": embed_t, "wcond": cond_t, "pre": pre, "cond": cond, "hid_all": hid_all, "low_all": low_all,
            "feat_all": feat_all, "lab_all": lab_all, "g_head": head_grad, "g_hbias": head_bias_grad, "loss": loss_part,
            "g_patch": patch_grad, "g_pbias": patch_bias_grad, "bin0": in_bias_grads[0], "bin1": in_bias_grads[1],
            "bout0": out_bias_grads[0], "bout1": out_bias_grads[1], "done_in": in_shard1, "done_out": out_shard1,
        },
    )
    merged = merged.astype(jnp.float32).reshape(devices, 32, 128)
    wide = MODEL_WIDTH // 128
    blocks = merged[:, :16]
    patch_total = blocks[:wide].transpose(1, 0, 2).reshape(PD, MODEL_WIDTH)
    head_total = blocks[wide : 3 * wide].reshape(wide, PO, 128).transpose(1, 0, 2).reshape(PO, MODEL_WIDTH)
    flat = blocks[3 * wide :].reshape(-1)
    rest = LAYERS * (IW + 2 * MODEL_WIDTH) + PO
    loss_total = jnp.sum(merged[:, 19, :3])
    bias_total = jnp.concatenate(
        [merged[:, 16, :cols].reshape(-1), merged[:, 17, :cols].reshape(-1), flat[:MODEL_WIDTH],
         merged[:, 20:23].reshape(devices, 384)[:, :cond_cols].reshape(-1), flat[MODEL_WIDTH : MODEL_WIDTH + rest]]
    )
    grad_norm = jnp.sqrt(
        jnp.sum(merged[:, 18, :3])
        + jnp.sum(head_total * head_total)
        + jnp.sum(patch_total * patch_total)
        + jnp.sum(bias_total * bias_total)
    )
    factor = jnp.minimum(1.0, clip_limit / grad_norm)
    own_patch = lax.dynamic_slice(patch_total, (0, me * cols), (PD, cols)).T
    embed_grad = jnp.concatenate([g_t1, g_t2, own_patch, g_cls[:, PD : PD + NCLS]], 1)
    embed_up = [a.T for a in adam_step(embed_t, embed_m.T, embed_v.T, embed_grad * factor)]
    cond_up = [a.T for a in adam_step(cond_t, cond_m.T, cond_v.T, g_cond * factor)]
    turn = (0, 2, 1)
    in_up = [
        a.transpose(turn)
        for a in adam_step(in_t, in_m.transpose(turn), in_v.transpose(turn), jnp.stack([in_shard0, in_shard1]) * factor)
    ]
    out_up = [
        a.transpose(turn)
        for a in adam_step(out_t, out_m.transpose(turn), out_v.transpose(turn), jnp.stack([out_shard0, out_shard1]) * factor)
    ]
    head_up = [a.T for a in adam_step(head_t, head_m.T, head_v.T, head_total * factor)]
    bias_up = adam_step(biases, bias_m, bias_v, bias_total * factor)
    return (loss_total, grad_norm, *embed_up, *cond_up, *in_up, *out_up, *head_up, *bias_up)


def fits(mesh):
    return mesh.shape["fsdp"] == 32


def solution(mesh):
    in_specs = (
        P("fsdp", None, None),
        P("fsdp", None, None),
        P("fsdp"),
        P("fsdp"),
        P(None, "fsdp"),
        P(None, "fsdp"),
        P(None, "fsdp"),
        P(None, "fsdp"),
        P(None, "fsdp"),
        P(None, "fsdp"),
        P(None, None, "fsdp"),
        P(None, None, "fsdp"),
        P(None, None, "fsdp"),
        P(None, None, "fsdp"),
        P(None, None, "fsdp"),
        P(None, None, "fsdp"),
        P(),
        P(),
        P(),
        P(),
        P(),
        P(),
    )
    out_specs = (
        P(),
        P(),
        P(None, "fsdp"),
        P(None, "fsdp"),
        P(None, "fsdp"),
        P(None, "fsdp"),
        P(None, "fsdp"),
        P(None, "fsdp"),
        P(None, None, "fsdp"),
        P(None, None, "fsdp"),
        P(None, None, "fsdp"),
        P(None, None, "fsdp"),
        P(None, None, "fsdp"),
        P(None, None, "fsdp"),
        P(),
        P(),
        P(),
        P(),
        P(),
        P(),
    )
    chosen = body if fits(mesh) else generic_body
    return jax.shard_map(chosen, mesh=mesh, in_specs=in_specs, out_specs=out_specs, check_vma=False)
```
